32 devices in a mesh: dp: 8 (over y, x, core), tensor: 4 (over z).
Axes of the slice: x: 2, y: 2, z: 4, core: 2. Of those that a mesh axis runs over, the one named last changes fastest.
Arguments:
- tokens: bfloat16 [12288, 2560], P(('dp', 'tensor')), may hold values from -6 to 6
- attention_gain: bfloat16 [2560], P('dp'), may hold values from 0.25 to 1.75
- query_weight: bfloat16 [2560, 2560], P('dp', 'tensor'), may hold values from -0.125 to 0.125
- key_weight: bfloat16 [2560, 640], P('dp', 'tensor'), may hold values from -0.125 to 0.125
- value_weight: bfloat16 [2560, 640], P('dp', 'tensor'), may hold values from -0.125 to 0.125
- output_weight: bfloat16 [2560, 2560], P('tensor', 'dp'), may hold values from -1.25 to 1.25
- feedforward_gain: bfloat16 [2560], P('dp'), may hold values from 0.25 to 1.75
- gate_weight: bfloat16 [2560, 6912], P('dp', 'tensor'), may hold values from -0.125 to 0.125
- up_weight: bfloat16 [2560, 6912], P('dp', 'tensor'), may hold values from -0.125 to 0.125
- down_weight: bfloat16 [6912, 2560], P('tensor', 'dp'), may hold values from -0.15625 to 0.15625
- cotangent: bfloat16 [12288, 2560], P(('dp', 'tensor')), may hold values from -6 to 6
- lengths: int32 [8, 3], P('dp'), may hold values from 1 to 1024, 1536 in all within a row
- storage_order: int32 [12288], P('dp'), may hold values from 0 to 1535, as said below
- sequence_order: int32 [12288], P('dp'), may hold values from 0 to 1535, as said below
- pad_mask: int32 [12288], P('dp'), may hold values 0 or 1
Outputs:
- layer_output: float32 [12288, 2560], P(('dp', 'tensor'))
- input_grad: float32 [12288, 2560], P(('dp', 'tensor'))
- attention_gain_grad: float32 [2560], P('dp')
- query_weight_grad: float32 [2560, 2560], P('dp', 'tensor')
- key_weight_grad: float32 [2560, 640], P('dp', 'tensor')
- value_weight_grad: float32 [2560, 640], P('dp', 'tensor')
- output_weight_grad: float32 [2560, 2560], P('tensor', 'dp')
- feedforward_gain_grad: float32 [2560], P('dp')
- gate_weight_grad: float32 [2560, 6912], P('dp', 'tensor')
- up_weight_grad: float32 [2560, 6912], P('dp', 'tensor')
- down_weight_grad: float32 [6912, 2560], P('tensor', 'dp')
The draws below stay inside these ranges and needn't reach their ends.
Inputs may be any that keep to these rules, and one draw needn't show every extreme that they name: Each group's 3 lengths add up to 1536, and the longest is 1024. `storage_order`: each group's 1536 entries are a permutation of its sequence positions. `sequence_order`: each group's 1536 entries are the inverse of that group's storage_order.
All inputs are finite; a program needn't handle non-finite values. No bound on the sum of `pad_mask` on one device may be relied on, other than what follows from the above.
Results may differ from the reference program's by a relative error of at most 0.02.
Values may be sent and summed in bfloat16 or wider, within the bound.
A program may use at most 320 MiB of HBM per device.

```python
import math
import jax
import jax.numpy as jnp
import numpy as np
from jax import lax

D = 2560
HEADS = 32
KV_HEADS = 8
HEAD_DIM = 80
FF = 6912
TOK_G = 1536
SEQ_MAX = 1024
NSEQ = 3
GROUPS = 8
TOKENS = 12288


def draw_orders(key):
    group_keys = jax.random.split(key, GROUPS)

    def one_order(group_key):
        return jax.random.permutation(group_key, TOK_G)
    return jax.vmap(one_order)(group_keys).astype(jnp.int32)


def draw_storage_order(key, part):
    orders = draw_orders(key)
    return orders.reshape(GROUPS * TOK_G)


def draw_sequence_order(key, part):
    orders = draw_orders(key)
    return jnp.argsort(orders, axis=1, stable=True).astype(jnp.int32).reshape(GROUPS * TOK_G)


def touch_ends(result, rng, least, largest):
    index_at = [jax.random.randint(jax.random.fold_in(rng, axis), (), 0, length) for axis, length in enumerate(result.shape)]
    main_axis = result.shape.index(max(result.shape))
    beside = index_at[:main_axis] + [(index_at[main_axis] + 1) % result.shape[main_axis]] + index_at[main_axis + 1:]
    return result.at[tuple(index_at)].set(least).at[tuple(beside)].set(largest)


def spiked(entries, key, source, target, parts, factor):
    def block_of(axis_at):
        return (jnp.arange(entries.shape[axis_at]) // (entries.shape[axis_at] // parts)).reshape((-1,) + (1,) * (entries.ndim - 1 - axis_at))

    near = jax.random.permutation(key, parts)[block_of(target)]
    other_side = (block_of(target) + parts // 2) % parts
    return jnp.where((block_of(source) == near) | (block_of(source) == other_side), factor * entries, entries)


def block_levels(key, dims, cuts, smallest, high):
    def one(dim, parts):
        draws = jax.random.uniform(jax.random.fold_in(jax.random.fold_in(key, 6), dim), (parts,), jnp.float32, smallest / len(cuts), high / len(cuts))
        return jnp.repeat(jnp.exp(draws), dims[dim] // parts).reshape((-1,) + (1,) * (len(dims) - dim - 1))

    factor_of = one(*cuts[0])
    for cut in cuts[1:]:
        factor_of = factor_of * one(*cut)
    return factor_of


def length_profile(number_of, total, reach, skew):
    weights = [(1 << 20) // math.isqrt(rank ** skew) + 1 for rank in range(2, number_of + 1)]
    spare, counts = total - reach - (number_of - 1), [1] * (number_of - 1)
    while spare > 0:
        free = [i for i in range(number_of - 1) if counts[i] < reach]
        whole, remaining = sum([weights[i] for i in free]), spare
        for i in free:
            addition = min(reach - counts[i], max(1, remaining * weights[i] // whole), spare)
            counts[i] = counts[i] + addition
            spare = spare - addition
    return np.array([reach] + counts)


def uneven_parts(rng, number_of, total, bound, slope):
    if number_of == 2:
        one = jax.random.randint(rng, (), max(1, total - bound), min(bound, total - 1) + 1)
        return jnp.stack([one, total - one])
    sizes = jnp.asarray(length_profile(number_of, total, bound, slope), jnp.int32)
    couples = (number_of - 1) // 2
    donor, taker = sizes[1:1 + 2 * couples:2], sizes[2:2 + 2 * couples:2]
    slack = jnp.minimum(donor - 1, bound - taker)
    shifted = jax.random.randint(jax.random.fold_in(rng, 1), (couples,), 0, 1 << 20) % (slack + 1)
    sizes = sizes.at[1:1 + 2 * couples:2].set(donor - shifted).at[2:2 + 2 * couples:2].set(taker + shifted)
    return sizes[jax.random.permutation(jax.random.fold_in(rng, 2), number_of)]


def normal_values(key, shape, deviation, bound, pieces=(), kind=jnp.bfloat16):
    entries = jax.random.normal(key, shape, jnp.float32) * deviation
    if len(pieces) > 0:
        entries = block_levels(key, shape, pieces, -0.22, 0.18) * entries
    return jnp.clip(entries, min=-bound, max=bound).astype(kind)


def gaussian_with(rng, extent, width, reach, cuts, heavy, kind=jnp.bfloat16):
    entries = width * jax.random.normal(rng, extent, jnp.float32)
    if cuts:
        entries = entries * block_levels(rng, extent, cuts, -0.22, 0.18)
    return jnp.clip(spiked(entries, jax.random.fold_in(rng, 3), *heavy), -reach, reach).astype(kind)


def setup_inputs(seed: int = 0) -> dict:
    streams_of = jax.random.split(jax.random.key(seed), 16)
    tokens = normal_values(streams_of[0], (TOKENS, D), 1.0, 6.0, ((0, 32),))
    attention_gain = jnp.clip(1.0 + 0.15 * jax.random.normal(streams_of[1], (D,), jnp.float32), 0.25, 1.75).astype(jnp.bfloat16)
    query_weight = normal_values(streams_of[2], (D, HEADS * HEAD_DIM), D ** -0.5, 0.125, ((0, 8), (1, 4)))
    key_weight = normal_values(streams_of[3], (D, KV_HEADS * HEAD_DIM), D ** -0.5, 0.125, ((0, 8), (1, 4)))
    value_weight = normal_values(streams_of[4], (D, KV_HEADS * HEAD_DIM), D ** -0.5, 0.125, ((0, 8), (1, 4)))
    output_weight = normal_values(streams_of[5], (HEADS * HEAD_DIM, D), (max(D // 128, 8)) ** -0.5, 1.25, ((0, 4), (1, 8)))
    feedforward_gain = jnp.clip(1.0 + 0.15 * jax.random.normal(streams_of[6], (D,), jnp.float32), 0.25, 1.75).astype(jnp.bfloat16)
    gate_weight = normal_values(streams_of[7], (D, FF), D ** -0.5, 0.125, ((0, 8), (1, 4)))
    up_weight = normal_values(streams_of[8], (D, FF), D ** -0.5, 0.125, ((0, 8), (1, 4)))
    down_weight = normal_values(streams_of[9], (FF, D), (FF // 4) ** -0.5, 0.15625, ((0, 4), (1, 8)))
    cotangent = gaussian_with(streams_of[10], (TOKENS, D), 1.0, 6.0, ((0, 32),), (0, 1, 32, 2.75))
    lengths = jax.vmap(lambda own: uneven_parts(own, NSEQ, TOK_G, SEQ_MAX, 2))(jax.random.split(streams_of[11], GROUPS)).reshape((GROUPS, NSEQ)).astype(jnp.int32)
    storage_order = draw_storage_order(jax.random.fold_in(streams_of[15], 71), 0)
    sequence_order = draw_sequence_order(jax.random.fold_in(streams_of[15], 71), 0)
    pad_mask = touch_ends((jax.random.randint(streams_of[14], (TOKENS,), 0, 8) < 7).astype(jnp.int32), jax.random.fold_in(streams_of[14], 1), 0, 1)
    return dict(tokens=tokens, attention_gain=attention_gain, query_weight=query_weight, key_weight=key_weight, value_weight=value_weight, output_weight=output_weight, feedforward_gain=feedforward_gain, gate_weight=gate_weight, up_weight=up_weight, down_weight=down_weight, cotangent=cotangent, lengths=lengths, storage_order=storage_order, sequence_order=sequence_order, pad_mask=pad_mask)


@jax.custom_vjp
def low(v):
    return lax.optimization_barrier(v.astype(jnp.bfloat16)).astype(jnp.float32)

@jax.custom_vjp
def low_back(v):
    return v

def low_keep(v):
    return (low(v), None)

def low_pass(kept, grad):
    return (grad,)

def back_keep(v):
    return (v, None)

def back_low(kept, grad):
    return (low(grad),)
low.defvjp(low_keep, low_pass)
low_back.defvjp(back_keep, back_low)
highest = lax.Precision.HIGHEST
epsilon = 1e-05
rope_base = 10000.0

def product(left, right):
    return jnp.dot(left, right, precision=highest, preferred_element_type=jnp.float32)

def inverse_root(vectors):
    return lax.rsqrt(lax.optimization_barrier(jnp.mean(vectors * vectors, axis=-1, keepdims=True)) + epsilon)

def sequence_layout(length_row, token_count):
    sequence_ends = jnp.cumsum(length_row).astype(jnp.int32)
    sequence_starts = sequence_ends - length_row
    places = jnp.arange(token_count, dtype=jnp.int32)
    members = lax.optimization_barrier(jnp.sum((places[:, None] >= sequence_ends[None, :]).astype(jnp.int32), axis=1))
    chosen = members[:, None] == jnp.arange(length_row.shape[0], dtype=jnp.int32)[None, :]
    first_place = lax.optimization_barrier(jnp.sum(jnp.where(chosen, sequence_starts[None, :], 0), axis=1))
    return (members, places - first_place)

def rotary_tables(positions, head_width):
    half_width = head_width // 2
    frequency = jnp.exp(jnp.arange(half_width, dtype=jnp.float32) * (-2.0 * math.log(rope_base) / head_width))
    angles = positions.astype(jnp.float32)[:, None] * frequency[None, :]
    return (jnp.cos(angles), jnp.sin(angles))

def rotate(vectors, cosine_table, sine_table):
    half_width = vectors.shape[-1] // 2
    leading = vectors[..., :half_width]
    trailing = vectors[..., half_width:]
    cosine = cosine_table[:, None, :]
    sine_part = sine_table[:, None, :]
    return jnp.concatenate([leading * cosine - trailing * sine_part, trailing * cosine + leading * sine_part], axis=-1)

def attend_group(query_heads, key_heads, value_heads, members, pad_keys):
    token_count = query_heads.shape[0]
    block_rows = math.gcd(token_count, 512)
    head_group = query_heads.shape[1] // key_heads.shape[1]
    wide_keys = jnp.repeat(key_heads, head_group, axis=1)
    wide_values = jnp.repeat(value_heads, head_group, axis=1)
    columns = jnp.arange(token_count, dtype=jnp.int32)
    score_scale = 1.0 / math.sqrt(query_heads.shape[2])

    def one_block(block_start):
        row_index = block_start + jnp.arange(block_rows, dtype=jnp.int32)
        query_block = lax.dynamic_slice_in_dim(query_heads, block_start, block_rows, 0)
        owners = lax.dynamic_slice_in_dim(members, block_start, block_rows, 0)
        allowed = (owners[:, None] == members[None, :]) & (columns[None, :] <= row_index[:, None]) & ((pad_keys[None, :] == 1) | (columns[None, :] == row_index[:, None]))
        scores = low_back(jnp.einsum('qhe,khe->hqk', query_block, wide_keys, precision=highest) * score_scale)
        scores = jnp.where(allowed[None], scores, -1e+30)
        row_top = lax.optimization_barrier(jnp.max(scores, axis=-1, keepdims=True))
        exponent = jnp.exp(scores - row_top)
        probability = exponent / lax.optimization_barrier(jnp.sum(exponent, axis=-1, keepdims=True))
        return jnp.einsum('hqk,khe->qhe', low(probability), wide_values, precision=highest)
    block_starts = jnp.arange(token_count // block_rows, dtype=jnp.int32) * block_rows
    results = lax.map(jax.checkpoint(one_block), block_starts)
    return results.reshape(query_heads.shape)

def layer(tokens, attention_gain, query_weight, key_weight, value_weight, output_weight, feedforward_gain, gate_weight, up_weight, down_weight, members, cosine_table, sine_table, sequence_rows, storage_rows, pad_keys):
    normed = low(tokens * inverse_root(tokens) * attention_gain)
    query_rows = low_back(product(normed, query_weight))
    key_rows = low_back(product(normed, key_weight))
    value_rows = low_back(product(normed, value_weight))

    def to_heads(vectors):
        return vectors[sequence_rows].reshape(GROUPS * TOK_G, -1, HEAD_DIM)

    def by_group(vectors):
        return vectors.reshape(GROUPS, TOK_G, vectors.shape[1], HEAD_DIM)
    query_heads = low(rotate(to_heads(query_rows), cosine_table, sine_table))
    key_heads = low(rotate(to_heads(key_rows), cosine_table, sine_table))
    value_heads = low(to_heads(value_rows))

    def attend_item(group_item):
        return attend_group(*group_item)
    attended = lax.map(attend_item, (by_group(query_heads), by_group(key_heads), by_group(value_heads), members, pad_keys))
    attended = low(low_back(attended.reshape(GROUPS * TOK_G, HEADS * HEAD_DIM)))
    attention_out = low_back(product(attended[storage_rows], output_weight))
    residual = tokens + attention_out
    normed_ffn = low(residual * inverse_root(residual) * feedforward_gain)
    gate_values = low_back(product(normed_ffn, gate_weight))
    up_values = low_back(product(normed_ffn, up_weight))
    hidden = low(gate_values * jax.nn.sigmoid(gate_values) * up_values)
    return residual + low_back(product(hidden, down_weight))

def reference(tokens, attention_gain, query_weight, key_weight, value_weight, output_weight, feedforward_gain, gate_weight, up_weight, down_weight, cotangent, lengths, storage_order, sequence_order, pad_mask):

    def layout_row(length_row):
        return sequence_layout(length_row, TOK_G)
    members, positions = jax.vmap(layout_row)(lengths)
    cosine_table, sine_table = rotary_tables(positions.reshape(GROUPS * TOK_G), HEAD_DIM)
    offsets = jnp.arange(GROUPS * TOK_G, dtype=jnp.int32) // TOK_G * TOK_G
    sequence_rows = (sequence_order + offsets).astype(jnp.int32)
    storage_rows = (storage_order + offsets).astype(jnp.int32)
    pad_keys = pad_mask.reshape(GROUPS, TOK_G)
    float_args = tuple((item.astype(jnp.float32) for item in (tokens, attention_gain, query_weight, key_weight, value_weight, output_weight, feedforward_gain, gate_weight, up_weight, down_weight)))

    def forward(*weights_in):
        return layer(*weights_in, members, cosine_table, sine_table, sequence_rows, storage_rows, pad_keys)
    layer_out, pullback = jax.vjp(forward, *float_args)
    gradients = pullback(cotangent.astype(jnp.float32))
    return (layer_out, gradients[0], gradients[1], gradients[2], gradients[3], gradients[4], gradients[5], gradients[6], gradients[7], gradients[8], gradients[9])
```

```python
import functools
import math

import jax
import jax.numpy as jnp
from jax import lax
from jax.experimental import pallas as pl
from jax.experimental.pallas import tpu as pltpu
from jax.sharding import PartitionSpec as P

HEAD_DIM = 80
HALF = HEAD_DIM // 2
QUERY_BLOCK = 128
KEY_BLOCK = 256
MASKED = -1e30
VMEM_LIMIT = 48 * 1024 * 1024

epsilon = 1e-05
rope_base = 10000.0
AXES = ("dp", "tensor")


def contract(left, right, left_dim, right_dim, out_type=jnp.float32):
    product = lax.dot_general(
        left,
        right,
        (((left_dim,), (right_dim,)), ((), ())),
        preferred_element_type=jnp.float32,
    )
    return product.astype(out_type)


def inverse_root(vectors):
    return lax.rsqrt(jnp.mean(vectors * vectors, axis=-1, keepdims=True) + epsilon)


class Placement:
    def __init__(self, dp_count, tensor_count):
        self.dp_count = dp_count
        self.tensor_count = tensor_count
        self.chips = dp_count // 2
        self.low = tensor_count // 2
        dp_index = lax.axis_index("dp")
        tensor_index = lax.axis_index("tensor")
        self.p = dp_index // 2
        self.c = dp_index % 2
        self.th = tensor_index // self.low
        self.tl = tensor_index % self.low
        self.home = self.c == self.th

    def move(self, array, target):
        pairs = []
        for p in range(self.chips):
            for c in range(2):
                for th in range(2):
                    for tl in range(self.low):
                        goal = target(p, c, th, tl)
                        if goal is not None:
                            pairs.append((self.flat(p, c, th, tl), self.flat(*goal)))
        return lax.ppermute(array, AXES, pairs)

    def flat(self, p, c, th, tl):
        return (2 * p + c) * self.tensor_count + th * self.low + tl

    def to_core(self, array):
        return self.move(array, lambda p, c, th, tl: (p, 1 - c, th, tl))

    def to_chip(self, array, step):
        return self.move(array, lambda p, c, th, tl: (p ^ step, c, th, tl))

    def to_low(self, array, step):
        return self.move(array, lambda p, c, th, tl: (p, c, th, (tl + step) % self.low))

    def cross(self, array):
        return self.move(
            array, lambda p, c, th, tl: (p, 1 - c, 1 - th, tl) if c != th else None
        )

    def home_turn(self, array):
        return self.move(
            array, lambda p, c, th, tl: (p, c, 1 - th, tl) if c == th else (p, 1 - c, th, tl)
        )

    def away_turn(self, array):
        return self.move(
            array, lambda p, c, th, tl: (p, 1 - c, th, tl) if c == th else (p, c, 1 - th, tl)
        )

    def swap(self, array):
        return jnp.where(self.home, array, self.cross(array))

    def relative_features(self, array):
        width = array.shape[-1] // self.chips
        return jnp.concatenate(
            [
                lax.dynamic_slice_in_dim(array, (self.p ^ step) * width, width, array.ndim - 1)
                for step in range(self.chips)
            ],
            axis=-1,
        )

    def gather_rows(self, own):
        same = [own] + [self.to_low(own, self.low - step) for step in range(1, self.low)]
        blocks = []
        for block in same:
            blocks.append(block)
            blocks.append(self.to_core(block))
        return blocks

    def scatter_rows(self, blocks):
        total = None
        for step in list(range(1, self.low)) + [0]:
            mine, others = blocks[2 * step], blocks[2 * step + 1]
            pair = mine.astype(jnp.float32) + self.to_core(others).astype(jnp.float32)
            if step:
                pair = self.to_low(pair.astype(jnp.bfloat16), step).astype(jnp.float32)
            total = pair if total is None else total + pair
        return total

    def gather_weight(self, shard):
        turned = self.home_turn(shard)
        crossed = self.cross(shard)
        mine = jnp.where(self.home, shard, turned)
        other = jnp.where(self.home, turned, crossed)
        first = jnp.where(self.c == 0, mine, other)
        second = jnp.where(self.c == 0, other, mine)
        if self.chips == 4:
            units = [[first, second], None, None, None]
            unit = jnp.stack([first, second])
            by_x = self.to_chip(unit, 1)
            by_y = self.to_chip(unit, 2)
            diagonal_first = self.to_chip(by_y[0], 1)
            diagonal_second = self.to_chip(by_x[1], 2)
            units = [first, second, by_x[0], by_x[1], by_y[0], by_y[1], diagonal_first, diagonal_second]
        else:
            unit = jnp.stack([first, second])
            units = [first, second]
            for step in range(1, self.chips):
                arrived = self.to_chip(unit, step)
                units += [arrived[0], arrived[1]]
        return jnp.concatenate(units, axis=0)

    def scatter_weight(self, partial):
        rows = partial.shape[0] // self.dp_count
        units = partial.reshape(self.chips, 2, rows, partial.shape[1])

        def low(value):
            return value.astype(jnp.bfloat16)

        def wide(value):
            return value.astype(jnp.float32)

        if self.chips == 4:
            by_x = self.to_chip(units[3, 0], 1)
            by_y = self.to_chip(units[3, 1], 2)
            unit_x = jnp.stack([units[1, 0], low(wide(units[1, 1]) + wide(by_y))])
            unit_y = jnp.stack([low(wide(units[2, 0]) + wide(by_x)), units[2, 1]])
            total = (
                wide(units[0])
                + wide(self.to_chip(unit_x, 1))
                + wide(self.to_chip(unit_y, 2))
            )
        else:
            total = wide(units[0])
            for step in range(1, self.chips):
                total = total + wide(self.to_chip(units[step], step))
        mine = jnp.where(self.c == 0, total[0], total[1])
        other = jnp.where(self.c == 0, total[1], total[0])
        turned = self.away_turn(low(jnp.where(self.home, other, mine)))
        crossed = self.cross(low(other))
        return jnp.where(self.home, mine, wide(crossed)) + wide(turned)

    def sum_tensor(self, array):
        for bit in range(self.tensor_count.bit_length() - 1):
            step = 1 << bit

            def target(p, c, th, tl, step=step):
                moved = (th * self.low + tl) ^ step
                return (p, c, moved // self.low, moved % self.low)

            array = array + self.move(array, target)
        return array


def project_kernel(heads, tokens_ref, gain_ref, weight_ref, cosine_ref, sine_ref, normed_ref, out_ref):
    tokens = tokens_ref[...].astype(jnp.float32)
    root = lax.rsqrt(jnp.mean(tokens * tokens, axis=-1, keepdims=True) + epsilon)
    normed = (tokens * root * gain_ref[...]).astype(jnp.bfloat16)
    normed_ref[...] = normed
    rows = jnp.dot(normed, weight_ref[...], preferred_element_type=jnp.float32)
    cosine, sine = cosine_ref[...], sine_ref[...]
    pieces = []
    for head in range(heads):
        leading = rows[:, head * HEAD_DIM : head * HEAD_DIM + HALF]
        trailing = rows[:, head * HEAD_DIM + HALF : (head + 1) * HEAD_DIM]
        pieces.append(leading * cosine - trailing * sine)
        pieces.append(trailing * cosine + leading * sine)
    pieces.append(rows[:, heads * HEAD_DIM : out_ref.shape[1]])
    out_ref[...] = jnp.concatenate(pieces, axis=1).astype(jnp.bfloat16)


def project(tokens, gain, weight, cosine, sine, rotated_heads, out_columns):
    count, width = tokens.shape
    block = math.gcd(count, 256)
    return pl.pallas_call(
        functools.partial(project_kernel, rotated_heads),
        grid=(count // block,),
        in_specs=[
            pl.BlockSpec((block, width), lambda i: (i, 0)),
            pl.BlockSpec((1, width), lambda i: (0, 0)),
            pl.BlockSpec(weight.shape, lambda i: (0, 0)),
            pl.BlockSpec((block, HALF), lambda i: (i, 0)),
            pl.BlockSpec((block, HALF), lambda i: (i, 0)),
        ],
        out_specs=[
            pl.BlockSpec((block, width), lambda i: (i, 0)),
            pl.BlockSpec((block, out_columns), lambda i: (i, 0)),
        ],
        out_shape=[
            jax.ShapeDtypeStruct((count, width), jnp.bfloat16),
            jax.ShapeDtypeStruct((count, out_columns), jnp.bfloat16),
        ],
        compiler_params=pltpu.CompilerParams(vmem_limit_bytes=VMEM_LIMIT),
        cost_estimate=pl.CostEstimate(
            flops=2 * count * width * weight.shape[1],
            bytes_accessed=4 * count * width + 2 * weight.size,
            transcendentals=0,
        ),
        name="project",
    )(tokens, gain, weight, cosine, sine)


def block_bias(key_start, query_start, start_row, pad_column):
    shape = (pad_column.shape[0], start_row.shape[1])
    keys = key_start + lax.broadcasted_iota(jnp.int32, shape, 0)
    queries = query_start + lax.broadcasted_iota(jnp.int32, shape, 1)
    allowed = ((keys >= start_row) & (keys <= queries) & (pad_column == 1)) | (keys == queries)
    return jnp.where(allowed, 0.0, MASKED)


def stack_heads(rows, first, group):
    return jnp.concatenate(
        [rows[:, (first + g) * HEAD_DIM : (first + g + 1) * HEAD_DIM] for g in range(group)], axis=0
    )


def times(left, right, left_dim, right_dim):
    return lax.dot_general(
        left, right, (((left_dim,), (right_dim,)), ((), ())), preferred_element_type=jnp.float32
    )


def attend_kernel(
    kv_heads, group, first_ref, query_ref, all_ref, start_ref, pad_ref, out_ref, total_ref, key_heads, value_turned
):
    step = pl.program_id(0)
    heads = kv_heads * group
    query_rows = query_ref.shape[0]
    scale = 1.0 / math.sqrt(HEAD_DIM)

    @pl.when(step == 0)
    def _():
        for k in range(kv_heads):
            at = (heads + k) * HEAD_DIM
            key_heads[k] = all_ref[:, at : at + HEAD_DIM]
            at = (heads + kv_heads + k) * HEAD_DIM
            value_turned[k] = all_ref[:, at : at + HEAD_DIM].astype(jnp.float32).T.astype(jnp.bfloat16)

    query_start = step * query_rows
    last = (query_start + query_rows - 1) // KEY_BLOCK + 1
    pieces = []
    for k in range(kv_heads):
        queries = stack_heads(query_ref[:, : heads * HEAD_DIM], k * group, group)

        def body(block, carry, k=k, queries=queries):
            top, total, mixed = carry
            at = pl.multiple_of(block * KEY_BLOCK, KEY_BLOCK)
            bias = block_bias(at, query_start, start_ref[...], pad_ref[pl.ds(at, KEY_BLOCK), :])
            bias = jnp.concatenate([bias] * group, axis=1)
            scores = times(key_heads[k, pl.ds(at, KEY_BLOCK), :], queries, 1, 1) * scale + bias
            new_top = jnp.maximum(top, jnp.max(scores, axis=0, keepdims=True))
            weight = jnp.exp(scores - new_top)
            shrink = jnp.exp(top - new_top)
            total = total * shrink + jnp.sum(weight, axis=0, keepdims=True)
            mixed = mixed * shrink + times(
                value_turned[k, :, pl.ds(at, KEY_BLOCK)], weight.astype(jnp.bfloat16), 1, 0
            )
            return new_top, total, mixed

        columns = group * query_rows
        top, total, mixed = lax.fori_loop(
            first_ref[step],
            last,
            body,
            (
                jnp.full((1, columns), MASKED, jnp.float32),
                jnp.zeros((1, columns), jnp.float32),
                jnp.zeros((HEAD_DIM, columns), jnp.float32),
            ),
        )
        mixed = mixed / total
        log_total = top + jnp.log(total)
        for g in range(group):
            span = slice(g * query_rows, (g + 1) * query_rows)
            pieces.append(mixed[:, span].T)
            total_ref[k * group + g : k * group + g + 1, :] = log_total[:, span]
    out_ref[...] = jnp.concatenate(pieces, axis=1).astype(jnp.bfloat16)


def attend(first, heads_all, start_row, pad_column, kv_heads, group):
    count, columns = heads_all.shape
    heads = kv_heads * group
    block = math.gcd(count, QUERY_BLOCK)
    return pl.pallas_call(
        functools.partial(attend_kernel, kv_heads, group),
        grid_spec=pltpu.PrefetchScalarGridSpec(
            num_scalar_prefetch=1,
            grid=(count // block,),
            in_specs=[
                pl.BlockSpec((block, columns), lambda i, first: (i, 0)),
                pl.BlockSpec((count, columns), lambda i, first: (0, 0)),
                pl.BlockSpec((1, block), lambda i, first: (0, i)),
                pl.BlockSpec((count, 1), lambda i, first: (0, 0)),
            ],
            out_specs=[
                pl.BlockSpec((block, heads * HEAD_DIM), lambda i, first: (i, 0)),
                pl.BlockSpec((heads, block), lambda i, first: (0, i)),
            ],
            scratch_shapes=[
                pltpu.VMEM((kv_heads, count, HEAD_DIM), jnp.bfloat16),
                pltpu.VMEM((kv_heads, HEAD_DIM, count), jnp.bfloat16),
            ],
        ),
        out_shape=[
            jax.ShapeDtypeStruct((count, heads * HEAD_DIM), jnp.bfloat16),
            jax.ShapeDtypeStruct((heads, count), jnp.float32),
        ],
        compiler_params=pltpu.CompilerParams(vmem_limit_bytes=VMEM_LIMIT),
        cost_estimate=pl.CostEstimate(
            flops=60 * 10**9, bytes_accessed=count * columns * 4, transcendentals=0
        ),
        name="attend",
    )(first, heads_all, heads_all, start_row, pad_column)


def attend_back_kernel(
    kv_heads,
    group,
    first_ref,
    query_ref,
    all_ref,
    start_ref,
    pad_ref,
    total_ref,
    attended_ref,
    grad_ref,
    cosine_turned_ref,
    sine_turned_ref,
    cosine_ref,
    sine_ref,
    grad_query_ref,
    grad_rest_ref,
    key_heads,
    value_heads,
    key_turned,
    grad_keys,
    grad_values,
):
    step = pl.program_id(0)
    heads = kv_heads * group
    query_rows = query_ref.shape[0]
    scale = 1.0 / math.sqrt(HEAD_DIM)

    @pl.when(step == 0)
    def _():
        for k in range(kv_heads):
            at = (heads + k) * HEAD_DIM
            keys = all_ref[:, at : at + HEAD_DIM]
            key_heads[k] = keys
            key_turned[k] = keys.astype(jnp.float32).T.astype(jnp.bfloat16)
            at = (heads + kv_heads + k) * HEAD_DIM
            value_heads[k] = all_ref[:, at : at + HEAD_DIM]
        grad_keys[...] = jnp.zeros_like(grad_keys)
        grad_values[...] = jnp.zeros_like(grad_values)

    query_start = step * query_rows
    last = (query_start + query_rows - 1) // KEY_BLOCK + 1
    cosine = cosine_turned_ref[...]
    sine = sine_turned_ref[...]
    pieces = []
    for k in range(kv_heads):
        queries = stack_heads(query_ref[:, : heads * HEAD_DIM], k * group, group)
        grads = stack_heads(grad_ref[...], k * group, group)
        attended = stack_heads(attended_ref[...], k * group, group)
        inner = jnp.sum(
            (grads.astype(jnp.float32) * attended.astype(jnp.float32)).T, axis=0, keepdims=True
        )
        log_total = jnp.concatenate(
            [total_ref[k * group + g : k * group + g + 1, :] for g in range(group)], axis=1
        )

        def body(block, turned, k=k, queries=queries, grads=grads, inner=inner, log_total=log_total):
            at = pl.multiple_of(block * KEY_BLOCK, KEY_BLOCK)
            span = pl.ds(at, KEY_BLOCK)
            bias = block_bias(at, query_start, start_ref[...], pad_ref[span, :])
            bias = jnp.concatenate([bias] * group, axis=1)
            scores = times(key_heads[k, span, :], queries, 1, 1) * scale + bias
            weight = jnp.exp(scores - log_total)
            grad_weight = times(value_heads[k, span, :], grads, 1, 1)
            grad_scores = (weight * (grad_weight - inner)).astype(jnp.bfloat16)
            grad_values[k, span, :] += times(weight.astype(jnp.bfloat16), grads, 1, 0)
            grad_keys[k, span, :] += times(grad_scores, queries, 1, 0)
            return turned + times(key_turned[k, :, span], grad_scores, 1, 0)

        turned = lax.fori_loop(
            first_ref[step], last, body, jnp.zeros((HEAD_DIM, group * query_rows), jnp.float32)
        )
        turned = turned * scale
        for g in range(group):
            part = turned[:, g * query_rows : (g + 1) * query_rows]
            leading, trailing = part[:HALF], part[HALF:]
            back = jnp.concatenate(
                [leading * cosine + trailing * sine, trailing * cosine - leading * sine], axis=0
            )
            pieces.append(back.T)
    grad_query_ref[...] = jnp.concatenate(pieces, axis=1).astype(jnp.bfloat16)

    @pl.when(step == pl.num_programs(0) - 1)
    def _():
        rest = []
        for k in range(kv_heads):
            leading = grad_keys[k][:, :HALF] * scale
            trailing = grad_keys[k][:, HALF:] * scale
            rest.append(leading * cosine_ref[...] + trailing * sine_ref[...])
            rest.append(trailing * cosine_ref[...] - leading * sine_ref[...])
        for k in range(kv_heads):
            rest.append(grad_values[k])
        grad_rest_ref[...] = jnp.concatenate(rest, axis=1).astype(jnp.bfloat16)


def attend_back(
    first, heads_all, start_row, pad_column, log_totals, attended, grad_attended, cosine, sine, kv_heads, group
):
    count, columns = heads_all.shape
    heads = kv_heads * group
    block = math.gcd(count, QUERY_BLOCK)
    width = heads * HEAD_DIM
    rest = 2 * kv_heads * HEAD_DIM
    return pl.pallas_call(
        functools.partial(attend_back_kernel, kv_heads, group),
        grid_spec=pltpu.PrefetchScalarGridSpec(
            num_scalar_prefetch=1,
            grid=(count // block,),
            in_specs=[
                pl.BlockSpec((block, columns), lambda i, first: (i, 0)),
                pl.BlockSpec((count, columns), lambda i, first: (0, 0)),
                pl.BlockSpec((1, block), lambda i, first: (0, i)),
                pl.BlockSpec((count, 1), lambda i, first: (0, 0)),
                pl.BlockSpec((heads, block), lambda i, first: (0, i)),
                pl.BlockSpec((block, width), lambda i, first: (i, 0)),
                pl.BlockSpec((block, width), lambda i, first: (i, 0)),
                pl.BlockSpec((HALF, block), lambda i, first: (0, i)),
                pl.BlockSpec((HALF, block), lambda i, first: (0, i)),
                pl.BlockSpec((count, HALF), lambda i, first: (0, 0)),
                pl.BlockSpec((count, HALF), lambda i, first: (0, 0)),
            ],
            out_specs=[
                pl.BlockSpec((block, width), lambda i, first: (i, 0)),
                pl.BlockSpec((count, rest), lambda i, first: (0, 0)),
            ],
            scratch_shapes=[
                pltpu.VMEM((kv_heads, count, HEAD_DIM), jnp.bfloat16),
                pltpu.VMEM((kv_heads, count, HEAD_DIM), jnp.bfloat16),
                pltpu.VMEM((kv_heads, HEAD_DIM, count), jnp.bfloat16),
                pltpu.VMEM((kv_heads, count, HEAD_DIM), jnp.float32),
                pltpu.VMEM((kv_heads, count, HEAD_DIM), jnp.float32),
            ],
        ),
        out_shape=[
            jax.ShapeDtypeStruct((count, width), jnp.bfloat16),
            jax.ShapeDtypeStruct((count, rest), jnp.bfloat16),
        ],
        compiler_params=pltpu.CompilerParams(vmem_limit_bytes=VMEM_LIMIT),
        cost_estimate=pl.CostEstimate(
            flops=120 * 10**9, bytes_accessed=count * columns * 8, transcendentals=0
        ),
        name="attend_back",
    )(
        first,
        heads_all,
        heads_all,
        start_row,
        pad_column,
        log_totals,
        attended,
        grad_attended,
        cosine.T,
        sine.T,
        cosine,
        sine,
    )


def starts_of(positions, length_row):
    ends = jnp.cumsum(length_row)
    inside = positions[:, None] >= ends[None, :]
    return jnp.sum(jnp.where(inside, length_row[None, :], 0), axis=1)


def rotary_tables(positions):
    frequency = jnp.exp(
        jnp.arange(HALF, dtype=jnp.float32) * (-2.0 * math.log(rope_base) / HEAD_DIM)
    )
    angles = positions.astype(jnp.float32)[:, None] * frequency[None, :]
    return (jnp.cos(angles), jnp.sin(angles))


def per_device(
    dp_count,
    tensor_count,
    tokens,
    attention_gain,
    query_weight,
    key_weight,
    value_weight,
    output_weight,
    feedforward_gain,
    gate_weight,
    up_weight,
    down_weight,
    cotangent,
    lengths,
    storage_order,
    sequence_order,
    pad_mask,
):
    place = Placement(dp_count, tensor_count)
    count = storage_order.shape[0]
    rows = count // tensor_count
    kv_heads = key_weight.shape[1] // HEAD_DIM
    heads = query_weight.shape[1] // HEAD_DIM
    group = heads // kv_heads
    head_columns = (heads + 2 * kv_heads) * HEAD_DIM

    tokens_own = place.swap(place.relative_features(tokens))
    first_weight = place.gather_weight(
        jnp.concatenate(
            [query_weight, key_weight, value_weight, attention_gain[:, None], feedforward_gain[:, None]],
            axis=1,
        )
    )
    tokens_all = jnp.concatenate(place.gather_rows(tokens_own), axis=0)
    output_turned = place.gather_weight(output_weight.T)
    gate_full = place.gather_weight(gate_weight)
    up_full = place.gather_weight(up_weight)
    down_turned = place.gather_weight(down_weight.T)
    cot_own = place.swap(place.relative_features(cotangent))
    cot_all = jnp.concatenate(place.gather_rows(cot_own), axis=0)

    numbers = jnp.concatenate([storage_order, pad_mask, lengths[0]])
    numbers = jnp.where(place.home, numbers, place.to_core(numbers))
    pad_column = numbers[count : 2 * count][:, None]
    length_row = numbers[2 * count :]
    quarters = numbers[:count].reshape(2, place.low, rows)
    order = []
    for step in range(place.low):
        for other in range(2):
            quarter = lax.dynamic_index_in_dim(quarters, place.c ^ other, 0, keepdims=False)
            order.append(
                lax.dynamic_index_in_dim(quarter, (place.tl + step) % place.low, 0, keepdims=False)
            )
    order = jnp.concatenate(order)

    places = jnp.arange(count, dtype=jnp.int32)
    starts = starts_of(places, length_row)
    cosine, sine = rotary_tables(places - starts)
    cosine_stored, sine_stored = rotary_tables(order - starts_of(order, length_row))
    to_sequence = (places[:, None] == order[None, :]).astype(jnp.bfloat16)
    to_storage = (order[:, None] == places[None, :]).astype(jnp.bfloat16)
    first_blocks = starts[:: math.gcd(count, QUERY_BLOCK)] // KEY_BLOCK
    start_row = starts[None, :]

    attention_scale = first_weight[:, head_columns].astype(jnp.float32)[None, :]
    feedforward_scale = first_weight[:, head_columns + 1].astype(jnp.float32)[None, :]
    normed, heads_stored = project(
        tokens_all,
        attention_scale,
        first_weight,
        cosine_stored,
        sine_stored,
        heads + kv_heads,
        head_columns,
    )
    heads_all = contract(to_sequence, heads_stored, 1, 0, jnp.bfloat16)
    attended, log_totals = attend(first_blocks, heads_all, start_row, pad_column, kv_heads, group)
    attended_stored = contract(to_storage, attended, 1, 0, jnp.bfloat16)

    def split_rows(array):
        return [array[i * rows : (i + 1) * rows] for i in range(tensor_count)]

    attention_out = place.scatter_rows(
        split_rows(contract(attended_stored, output_turned, 1, 1, jnp.bfloat16))
    )
    residual = tokens_own.astype(jnp.float32) + attention_out

    root = inverse_root(residual)
    normed_ffn = jnp.concatenate(
        place.gather_rows((residual * root * feedforward_scale).astype(jnp.bfloat16)), axis=0
    )
    gate_values = contract(normed_ffn, gate_full, 1, 0)
    up_values = contract(normed_ffn, up_full, 1, 0)
    sigmoid = jax.nn.sigmoid(gate_values)
    hidden = (gate_values * sigmoid * up_values).astype(jnp.bfloat16)
    layer_own = residual + place.scatter_rows(
        split_rows(contract(hidden, down_turned, 1, 1, jnp.bfloat16))
    )

    def leave(own):
        arrived = place.cross(own.astype(jnp.bfloat16)).astype(jnp.float32)
        return place.relative_features(jnp.where(place.home, own, arrived))

    layer_output = leave(layer_own)

    grad_hidden = contract(cot_all, down_turned, 1, 0)
    grad_gate = (grad_hidden * up_values * sigmoid * (1.0 + gate_values * (1.0 - sigmoid))).astype(
        jnp.bfloat16
    )
    grad_up = (grad_hidden * gate_values * sigmoid).astype(jnp.bfloat16)
    grad_normed_ffn = place.scatter_rows(
        split_rows(
            (contract(grad_gate, gate_full, 1, 1) + contract(grad_up, up_full, 1, 1)).astype(jnp.bfloat16)
        )
    )
    down_grad = place.scatter_weight(contract(cot_all, hidden, 0, 0, jnp.bfloat16))
    gate_grad = place.scatter_weight(contract(normed_ffn, grad_gate, 0, 0, jnp.bfloat16))
    up_grad = place.scatter_weight(contract(normed_ffn, grad_up, 0, 0, jnp.bfloat16))
    unit_rows = residual * root
    scaled = grad_normed_ffn * feedforward_scale
    feedforward_part = jnp.sum(grad_normed_ffn * unit_rows, axis=0)
    grad_residual = cot_own.astype(jnp.float32) + root * (
        scaled - unit_rows * jnp.mean(scaled * unit_rows, axis=-1, keepdims=True)
    )

    grad_rows = jnp.concatenate(place.gather_rows(grad_residual.astype(jnp.bfloat16)), axis=0)
    grad_attended = contract(grad_rows, output_turned, 1, 0, jnp.bfloat16)
    grad_attended = contract(to_sequence, grad_attended, 1, 0, jnp.bfloat16)
    output_grad = place.scatter_weight(contract(grad_rows, attended_stored, 0, 0, jnp.bfloat16))
    grad_query, grad_rest = attend_back(
        first_blocks,
        heads_all,
        start_row,
        pad_column,
        log_totals,
        attended,
        grad_attended,
        cosine,
        sine,
        kv_heads,
        group,
    )
    grad_heads = contract(
        to_storage, jnp.concatenate([grad_query, grad_rest], axis=1), 1, 0, jnp.bfloat16
    )
    grad_normed_part = contract(grad_heads, first_weight[:, :head_columns], 1, 1)
    grad_normed = place.scatter_rows(split_rows(grad_normed_part.astype(jnp.bfloat16)))
    tokens_wide = tokens_all.astype(jnp.float32)
    attention_part = jnp.sum(grad_normed_part * (tokens_wide * inverse_root(tokens_wide)), axis=0)
    first_grad = place.scatter_weight(
        jnp.concatenate(
            [
                contract(normed, grad_heads, 0, 0, jnp.bfloat16),
                attention_part.astype(jnp.bfloat16)[:, None],
                feedforward_part.astype(jnp.bfloat16)[:, None],
            ],
            axis=1,
        )
    )
    gain_grads = place.sum_tensor(first_grad[:, head_columns:])
    own_wide = tokens_own.astype(jnp.float32)
    root_own = inverse_root(own_wide)
    unit_rows = own_wide * root_own
    scaled = grad_normed * attention_scale
    input_grad = grad_residual + root_own * (
        scaled - unit_rows * jnp.mean(scaled * unit_rows, axis=-1, keepdims=True)
    )
    query_columns = heads * HEAD_DIM
    key_columns = kv_heads * HEAD_DIM
    return (
        layer_output,
        leave(input_grad),
        gain_grads[:, 0],
        first_grad[:, :query_columns],
        first_grad[:, query_columns : query_columns + key_columns],
        first_grad[:, query_columns + key_columns : head_columns],
        output_grad.T,
        gain_grads[:, 1],
        gate_grad,
        up_grad,
        down_grad.T,
    )


def solution(mesh):
    placed = (
        P(("dp", "tensor"), None),
        P("dp"),
        P("dp", "tensor"),
        P("dp", "tensor"),
        P("dp", "tensor"),
        P("tensor", "dp"),
        P("dp"),
        P("dp", "tensor"),
        P("dp", "tensor"),
        P("tensor", "dp"),
        P(("dp", "tensor"), None),
        P("dp", None),
        P("dp"),
        P("dp"),
        P("dp"),
    )
    return jax.shard_map(
        functools.partial(per_device, mesh.shape["dp"], mesh.shape["tensor"]),
        mesh=mesh,
        in_specs=placed,
        out_specs=(
            P(("dp", "tensor"), None),
            P(("dp", "tensor"), None),
            P("dp"),
            P("dp", "tensor"),
            P("dp", "tensor"),
            P("dp", "tensor"),
            P("tensor", "dp"),
            P("dp"),
            P("dp", "tensor"),
            P("dp", "tensor"),
            P("tensor", "dp"),
        ),
        check_vma=False,
    )
```

```python
import functools
import math

import jax
import jax.numpy as jnp
from jax import lax
from jax.experimental import pallas as pl
from jax.experimental.pallas import tpu as pltpu
from jax.sharding import PartitionSpec as P

HEAD_DIM = 80
HALF = HEAD_DIM // 2
QUERY_BLOCK = 128
KEY_BLOCK = 256
MASKED = -1e30
VMEM_LIMIT = 48 * 1024 * 1024
LINK_VMEM_LIMIT = 60 * 1024 * 1024

epsilon = 1e-05
rope_base = 10000.0
AXES = ("dp", "tensor")


def contract(left, right, left_dim, right_dim, out_type=jnp.float32):
    product = lax.dot_general(
        left,
        right,
        (((left_dim,), (right_dim,)), ((), ())),
        preferred_element_type=jnp.float32,
    )
    return product.astype(out_type)


def after(value, *earlier):
    return lax.optimization_barrier((value,) + earlier)[0]


def inverse_root(vectors):
    return lax.rsqrt(jnp.mean(vectors * vectors, axis=-1, keepdims=True) + epsilon)


class Placement:
    def __init__(self, dp_count, tensor_count):
        self.dp_count = dp_count
        self.tensor_count = tensor_count
        self.chips = dp_count // 2
        self.low = tensor_count // 2
        dp_index = lax.axis_index("dp")
        tensor_index = lax.axis_index("tensor")
        self.p = dp_index // 2
        self.c = dp_index % 2
        self.th = tensor_index // self.low
        self.tl = tensor_index % self.low
        self.home = self.c == self.th

    def move(self, array, target):
        pairs = []
        for p in range(self.chips):
            for c in range(2):
                for th in range(2):
                    for tl in range(self.low):
                        goal = target(p, c, th, tl)
                        if goal is not None:
                            pairs.append((self.flat(p, c, th, tl), self.flat(*goal)))
        return lax.ppermute(array, AXES, pairs)

    def flat(self, p, c, th, tl):
        return (2 * p + c) * self.tensor_count + th * self.low + tl

    def to_core(self, array):
        return self.move(array, lambda p, c, th, tl: (p, 1 - c, th, tl))

    def to_chip(self, array, step):
        return self.move(array, lambda p, c, th, tl: (p ^ step, c, th, tl))

    def to_low(self, array, step):
        return self.move(array, lambda p, c, th, tl: (p, c, th, (tl + step) % self.low))

    def cross(self, array):
        return self.move(
            array, lambda p, c, th, tl: (p, 1 - c, 1 - th, tl) if c != th else None
        )

    def home_turn(self, array):
        return self.move(
            array, lambda p, c, th, tl: (p, c, 1 - th, tl) if c == th else (p, 1 - c, th, tl)
        )

    def away_turn(self, array):
        return self.move(
            array, lambda p, c, th, tl: (p, 1 - c, th, tl) if c == th else (p, c, 1 - th, tl)
        )

    def swap(self, array):
        return jnp.where(self.home, array, self.cross(array))

    def quarter_rows(self, array, step, other):
        rows = array.shape[0] // self.tensor_count
        index = (self.c ^ other) * self.low + (self.tl + step) % self.low
        return lax.dynamic_slice_in_dim(array, index * rows, rows, 0)

    def scatter_rows(self, partial):
        total = None
        for step in list(range(1, self.low)) + [0]:
            mine = self.quarter_rows(partial, step, 0)
            others = self.quarter_rows(partial, step, 1)
            pair = mine.astype(jnp.float32) + self.to_core(others).astype(jnp.float32)
            if step:
                pair = self.to_low(pair.astype(jnp.bfloat16), step).astype(jnp.float32)
            total = pair if total is None else total + pair
        return total


def project_kernel(heads, tokens_ref, gain_ref, weight_ref, cosine_ref, sine_ref, normed_ref, out_ref):
    tokens = tokens_ref[...].astype(jnp.float32)
    root = lax.rsqrt(jnp.mean(tokens * tokens, axis=-1, keepdims=True) + epsilon)
    normed = (tokens * root * gain_ref[...]).astype(jnp.bfloat16)
    normed_ref[...] = normed
    rows = jnp.dot(normed, weight_ref[...], preferred_element_type=jnp.float32)
    cosine, sine = cosine_ref[...], sine_ref[...]
    pieces = []
    for head in range(heads):
        leading = rows[:, head * HEAD_DIM : head * HEAD_DIM + HALF]
        trailing = rows[:, head * HEAD_DIM + HALF : (head + 1) * HEAD_DIM]
        pieces.append(leading * cosine - trailing * sine)
        pieces.append(trailing * cosine + leading * sine)
    pieces.append(rows[:, heads * HEAD_DIM : out_ref.shape[1]])
    out_ref[...] = jnp.concatenate(pieces, axis=1).astype(jnp.bfloat16)


def project(tokens, gain, weight, cosine, sine, rotated_heads, out_columns):
    count, width = tokens.shape
    block = math.gcd(count, 256)
    return pl.pallas_call(
        functools.partial(project_kernel, rotated_heads),
        grid=(count // block,),
        in_specs=[
            pl.BlockSpec((block, width), lambda i: (i, 0)),
            pl.BlockSpec((1, width), lambda i: (0, 0)),
            pl.BlockSpec(weight.shape, lambda i: (0, 0)),
            pl.BlockSpec((block, HALF), lambda i: (i, 0)),
            pl.BlockSpec((block, HALF), lambda i: (i, 0)),
        ],
        out_specs=[
            pl.BlockSpec((block, width), lambda i: (i, 0)),
            pl.BlockSpec((block, out_columns), lambda i: (i, 0)),
        ],
        out_shape=[
            jax.ShapeDtypeStruct((count, width), jnp.bfloat16),
            jax.ShapeDtypeStruct((count, out_columns), jnp.bfloat16),
        ],
        compiler_params=pltpu.CompilerParams(vmem_limit_bytes=VMEM_LIMIT),
        cost_estimate=pl.CostEstimate(
            flops=2 * count * width * weight.shape[1],
            bytes_accessed=4 * count * width + 2 * weight.size,
            transcendentals=0,
        ),
        name="project",
    )(tokens, gain, weight, cosine, sine)


def block_bias(key_start, query_start, start_row, pad_column):
    shape = (pad_column.shape[0], start_row.shape[1])
    keys = key_start + lax.broadcasted_iota(jnp.int32, shape, 0)
    queries = query_start + lax.broadcasted_iota(jnp.int32, shape, 1)
    allowed = ((keys >= start_row) & (keys <= queries) & (pad_column == 1)) | (keys == queries)
    return jnp.where(allowed, 0.0, MASKED)


def stack_heads(rows, first, group):
    return jnp.concatenate(
        [rows[:, (first + g) * HEAD_DIM : (first + g + 1) * HEAD_DIM] for g in range(group)], axis=0
    )


def times(left, right, left_dim, right_dim):
    return lax.dot_general(
        left, right, (((left_dim,), (right_dim,)), ((), ())), preferred_element_type=jnp.float32
    )


def attend_kernel(
    kv_heads, group, first_ref, query_ref, all_ref, start_ref, pad_ref, out_ref, total_ref, key_heads, value_turned
):
    step = pl.program_id(0)
    heads = kv_heads * group
    query_rows = query_ref.shape[0]
    scale = 1.0 / math.sqrt(HEAD_DIM)

    @pl.when(step == 0)
    def _():
        for k in range(kv_heads):
            at = (heads + k) * HEAD_DIM
            key_heads[k] = all_ref[:, at : at + HEAD_DIM]
            at = (heads + kv_heads + k) * HEAD_DIM
            value_turned[k] = all_ref[:, at : at + HEAD_DIM].astype(jnp.float32).T.astype(jnp.bfloat16)

    query_start = step * query_rows
    last = (query_start + query_rows - 1) // KEY_BLOCK + 1
    pieces = []
    for k in range(kv_heads):
        queries = stack_heads(query_ref[:, : heads * HEAD_DIM], k * group, group)

        def body(block, carry, k=k, queries=queries):
            top, total, mixed = carry
            at = pl.multiple_of(block * KEY_BLOCK, KEY_BLOCK)
            bias = block_bias(at, query_start, start_ref[...], pad_ref[pl.ds(at, KEY_BLOCK), :])
            bias = jnp.concatenate([bias] * group, axis=1)
            scores = times(key_heads[k, pl.ds(at, KEY_BLOCK), :], queries, 1, 1) * scale + bias
            new_top = jnp.maximum(top, jnp.max(scores, axis=0, keepdims=True))
            weight = jnp.exp(scores - new_top)
            shrink = jnp.exp(top - new_top)
            total = total * shrink + jnp.sum(weight, axis=0, keepdims=True)
            mixed = mixed * shrink + times(
                value_turned[k, :, pl.ds(at, KEY_BLOCK)], weight.astype(jnp.bfloat16), 1, 0
            )
            return new_top, total, mixed

        columns = group * query_rows
        top, total, mixed = lax.fori_loop(
            first_ref[step],
            last,
            body,
            (
                jnp.full((1, columns), MASKED, jnp.float32),
                jnp.zeros((1, columns), jnp.float32),
                jnp.zeros((HEAD_DIM, columns), jnp.float32),
            ),
        )
        mixed = mixed / total
        log_total = top + jnp.log(total)
        for g in range(group):
            span = slice(g * query_rows, (g + 1) * query_rows)
            pieces.append(mixed[:, span].T)
            total_ref[k * group + g : k * group + g + 1, :] = log_total[:, span]
    out_ref[...] = jnp.concatenate(pieces, axis=1).astype(jnp.bfloat16)


def attend(first, heads_all, start_row, pad_column, kv_heads, group):
    count, columns = heads_all.shape
    heads = kv_heads * group
    block = math.gcd(count, QUERY_BLOCK)
    return pl.pallas_call(
        functools.partial(attend_kernel, kv_heads, group),
        grid_spec=pltpu.PrefetchScalarGridSpec(
            num_scalar_prefetch=1,
            grid=(count // block,),
            in_specs=[
                pl.BlockSpec((block, columns), lambda i, first: (i, 0)),
                pl.BlockSpec((count, columns), lambda i, first: (0, 0)),
                pl.BlockSpec((1, block), lambda i, first: (0, i)),
                pl.BlockSpec((count, 1), lambda i, first: (0, 0)),
            ],
            out_specs=[
                pl.BlockSpec((block, heads * HEAD_DIM), lambda i, first: (i, 0)),
                pl.BlockSpec((heads, block), lambda i, first: (0, i)),
            ],
            scratch_shapes=[
                pltpu.VMEM((kv_heads, count, HEAD_DIM), jnp.bfloat16),
                pltpu.VMEM((kv_heads, HEAD_DIM, count), jnp.bfloat16),
            ],
        ),
        out_shape=[
            jax.ShapeDtypeStruct((count, heads * HEAD_DIM), jnp.bfloat16),
            jax.ShapeDtypeStruct((heads, count), jnp.float32),
        ],
        compiler_params=pltpu.CompilerParams(vmem_limit_bytes=VMEM_LIMIT),
        cost_estimate=pl.CostEstimate(
            flops=60 * 10**9, bytes_accessed=count * columns * 4, transcendentals=0
        ),
        name="attend",
    )(first, heads_all, heads_all, start_row, pad_column)


def attend_back_kernel(
    kv_heads,
    group,
    first_ref,
    query_ref,
    all_ref,
    start_ref,
    pad_ref,
    total_ref,
    attended_ref,
    grad_ref,
    cosine_turned_ref,
    sine_turned_ref,
    cosine_ref,
    sine_ref,
    grad_query_ref,
    grad_rest_ref,
    key_heads,
    value_heads,
    key_turned,
    grad_keys,
    grad_values,
):
    step = pl.program_id(0)
    heads = kv_heads * group
    query_rows = query_ref.shape[0]
    scale = 1.0 / math.sqrt(HEAD_DIM)

    @pl.when(step == 0)
    def _():
        for k in range(kv_heads):
            at = (heads + k) * HEAD_DIM
            keys = all_ref[:, at : at + HEAD_DIM]
            key_heads[k] = keys
            key_turned[k] = keys.astype(jnp.float32).T.astype(jnp.bfloat16)
            at = (heads + kv_heads + k) * HEAD_DIM
            value_heads[k] = all_ref[:, at : at + HEAD_DIM]
        grad_keys[...] = jnp.zeros_like(grad_keys)
        grad_values[...] = jnp.zeros_like(grad_values)

    query_start = step * query_rows
    last = (query_start + query_rows - 1) // KEY_BLOCK + 1
    cosine = cosine_turned_ref[...]
    sine = sine_turned_ref[...]
    pieces = []
    for k in range(kv_heads):
        queries = stack_heads(query_ref[:, : heads * HEAD_DIM], k * group, group)
        grads = stack_heads(grad_ref[...], k * group, group)
        attended = stack_heads(attended_ref[...], k * group, group)
        inner = jnp.sum(
            (grads.astype(jnp.float32) * attended.astype(jnp.float32)).T, axis=0, keepdims=True
        )
        log_total = jnp.concatenate(
            [total_ref[k * group + g : k * group + g + 1, :] for g in range(group)], axis=1
        )

        def body(block, turned, k=k, queries=queries, grads=grads, inner=inner, log_total=log_total):
            at = pl.multiple_of(block * KEY_BLOCK, KEY_BLOCK)
            span = pl.ds(at, KEY_BLOCK)
            bias = block_bias(at, query_start, start_ref[...], pad_ref[span, :])
            bias = jnp.concatenate([bias] * group, axis=1)
            scores = times(key_heads[k, span, :], queries, 1, 1) * scale + bias
            weight = jnp.exp(scores - log_total)
            grad_weight = times(value_heads[k, span, :], grads, 1, 1)
            grad_scores = (weight * (grad_weight - inner)).astype(jnp.bfloat16)
            grad_values[k, span, :] += times(weight.astype(jnp.bfloat16), grads, 1, 0)
            grad_keys[k, span, :] += times(grad_scores, queries, 1, 0)
            return turned + times(key_turned[k, :, span], grad_scores, 1, 0)

        turned = lax.fori_loop(
            first_ref[step], last, body, jnp.zeros((HEAD_DIM, group * query_rows), jnp.float32)
        )
        turned = turned * scale
        for g in range(group):
            part = turned[:, g * query_rows : (g + 1) * query_rows]
            leading, trailing = part[:HALF], part[HALF:]
            back = jnp.concatenate(
                [leading * cosine + trailing * sine, trailing * cosine - leading * sine], axis=0
            )
            pieces.append(back.T)
    grad_query_ref[...] = jnp.concatenate(pieces, axis=1).astype(jnp.bfloat16)

    @pl.when(step == pl.num_programs(0) - 1)
    def _():
        rest = []
        for k in range(kv_heads):
            leading = grad_keys[k][:, :HALF] * scale
            trailing = grad_keys[k][:, HALF:] * scale
            rest.append(leading * cosine_ref[...] + trailing * sine_ref[...])
            rest.append(trailing * cosine_ref[...] - leading * sine_ref[...])
        for k in range(kv_heads):
            rest.append(grad_values[k])
        grad_rest_ref[...] = jnp.concatenate(rest, axis=1).astype(jnp.bfloat16)


def attend_back(
    first, heads_all, start_row, pad_column, log_totals, attended, grad_attended, cosine, sine, kv_heads, group
):
    count, columns = heads_all.shape
    heads = kv_heads * group
    block = math.gcd(count, QUERY_BLOCK)
    width = heads * HEAD_DIM
    rest = 2 * kv_heads * HEAD_DIM
    return pl.pallas_call(
        functools.partial(attend_back_kernel, kv_heads, group),
        grid_spec=pltpu.PrefetchScalarGridSpec(
            num_scalar_prefetch=1,
            grid=(count // block,),
            in_specs=[
                pl.BlockSpec((block, columns), lambda i, first: (i, 0)),
                pl.BlockSpec((count, columns), lambda i, first: (0, 0)),
                pl.BlockSpec((1, block), lambda i, first: (0, i)),
                pl.BlockSpec((count, 1), lambda i, first: (0, 0)),
                pl.BlockSpec((heads, block), lambda i, first: (0, i)),
                pl.BlockSpec((block, width), lambda i, first: (i, 0)),
                pl.BlockSpec((block, width), lambda i, first: (i, 0)),
                pl.BlockSpec((HALF, block), lambda i, first: (0, i)),
                pl.BlockSpec((HALF, block), lambda i, first: (0, i)),
                pl.BlockSpec((count, HALF), lambda i, first: (0, 0)),
                pl.BlockSpec((count, HALF), lambda i, first: (0, 0)),
            ],
            out_specs=[
                pl.BlockSpec((block, width), lambda i, first: (i, 0)),
                pl.BlockSpec((count, rest), lambda i, first: (0, 0)),
            ],
            scratch_shapes=[
                pltpu.VMEM((kv_heads, count, HEAD_DIM), jnp.bfloat16),
                pltpu.VMEM((kv_heads, count, HEAD_DIM), jnp.bfloat16),
                pltpu.VMEM((kv_heads, HEAD_DIM, count), jnp.bfloat16),
                pltpu.VMEM((kv_heads, count, HEAD_DIM), jnp.float32),
                pltpu.VMEM((kv_heads, count, HEAD_DIM), jnp.float32),
            ],
        ),
        out_shape=[
            jax.ShapeDtypeStruct((count, width), jnp.bfloat16),
            jax.ShapeDtypeStruct((count, rest), jnp.bfloat16),
        ],
        compiler_params=pltpu.CompilerParams(vmem_limit_bytes=VMEM_LIMIT),
        cost_estimate=pl.CostEstimate(
            flops=120 * 10**9, bytes_accessed=count * columns * 8, transcendentals=0
        ),
        name="attend_back",
    )(
        first,
        heads_all,
        heads_all,
        start_row,
        pad_column,
        log_totals,
        attended,
        grad_attended,
        cosine.T,
        sine.T,
        cosine,
        sine,
    )


MESH = pl.DeviceIdType.MESH
CHUNK = 64


class Links:
    def __init__(self, dp_count, tensor_count, send, recv, local):
        self.chips, self.low = dp_count // 2, tensor_count // 2
        self.send, self.recv, self.local = send, recv, local
        self.used = 0
        self.used_local = 0
        self.unsent = []
        self.all_low = False
        dp_index, tensor_index = lax.axis_index("dp"), lax.axis_index("tensor")
        self.dp_index, self.tensor_index = dp_index, tensor_index
        self.p, self.c = dp_index // 2, dp_index % 2
        self.th, self.tl = tensor_index // self.low, tensor_index % self.low
        self.home = self.c == self.th
        self.away = self.c != self.th
        self.quarter = self.c * self.low + self.tl

    def at(self, p, c, th, tl):
        return (2 * p + c, th * self.low + tl)

    def chip(self, step):
        p = self.p
        moved = p
        for bit in (1, 2, 4):
            if step & bit:
                moved = moved + bit * (1 - 2 * ((p // bit) % 2))
        return moved

    def chip_peer(self, step):
        return self.at(self.chip(step), self.c, self.th, self.tl)

    def core_peer(self):
        return self.at(self.p, 1 - self.c, self.th, self.tl)

    def low_peer(self, step):
        return self.at(self.p, self.c, self.th, (self.tl + step) % self.low)

    def cross_peer(self):
        return self.at(self.p, 1 - self.c, 1 - self.th, self.tl)

    def partner(self):
        return self.at(self.p, self.c, 1 - self.th, self.tl)

    def chip_steps(self):
        return (1, 2) if self.chips == 4 else tuple(range(1, self.chips))

    def enter(self):
        peers = [self.core_peer(), self.cross_peer(), self.partner()]
        peers += [self.chip_peer(step) for step in self.chip_steps()]
        peers += [self.low_peer(step) for step in range(1, self.low)]
        if self.all_low:
            peers += [
                self.at(self.p, self.c, 1 - self.th, (self.tl + step) % self.low)
                for step in range(1, self.low)
            ]
        barrier = pltpu.get_barrier_semaphore()
        for peer in peers:
            pl.semaphore_signal(barrier, inc=1, device_id=peer, device_id_type=MESH)
        pl.semaphore_wait(barrier, len(peers))

    def copy(self, source, target, peer, when=None):
        slot = self.used
        self.used += 1

        def make():
            return pltpu.make_async_remote_copy(
                src_ref=source,
                dst_ref=target,
                send_sem=self.send.at[slot],
                recv_sem=self.recv.at[slot],
                device_id=peer,
                device_id_type=MESH,
            )

        item = Item(make, when)
        self.unsent.append(item)
        return item

    def local_slot(self):
        self.used_local += 1
        return self.used_local - 1

    def keep(self, source, target, when=None):
        slot = self.used_local
        self.used_local += 1
        return Item(lambda: pltpu.make_async_copy(source, target, self.local.at[slot]), when)

    def drop(self, items):
        self.unsent = [item for item in self.unsent if item not in items]

    def leave(self):
        for item in self.unsent:
            item.sent()


class Item:
    def __init__(self, make, when):
        self.make, self.when = make, when

    def run(self, action):
        if self.when is None:
            action(self.make())
        else:
            pl.when(self.when)(lambda: action(self.make()))

    def start(self):
        self.run(lambda copy: copy.start())

    def arrived(self):
        self.run(lambda copy: copy.wait_recv())

    def sent(self):
        self.run(lambda copy: copy.wait_send())

    def done(self):
        self.run(lambda copy: copy.wait())


class WeightGather:
    def __init__(self, links, shard, full):
        self.links, self.shard, self.full = links, shard, full
        rows = shard.shape[0]
        self.rows = rows
        mine = full.at[pl.ds(links.dp_index * rows, rows)]
        home_int = links.home.astype(jnp.int32)
        self.first = links.copy(
            shard,
            mine,
            links.at(
                links.p,
                home_int * links.c + (1 - home_int) * (1 - links.c),
                home_int * (1 - links.th) + (1 - home_int) * links.th,
                links.tl,
            ),
        )
        self.second = links.copy(shard, mine, links.cross_peer(), links.away)
        self.own = links.keep(shard, mine, links.home)
        unit = 2 * rows
        self.direct = []
        self.forward = []
        here = full.at[pl.ds(links.p * unit, unit)]
        for step in links.chip_steps():
            self.direct.append(links.copy(here, here, links.chip_peer(step)))
        if links.chips == 4:
            top = full.at[pl.ds(links.chip(2) * unit, rows)]
            bottom = full.at[pl.ds(links.chip(1) * unit + rows, rows)]
            self.forward.append(links.copy(top, top, links.chip_peer(1)))
            self.forward.append(links.copy(bottom, bottom, links.chip_peer(2)))

    def turn(self):
        self.first.start()
        self.second.start()
        self.own.start()

    def settle_unit(self):
        self.first.arrived()
        self.second.arrived()
        self.own.done()

    def spread(self):
        self.settle_unit()
        self.spread_unit()

    def spread_unit(self):
        for item in self.direct:
            item.start()

    def pass_on(self):
        for item in self.direct:
            item.arrived()
        for item in self.forward:
            item.start()

    def finish(self):
        for item in self.forward:
            item.arrived()


class RowGather:
    def __init__(self, links, full, rows):
        self.links = links
        mine = full.at[pl.ds(links.quarter * rows, rows)]
        self.to_core = links.copy(mine, mine, links.core_peer())
        self.to_low = []
        self.onward = []
        for step in range(1, links.low):
            self.to_low.append(links.copy(mine, mine, links.low_peer(step)))
            came = (links.tl + links.low - step) % links.low
            block = full.at[pl.ds((links.c * links.low + came) * rows, rows)]
            self.onward.append(links.copy(block, block, links.core_peer()))

    def start(self):
        for item in self.to_low:
            item.start()
        self.to_core.start()

    def pass_on(self):
        for arriving, item in zip(self.to_low, self.onward):
            arriving.arrived()
            item.start()

    def finish(self):
        self.to_core.arrived()
        for item in self.onward:
            item.arrived()


class RowScatter:
    def __init__(self, links, partial, mine, others, sums, arrivals, rows):
        self.links, self.rows = links, rows
        self.mine, self.others, self.sums, self.arrivals = mine, others, sums, arrivals
        low = links.low
        self.load = links.keep(partial.at[pl.ds(links.c * low * rows, low * rows)], mine)
        self.swap = links.copy(
            partial.at[pl.ds((1 - links.c) * low * rows, low * rows)], others, links.core_peer()
        )
        self.sends = [
            links.copy(sums.at[step - 1], arrivals.at[step - 1], links.low_peer(step))
            for step in range(1, low)
        ]

    def start(self):
        self.swap.start()
        self.load.start()

    def send_sums(self):
        self.load.done()
        self.swap.arrived()
        for step in range(1, self.links.low):
            base = ((self.links.tl + step) % self.links.low) * self.rows

            @pl.loop(0, self.rows // CHUNK)
            def _(i, base=base, step=step):
                span = pl.ds(pl.multiple_of(base + i * CHUNK, CHUNK), CHUNK)
                total = self.mine[span].astype(jnp.float32) + self.others[span].astype(jnp.float32)
                self.sums[step - 1, pl.ds(pl.multiple_of(i * CHUNK, CHUNK), CHUNK)] = total.astype(jnp.bfloat16)

            self.sends[step - 1].start()

    def collect(self, use):
        for item in self.sends:
            item.arrived()
        base = self.links.tl * self.rows

        @pl.loop(0, self.rows // CHUNK)
        def _(i):
            at = pl.multiple_of(i * CHUNK, CHUNK)
            span = pl.ds(pl.multiple_of(base + at, CHUNK), CHUNK)
            total = self.mine[span].astype(jnp.float32) + self.others[span].astype(jnp.float32)
            for step in range(1, self.links.low):
                total = total + self.arrivals[step - 1, pl.ds(at, CHUNK)].astype(jnp.float32)
            use(pl.ds(at, CHUNK), total)


def scatter_scratch(low, rows, width):
    return [
        pltpu.VMEM((low * rows, width), jnp.bfloat16),
        pltpu.VMEM((low * rows, width), jnp.bfloat16),
        pltpu.VMEM((low - 1, rows, width), jnp.bfloat16),
        pltpu.VMEM((low - 1, rows, width), jnp.bfloat16),
    ]


def semaphores(count, local_count):
    return [
        pltpu.SemaphoreType.DMA((count,)),
        pltpu.SemaphoreType.DMA((count,)),
        pltpu.SemaphoreType.DMA((local_count,)),
    ]


def anywhere(count):
    return [pl.BlockSpec(memory_space=pl.ANY)] * count


def in_vmem(count):
    return [pl.BlockSpec(memory_space=pltpu.VMEM)] * count


def link_params(number):
    return pltpu.CompilerParams(
        collective_id=number, has_side_effects=True, vmem_limit_bytes=LINK_VMEM_LIMIT
    )


ADD_ROWS = 32


def row_loop(rows, body):
    @pl.loop(0, rows // ADD_ROWS)
    def _(i):
        body(pl.ds(pl.multiple_of(i * ADD_ROWS, ADD_ROWS), ADD_ROWS))


class WeightScatter:
    def __init__(self, links, partial, result, inbox, turned, sums, leaving, stage):
        self.links, self.partial, self.result = links, partial, result
        self.inbox, self.turned, self.sums, self.leaving = inbox, turned, sums, leaving
        rows = partial.shape[0] // (2 * links.chips)
        self.rows = rows
        width = partial.shape[1]
        self.stage = [stage.at[i, pl.ds(0, rows), pl.ds(0, width)] for i in range(3)]
        self.both = links.chips == 4
        self.loads = [
            links.local_slot() for _ in range(3)
        ]
        if self.both:
            x_peer, y_peer = links.chip_peer(1), links.chip_peer(2)
            self.before = [
                links.copy(self.part(3, 0), inbox.at[0], x_peer),
                links.copy(self.part(3, 1), inbox.at[1], y_peer),
            ]
            self.direct = [
                links.copy(self.part(1, 0), inbox.at[2], x_peer),
                links.copy(self.part(2, 1), inbox.at[3], y_peer),
            ]
            self.summed = [
                links.copy(sums.at[0], inbox.at[4], y_peer),
                links.copy(sums.at[1], inbox.at[5], x_peer),
            ]
            self.arrivals = ((2, 4), (5, 3))
        else:
            self.before, self.summed, self.direct = [], [], []
            for step in links.chip_steps():
                for half in range(2):
                    at = 2 * (step - 1) + half
                    self.direct.append(
                        links.copy(self.part(step, half), inbox.at[at], links.chip_peer(step))
                    )
            self.arrivals = tuple(
                tuple(2 * (step - 1) + half for step in links.chip_steps()) for half in range(2)
            )
        home_int = links.home.astype(jnp.int32)
        self.first = links.copy(
            leaving.at[0],
            turned.at[0],
            links.at(
                links.p,
                home_int * (1 - links.c) + (1 - home_int) * links.c,
                home_int * links.th + (1 - home_int) * (1 - links.th),
                links.tl,
            ),
        )
        self.second = links.copy(leaving.at[1], turned.at[1], links.cross_peer(), links.away)

    def part(self, step, half):
        start = (2 * self.links.chip(step) + half) * self.rows
        return self.partial.at[pl.ds(start, self.rows)]

    def load(self, sources):
        copies = [
            pltpu.make_async_copy(source, stage, self.links.local.at[slot])
            for source, stage, slot in zip(sources, self.stage, self.loads)
        ]
        for copy in copies:
            copy.start()
        for copy in copies:
            copy.wait()

    def start(self, which):
        for item in getattr(self, which):
            item.start()

    def arrived(self, which):
        for item in getattr(self, which):
            item.arrived()

    def add_before(self):
        if not self.both:
            return
        self.arrived("before")
        for index, part in ((0, self.part(2, 0)), (1, self.part(1, 1))):
            self.load([part, self.inbox.at[index]])

            def body(span, index=index):
                total = self.stage[0][span].astype(jnp.float32) + self.stage[1][span].astype(jnp.float32)
                self.sums[index, span] = total.astype(jnp.bfloat16)

            row_loop(self.rows, body)
            self.summed[index].start()

    def turn(self):
        links = self.links
        for half in range(2):
            sources = [self.part(0, half)] + [self.inbox.at[at] for at in self.arrivals[half]]
            kept = links.c == half
            if len(sources) == 3:
                self.load(sources)

                def body(span, half=half, kept=kept):
                    total = self.stage[0][span].astype(jnp.float32)
                    total = total + self.stage[1][span].astype(jnp.float32)
                    self.settle(span, total + self.stage[2][span].astype(jnp.float32), kept)

                row_loop(self.rows, body)
            else:
                self.fold(sources, kept)
        self.first.start()
        self.second.start()

    def fold(self, sources, kept):
        rows = self.rows
        total = self.total
        self.load(sources[:1])
        row_loop(rows, lambda span: total.__setitem__(span, self.stage[0][span].astype(jnp.float32)))
        for source in sources[1:]:
            self.load([source])

            def body(span):
                total[span] = total[span] + self.stage[0][span].astype(jnp.float32)

            row_loop(rows, body)
        row_loop(rows, lambda span: self.settle(span, total[span], kept))

    def settle(self, span, total, kept):
        low = total.astype(jnp.bfloat16)
        links = self.links

        @pl.when(kept & links.home)
        def _():
            self.result[span] = total

        @pl.when(kept & links.away)
        def _():
            self.leaving[0, span] = low

        @pl.when(jnp.logical_not(kept) & links.home)
        def _():
            self.leaving[0, span] = low

        @pl.when(jnp.logical_not(kept) & links.away)
        def _():
            self.leaving[1, span] = low

    def finish(self):
        links = self.links
        self.first.arrived()
        self.second.arrived()

        @pl.when(links.home)
        def _():
            def body(span):
                self.result[span] = self.result[span] + self.turned[0, span].astype(jnp.float32)

            row_loop(self.rows, body)

        @pl.when(links.away)
        def _():
            def body(span):
                self.result[span] = self.turned[1, span].astype(jnp.float32) + self.turned[0, span].astype(
                    jnp.float32
                )

            row_loop(self.rows, body)


def weight_scatter_scratch(chips, rows, width):
    return [pltpu.VMEM((2, rows, width), jnp.bfloat16)] * 3


def inbox_shape(chips, rows, width):
    count = 6 if chips == 4 else 2 * (chips - 1)
    return jax.ShapeDtypeStruct((count, rows, width), jnp.bfloat16)


def scatter_shapes(chips, partial):
    rows = partial.shape[0] // (2 * chips)
    width = partial.shape[1]
    return rows, width


def tail_kernel(
    dp_count,
    tensor_count,
    gain_column,
    partial,
    grad_gate,
    grad_up,
    grad_output,
    grad_first,
    own_ref,
    grad_residual_ref,
    gain_ref,
    input_ref,
    gate_ref,
    up_ref,
    output_ref,
    first_ref,
    gate_in,
    up_in,
    output_in,
    first_in,
    *scratch,
):
    gate_work, up_work, output_work, first_work = (scratch[3 * i : 3 * i + 3] for i in range(4))
    stage, leaving, crossed, mine, others, sums, arrivals, gains_out, gains_in, total = scratch[12:22]
    links = Links(dp_count, tensor_count, *scratch[22:])
    links.all_low = True
    rows = own_ref.shape[0]
    scatter = RowScatter(links, partial, mine, others, sums, arrivals, rows)
    crossing = links.copy(leaving, crossed, links.cross_peer(), links.away)
    weights = []
    for grad, result, inbox, work in (
        (grad_gate, gate_ref, gate_in, gate_work),
        (grad_up, up_ref, up_in, up_work),
        (grad_output, output_ref, output_in, output_work),
        (grad_first, first_ref, first_in, first_work),
    ):
        turned, added, turning = work
        made = WeightScatter(links, grad, result, inbox, turned, added, turning, stage)
        made.total = None if made.both else total.at[pl.ds(0, made.rows), pl.ds(0, grad.shape[1])]
        weights.append(made)
    gate, up, output, first = weights
    gain_sends = []
    for step in range(1, tensor_count):
        other = (links.tensor_index + step) % tensor_count
        gain_sends.append(
            links.copy(gains_out, gains_in.at[step - 1], links.at(links.p, links.c, other // links.low, other % links.low))
        )

    links.enter()
    gate.start("before")
    scatter.start()
    gate.start("direct")
    scatter.send_sums()
    gate.add_before()

    def use(span, grad_normed):
        own = own_ref[span].astype(jnp.float32)
        root = lax.rsqrt(jnp.mean(own * own, axis=-1, keepdims=True) + epsilon)
        unit = own * root
        scaled = grad_normed * gain_ref[...]
        grad = grad_residual_ref[span] + root * (
            scaled - unit * jnp.mean(scaled * unit, axis=-1, keepdims=True)
        )
        input_ref[span] = grad
        leaving[span] = grad.astype(jnp.bfloat16)

    gate.arrived("direct")
    up.start("before")
    scatter.collect(use)
    crossing.start()
    gate.arrived("summed")
    up.start("direct")
    gate.turn()
    up.add_before()
    up.arrived("direct")
    output.start("before")
    output.start("direct")
    up.arrived("summed")
    first.start("before")
    up.turn()
    output.add_before()
    gate.finish()
    output.arrived("direct")
    first.start("direct")
    first.add_before()
    output.arrived("summed")
    output.turn()
    crossing.arrived()

    @pl.when(links.away)
    def _():
        def body(span):
            input_ref[span] = crossed[span].astype(jnp.float32)

        row_loop(rows, body)

    first.arrived("direct")
    first.arrived("summed")
    first.turn()
    up.finish()
    output.finish()
    first.finish()
    width = first_ref.shape[1]
    gains_out[...] = first_ref[:, width - 128 :]
    for item in gain_sends:
        item.start()
    for item in gain_sends:
        item.arrived()
    summed = gains_out[...]
    for step in range(1, tensor_count):
        summed = summed + gains_in[step - 1]
    column = width - 128 + lax.broadcasted_iota(jnp.int32, summed.shape, 1)
    first_ref[:, width - 128 :] = jnp.where(column >= gain_column, summed, gains_out[...])
    links.leave()


def tail(dp_count, tensor_count, gain_column, partial, grads, own, grad_residual, gain):
    rows, width = own.shape
    low, chips = tensor_count // 2, dp_count // 2
    shapes = [scatter_shapes(chips, grad) for grad in grads]
    widest = max(columns for _, columns in shapes)
    most = shapes[0][0]
    scratch = []
    for block, columns in shapes:
        scratch += weight_scatter_scratch(chips, block, columns)
    scratch += [
        pltpu.VMEM((3, most, widest), jnp.bfloat16),
        pltpu.VMEM((rows, width), jnp.bfloat16),
        pltpu.VMEM((rows, width), jnp.bfloat16),
    ]
    scratch += scatter_scratch(low, rows, width)
    scratch += [
        pltpu.VMEM((most, 128), jnp.float32),
        pltpu.VMEM((tensor_count - 1, most, 128), jnp.float32),
        pltpu.VMEM((most, widest) if chips != 4 else (8, 128), jnp.float32),
    ]
    results = pl.pallas_call(
        functools.partial(tail_kernel, dp_count, tensor_count, gain_column),
        out_shape=[jax.ShapeDtypeStruct((rows, width), jnp.float32)]
        + [jax.ShapeDtypeStruct(shape, jnp.float32) for shape in shapes]
        + [inbox_shape(chips, *shape) for shape in shapes],
        in_specs=anywhere(5) + in_vmem(3),
        out_specs=in_vmem(5) + anywhere(4),
        scratch_shapes=scratch + semaphores(96, 24),
        compiler_params=link_params(3),
        name="tail",
    )(partial, *grads, own, grad_residual, gain)
    return results[:5]


def gather_first_kernel(
    dp_count, tensor_count, tokens, first, output, gate, tokens_all, first_full, output_full, gate_full, *sems
):
    links = Links(dp_count, tensor_count, *sems)
    rows = tokens.shape[0]
    mine = tokens_all.at[pl.ds(links.tensor_index * rows, rows)]
    crossing = links.copy(tokens, mine, links.cross_peer(), links.away)
    staying = links.keep(tokens, mine, links.home)
    gather_tokens = RowGather(links, tokens_all, rows)
    weights = [
        WeightGather(links, shard, full)
        for shard, full in ((first, first_full), (output, output_full), (gate, gate_full))
    ]
    links.enter()
    weights[0].turn()
    crossing.start()
    staying.start()

    @pl.when(links.home)
    def _():
        staying.make().wait()
        gather_tokens.start()

    weights[0].spread()
    weights[1].turn()

    @pl.when(links.away)
    def _():
        crossing.make().wait_recv()
        gather_tokens.start()

    weights[1].spread()
    weights[2].turn()
    weights[0].pass_on()
    gather_tokens.pass_on()
    weights[1].pass_on()
    weights[0].finish()
    gather_tokens.finish()
    weights[1].finish()
    weights[2].settle_unit()
    links.drop(weights[2].direct + weights[2].forward)
    links.leave()


def gather_first(dp_count, tensor_count, tokens, first, output, gate):
    def full(shard, times):
        return jax.ShapeDtypeStruct((shard.shape[0] * times, shard.shape[1]), shard.dtype)

    return pl.pallas_call(
        functools.partial(gather_first_kernel, dp_count, tensor_count),
        out_shape=[
            full(tokens, tensor_count),
            full(first, dp_count),
            full(output, dp_count),
            full(gate, dp_count),
        ],
        in_specs=in_vmem(4),
        out_specs=anywhere(4),
        scratch_shapes=semaphores(64, 8),
        compiler_params=link_params(0),
        name="gather_first",
    )(tokens, first, output, gate)


def middle_kernel(
    dp_count,
    tensor_count,
    moved_units,
    partial,
    tokens_all,
    cot,
    up,
    up_turned,
    up_crossed,
    down,
    gate_part,
    *rest,
):
    gate_units, rest = rest[:moved_units], rest[moved_units:]
    gain_ref, residual_ref, normed_all, cot_all, up_full, down_full, gate_full = rest[:7]
    own, normed, mine, others, sums, arrivals = rest[7:13]
    links = Links(dp_count, tensor_count, *rest[13:])
    rows = cot.shape[0]
    scatter = RowScatter(links, partial, mine, others, sums, arrivals, rows)
    gather_normed = RowGather(links, normed_all, rows)
    gather_cot = RowGather(links, cot_all, rows)
    gate_gather = WeightGather(links, up, gate_full)
    up_gather = WeightGather(links, up, up_full)
    down_gather = WeightGather(links, down, down_full)
    shard = up.shape[0]
    here = up_full.at[pl.ds(links.dp_index * shard, shard)]
    beside = up_full.at[pl.ds((2 * links.p + 1 - links.c) * shard, shard)]
    quarter = pl.ds(links.quarter * rows, rows)
    placements = [
        links.keep(up, here, links.home),
        links.keep(up_turned, beside, links.home),
        links.keep(up_turned, here, links.away),
        links.keep(up_crossed, beside, links.away),
    ]
    gate_placements = [
        links.keep(unit, gate_full.at[pl.ds(links.chip(step) * 2 * shard, 2 * shard)])
        for step, unit in zip(links.chip_steps(), gate_units)
    ]
    cot_crossing = links.copy(cot, cot_all.at[pl.ds(links.tensor_index * rows, rows)], links.cross_peer(), links.away)
    cot_staying = links.keep(cot, cot_all.at[quarter], links.home)
    load = links.keep(tokens_all.at[quarter], own)
    store = links.keep(normed, normed_all.at[quarter])
    links.drop([up_gather.first, up_gather.second, gate_gather.first, gate_gather.second] + gate_gather.direct)
    links.enter()
    scatter.start()
    load.start()
    for item in gate_placements + placements:
        item.start()
    for item in gate_placements:
        item.done()
    for item in gate_gather.forward:
        item.start()
    for item in placements:
        item.done()
    scatter.send_sums()
    up_gather.spread_unit()
    down_gather.turn()
    cot_staying.start()
    load.done()

    def use(span, total):
        residual = own[span].astype(jnp.float32) + total
        residual_ref[span] = residual
        root = lax.rsqrt(jnp.mean(residual * residual, axis=-1, keepdims=True) + epsilon)
        normed[span] = (residual * root * gain_ref[...]).astype(jnp.bfloat16)

    scatter.collect(use)
    store.start()
    store.done()
    gather_normed.start()
    down_gather.settle_unit()
    cot_crossing.start()
    up_gather.pass_on()
    down_gather.spread_unit()
    gate_gather.finish()
    gather_normed.pass_on()
    cot_staying.done()
    cot_crossing.arrived()
    gather_cot.start()
    up_gather.finish()
    down_gather.pass_on()
    gather_normed.finish()
    gather_cot.pass_on()
    down_gather.finish()
    gather_cot.finish()
    links.leave()


def middle(
    dp_count, tensor_count, partial, tokens_all, cot, up, up_turned, up_crossed, down, gate_part, gate_units, gain
):
    rows, width = cot.shape
    low = tensor_count // 2

    def full(shard, times):
        return jax.ShapeDtypeStruct((shard.shape[0] * times, shard.shape[1]), shard.dtype)

    return pl.pallas_call(
        functools.partial(middle_kernel, dp_count, tensor_count, len(gate_units)),
        out_shape=[
            jax.ShapeDtypeStruct((rows, width), jnp.float32),
            full(cot, tensor_count),
            full(cot, tensor_count),
            full(up, dp_count),
            full(down, dp_count),
            jax.ShapeDtypeStruct(gate_part.shape, gate_part.dtype),
        ],
        in_specs=anywhere(2) + in_vmem(5) + anywhere(1) + in_vmem(len(gate_units) + 1),
        out_specs=in_vmem(1) + anywhere(5),
        scratch_shapes=[pltpu.VMEM((rows, width), jnp.bfloat16)] * 2
        + scatter_scratch(low, rows, width)
        + semaphores(64, 24),
        input_output_aliases={7: 5},
        compiler_params=link_params(1),
        name="middle",
    )(partial, tokens_all, cot, up, up_turned, up_crossed, down, gate_part, *gate_units, gain)


def turn_back_kernel(
    dp_count,
    tensor_count,
    partial,
    cot_all,
    grad_down,
    residual_ref,
    gain_ref,
    grad_residual_ref,
    gain_part_ref,
    down_ref,
    grad_rows,
    down_in,
    own,
    low_grad,
    turned,
    added,
    turning,
    stage,
    total_ref,
    mine,
    others,
    sums,
    arrivals,
    *sems,
):
    links = Links(dp_count, tensor_count, *sems)
    rows = residual_ref.shape[0]
    down = WeightScatter(links, grad_down, down_ref, down_in, turned, added, turning, stage)
    down.total = total_ref
    scatter = RowScatter(links, partial, mine, others, sums, arrivals, rows)
    gather = RowGather(links, grad_rows, rows)
    quarter = pl.ds(links.quarter * rows, rows)
    load = links.keep(cot_all.at[quarter], own)
    store = links.keep(low_grad, grad_rows.at[quarter])
    links.enter()
    scatter.start()
    load.start()
    down.start("before")
    down.start("direct")
    scatter.send_sums()
    load.done()
    down.add_before()
    gain_part_ref[...] = jnp.zeros_like(gain_part_ref)

    def use(span, grad_normed):
        residual = residual_ref[span]
        root = lax.rsqrt(jnp.mean(residual * residual, axis=-1, keepdims=True) + epsilon)
        unit = residual * root
        gain_part_ref[...] += jnp.sum(grad_normed * unit, axis=0, keepdims=True)
        scaled = grad_normed * gain_ref[...]
        grad = own[span].astype(jnp.float32) + root * (
            scaled - unit * jnp.mean(scaled * unit, axis=-1, keepdims=True)
        )
        grad_residual_ref[span] = grad
        low_grad[span] = grad.astype(jnp.bfloat16)

    scatter.collect(use)
    store.start()
    store.done()
    gather.start()
    down.arrived("direct")
    down.arrived("summed")
    down.turn()
    gather.pass_on()
    down.finish()
    gather.finish()
    links.leave()


def turn_back(dp_count, tensor_count, partial, cot_all, grad_down, residual, gain):
    rows, width = residual.shape
    low, chips = tensor_count // 2, dp_count // 2
    block, columns = scatter_shapes(chips, grad_down)
    return pl.pallas_call(
        functools.partial(turn_back_kernel, dp_count, tensor_count),
        out_shape=[
            jax.ShapeDtypeStruct((rows, width), jnp.float32),
            jax.ShapeDtypeStruct((1, width), jnp.float32),
            jax.ShapeDtypeStruct((block, columns), jnp.float32),
            jax.ShapeDtypeStruct((rows * tensor_count, width), jnp.bfloat16),
            inbox_shape(chips, block, columns),
        ],
        in_specs=anywhere(3) + in_vmem(2),
        out_specs=in_vmem(3) + anywhere(2),
        scratch_shapes=[pltpu.VMEM((rows, width), jnp.bfloat16)] * 2
        + weight_scatter_scratch(chips, block, columns)
        + [
            pltpu.VMEM((3, block, columns), jnp.bfloat16),
            pltpu.VMEM((block, columns) if chips != 4 else (8, 128), jnp.float32),
        ]
        + scatter_scratch(low, rows, width)
        + semaphores(48, 16),
        compiler_params=link_params(2),
        name="turn_back",
    )(partial, cot_all, grad_down, residual, gain)[:4]


def starts_of(positions, length_row):
    ends = jnp.cumsum(length_row)
    inside = positions[:, None] >= ends[None, :]
    return jnp.sum(jnp.where(inside, length_row[None, :], 0), axis=1)


def rotary_tables(positions):
    frequency = jnp.exp(
        jnp.arange(HALF, dtype=jnp.float32) * (-2.0 * math.log(rope_base) / HEAD_DIM)
    )
    angles = positions.astype(jnp.float32)[:, None] * frequency[None, :]
    return (jnp.cos(angles), jnp.sin(angles))


def per_device(
    dp_count,
    tensor_count,
    tokens,
    attention_gain,
    query_weight,
    key_weight,
    value_weight,
    output_weight,
    feedforward_gain,
    gate_weight,
    up_weight,
    down_weight,
    cotangent,
    lengths,
    storage_order,
    sequence_order,
    pad_mask,
):
    place = Placement(dp_count, tensor_count)
    count = storage_order.shape[0]
    rows = count // tensor_count
    kv_heads = key_weight.shape[1] // HEAD_DIM
    heads = query_weight.shape[1] // HEAD_DIM
    group = heads // kv_heads
    head_columns = (heads + 2 * kv_heads) * HEAD_DIM

    hidden_units = gate_weight.shape[1]
    hidden_padded = -(-hidden_units // 128) * 128
    output_padded = -(-heads * HEAD_DIM // 128) * 128
    first_padded = -(-(head_columns + 2) // 128) * 128

    def wide(array, columns):
        return jnp.pad(array, ((0, 0), (0, columns - array.shape[1])))

    gate_shard = wide(gate_weight, hidden_padded)
    up_shard = wide(up_weight, hidden_padded)
    down_shard = wide(down_weight.T, hidden_padded)
    tokens_all, first_weight, output_turned, gate_part = gather_first(
        dp_count,
        tensor_count,
        tokens,
        wide(
            jnp.concatenate(
                [query_weight, key_weight, value_weight, attention_gain[:, None], feedforward_gain[:, None]],
                axis=1,
            ),
            first_padded,
        ),
        wide(output_weight.T, output_padded),
        gate_shard,
    )
    output_turned = output_turned[:, : heads * HEAD_DIM]
    late_up = after(up_shard, tokens_all)
    up_turned = place.home_turn(late_up)
    up_crossed = place.cross(late_up)
    unit = gate_part.shape[0] // place.chips
    gate_unit = lax.dynamic_slice_in_dim(gate_part, place.p * unit, unit, 0)
    steps = (1, 2) if place.chips == 4 else tuple(range(1, place.chips))
    gate_units = [place.to_chip(gate_unit, step) for step in steps]

    numbers = jnp.concatenate([storage_order, pad_mask, lengths[0]])
    numbers = jnp.where(place.home, numbers, place.to_core(numbers))
    pad_column = numbers[count : 2 * count][:, None]
    length_row = numbers[2 * count :]
    order = numbers[:count]

    places = jnp.arange(count, dtype=jnp.int32)
    starts = starts_of(places, length_row)
    cosine, sine = rotary_tables(places - starts)
    cosine_stored, sine_stored = rotary_tables(order - starts_of(order, length_row))
    to_sequence = (places[:, None] == order[None, :]).astype(jnp.bfloat16)
    to_storage = (order[:, None] == places[None, :]).astype(jnp.bfloat16)
    first_blocks = starts[:: math.gcd(count, QUERY_BLOCK)] // KEY_BLOCK
    start_row = starts[None, :]

    attention_scale = first_weight[:, head_columns].astype(jnp.float32)[None, :]
    feedforward_scale = first_weight[:, head_columns + 1].astype(jnp.float32)[None, :]
    normed, heads_stored = project(
        tokens_all,
        attention_scale,
        first_weight,
        cosine_stored,
        sine_stored,
        heads + kv_heads,
        head_columns,
    )
    heads_all = contract(to_sequence, heads_stored, 1, 0, jnp.bfloat16)
    attended, log_totals = attend(first_blocks, heads_all, start_row, pad_column, kv_heads, group)
    attended_stored = contract(to_storage, attended, 1, 0, jnp.bfloat16)

    residual, normed_ffn, cot_all, up_full, down_turned, gate_full = middle(
        dp_count,
        tensor_count,
        contract(attended_stored, output_turned, 1, 1, jnp.bfloat16),
        tokens_all,
        cotangent,
        up_shard,
        up_turned,
        up_crossed,
        down_shard,
        gate_part,
        gate_units,
        feedforward_scale,
    )
    gate_values = contract(normed_ffn, gate_full, 1, 0)
    up_values = contract(normed_ffn, up_full, 1, 0)
    sigmoid = jax.nn.sigmoid(gate_values)
    hidden = (gate_values * sigmoid * up_values).astype(jnp.bfloat16)

    def leave(own):
        arrived = place.cross(own.astype(jnp.bfloat16)).astype(jnp.float32)
        return jnp.where(place.home, own, arrived)

    grad_hidden = contract(cot_all, down_turned, 1, 0)
    grad_gate = (grad_hidden * up_values * sigmoid * (1.0 + gate_values * (1.0 - sigmoid))).astype(
        jnp.bfloat16
    )
    grad_up = (grad_hidden * gate_values * sigmoid).astype(jnp.bfloat16)
    grad_part = (contract(grad_gate, gate_full, 1, 1) + contract(grad_up, up_full, 1, 1)).astype(
        jnp.bfloat16
    )
    down_part_grad = contract(cot_all, hidden, 0, 0, jnp.bfloat16)
    grad_residual, feedforward_part, down_grad, grad_rows = turn_back(
        dp_count, tensor_count, grad_part, cot_all, down_part_grad, residual, feedforward_scale
    )
    late_hidden = after(hidden, grad_rows)
    down_part = contract(late_hidden, down_turned, 1, 1, jnp.bfloat16)

    layer_own = residual + place.scatter_rows(down_part)
    layer_output = leave(layer_own)
    grad_attended = contract(grad_rows, output_turned, 1, 0, jnp.bfloat16)
    grad_attended = contract(to_sequence, grad_attended, 1, 0, jnp.bfloat16)
    late_rows, late_gate, late_up_grad = lax.optimization_barrier((normed_ffn, grad_gate, grad_up, grad_rows))[:3]
    grads = [
        contract(late_rows, late_gate, 0, 0, jnp.bfloat16),
        contract(late_rows, late_up_grad, 0, 0, jnp.bfloat16),
        wide(contract(grad_rows, attended_stored, 0, 0, jnp.bfloat16), output_padded),
    ]
    grad_query, grad_rest = attend_back(
        first_blocks,
        heads_all,
        start_row,
        pad_column,
        log_totals,
        attended,
        grad_attended,
        cosine,
        sine,
        kv_heads,
        group,
    )
    grad_heads = contract(
        to_storage, jnp.concatenate([grad_query, grad_rest], axis=1), 1, 0, jnp.bfloat16
    )
    grad_normed_part = contract(grad_heads, first_weight[:, :head_columns], 1, 1)
    tokens_wide = tokens_all.astype(jnp.float32)
    attention_part = jnp.sum(grad_normed_part * (tokens_wide * inverse_root(tokens_wide)), axis=0)
    grads.append(
        wide(
            jnp.concatenate(
                [
                    contract(normed, grad_heads, 0, 0, jnp.bfloat16),
                    attention_part.astype(jnp.bfloat16)[:, None],
                    feedforward_part[0].astype(jnp.bfloat16)[:, None],
                ],
                axis=1,
            ),
            first_padded,
        )
    )
    input_grad, gate_grad, up_grad, output_grad, first_grad = tail(
        dp_count,
        tensor_count,
        head_columns,
        grad_normed_part.astype(jnp.bfloat16),
        grads,
        place.quarter_rows(tokens_all, 0, 0),
        grad_residual,
        attention_scale,
    )
    query_columns = heads * HEAD_DIM
    key_columns = kv_heads * HEAD_DIM
    return (
        layer_output,
        input_grad,
        first_grad[:, head_columns],
        first_grad[:, :query_columns],
        first_grad[:, query_columns : query_columns + key_columns],
        first_grad[:, query_columns + key_columns : head_columns],
        output_grad[:, :query_columns].T,
        first_grad[:, head_columns + 1],
        gate_grad[:, :hidden_units],
        up_grad[:, :hidden_units],
        down_grad[:, :hidden_units].T,
    )


def solution(mesh):
    placed = (
        P(("dp", "tensor"), None),
        P("dp"),
        P("dp", "tensor"),
        P("dp", "tensor"),
        P("dp", "tensor"),
        P("tensor", "dp"),
        P("dp"),
        P("dp", "tensor"),
        P("dp", "tensor"),
        P("tensor", "dp"),
        P(("dp", "tensor"), None),
        P("dp", None),
        P("dp"),
        P("dp"),
        P("dp"),
    )
    return jax.shard_map(
        functools.partial(per_device, mesh.shape["dp"], mesh.shape["tensor"]),
        mesh=mesh,
        in_specs=placed,
        out_specs=(
            P(("dp", "tensor"), None),
            P(("dp", "tensor"), None),
            P("dp"),
            P("dp", "tensor"),
            P("dp", "tensor"),
            P("dp", "tensor"),
            P("tensor", "dp"),
            P("dp"),
            P("dp", "tensor"),
            P("dp", "tensor"),
            P("tensor", "dp"),
        ),
        check_vma=False,
    )
```

```python
import functools
import math

import jax
import jax.numpy as jnp
from jax import lax
from jax.experimental import pallas as pl
from jax.experimental.pallas import tpu as pltpu
from jax.sharding import PartitionSpec as P

HEAD_DIM = 80
HALF = HEAD_DIM // 2
QUERY_BLOCK = 128
KEY_BLOCK = 256
MASKED = -1e30
VMEM_LIMIT = 48 * 1024 * 1024
LINK_VMEM_LIMIT = 60 * 1024 * 1024

epsilon = 1e-05
rope_base = 10000.0
AXES = ("dp", "tensor")


def contract(left, right, left_dim, right_dim, out_type=jnp.float32):
    product = lax.dot_general(
        left,
        right,
        (((left_dim,), (right_dim,)), ((), ())),
        preferred_element_type=jnp.float32,
    )
    return product.astype(out_type)


def after(value, *earlier):
    return lax.optimization_barrier((value,) + earlier)[0]


def inverse_root(vectors):
    return lax.rsqrt(jnp.mean(vectors * vectors, axis=-1, keepdims=True) + epsilon)


class Placement:
    def __init__(self, dp_count, tensor_count):
        self.dp_count = dp_count
        self.tensor_count = tensor_count
        self.chips = dp_count // 2
        self.low = tensor_count // 2
        dp_index = lax.axis_index("dp")
        tensor_index = lax.axis_index("tensor")
        self.p = dp_index // 2
        self.c = dp_index % 2
        self.th = tensor_index // self.low
        self.tl = tensor_index % self.low
        self.home = self.c == self.th

    def move(self, array, target):
        pairs = []
        for p in range(self.chips):
            for c in range(2):
                for th in range(2):
                    for tl in range(self.low):
                        goal = target(p, c, th, tl)
                        if goal is not None:
                            pairs.append((self.flat(p, c, th, tl), self.flat(*goal)))
        return lax.ppermute(array, AXES, pairs)

    def flat(self, p, c, th, tl):
        return (2 * p + c) * self.tensor_count + th * self.low + tl

    def to_core(self, array):
        return self.move(array, lambda p, c, th, tl: (p, 1 - c, th, tl))

    def to_chip(self, array, step):
        return self.move(array, lambda p, c, th, tl: (p ^ step, c, th, tl))

    def to_low(self, array, step):
        return self.move(array, lambda p, c, th, tl: (p, c, th, (tl + step) % self.low))

    def cross(self, array):
        return self.move(
            array, lambda p, c, th, tl: (p, 1 - c, 1 - th, tl) if c != th else None
        )

    def home_turn(self, array):
        return self.move(
            array, lambda p, c, th, tl: (p, c, 1 - th, tl) if c == th else (p, 1 - c, th, tl)
        )

    def away_turn(self, array):
        return self.move(
            array, lambda p, c, th, tl: (p, 1 - c, th, tl) if c == th else (p, c, 1 - th, tl)
        )

    def swap(self, array):
        return jnp.where(self.home, array, self.cross(array))

    def quarter_rows(self, array, step, other):
        rows = array.shape[0] // self.tensor_count
        index = (self.c ^ other) * self.low + (self.tl + step) % self.low
        return lax.dynamic_slice_in_dim(array, index * rows, rows, 0)

    def pair_rows(self, partial):
        return [
            self.quarter_rows(partial, step, 0).astype(jnp.float32)
            + self.to_core(self.quarter_rows(partial, step, 1)).astype(jnp.float32)
            for step in range(self.low)
        ]

    def sum_rows(self, pairs):
        total = pairs[0]
        for step in range(1, self.low):
            total = total + self.to_low(pairs[step].astype(jnp.bfloat16), step).astype(jnp.float32)
        return total


def project_kernel(heads, tokens_ref, gain_ref, weight_ref, cosine_ref, sine_ref, normed_ref, out_ref, root_ref):
    tokens = tokens_ref[...].astype(jnp.float32)
    root = lax.rsqrt(jnp.mean(tokens * tokens, axis=-1, keepdims=True) + epsilon)
    root_ref[...] = root
    normed = (tokens * root * gain_ref[...]).astype(jnp.bfloat16)
    normed_ref[...] = normed
    rows = jnp.dot(normed, weight_ref[...], preferred_element_type=jnp.float32)
    cosine, sine = cosine_ref[...].T, sine_ref[...].T
    pieces = []
    for head in range(heads):
        leading = rows[:, head * HEAD_DIM : head * HEAD_DIM + HALF]
        trailing = rows[:, head * HEAD_DIM + HALF : (head + 1) * HEAD_DIM]
        pieces.append(leading * cosine - trailing * sine)
        pieces.append(trailing * cosine + leading * sine)
    pieces.append(rows[:, heads * HEAD_DIM : out_ref.shape[1]])
    out_ref[...] = jnp.concatenate(pieces, axis=1).astype(jnp.bfloat16)


def project(tokens, gain, weight, cosine, sine, rotated_heads, out_columns):
    count, width = tokens.shape
    block = math.gcd(count, 256)
    return pl.pallas_call(
        functools.partial(project_kernel, rotated_heads),
        grid=(count // block,),
        in_specs=[
            pl.BlockSpec((block, width), lambda i: (i, 0)),
            pl.BlockSpec((1, width), lambda i: (0, 0)),
            pl.BlockSpec(weight.shape, lambda i: (0, 0)),
            pl.BlockSpec((HALF, block), lambda i: (0, i)),
            pl.BlockSpec((HALF, block), lambda i: (0, i)),
        ],
        out_specs=[
            pl.BlockSpec((block, width), lambda i: (i, 0)),
            pl.BlockSpec((block, out_columns), lambda i: (i, 0)),
            pl.BlockSpec((block, 1), lambda i: (i, 0)),
        ],
        out_shape=[
            jax.ShapeDtypeStruct((count, width), jnp.bfloat16),
            jax.ShapeDtypeStruct((count, out_columns), jnp.bfloat16),
            jax.ShapeDtypeStruct((count, 1), jnp.float32),
        ],
        compiler_params=pltpu.CompilerParams(vmem_limit_bytes=VMEM_LIMIT),
        cost_estimate=pl.CostEstimate(
            flops=2 * count * width * weight.shape[1],
            bytes_accessed=4 * count * width + 2 * weight.size,
            transcendentals=0,
        ),
        name="project",
    )(tokens, gain, weight, cosine, sine)


def block_bias(key_start, query_start, start_row, pad_column):
    shape = (pad_column.shape[0], start_row.shape[1])
    keys = key_start + lax.broadcasted_iota(jnp.int32, shape, 0)
    queries = query_start + lax.broadcasted_iota(jnp.int32, shape, 1)
    allowed = ((keys >= start_row) & (keys <= queries) & (pad_column == 1)) | (keys == queries)
    return jnp.where(allowed, 0.0, MASKED)


def stack_heads(rows, first, group):
    return jnp.concatenate(
        [rows[:, (first + g) * HEAD_DIM : (first + g + 1) * HEAD_DIM] for g in range(group)], axis=0
    )


def times(left, right, left_dim, right_dim):
    return lax.dot_general(
        left, right, (((left_dim,), (right_dim,)), ((), ())), preferred_element_type=jnp.float32
    )


def attend_kernel(
    kv_heads, group, first_ref, query_ref, all_ref, start_ref, pad_ref, out_ref, total_ref, key_heads, value_turned
):
    step = pl.program_id(0)
    heads = kv_heads * group
    query_rows = query_ref.shape[0]
    scale = 1.0 / math.sqrt(HEAD_DIM)

    @pl.when(step == 0)
    def _():
        for k in range(kv_heads):
            at = (heads + k) * HEAD_DIM
            key_heads[k] = all_ref[:, at : at + HEAD_DIM]
            at = (heads + kv_heads + k) * HEAD_DIM
            value_turned[k] = all_ref[:, at : at + HEAD_DIM].astype(jnp.float32).T.astype(jnp.bfloat16)

    query_start = step * query_rows
    last = (query_start + query_rows - 1) // KEY_BLOCK + 1
    pieces = []
    for k in range(kv_heads):
        queries = stack_heads(query_ref[:, : heads * HEAD_DIM], k * group, group)

        def body(block, carry, k=k, queries=queries):
            top, total, mixed = carry
            at = pl.multiple_of(block * KEY_BLOCK, KEY_BLOCK)
            bias = block_bias(at, query_start, start_ref[...], pad_ref[pl.ds(at, KEY_BLOCK), :])
            bias = jnp.concatenate([bias] * group, axis=1)
            scores = times(key_heads[k, pl.ds(at, KEY_BLOCK), :], queries, 1, 1) * scale + bias
            new_top = jnp.maximum(top, jnp.max(scores, axis=0, keepdims=True))
            weight = jnp.exp(scores - new_top)
            shrink = jnp.exp(top - new_top)
            total = total * shrink + jnp.sum(weight, axis=0, keepdims=True)
            mixed = mixed * shrink + times(
                value_turned[k, :, pl.ds(at, KEY_BLOCK)], weight.astype(jnp.bfloat16), 1, 0
            )
            return new_top, total, mixed

        columns = group * query_rows
        top, total, mixed = lax.fori_loop(
            first_ref[step],
            last,
            body,
            (
                jnp.full((1, columns), MASKED, jnp.float32),
                jnp.zeros((1, columns), jnp.float32),
                jnp.zeros((HEAD_DIM, columns), jnp.float32),
            ),
        )
        mixed = mixed / total
        log_total = top + jnp.log(total)
        for g in range(group):
            span = slice(g * query_rows, (g + 1) * query_rows)
            pieces.append(mixed[:, span].T)
            total_ref[k * group + g : k * group + g + 1, :] = log_total[:, span]
    out_ref[...] = jnp.concatenate(pieces, axis=1).astype(jnp.bfloat16)


def attend(first, heads_all, start_row, pad_column, kv_heads, group):
    count, columns = heads_all.shape
    heads = kv_heads * group
    block = math.gcd(count, QUERY_BLOCK)
    return pl.pallas_call(
        functools.partial(attend_kernel, kv_heads, group),
        grid_spec=pltpu.PrefetchScalarGridSpec(
            num_scalar_prefetch=1,
            grid=(count // block,),
            in_specs=[
                pl.BlockSpec((block, columns), lambda i, first: (i, 0)),
                pl.BlockSpec((count, columns), lambda i, first: (0, 0)),
                pl.BlockSpec((1, block), lambda i, first: (0, i)),
                pl.BlockSpec((count, 1), lambda i, first: (0, 0)),
            ],
            out_specs=[
                pl.BlockSpec((block, heads * HEAD_DIM), lambda i, first: (i, 0)),
                pl.BlockSpec((heads, block), lambda i, first: (0, i)),
            ],
            scratch_shapes=[
                pltpu.VMEM((kv_heads, count, HEAD_DIM), jnp.bfloat16),
                pltpu.VMEM((kv_heads, HEAD_DIM, count), jnp.bfloat16),
            ],
        ),
        out_shape=[
            jax.ShapeDtypeStruct((count, heads * HEAD_DIM), jnp.bfloat16),
            jax.ShapeDtypeStruct((heads, count), jnp.float32),
        ],
        compiler_params=pltpu.CompilerParams(vmem_limit_bytes=VMEM_LIMIT),
        cost_estimate=pl.CostEstimate(
            flops=50 * 10**9, bytes_accessed=count * columns, transcendentals=0
        ),
        name="attend",
    )(first, heads_all, heads_all, start_row, pad_column)


def attend_back_kernel(
    kv_heads,
    group,
    first_ref,
    query_ref,
    all_ref,
    start_ref,
    pad_ref,
    total_ref,
    attended_ref,
    grad_ref,
    cosine_turned_ref,
    sine_turned_ref,
    cosine_all_ref,
    sine_all_ref,
    grad_query_ref,
    grad_rest_ref,
    key_heads,
    value_heads,
    key_turned,
    grad_keys,
    grad_values,
):
    step = pl.program_id(0)
    heads = kv_heads * group
    query_rows = query_ref.shape[0]
    scale = 1.0 / math.sqrt(HEAD_DIM)

    @pl.when(step == 0)
    def _():
        for k in range(kv_heads):
            at = (heads + k) * HEAD_DIM
            keys = all_ref[:, at : at + HEAD_DIM]
            key_heads[k] = keys
            key_turned[k] = keys.astype(jnp.float32).T.astype(jnp.bfloat16)
            at = (heads + kv_heads + k) * HEAD_DIM
            value_heads[k] = all_ref[:, at : at + HEAD_DIM]
        grad_keys[...] = jnp.zeros_like(grad_keys)
        grad_values[...] = jnp.zeros_like(grad_values)

    query_start = step * query_rows
    last = (query_start + query_rows - 1) // KEY_BLOCK + 1
    cosine = cosine_turned_ref[...]
    sine = sine_turned_ref[...]
    pieces = []
    for k in range(kv_heads):
        queries = stack_heads(query_ref[:, : heads * HEAD_DIM], k * group, group)
        grads = stack_heads(grad_ref[...], k * group, group)
        attended = stack_heads(attended_ref[...], k * group, group)
        inner = jnp.sum(
            (grads.astype(jnp.float32) * attended.astype(jnp.float32)).T, axis=0, keepdims=True
        )
        log_total = jnp.concatenate(
            [total_ref[k * group + g : k * group + g + 1, :] for g in range(group)], axis=1
        )

        def body(block, turned, k=k, queries=queries, grads=grads, inner=inner, log_total=log_total):
            at = pl.multiple_of(block * KEY_BLOCK, KEY_BLOCK)
            span = pl.ds(at, KEY_BLOCK)
            bias = block_bias(at, query_start, start_ref[...], pad_ref[span, :])
            bias = jnp.concatenate([bias] * group, axis=1)
            scores = times(key_heads[k, span, :], queries, 1, 1) * scale + bias
            weight = jnp.exp(scores - log_total)
            grad_weight = times(value_heads[k, span, :], grads, 1, 1)
            grad_scores = (weight * (grad_weight - inner)).astype(jnp.bfloat16)
            grad_values[k, span, :] += times(weight.astype(jnp.bfloat16), grads, 1, 0)
            grad_keys[k, span, :] += times(grad_scores, queries, 1, 0)
            return turned + times(key_turned[k, :, span], grad_scores, 1, 0)

        turned = lax.fori_loop(
            first_ref[step], last, body, jnp.zeros((HEAD_DIM, group * query_rows), jnp.float32)
        )
        turned = turned * scale
        for g in range(group):
            part = turned[:, g * query_rows : (g + 1) * query_rows]
            leading, trailing = part[:HALF], part[HALF:]
            back = jnp.concatenate(
                [leading * cosine + trailing * sine, trailing * cosine - leading * sine], axis=0
            )
            pieces.append(back.T)
    grad_query_ref[...] = jnp.concatenate(pieces, axis=1).astype(jnp.bfloat16)

    @pl.when(step == pl.num_programs(0) - 1)
    def _():
        rest = []
        cosine_all, sine_all = cosine_all_ref[...].T, sine_all_ref[...].T
        for k in range(kv_heads):
            leading = grad_keys[k][:, :HALF] * scale
            trailing = grad_keys[k][:, HALF:] * scale
            rest.append(leading * cosine_all + trailing * sine_all)
            rest.append(trailing * cosine_all - leading * sine_all)
        for k in range(kv_heads):
            rest.append(grad_values[k])
        grad_rest_ref[...] = jnp.concatenate(rest, axis=1).astype(jnp.bfloat16)


def attend_back(
    first, heads_all, start_row, pad_column, log_totals, attended, grad_attended, cosine, sine, kv_heads, group
):
    count, columns = heads_all.shape
    heads = kv_heads * group
    block = math.gcd(count, QUERY_BLOCK)
    width = heads * HEAD_DIM
    rest = 2 * kv_heads * HEAD_DIM
    return pl.pallas_call(
        functools.partial(attend_back_kernel, kv_heads, group),
        grid_spec=pltpu.PrefetchScalarGridSpec(
            num_scalar_prefetch=1,
            grid=(count // block,),
            in_specs=[
                pl.BlockSpec((block, columns), lambda i, first: (i, 0)),
                pl.BlockSpec((count, columns), lambda i, first: (0, 0)),
                pl.BlockSpec((1, block), lambda i, first: (0, i)),
                pl.BlockSpec((count, 1), lambda i, first: (0, 0)),
                pl.BlockSpec((heads, block), lambda i, first: (0, i)),
                pl.BlockSpec((block, width), lambda i, first: (i, 0)),
                pl.BlockSpec((block, width), lambda i, first: (i, 0)),
                pl.BlockSpec((HALF, block), lambda i, first: (0, i)),
                pl.BlockSpec((HALF, block), lambda i, first: (0, i)),
                pl.BlockSpec((HALF, count), lambda i, first: (0, 0)),
                pl.BlockSpec((HALF, count), lambda i, first: (0, 0)),
            ],
            out_specs=[
                pl.BlockSpec((block, width), lambda i, first: (i, 0)),
                pl.BlockSpec((count, rest), lambda i, first: (0, 0)),
            ],
            scratch_shapes=[
                pltpu.VMEM((kv_heads, count, HEAD_DIM), jnp.bfloat16),
                pltpu.VMEM((kv_heads, count, HEAD_DIM), jnp.bfloat16),
                pltpu.VMEM((kv_heads, HEAD_DIM, count), jnp.bfloat16),
                pltpu.VMEM((kv_heads, count, HEAD_DIM), jnp.float32),
                pltpu.VMEM((kv_heads, count, HEAD_DIM), jnp.float32),
            ],
        ),
        out_shape=[
            jax.ShapeDtypeStruct((count, width), jnp.bfloat16),
            jax.ShapeDtypeStruct((count, rest), jnp.bfloat16),
        ],
        compiler_params=pltpu.CompilerParams(vmem_limit_bytes=VMEM_LIMIT),
        cost_estimate=pl.CostEstimate(
            flops=50 * 10**9, bytes_accessed=count * columns, transcendentals=0
        ),
        name="attend_back",
    )(
        first,
        heads_all,
        heads_all,
        start_row,
        pad_column,
        log_totals,
        attended,
        grad_attended,
        cosine,
        sine,
        cosine,
        sine,
    )


MESH = pl.DeviceIdType.MESH
CHUNK = 64


class Links:
    def __init__(self, dp_count, tensor_count, send, recv, local):
        self.chips, self.low = dp_count // 2, tensor_count // 2
        self.send, self.recv, self.local = send, recv, local
        self.used = 0
        self.used_local = 0
        self.unsent = []
        self.all_low = False
        dp_index, tensor_index = lax.axis_index("dp"), lax.axis_index("tensor")
        self.dp_index, self.tensor_index = dp_index, tensor_index
        self.p, self.c = dp_index // 2, dp_index % 2
        self.th, self.tl = tensor_index // self.low, tensor_index % self.low
        self.home = self.c == self.th
        self.away = self.c != self.th
        self.quarter = self.c * self.low + self.tl

    def at(self, p, c, th, tl):
        return (2 * p + c, th * self.low + tl)

    def chip(self, step):
        p = self.p
        moved = p
        for bit in (1, 2, 4):
            if step & bit:
                moved = moved + bit * (1 - 2 * ((p // bit) % 2))
        return moved

    def chip_peer(self, step):
        return self.at(self.chip(step), self.c, self.th, self.tl)

    def core_peer(self):
        return self.at(self.p, 1 - self.c, self.th, self.tl)

    def low_peer(self, step):
        return self.at(self.p, self.c, self.th, (self.tl + step) % self.low)

    def cross_peer(self):
        return self.at(self.p, 1 - self.c, 1 - self.th, self.tl)

    def turn_peer(self):
        home = self.home.astype(jnp.int32)
        return self.at(
            self.p,
            home * self.c + (1 - home) * (1 - self.c),
            home * (1 - self.th) + (1 - home) * self.th,
            self.tl,
        )

    def partner(self):
        return self.at(self.p, self.c, 1 - self.th, self.tl)

    def chip_steps(self):
        return (1, 2) if self.chips == 4 else tuple(range(1, self.chips))

    def enter(self):
        peers = [self.core_peer(), self.cross_peer(), self.partner()]
        peers += [self.chip_peer(step) for step in self.chip_steps()]
        peers += [self.low_peer(step) for step in range(1, self.low)]
        if self.all_low:
            peers += [
                self.at(self.p, self.c, 1 - self.th, (self.tl + step) % self.low)
                for step in range(1, self.low)
            ]
        barrier = pltpu.get_barrier_semaphore()
        for peer in peers:
            pl.semaphore_signal(barrier, inc=1, device_id=peer, device_id_type=MESH)
        pl.semaphore_wait(barrier, len(peers))

    def copy(self, source, target, peer, when=None):
        slot = self.used
        self.used += 1

        def make():
            return pltpu.make_async_remote_copy(
                src_ref=source,
                dst_ref=target,
                send_sem=self.send.at[slot],
                recv_sem=self.recv.at[slot],
                device_id=peer,
                device_id_type=MESH,
            )

        item = Item(make, when)
        self.unsent.append(item)
        return item

    def local_slot(self):
        self.used_local += 1
        return self.used_local - 1

    def keep(self, source, target, when=None):
        slot = self.used_local
        self.used_local += 1
        return Item(lambda: pltpu.make_async_copy(source, target, self.local.at[slot]), when)

    def drop(self, items):
        self.unsent = [item for item in self.unsent if item not in items]

    def leave(self):
        for item in self.unsent:
            item.sent()


class Item:
    def __init__(self, make, when):
        self.make, self.when = make, when

    def run(self, action):
        if self.when is None:
            action(self.make())
        else:
            pl.when(self.when)(lambda: action(self.make()))

    def start(self):
        self.run(lambda copy: copy.start())

    def arrived(self):
        self.run(lambda copy: copy.wait_recv())

    def sent(self):
        self.run(lambda copy: copy.wait_send())

    def done(self):
        self.run(lambda copy: copy.wait())


class UnitGather:
    def __init__(self, links, shard, unit):
        rows = shard.shape[0]
        mine = unit.at[pl.ds(links.c * rows, rows)]
        self.first = links.copy(shard, mine, links.turn_peer())
        self.second = links.copy(shard, mine, links.cross_peer(), links.away)
        self.own = links.keep(shard, mine, links.home)

    def turn(self):
        self.first.start()
        self.second.start()
        self.own.start()

    def settle_unit(self):
        self.first.arrived()
        self.second.arrived()
        self.own.done()


class WeightGather:
    def __init__(self, links, shard, full):
        self.links, self.shard, self.full = links, shard, full
        rows = shard.shape[0]
        self.rows = rows
        mine = full.at[pl.ds(links.dp_index * rows, rows)]
        self.first = links.copy(shard, mine, links.turn_peer())
        self.second = links.copy(shard, mine, links.cross_peer(), links.away)
        self.own = links.keep(shard, mine, links.home)
        unit = 2 * rows
        self.direct = []
        self.forward = []
        here = full.at[pl.ds(links.p * unit, unit)]
        for step in links.chip_steps():
            self.direct.append(links.copy(here, here, links.chip_peer(step)))
        if links.chips == 4:
            top = full.at[pl.ds(links.chip(2) * unit, rows)]
            bottom = full.at[pl.ds(links.chip(1) * unit + rows, rows)]
            self.forward.append(links.copy(top, top, links.chip_peer(1)))
            self.forward.append(links.copy(bottom, bottom, links.chip_peer(2)))

    def turn(self):
        self.first.start()
        self.second.start()
        self.own.start()

    def settle_unit(self):
        self.first.arrived()
        self.second.arrived()
        self.own.done()

    def spread(self):
        self.settle_unit()
        self.spread_unit()

    def spread_unit(self):
        for item in self.direct:
            item.start()

    def pass_on(self):
        for item in self.direct:
            item.arrived()
        for item in self.forward:
            item.start()

    def finish(self):
        for item in self.forward:
            item.arrived()


class RowGather:
    def __init__(self, links, full, rows):
        self.links = links
        mine = full.at[pl.ds(links.quarter * rows, rows)]
        self.to_core = links.copy(mine, mine, links.core_peer())
        self.to_low = []
        self.onward = []
        for step in range(1, links.low):
            self.to_low.append(links.copy(mine, mine, links.low_peer(step)))
            came = (links.tl + links.low - step) % links.low
            block = full.at[pl.ds((links.c * links.low + came) * rows, rows)]
            self.onward.append(links.copy(block, block, links.core_peer()))

    def start(self):
        for item in self.to_low:
            item.start()
        self.to_core.start()

    def pass_on(self):
        for arriving, item in zip(self.to_low, self.onward):
            arriving.arrived()
            item.start()

    def finish(self):
        self.to_core.arrived()
        for item in self.onward:
            item.arrived()


class RowScatter:
    def __init__(self, links, partial, mine, others, sums, arrivals, rows):
        self.links, self.rows = links, rows
        self.mine, self.others, self.sums, self.arrivals = mine, others, sums, arrivals
        low = links.low
        self.load = links.keep(partial.at[pl.ds(links.c * low * rows, low * rows)], mine)
        self.swap = links.copy(
            partial.at[pl.ds((1 - links.c) * low * rows, low * rows)], others, links.core_peer()
        )
        self.sends = [
            links.copy(sums.at[step - 1], arrivals.at[step - 1], links.low_peer(step))
            for step in range(1, low)
        ]

    def start(self):
        self.swap.start()
        self.load.start()

    def send_sums(self):
        self.load.done()
        self.swap.arrived()
        for step in range(1, self.links.low):
            base = ((self.links.tl + step) % self.links.low) * self.rows

            @pl.loop(0, self.rows // CHUNK)
            def _(i, base=base, step=step):
                span = pl.ds(pl.multiple_of(base + i * CHUNK, CHUNK), CHUNK)
                total = self.mine[span].astype(jnp.float32) + self.others[span].astype(jnp.float32)
                self.sums[step - 1, pl.ds(pl.multiple_of(i * CHUNK, CHUNK), CHUNK)] = total.astype(jnp.bfloat16)

            self.sends[step - 1].start()

    def collect(self, use):
        for item in self.sends:
            item.arrived()
        base = self.links.tl * self.rows

        @pl.loop(0, self.rows // CHUNK)
        def _(i):
            at = pl.multiple_of(i * CHUNK, CHUNK)
            span = pl.ds(pl.multiple_of(base + at, CHUNK), CHUNK)
            total = self.mine[span].astype(jnp.float32) + self.others[span].astype(jnp.float32)
            for step in range(1, self.links.low):
                total = total + self.arrivals[step - 1, pl.ds(at, CHUNK)].astype(jnp.float32)
            use(pl.ds(at, CHUNK), total)


def scatter_scratch(low, rows, width):
    return [
        pltpu.VMEM((low * rows, width), jnp.bfloat16),
        pltpu.VMEM((low * rows, width), jnp.bfloat16),
        pltpu.VMEM((low - 1, rows, width), jnp.bfloat16),
        pltpu.VMEM((low - 1, rows, width), jnp.bfloat16),
    ]


def semaphores(count, local_count):
    return [
        pltpu.SemaphoreType.DMA((count,)),
        pltpu.SemaphoreType.DMA((count,)),
        pltpu.SemaphoreType.DMA((local_count,)),
    ]


def anywhere(count):
    return [pl.BlockSpec(memory_space=pl.ANY)] * count


def in_vmem(count):
    return [pl.BlockSpec(memory_space=pltpu.VMEM)] * count


def link_params(number):
    return pltpu.CompilerParams(
        collective_id=number, has_side_effects=True, vmem_limit_bytes=LINK_VMEM_LIMIT
    )


ADD_ROWS = 32


def cut(columns, most):
    half = columns // 2
    return half if columns > most and half % 128 == 0 else columns


def product(left, right, out, left_dim, right_dim, rows, columns, finish=None, extra=(), extra_out=()):
    depth = left.shape[left_dim]
    count, width = out.shape
    rows, columns = math.gcd(count, rows), cut(width, columns)

    def body(left_ref, right_ref, *refs):
        value = times(left_ref[...], right_ref[...], left_dim, right_dim)
        if finish is None:
            refs[0][...] = value.astype(refs[0].dtype)
        else:
            finish(value, *refs)

    def block(shape, index):
        return pl.BlockSpec(shape, index)

    left_spec = (
        block((rows, depth), lambda j, i: (i, 0)) if left_dim == 1 else block((depth, rows), lambda j, i: (0, i))
    )
    right_spec = (
        block((columns, depth), lambda j, i: (j, 0))
        if right_dim == 1
        else block((depth, columns), lambda j, i: (0, j))
    )
    whole = block((rows, columns), lambda j, i: (i, j))
    extra_specs = [
        whole if ref.shape[1] == width else block((rows, ref.shape[1]), lambda j, i: (i, 0)) for ref in extra
    ]
    pltpu.emit_pipeline(
        body,
        grid=(width // columns, count // rows),
        in_specs=[left_spec, right_spec] + extra_specs,
        out_specs=[whole] * (1 + len(extra_out)),
    )(left, right, *extra, out, *extra_out)


def row_loop(rows, body):
    @pl.loop(0, rows // ADD_ROWS)
    def _(i):
        body(pl.ds(pl.multiple_of(i * ADD_ROWS, ADD_ROWS), ADD_ROWS))


class WeightScatter:
    def __init__(self, links, partial, result, inbox, turned, sums, leaving, stage):
        self.links, self.partial, self.result = links, partial, result
        self.inbox, self.turned, self.sums, self.leaving = inbox, turned, sums, leaving
        rows = partial.shape[0] // (2 * links.chips)
        self.rows = rows
        width = partial.shape[1]
        self.stage = [stage.at[i, pl.ds(0, rows), pl.ds(0, width)] for i in range(3)]
        self.both = links.chips == 4
        self.loads = [
            links.local_slot() for _ in range(3)
        ]
        if self.both:
            x_peer, y_peer = links.chip_peer(1), links.chip_peer(2)
            self.before = [
                links.copy(self.part(3, 0), inbox.at[0], x_peer),
                links.copy(self.part(3, 1), inbox.at[1], y_peer),
            ]
            self.direct = [
                links.copy(self.part(1, 0), inbox.at[2], x_peer),
                links.copy(self.part(2, 1), inbox.at[3], y_peer),
            ]
            self.summed = [
                links.copy(sums.at[0], inbox.at[4], y_peer),
                links.copy(sums.at[1], inbox.at[5], x_peer),
            ]
            self.arrivals = ((2, 4), (5, 3))
        else:
            self.before, self.summed, self.direct = [], [], []
            for step in links.chip_steps():
                for half in range(2):
                    at = 2 * (step - 1) + half
                    self.direct.append(
                        links.copy(self.part(step, half), inbox.at[at], links.chip_peer(step))
                    )
            self.arrivals = tuple(
                tuple(2 * (step - 1) + half for step in links.chip_steps()) for half in range(2)
            )
        home_int = links.home.astype(jnp.int32)
        self.first = links.copy(
            leaving.at[0],
            turned.at[0],
            links.at(
                links.p,
                home_int * (1 - links.c) + (1 - home_int) * links.c,
                home_int * links.th + (1 - home_int) * (1 - links.th),
                links.tl,
            ),
        )
        self.second = links.copy(leaving.at[1], turned.at[1], links.cross_peer(), links.away)

    def part(self, step, half):
        start = (2 * self.links.chip(step) + half) * self.rows
        return self.partial.at[pl.ds(start, self.rows)]

    def load(self, sources):
        copies = [
            pltpu.make_async_copy(source, stage, self.links.local.at[slot])
            for source, stage, slot in zip(sources, self.stage, self.loads)
        ]
        for copy in copies:
            copy.start()
        for copy in copies:
            copy.wait()

    def start(self, which):
        for item in getattr(self, which):
            item.start()

    def arrived(self, which):
        for item in getattr(self, which):
            item.arrived()

    def add_before(self):
        if not self.both:
            self.start("direct")
            return
        self.arrived("before")
        self.start("direct")
        for index, part in ((0, self.part(2, 0)), (1, self.part(1, 1))):
            self.load([part, self.inbox.at[index]])

            def body(span, index=index):
                total = self.stage[0][span].astype(jnp.float32) + self.stage[1][span].astype(jnp.float32)
                self.sums[index, span] = total.astype(jnp.bfloat16)

            row_loop(self.rows, body)
            self.summed[index].start()

    def turn(self):
        self.reduce()
        self.send_turned()

    def send_turned(self):
        self.first.start()
        self.second.start()

    def reduce(self):
        links = self.links
        for half in range(2):
            sources = [self.part(0, half)] + [self.inbox.at[at] for at in self.arrivals[half]]
            kept = links.c == half
            if len(sources) == 3:
                self.load(sources)

                def body(span, half=half, kept=kept):
                    total = self.stage[0][span].astype(jnp.float32)
                    total = total + self.stage[1][span].astype(jnp.float32)
                    self.settle(span, total + self.stage[2][span].astype(jnp.float32), kept)

                row_loop(self.rows, body)
            else:
                self.fold(sources, kept)

    def fold(self, sources, kept):
        rows = self.rows
        total = self.total
        self.load(sources[:1])
        row_loop(rows, lambda span: total.__setitem__(span, self.stage[0][span].astype(jnp.float32)))
        for source in sources[1:]:
            self.load([source])

            def body(span):
                total[span] = total[span] + self.stage[0][span].astype(jnp.float32)

            row_loop(rows, body)
        row_loop(rows, lambda span: self.settle(span, total[span], kept))

    def settle(self, span, total, kept):
        low = total.astype(jnp.bfloat16)
        links = self.links

        @pl.when(kept & links.home)
        def _():
            self.result[span] = total

        @pl.when(kept & links.away)
        def _():
            self.leaving[0, span] = low

        @pl.when(jnp.logical_not(kept) & links.home)
        def _():
            self.leaving[0, span] = low

        @pl.when(jnp.logical_not(kept) & links.away)
        def _():
            self.leaving[1, span] = low

    def finish(self):
        links = self.links
        self.first.arrived()
        self.second.arrived()

        @pl.when(links.home)
        def _():
            def body(span):
                self.result[span] = self.result[span] + self.turned[0, span].astype(jnp.float32)

            row_loop(self.rows, body)

        @pl.when(links.away)
        def _():
            def body(span):
                self.result[span] = self.turned[1, span].astype(jnp.float32) + self.turned[0, span].astype(
                    jnp.float32
                )

            row_loop(self.rows, body)


def weight_scatter_scratch(chips, rows, width):
    return [pltpu.VMEM((2, rows, width), jnp.bfloat16)] * 3


def inbox_shape(chips, rows, width):
    count = 6 if chips == 4 else 2 * (chips - 1)
    return jax.ShapeDtypeStruct((count, rows, width), jnp.bfloat16)


def scatter_shapes(chips, partial):
    rows = partial.shape[0] // (2 * chips)
    width = partial.shape[1]
    return rows, width


def tail_kernel(
    dp_count,
    tensor_count,
    gain_column,
    partial,
    tokens_all,
    grad_up,
    grad_rows,
    attended,
    normed,
    grad_heads,
    gain_parts,
    grad_residual_ref,
    gain_ref,
    input_ref,
    up_ref,
    output_ref,
    first_ref,
    up_in,
    output_in,
    first_in,
    grad_output,
    grad_first,
    *scratch,
):
    up_work, output_work, first_work = (scratch[3 * i : 3 * i + 3] for i in range(3))
    stage, own_ref, leaving, crossed, mine, others, sums, arrivals, gains_out, gains_in, total = scratch[9:20]
    links = Links(dp_count, tensor_count, *scratch[20:])
    links.all_low = True
    rows = own_ref.shape[0]
    load_own = links.keep(tokens_all.at[pl.ds(links.quarter * rows, rows)], own_ref)
    scatter = RowScatter(links, partial, mine, others, sums, arrivals, rows)
    crossing = links.copy(leaving, crossed, links.cross_peer(), links.away)
    weights = []
    for grad, result, inbox, work in (
        (grad_up, up_ref, up_in, up_work),
        (grad_output, output_ref, output_in, output_work),
        (grad_first, first_ref, first_in, first_work),
    ):
        turned, added, turning = work
        made = WeightScatter(links, grad, result, inbox, turned, added, turning, stage)
        made.total = None if made.both else total.at[pl.ds(0, made.rows), pl.ds(0, grad.shape[1])]
        weights.append(made)
    up, output, first = weights
    gain_sends = []
    for step in range(1, tensor_count):
        other = (links.tensor_index + step) % tensor_count
        gain_sends.append(
            links.copy(gains_out, gains_in.at[step - 1], links.at(links.p, links.c, other // links.low, other % links.low))
        )

    links.enter()
    scatter.start()
    load_own.start()
    up.start("before")
    scatter.send_sums()
    load_own.done()

    def finish(value, parts_ref, out_ref):
        columns = value.shape[1]
        out_ref[:, : columns - 128] = value[:, : columns - 128].astype(jnp.bfloat16)
        out_ref[:, columns - 128 :] = (value[:, columns - 128 :] + parts_ref[...]).astype(jnp.bfloat16)

    product(normed, grad_heads, grad_first, 0, 0, 512, 1024, finish, (gain_parts,))
    up.add_before()
    product(grad_rows, attended, grad_output, 0, 0, 512, 1024)

    def use(span, grad_normed):
        own = own_ref[span].astype(jnp.float32)
        root = lax.rsqrt(jnp.mean(own * own, axis=-1, keepdims=True) + epsilon)
        unit = own * root
        scaled = grad_normed * gain_ref[...]
        grad = grad_residual_ref[span] + root * (
            scaled - unit * jnp.mean(scaled * unit, axis=-1, keepdims=True)
        )
        input_ref[span] = grad
        leaving[span] = grad.astype(jnp.bfloat16)

    scatter.collect(use)
    crossing.start()
    up.arrived("direct")
    up.arrived("summed")
    first.start("before")
    up.turn()
    first.add_before()
    output.start("before")
    first.arrived("direct")
    first.arrived("summed")
    first.turn()
    output.add_before()
    crossing.arrived()

    @pl.when(links.away)
    def _():
        def body(span):
            input_ref[span] = crossed[span].astype(jnp.float32)

        row_loop(rows, body)

    output.arrived("direct")
    output.arrived("summed")
    output.turn()
    up.finish()
    first.finish()
    width = first_ref.shape[1]
    gains_out[...] = first_ref[:, width - 128 :]
    for item in gain_sends:
        item.start()
    output.finish()
    for item in gain_sends:
        item.arrived()
    summed = gains_out[...]
    for step in range(1, tensor_count):
        summed = summed + gains_in[step - 1]
    column = width - 128 + lax.broadcasted_iota(jnp.int32, summed.shape, 1)
    first_ref[:, width - 128 :] = jnp.where(column >= gain_column, summed, gains_out[...])
    links.leave()


def tail(
    dp_count,
    tensor_count,
    gain_column,
    partial,
    tokens_all,
    grad_up,
    grad_rows,
    attended,
    normed,
    grad_heads,
    gain_parts,
    grad_residual,
    gain,
):
    rows, width = grad_residual.shape
    low, chips = tensor_count // 2, dp_count // 2
    features = grad_up.shape[0]
    partials = [
        grad_up,
        jax.ShapeDtypeStruct((features, attended.shape[1]), jnp.bfloat16),
        jax.ShapeDtypeStruct((features, grad_heads.shape[1]), jnp.bfloat16),
    ]
    shapes = [scatter_shapes(chips, grad) for grad in partials]
    widest = max(columns for _, columns in shapes)
    most = shapes[0][0]
    scratch = []
    for block, columns in shapes:
        scratch += weight_scatter_scratch(chips, block, columns)
    scratch += [pltpu.VMEM((3, most, widest), jnp.bfloat16)]
    scratch += [pltpu.VMEM((rows, width), jnp.bfloat16)] * 3
    scratch += scatter_scratch(low, rows, width)
    scratch += [
        pltpu.VMEM((most, 128), jnp.float32),
        pltpu.VMEM((tensor_count - 1, most, 128), jnp.float32),
        pltpu.VMEM((most, widest) if chips != 4 else (8, 128), jnp.float32),
    ]
    return pl.pallas_call(
        functools.partial(tail_kernel, dp_count, tensor_count, gain_column),
        out_shape=[jax.ShapeDtypeStruct((rows, width), jnp.float32)]
        + [jax.ShapeDtypeStruct(shape, jnp.float32) for shape in shapes]
        + [inbox_shape(chips, *shape) for shape in shapes]
        + partials[1:],
        in_specs=anywhere(8) + in_vmem(2),
        out_specs=in_vmem(4) + anywhere(5),
        scratch_shapes=scratch + semaphores(96, 24),
        compiler_params=link_params(3),
        name="tail",
    )(
        partial,
        tokens_all,
        grad_up,
        grad_rows,
        attended,
        normed,
        grad_heads,
        gain_parts,
        grad_residual,
        gain,
    )[:4]


def gather_first_kernel(
    dp_count, tensor_count, tokens, first, output, gate, tokens_all, first_full, output_full, gate_unit, *sems
):
    links = Links(dp_count, tensor_count, *sems)
    rows = tokens.shape[0]
    mine = tokens_all.at[pl.ds(links.tensor_index * rows, rows)]
    crossing = links.copy(tokens, mine, links.cross_peer(), links.away)
    staying = links.keep(tokens, mine, links.home)
    gather_tokens = RowGather(links, tokens_all, rows)
    weights = [
        WeightGather(links, shard, full)
        for shard, full in ((first, first_full), (output, output_full))
    ]
    weights.append(UnitGather(links, gate, gate_unit))
    links.enter()
    weights[0].turn()
    crossing.start()
    staying.start()

    @pl.when(links.home)
    def _():
        staying.make().wait()
        gather_tokens.start()

    weights[0].spread()
    weights[1].turn()

    @pl.when(links.away)
    def _():
        crossing.make().wait_recv()
        gather_tokens.start()

    weights[1].spread()
    weights[2].turn()
    weights[0].pass_on()
    gather_tokens.pass_on()
    weights[1].pass_on()
    weights[0].finish()
    gather_tokens.finish()
    weights[1].finish()
    weights[2].settle_unit()
    links.leave()


def gather_first(dp_count, tensor_count, tokens, first, output, gate):
    def full(shard, times):
        return jax.ShapeDtypeStruct((shard.shape[0] * times, shard.shape[1]), shard.dtype)

    return pl.pallas_call(
        functools.partial(gather_first_kernel, dp_count, tensor_count),
        out_shape=[
            full(tokens, tensor_count),
            full(first, dp_count),
            full(output, dp_count),
            full(gate, 2),
        ],
        in_specs=in_vmem(4),
        out_specs=anywhere(4),
        scratch_shapes=semaphores(64, 8),
        compiler_params=link_params(0),
        name="gather_first",
    )(tokens, first, output, gate)


def middle_kernel(
    dp_count,
    tensor_count,
    moved_units,
    partial,
    tokens_all,
    cot,
    up,
    up_turned,
    up_crossed,
    down,
    gate_unit,
    *rest,
):
    gate_units, rest = rest[:moved_units], rest[moved_units:]
    gain_ref, residual_ref, normed_all, cot_all, up_full, down_full, gate_full = rest[:7]
    gate_values, up_values, hidden = rest[7:10]
    own, normed, mine, others, sums, arrivals = rest[10:16]
    links = Links(dp_count, tensor_count, *rest[16:])
    rows = cot.shape[0]
    scatter = RowScatter(links, partial, mine, others, sums, arrivals, rows)
    gather_normed = RowGather(links, normed_all, rows)
    gather_cot = RowGather(links, cot_all, rows)
    gate_gather = WeightGather(links, up, gate_full)
    up_gather = WeightGather(links, up, up_full)
    down_gather = WeightGather(links, down, down_full)
    shard = up.shape[0]
    here = up_full.at[pl.ds(links.dp_index * shard, shard)]
    beside = up_full.at[pl.ds((2 * links.p + 1 - links.c) * shard, shard)]
    quarter = pl.ds(links.quarter * rows, rows)
    placements = [
        links.keep(up, here, links.home),
        links.keep(up_turned, beside, links.home),
        links.keep(up_turned, here, links.away),
        links.keep(up_crossed, beside, links.away),
    ]
    gate_placements = [
        links.keep(unit, gate_full.at[pl.ds(links.chip(step) * 2 * shard, 2 * shard)])
        for step, unit in zip((0,) + links.chip_steps(), (gate_unit,) + tuple(gate_units))
    ]
    cot_crossing = links.copy(cot, cot_all.at[pl.ds(links.tensor_index * rows, rows)], links.cross_peer(), links.away)
    cot_staying = links.keep(cot, cot_all.at[quarter], links.home)
    load = links.keep(tokens_all.at[quarter], own)
    store = links.keep(normed, normed_all.at[quarter])
    links.drop([up_gather.first, up_gather.second, gate_gather.first, gate_gather.second] + gate_gather.direct)
    links.enter()
    scatter.start()
    load.start()
    for item in gate_placements + placements:
        item.start()
    for item in gate_placements:
        item.done()
    for item in gate_gather.forward:
        item.start()
    for item in placements:
        item.done()
    scatter.send_sums()
    up_gather.spread_unit()
    down_gather.turn()
    cot_staying.start()
    load.done()

    def use(span, total):
        residual = own[span].astype(jnp.float32) + total
        residual_ref[span] = residual
        root = lax.rsqrt(jnp.mean(residual * residual, axis=-1, keepdims=True) + epsilon)
        normed[span] = (residual * root * gain_ref[...]).astype(jnp.bfloat16)

    scatter.collect(use)
    store.start()
    store.done()
    gather_normed.start()
    down_gather.settle_unit()
    cot_crossing.start()
    up_gather.pass_on()
    down_gather.spread_unit()
    gate_gather.finish()
    gather_normed.pass_on()
    cot_staying.done()
    cot_crossing.arrived()
    gather_cot.start()
    up_gather.finish()
    gather_normed.finish()
    product(normed_all, gate_full, gate_values, 1, 0, 512, 1024)
    down_gather.pass_on()
    gather_cot.pass_on()

    def finish(up, gate_ref, up_ref, hidden_ref):
        gate = gate_ref[...]
        up_ref[...] = up
        hidden_ref[...] = (gate * jax.nn.sigmoid(gate) * up).astype(jnp.bfloat16)

    product(normed_all, up_full, up_values, 1, 0, 256, 1024, finish, (gate_values,), (hidden,))
    down_gather.finish()
    gather_cot.finish()
    links.leave()


def middle(
    dp_count, tensor_count, partial, tokens_all, cot, up, up_turned, up_crossed, down, gate_unit, gate_units, gain
):
    rows, width = cot.shape
    low = tensor_count // 2

    def full(shard, times):
        return jax.ShapeDtypeStruct((shard.shape[0] * times, shard.shape[1]), shard.dtype)

    return pl.pallas_call(
        functools.partial(middle_kernel, dp_count, tensor_count, len(gate_units)),
        out_shape=[
            jax.ShapeDtypeStruct((rows, width), jnp.float32),
            full(cot, tensor_count),
            full(cot, tensor_count),
            full(up, dp_count),
            full(down, dp_count),
            full(gate_unit, dp_count // 2),
            jax.ShapeDtypeStruct((rows * tensor_count, up.shape[1]), jnp.float32),
            jax.ShapeDtypeStruct((rows * tensor_count, up.shape[1]), jnp.float32),
            jax.ShapeDtypeStruct((rows * tensor_count, up.shape[1]), jnp.bfloat16),
        ],
        in_specs=anywhere(2) + in_vmem(len(gate_units) + 7),
        out_specs=in_vmem(1) + anywhere(8),
        scratch_shapes=[pltpu.VMEM((rows, width), jnp.bfloat16)] * 2
        + scatter_scratch(low, rows, width)
        + semaphores(64, 24),
        compiler_params=link_params(1),
        name="middle",
    )(partial, tokens_all, cot, up, up_turned, up_crossed, down, gate_unit, *gate_units, gain)


def turn_back_kernel(
    dp_count,
    tensor_count,
    partial,
    cot_all,
    grad_down,
    normed_ffn,
    gate_signal,
    up_signal,
    hidden,
    down_full,
    residual_ref,
    gain_ref,
    grad_residual_ref,
    gain_part_ref,
    down_ref,
    gate_ref,
    gate_turning,
    grad_rows,
    down_in,
    gate_in,
    grad_gate,
    grad_up,
    down_part,
    own,
    low_grad,
    turned,
    added,
    turning,
    gate_added,
    stage,
    total_ref,
    mine,
    others,
    sums,
    arrivals,
    *sems,
):
    links = Links(dp_count, tensor_count, *sems)
    rows = residual_ref.shape[0]
    down = WeightScatter(links, grad_down, down_ref, down_in, turned, added, turning, stage)
    gate = WeightScatter(links, grad_gate, gate_ref, gate_in, turned, gate_added, gate_turning, stage)
    down.total = gate.total = total_ref
    links.drop([gate.first, gate.second])
    scatter = RowScatter(links, partial, mine, others, sums, arrivals, rows)
    gather = RowGather(links, grad_rows, rows)
    quarter = pl.ds(links.quarter * rows, rows)
    load = links.keep(cot_all.at[quarter], own)
    store = links.keep(low_grad, grad_rows.at[quarter])
    links.enter()
    scatter.start()
    load.start()
    down.start("before")
    scatter.send_sums()
    load.done()
    product(normed_ffn, gate_signal, grad_gate, 0, 0, 512, 1024)
    down.add_before()
    gain_part_ref[...] = jnp.zeros_like(gain_part_ref)

    def use(span, grad_normed):
        residual = residual_ref[span]
        root = lax.rsqrt(jnp.mean(residual * residual, axis=-1, keepdims=True) + epsilon)
        unit = residual * root
        gain_part_ref[...] += jnp.sum(grad_normed * unit, axis=0, keepdims=True)
        scaled = grad_normed * gain_ref[...]
        grad = own[span].astype(jnp.float32) + root * (
            scaled - unit * jnp.mean(scaled * unit, axis=-1, keepdims=True)
        )
        grad_residual_ref[span] = grad
        low_grad[span] = grad.astype(jnp.bfloat16)

    scatter.collect(use)
    store.start()
    store.done()
    gather.start()
    gate.start("before")
    down.arrived("direct")
    down.arrived("summed")
    down.reduce()
    down.send_turned()
    gate.add_before()
    product(normed_ffn, up_signal, grad_up, 0, 0, 512, 1024)
    gather.pass_on()
    product(hidden, down_full, down_part, 1, 1, 512, 1024)
    gate.arrived("direct")
    gate.arrived("summed")
    down.finish()
    gather.finish()
    gate.reduce()
    links.leave()


def turn_back(
    dp_count,
    tensor_count,
    partial,
    cot_all,
    grad_down,
    normed_ffn,
    gate_signal,
    up_signal,
    hidden,
    down_full,
    residual,
    gain,
):
    rows, width = residual.shape
    low, chips = tensor_count // 2, dp_count // 2
    block, columns = scatter_shapes(chips, grad_down)
    return pl.pallas_call(
        functools.partial(turn_back_kernel, dp_count, tensor_count),
        out_shape=[
            jax.ShapeDtypeStruct((rows, width), jnp.float32),
            jax.ShapeDtypeStruct((1, width), jnp.float32),
            jax.ShapeDtypeStruct((block, columns), jnp.float32),
            jax.ShapeDtypeStruct((block, columns), jnp.float32),
            jax.ShapeDtypeStruct((2, block, columns), jnp.bfloat16),
            jax.ShapeDtypeStruct((rows * tensor_count, width), jnp.bfloat16),
            inbox_shape(chips, block, columns),
            inbox_shape(chips, block, columns),
            jax.ShapeDtypeStruct(grad_down.shape, jnp.bfloat16),
            jax.ShapeDtypeStruct(grad_down.shape, jnp.bfloat16),
            jax.ShapeDtypeStruct((rows * tensor_count, width), jnp.bfloat16),
        ],
        in_specs=anywhere(8) + in_vmem(2),
        out_specs=in_vmem(5) + anywhere(6),
        scratch_shapes=[pltpu.VMEM((rows, width), jnp.bfloat16)] * 2
        + weight_scatter_scratch(chips, block, columns)
        + [
            pltpu.VMEM((2, block, columns), jnp.bfloat16),
            pltpu.VMEM((3, block, columns), jnp.bfloat16),
            pltpu.VMEM((block, columns) if chips != 4 else (8, 128), jnp.float32),
        ]
        + scatter_scratch(low, rows, width)
        + semaphores(64, 24),
        compiler_params=link_params(2),
        name="turn_back",
    )(partial, cot_all, grad_down, normed_ffn, gate_signal, up_signal, hidden, down_full, residual, gain)


def starts_of(positions, length_row):
    ends = jnp.cumsum(length_row)
    inside = positions[:, None] >= ends[None, :]
    return jnp.sum(jnp.where(inside, length_row[None, :], 0), axis=1)


def rotary_tables(positions):
    frequency = jnp.exp(
        jnp.arange(HALF, dtype=jnp.float32) * (-2.0 * math.log(rope_base) / HEAD_DIM)
    )
    angles = positions.astype(jnp.float32)[None, :] * frequency[:, None]
    return (jnp.cos(angles), jnp.sin(angles))


def per_device(
    dp_count,
    tensor_count,
    tokens,
    attention_gain,
    query_weight,
    key_weight,
    value_weight,
    output_weight,
    feedforward_gain,
    gate_weight,
    up_weight,
    down_weight,
    cotangent,
    lengths,
    storage_order,
    sequence_order,
    pad_mask,
):
    place = Placement(dp_count, tensor_count)
    count = storage_order.shape[0]
    rows = count // tensor_count
    kv_heads = key_weight.shape[1] // HEAD_DIM
    heads = query_weight.shape[1] // HEAD_DIM
    group = heads // kv_heads
    head_columns = (heads + 2 * kv_heads) * HEAD_DIM

    hidden_units = gate_weight.shape[1]
    hidden_padded = -(-hidden_units // 128) * 128
    output_padded = -(-heads * HEAD_DIM // 128) * 128
    first_padded = -(-(head_columns + 2) // 128) * 128

    def wide(array, columns):
        return jnp.pad(array, ((0, 0), (0, columns - array.shape[1])))

    gate_shard = wide(gate_weight, hidden_padded)
    up_shard = wide(up_weight, hidden_padded)
    down_shard = wide(down_weight.T, hidden_padded)
    tokens_all, first_weight, output_turned, gate_unit = gather_first(
        dp_count,
        tensor_count,
        tokens,
        wide(
            jnp.concatenate(
                [query_weight, key_weight, value_weight, attention_gain[:, None], feedforward_gain[:, None]],
                axis=1,
            ),
            first_padded,
        ),
        wide(output_weight.T, output_padded),
        gate_shard,
    )
    output_turned = output_turned[:, : heads * HEAD_DIM]
    late_up = after(up_shard, tokens_all)
    up_turned = place.home_turn(late_up)
    up_crossed = place.cross(late_up)
    steps = (1, 2) if place.chips == 4 else tuple(range(1, place.chips))
    gate_units = [place.to_chip(gate_unit, step) for step in steps]

    numbers = jnp.concatenate([storage_order, pad_mask, lengths[0]])
    numbers = jnp.where(place.home, numbers, place.to_core(numbers))
    pad_column = numbers[count : 2 * count][:, None]
    length_row = numbers[2 * count :]
    order = numbers[:count]

    places = jnp.arange(count, dtype=jnp.int32)
    starts = starts_of(places, length_row)
    cosine, sine = rotary_tables(places - starts)
    cosine_stored, sine_stored = rotary_tables(order - starts_of(order, length_row))
    to_sequence = (places[:, None] == order[None, :]).astype(jnp.bfloat16)
    to_storage = (order[:, None] == places[None, :]).astype(jnp.bfloat16)
    first_blocks = starts[:: math.gcd(count, QUERY_BLOCK)] // KEY_BLOCK
    start_row = starts[None, :]

    attention_scale = first_weight[:, head_columns].astype(jnp.float32)[None, :]
    feedforward_scale = first_weight[:, head_columns + 1].astype(jnp.float32)[None, :]
    normed, heads_stored, token_roots = project(
        tokens_all,
        attention_scale,
        first_weight,
        cosine_stored,
        sine_stored,
        heads + kv_heads,
        head_columns,
    )
    heads_all = contract(to_sequence, heads_stored, 1, 0, jnp.bfloat16)
    attended, log_totals = attend(first_blocks, heads_all, start_row, pad_column, kv_heads, group)
    attended_stored = contract(to_storage, attended, 1, 0, jnp.bfloat16)

    residual, normed_ffn, cot_all, up_full, down_turned, gate_full, gate_values, up_values, hidden = middle(
        dp_count,
        tensor_count,
        contract(attended_stored, output_turned, 1, 1, jnp.bfloat16),
        tokens_all,
        cotangent,
        up_shard,
        up_turned,
        up_crossed,
        down_shard,
        gate_unit,
        gate_units,
        feedforward_scale,
    )
    sigmoid = jax.nn.sigmoid(gate_values)

    def leave(own):
        arrived = place.cross(own.astype(jnp.bfloat16)).astype(jnp.float32)
        return jnp.where(place.home, own, arrived)

    grad_hidden = contract(cot_all, down_turned, 1, 0)
    grad_gate = (grad_hidden * up_values * sigmoid * (1.0 + gate_values * (1.0 - sigmoid))).astype(
        jnp.bfloat16
    )
    grad_up = (grad_hidden * gate_values * sigmoid).astype(jnp.bfloat16)
    grad_part = (contract(grad_gate, gate_full, 1, 1) + contract(grad_up, up_full, 1, 1)).astype(
        jnp.bfloat16
    )
    turned_back = turn_back(
        dp_count,
        tensor_count,
        grad_part,
        cot_all,
        contract(cot_all, hidden, 0, 0, jnp.bfloat16),
        normed_ffn,
        grad_gate,
        grad_up,
        hidden,
        down_turned,
        residual,
        feedforward_scale,
    )
    grad_residual, feedforward_part, down_grad, gate_grad, gate_turning, grad_rows = turned_back[:6]
    up_part, down_part = turned_back[9:]
    gate_turned = place.away_turn(gate_turning[0])
    gate_crossed = place.cross(gate_turning[1])

    pairs = place.pair_rows(down_part)
    grad_attended = contract(grad_rows, output_turned, 1, 0, jnp.bfloat16)
    grad_attended = contract(to_sequence, grad_attended, 1, 0, jnp.bfloat16)
    grad_attended = after(grad_attended, *pairs)
    grad_query, grad_rest = attend_back(
        first_blocks,
        heads_all,
        start_row,
        pad_column,
        log_totals,
        attended,
        grad_attended,
        cosine,
        sine,
        kv_heads,
        group,
    )
    spare = jnp.zeros((count, first_padded - head_columns), jnp.bfloat16)
    grad_heads = contract(
        to_storage, jnp.concatenate([grad_query, grad_rest, spare], axis=1), 1, 0, jnp.bfloat16
    )
    grad_normed_part = contract(grad_heads, first_weight, 1, 1)
    tokens_wide = tokens_all.astype(jnp.float32)
    attention_part = jnp.sum(grad_normed_part * (tokens_wide * token_roots), axis=0)
    layer_own = after(residual, grad_query) + place.sum_rows(pairs)
    layer_output = leave(layer_own)
    gate_turned, gate_crossed = lax.optimization_barrier((gate_turned, gate_crossed, grad_query))[:2]
    gate_grad = jnp.where(place.home, gate_grad, gate_crossed.astype(jnp.float32)) + gate_turned.astype(
        jnp.float32
    )
    gain_parts = jnp.stack([attention_part, feedforward_part[0]], axis=1)
    before = head_columns - (first_padded - 128)
    gain_parts = jnp.pad(gain_parts, ((0, 0), (before, 126 - before)))
    input_grad, up_grad, output_grad, first_grad = tail(
        dp_count,
        tensor_count,
        head_columns,
        after(grad_normed_part.astype(jnp.bfloat16), layer_own),
        tokens_all,
        up_part,
        grad_rows,
        wide(attended_stored, output_padded),
        normed,
        grad_heads,
        gain_parts,
        grad_residual,
        attention_scale,
    )
    query_columns = heads * HEAD_DIM
    key_columns = kv_heads * HEAD_DIM
    return (
        layer_output,
        input_grad,
        first_grad[:, head_columns],
        first_grad[:, :query_columns],
        first_grad[:, query_columns : query_columns + key_columns],
        first_grad[:, query_columns + key_columns : head_columns],
        output_grad[:, :query_columns].T,
        first_grad[:, head_columns + 1],
        gate_grad[:, :hidden_units],
        up_grad[:, :hidden_units],
        down_grad[:, :hidden_units].T,
    )


def solution(mesh):
    placed = (
        P(("dp", "tensor"), None),
        P("dp"),
        P("dp", "tensor"),
        P("dp", "tensor"),
        P("dp", "tensor"),
        P("tensor", "dp"),
        P("dp"),
        P("dp", "tensor"),
        P("dp", "tensor"),
        P("tensor", "dp"),
        P(("dp", "tensor"), None),
        P("dp", None),
        P("dp"),
        P("dp"),
        P("dp"),
    )
    return jax.shard_map(
        functools.partial(per_device, mesh.shape["dp"], mesh.shape["tensor"]),
        mesh=mesh,
        in_specs=placed,
        out_specs=(
            P(("dp", "tensor"), None),
            P(("dp", "tensor"), None),
            P("dp"),
            P("dp", "tensor"),
            P("dp", "tensor"),
            P("dp", "tensor"),
            P("tensor", "dp"),
            P("dp"),
            P("dp", "tensor"),
            P("dp", "tensor"),
            P("tensor", "dp"),
        ),
        check_vma=False,
    )
```

```python
import functools
import math

import jax
import jax.numpy as jnp
from jax import lax
from jax.experimental import pallas as pl
from jax.experimental.pallas import tpu as pltpu
from jax.sharding import PartitionSpec as P

HEAD_DIM = 80
HALF = HEAD_DIM // 2
QUERY_BLOCK = 128
KEY_BLOCK = 256
MASKED = -1e30
VMEM_LIMIT = 48 * 1024 * 1024
LINK_VMEM_LIMIT = 60 * 1024 * 1024

epsilon = 1e-05
rope_base = 10000.0
AXES = ("dp", "tensor")


def contract(left, right, left_dim, right_dim, out_type=jnp.float32):
    product = lax.dot_general(
        left,
        right,
        (((left_dim,), (right_dim,)), ((), ())),
        preferred_element_type=jnp.float32,
    )
    return product.astype(out_type)


def after(value, *earlier):
    return lax.optimization_barrier((value,) + earlier)[0]


def inverse_root(vectors):
    return lax.rsqrt(jnp.mean(vectors * vectors, axis=-1, keepdims=True) + epsilon)


class Placement:
    def __init__(self, dp_count, tensor_count):
        self.dp_count = dp_count
        self.tensor_count = tensor_count
        self.chips = dp_count // 2
        self.low = tensor_count // 2
        dp_index = lax.axis_index("dp")
        tensor_index = lax.axis_index("tensor")
        self.p = dp_index // 2
        self.c = dp_index % 2
        self.th = tensor_index // self.low
        self.tl = tensor_index % self.low
        self.home = self.c == self.th

    def move(self, array, target):
        pairs = []
        for p in range(self.chips):
            for c in range(2):
                for th in range(2):
                    for tl in range(self.low):
                        goal = target(p, c, th, tl)
                        if goal is not None:
                            pairs.append((self.flat(p, c, th, tl), self.flat(*goal)))
        return lax.ppermute(array, AXES, pairs)

    def flat(self, p, c, th, tl):
        return (2 * p + c) * self.tensor_count + th * self.low + tl

    def to_core(self, array):
        return self.move(array, lambda p, c, th, tl: (p, 1 - c, th, tl))

    def to_chip(self, array, step):
        return self.move(array, lambda p, c, th, tl: (p ^ step, c, th, tl))

    def to_low(self, array, step):
        return self.move(array, lambda p, c, th, tl: (p, c, th, (tl + step) % self.low))

    def cross(self, array):
        return self.move(
            array, lambda p, c, th, tl: (p, 1 - c, 1 - th, tl) if c != th else None
        )

    def home_turn(self, array):
        return self.move(
            array, lambda p, c, th, tl: (p, c, 1 - th, tl) if c == th else (p, 1 - c, th, tl)
        )

    def away_to_home(self, array):
        return self.move(array, lambda p, c, th, tl: (p, c, 1 - th, tl) if c != th else None)

    def home_to_core(self, array):
        return self.move(array, lambda p, c, th, tl: (p, 1 - c, th, tl) if c == th else None)

    def swap(self, array):
        return jnp.where(self.home, array, self.cross(array))

    def quarter_rows(self, array, step, other):
        rows = array.shape[0] // self.tensor_count
        index = (self.c ^ other) * self.low + (self.tl + step) % self.low
        return lax.dynamic_slice_in_dim(array, index * rows, rows, 0)

    def plane_moves(self, partial):
        rows, columns = 2 * partial.shape[0] // self.dp_count, partial.shape[1]

        def unit(step):
            return lax.dynamic_slice(partial, ((self.p ^ step) * rows, 0), (rows, columns))

        return unit(0), [self.to_chip(unit(step), step) for step in range(self.chips - 1, 0, -1)]

    def plane_sum(self, own, moves):
        total = own.astype(jnp.float32)
        for arrived in moves:
            total = total + arrived.astype(jnp.float32)
        rows = own.shape[0] // 2
        sums = [total[:rows], total[rows:]]
        mine = jnp.where(self.c == 0, sums[0], sums[1])
        other = jnp.where(self.c == 0, sums[1], sums[0])
        leaving = jnp.stack(
            [jnp.where(self.home, other, mine).astype(jnp.bfloat16), other.astype(jnp.bfloat16)]
        )
        return mine, leaving

    def pair_rows(self, partial):
        return [
            self.quarter_rows(partial, step, 0).astype(jnp.float32)
            + self.to_core(self.quarter_rows(partial, step, 1)).astype(jnp.float32)
            for step in range(self.low)
        ]

    def sum_rows(self, pairs):
        total = pairs[0]
        for step in range(1, self.low):
            total = total + self.to_low(pairs[step].astype(jnp.bfloat16), step).astype(jnp.float32)
        return total


def project_kernel(heads, tokens_ref, gain_ref, weight_ref, cosine_ref, sine_ref, normed_ref, out_ref, root_ref):
    tokens = tokens_ref[...].astype(jnp.float32)
    root = lax.rsqrt(jnp.mean(tokens * tokens, axis=-1, keepdims=True) + epsilon)
    root_ref[...] = root
    normed = (tokens * root * gain_ref[...]).astype(jnp.bfloat16)
    normed_ref[...] = normed
    rows = jnp.dot(normed, weight_ref[...], preferred_element_type=jnp.float32)
    cosine, sine = cosine_ref[...].T, sine_ref[...].T
    pieces = []
    for head in range(heads):
        leading = rows[:, head * HEAD_DIM : head * HEAD_DIM + HALF]
        trailing = rows[:, head * HEAD_DIM + HALF : (head + 1) * HEAD_DIM]
        pieces.append(leading * cosine - trailing * sine)
        pieces.append(trailing * cosine + leading * sine)
    pieces.append(rows[:, heads * HEAD_DIM : out_ref.shape[1]])
    out_ref[...] = jnp.concatenate(pieces, axis=1).astype(jnp.bfloat16)


def project(tokens, gain, weight, cosine, sine, rotated_heads, out_columns):
    count, width = tokens.shape
    block = math.gcd(count, 256)
    return pl.pallas_call(
        functools.partial(project_kernel, rotated_heads),
        grid=(count // block,),
        in_specs=[
            pl.BlockSpec((block, width), lambda i: (i, 0)),
            pl.BlockSpec((1, width), lambda i: (0, 0)),
            pl.BlockSpec(weight.shape, lambda i: (0, 0)),
            pl.BlockSpec((HALF, block), lambda i: (0, i)),
            pl.BlockSpec((HALF, block), lambda i: (0, i)),
        ],
        out_specs=[
            pl.BlockSpec((block, width), lambda i: (i, 0)),
            pl.BlockSpec((block, out_columns), lambda i: (i, 0)),
            pl.BlockSpec((block, 1), lambda i: (i, 0)),
        ],
        out_shape=[
            jax.ShapeDtypeStruct((count, width), jnp.bfloat16),
            jax.ShapeDtypeStruct((count, out_columns), jnp.bfloat16),
            jax.ShapeDtypeStruct((count, 1), jnp.float32),
        ],
        compiler_params=pltpu.CompilerParams(vmem_limit_bytes=VMEM_LIMIT),
        cost_estimate=pl.CostEstimate(
            flops=2 * count * width * weight.shape[1],
            bytes_accessed=4 * count * width + 2 * weight.size,
            transcendentals=0,
        ),
        name="project",
    )(tokens, gain, weight, cosine, sine)


def block_bias(key_start, query_start, start_row, pad_column):
    shape = (pad_column.shape[0], start_row.shape[1])
    keys = key_start + lax.broadcasted_iota(jnp.int32, shape, 0)
    queries = query_start + lax.broadcasted_iota(jnp.int32, shape, 1)
    allowed = ((keys >= start_row) & (keys <= queries) & (pad_column == 1)) | (keys == queries)
    return jnp.where(allowed, 0.0, MASKED)


def stack_heads(rows, first, group):
    return jnp.concatenate(
        [rows[:, (first + g) * HEAD_DIM : (first + g + 1) * HEAD_DIM] for g in range(group)], axis=0
    )


def times(left, right, left_dim, right_dim):
    return lax.dot_general(
        left, right, (((left_dim,), (right_dim,)), ((), ())), preferred_element_type=jnp.float32
    )


def attend_kernel(
    kv_heads, group, first_ref, query_ref, all_ref, start_ref, pad_ref, out_ref, total_ref, key_heads, value_turned
):
    step = pl.program_id(0)
    heads = kv_heads * group
    query_rows = query_ref.shape[0]
    scale = 1.0 / math.sqrt(HEAD_DIM)

    @pl.when(step == 0)
    def _():
        for k in range(kv_heads):
            at = (heads + k) * HEAD_DIM
            key_heads[k] = all_ref[:, at : at + HEAD_DIM]
            at = (heads + kv_heads + k) * HEAD_DIM
            value_turned[k] = all_ref[:, at : at + HEAD_DIM].astype(jnp.float32).T.astype(jnp.bfloat16)

    query_start = step * query_rows
    last = (query_start + query_rows - 1) // KEY_BLOCK + 1
    pieces = []
    for k in range(kv_heads):
        queries = stack_heads(query_ref[:, : heads * HEAD_DIM], k * group, group)

        def body(block, carry, k=k, queries=queries):
            top, total, mixed = carry
            at = pl.multiple_of(block * KEY_BLOCK, KEY_BLOCK)
            bias = block_bias(at, query_start, start_ref[...], pad_ref[pl.ds(at, KEY_BLOCK), :])
            bias = jnp.concatenate([bias] * group, axis=1)
            scores = times(key_heads[k, pl.ds(at, KEY_BLOCK), :], queries, 1, 1) * scale + bias
            new_top = jnp.maximum(top, jnp.max(scores, axis=0, keepdims=True))
            weight = jnp.exp(scores - new_top)
            shrink = jnp.exp(top - new_top)
            total = total * shrink + jnp.sum(weight, axis=0, keepdims=True)
            mixed = mixed * shrink + times(
                value_turned[k, :, pl.ds(at, KEY_BLOCK)], weight.astype(jnp.bfloat16), 1, 0
            )
            return new_top, total, mixed

        columns = group * query_rows
        top, total, mixed = lax.fori_loop(
            first_ref[step],
            last,
            body,
            (
                jnp.full((1, columns), MASKED, jnp.float32),
                jnp.zeros((1, columns), jnp.float32),
                jnp.zeros((HEAD_DIM, columns), jnp.float32),
            ),
        )
        mixed = mixed / total
        log_total = top + jnp.log(total)
        for g in range(group):
            span = slice(g * query_rows, (g + 1) * query_rows)
            pieces.append(mixed[:, span].T)
            total_ref[k * group + g : k * group + g + 1, :] = log_total[:, span]
    out_ref[...] = jnp.concatenate(pieces, axis=1).astype(jnp.bfloat16)


def attend(first, heads_all, start_row, pad_column, kv_heads, group):
    count, columns = heads_all.shape
    heads = kv_heads * group
    block = math.gcd(count, QUERY_BLOCK)
    return pl.pallas_call(
        functools.partial(attend_kernel, kv_heads, group),
        grid_spec=pltpu.PrefetchScalarGridSpec(
            num_scalar_prefetch=1,
            grid=(count // block,),
            in_specs=[
                pl.BlockSpec((block, columns), lambda i, first: (i, 0)),
                pl.BlockSpec((count, columns), lambda i, first: (0, 0)),
                pl.BlockSpec((1, block), lambda i, first: (0, i)),
                pl.BlockSpec((count, 1), lambda i, first: (0, 0)),
            ],
            out_specs=[
                pl.BlockSpec((block, heads * HEAD_DIM), lambda i, first: (i, 0)),
                pl.BlockSpec((heads, block), lambda i, first: (0, i)),
            ],
            scratch_shapes=[
                pltpu.VMEM((kv_heads, count, HEAD_DIM), jnp.bfloat16),
                pltpu.VMEM((kv_heads, HEAD_DIM, count), jnp.bfloat16),
            ],
        ),
        out_shape=[
            jax.ShapeDtypeStruct((count, heads * HEAD_DIM), jnp.bfloat16),
            jax.ShapeDtypeStruct((heads, count), jnp.float32),
        ],
        compiler_params=pltpu.CompilerParams(vmem_limit_bytes=VMEM_LIMIT),
        cost_estimate=pl.CostEstimate(
            flops=50 * 10**9, bytes_accessed=count * columns, transcendentals=0
        ),
        name="attend",
    )(first, heads_all, heads_all, start_row, pad_column)


def attend_back_kernel(
    kv_heads,
    group,
    first_ref,
    query_ref,
    all_ref,
    start_ref,
    pad_ref,
    total_ref,
    attended_ref,
    grad_ref,
    cosine_turned_ref,
    sine_turned_ref,
    cosine_all_ref,
    sine_all_ref,
    grad_query_ref,
    grad_rest_ref,
    key_heads,
    value_heads,
    key_turned,
    grad_keys,
    grad_values,
):
    step = pl.program_id(0)
    heads = kv_heads * group
    query_rows = query_ref.shape[0]
    scale = 1.0 / math.sqrt(HEAD_DIM)

    @pl.when(step == 0)
    def _():
        for k in range(kv_heads):
            at = (heads + k) * HEAD_DIM
            keys = all_ref[:, at : at + HEAD_DIM]
            key_heads[k] = keys
            key_turned[k] = keys.astype(jnp.float32).T.astype(jnp.bfloat16)
            at = (heads + kv_heads + k) * HEAD_DIM
            value_heads[k] = all_ref[:, at : at + HEAD_DIM]
        grad_keys[...] = jnp.zeros_like(grad_keys)
        grad_values[...] = jnp.zeros_like(grad_values)

    query_start = step * query_rows
    last = (query_start + query_rows - 1) // KEY_BLOCK + 1
    cosine = cosine_turned_ref[...]
    sine = sine_turned_ref[...]
    pieces = []
    for k in range(kv_heads):
        queries = stack_heads(query_ref[:, : heads * HEAD_DIM], k * group, group)
        grads = stack_heads(grad_ref[...], k * group, group)
        attended = stack_heads(attended_ref[...], k * group, group)
        inner = jnp.sum(
            (grads.astype(jnp.float32) * attended.astype(jnp.float32)).T, axis=0, keepdims=True
        )
        log_total = jnp.concatenate(
            [total_ref[k * group + g : k * group + g + 1, :] for g in range(group)], axis=1
        )

        def body(block, turned, k=k, queries=queries, grads=grads, inner=inner, log_total=log_total):
            at = pl.multiple_of(block * KEY_BLOCK, KEY_BLOCK)
            span = pl.ds(at, KEY_BLOCK)
            bias = block_bias(at, query_start, start_ref[...], pad_ref[span, :])
            bias = jnp.concatenate([bias] * group, axis=1)
            scores = times(key_heads[k, span, :], queries, 1, 1) * scale + bias
            weight = jnp.exp(scores - log_total)
            grad_weight = times(value_heads[k, span, :], grads, 1, 1)
            grad_scores = (weight * (grad_weight - inner)).astype(jnp.bfloat16)
            grad_values[k, span, :] += times(weight.astype(jnp.bfloat16), grads, 1, 0)
            grad_keys[k, span, :] += times(grad_scores, queries, 1, 0)
            return turned + times(key_turned[k, :, span], grad_scores, 1, 0)

        turned = lax.fori_loop(
            first_ref[step], last, body, jnp.zeros((HEAD_DIM, group * query_rows), jnp.float32)
        )
        turned = turned * scale
        for g in range(group):
            part = turned[:, g * query_rows : (g + 1) * query_rows]
            leading, trailing = part[:HALF], part[HALF:]
            back = jnp.concatenate(
                [leading * cosine + trailing * sine, trailing * cosine - leading * sine], axis=0
            )
            pieces.append(back.T)
    grad_query_ref[...] = jnp.concatenate(pieces, axis=1).astype(jnp.bfloat16)

    @pl.when(step == pl.num_programs(0) - 1)
    def _():
        rest = []
        cosine_all, sine_all = cosine_all_ref[...].T, sine_all_ref[...].T
        for k in range(kv_heads):
            leading = grad_keys[k][:, :HALF] * scale
            trailing = grad_keys[k][:, HALF:] * scale
            rest.append(leading * cosine_all + trailing * sine_all)
            rest.append(trailing * cosine_all - leading * sine_all)
        for k in range(kv_heads):
            rest.append(grad_values[k])
        grad_rest_ref[...] = jnp.concatenate(rest, axis=1).astype(jnp.bfloat16)


def attend_back(
    first, heads_all, start_row, pad_column, log_totals, attended, grad_attended, cosine, sine, kv_heads, group
):
    count, columns = heads_all.shape
    heads = kv_heads * group
    block = math.gcd(count, QUERY_BLOCK)
    width = heads * HEAD_DIM
    rest = 2 * kv_heads * HEAD_DIM
    return pl.pallas_call(
        functools.partial(attend_back_kernel, kv_heads, group),
        grid_spec=pltpu.PrefetchScalarGridSpec(
            num_scalar_prefetch=1,
            grid=(count // block,),
            in_specs=[
                pl.BlockSpec((block, columns), lambda i, first: (i, 0)),
                pl.BlockSpec((count, columns), lambda i, first: (0, 0)),
                pl.BlockSpec((1, block), lambda i, first: (0, i)),
                pl.BlockSpec((count, 1), lambda i, first: (0, 0)),
                pl.BlockSpec((heads, block), lambda i, first: (0, i)),
                pl.BlockSpec((block, width), lambda i, first: (i, 0)),
                pl.BlockSpec((block, width), lambda i, first: (i, 0)),
                pl.BlockSpec((HALF, block), lambda i, first: (0, i)),
                pl.BlockSpec((HALF, block), lambda i, first: (0, i)),
                pl.BlockSpec((HALF, count), lambda i, first: (0, 0)),
                pl.BlockSpec((HALF, count), lambda i, first: (0, 0)),
            ],
            out_specs=[
                pl.BlockSpec((block, width), lambda i, first: (i, 0)),
                pl.BlockSpec((count, rest), lambda i, first: (0, 0)),
            ],
            scratch_shapes=[
                pltpu.VMEM((kv_heads, count, HEAD_DIM), jnp.bfloat16),
                pltpu.VMEM((kv_heads, count, HEAD_DIM), jnp.bfloat16),
                pltpu.VMEM((kv_heads, HEAD_DIM, count), jnp.bfloat16),
                pltpu.VMEM((kv_heads, count, HEAD_DIM), jnp.float32),
                pltpu.VMEM((kv_heads, count, HEAD_DIM), jnp.float32),
            ],
        ),
        out_shape=[
            jax.ShapeDtypeStruct((count, width), jnp.bfloat16),
            jax.ShapeDtypeStruct((count, rest), jnp.bfloat16),
        ],
        compiler_params=pltpu.CompilerParams(vmem_limit_bytes=VMEM_LIMIT),
        cost_estimate=pl.CostEstimate(
            flops=50 * 10**9, bytes_accessed=count * columns, transcendentals=0
        ),
        name="attend_back",
    )(
        first,
        heads_all,
        heads_all,
        start_row,
        pad_column,
        log_totals,
        attended,
        grad_attended,
        cosine,
        sine,
        cosine,
        sine,
    )


MESH = pl.DeviceIdType.MESH
CHUNK = 64


class Links:
    def __init__(self, dp_count, tensor_count, send, recv, local):
        self.chips, self.low = dp_count // 2, tensor_count // 2
        self.send, self.recv, self.local = send, recv, local
        self.used = 0
        self.used_local = 0
        self.unsent = []
        self.all_low = False
        dp_index, tensor_index = lax.axis_index("dp"), lax.axis_index("tensor")
        self.dp_index, self.tensor_index = dp_index, tensor_index
        self.p, self.c = dp_index // 2, dp_index % 2
        self.th, self.tl = tensor_index // self.low, tensor_index % self.low
        self.home = self.c == self.th
        self.away = self.c != self.th
        self.quarter = self.c * self.low + self.tl

    def at(self, p, c, th, tl):
        return (2 * p + c, th * self.low + tl)

    def chip(self, step):
        p = self.p
        moved = p
        for bit in (1, 2, 4):
            if step & bit:
                moved = moved + bit * (1 - 2 * ((p // bit) % 2))
        return moved

    def chip_peer(self, step):
        return self.at(self.chip(step), self.c, self.th, self.tl)

    def core_peer(self):
        return self.at(self.p, 1 - self.c, self.th, self.tl)

    def low_peer(self, step):
        return self.at(self.p, self.c, self.th, (self.tl + step) % self.low)

    def cross_peer(self):
        return self.at(self.p, 1 - self.c, 1 - self.th, self.tl)

    def turn_peer(self):
        home = self.home.astype(jnp.int32)
        return self.at(
            self.p,
            home * self.c + (1 - home) * (1 - self.c),
            home * (1 - self.th) + (1 - home) * self.th,
            self.tl,
        )

    def back_peer(self):
        home = self.home.astype(jnp.int32)
        return self.at(
            self.p,
            home * (1 - self.c) + (1 - home) * self.c,
            home * self.th + (1 - home) * (1 - self.th),
            self.tl,
        )

    def partner(self):
        return self.at(self.p, self.c, 1 - self.th, self.tl)

    def chip_steps(self):
        return (1, 2) if self.chips == 4 else tuple(range(1, self.chips))

    def enter(self):
        peers = [self.core_peer(), self.cross_peer(), self.partner()]
        peers += [self.chip_peer(step) for step in self.chip_steps()]
        peers += [self.low_peer(step) for step in range(1, self.low)]
        if self.all_low:
            peers += [
                self.at(self.p, self.c, 1 - self.th, (self.tl + step) % self.low)
                for step in range(1, self.low)
            ]
        barrier = pltpu.get_barrier_semaphore()
        for peer in peers:
            pl.semaphore_signal(barrier, inc=1, device_id=peer, device_id_type=MESH)
        pl.semaphore_wait(barrier, len(peers))

    def copy(self, source, target, peer, when=None):
        slot = self.used
        self.used += 1

        def make():
            return pltpu.make_async_remote_copy(
                src_ref=source,
                dst_ref=target,
                send_sem=self.send.at[slot],
                recv_sem=self.recv.at[slot],
                device_id=peer,
                device_id_type=MESH,
            )

        item = Item(make, when)
        self.unsent.append(item)
        return item

    def local_slot(self):
        self.used_local += 1
        return self.used_local - 1

    def keep(self, source, target, when=None):
        slot = self.used_local
        self.used_local += 1
        return Item(lambda: pltpu.make_async_copy(source, target, self.local.at[slot]), when)

    def drop(self, items):
        self.unsent = [item for item in self.unsent if item not in items]

    def leave(self):
        for item in self.unsent:
            item.sent()


class Item:
    def __init__(self, make, when):
        self.make, self.when = make, when

    def run(self, action):
        if self.when is None:
            action(self.make())
        else:
            pl.when(self.when)(lambda: action(self.make()))

    def start(self):
        self.run(lambda copy: copy.start())

    def arrived(self):
        self.run(lambda copy: copy.wait_recv())

    def sent(self):
        self.run(lambda copy: copy.wait_send())

    def done(self):
        self.run(lambda copy: copy.wait())


class UnitGather:
    def __init__(self, links, shard, unit):
        rows = shard.shape[0]
        mine = unit.at[pl.ds(links.c * rows, rows)]
        self.first = links.copy(shard, mine, links.turn_peer())
        self.second = links.copy(shard, mine, links.cross_peer(), links.away)
        self.own = links.keep(shard, mine, links.home)

    def turn(self):
        self.first.start()
        self.second.start()
        self.own.start()

    def settle_unit(self):
        self.first.arrived()
        self.second.arrived()
        self.own.done()


class WeightGather:
    def __init__(self, links, shard, full):
        self.links, self.shard, self.full = links, shard, full
        rows = shard.shape[0]
        self.rows = rows
        mine = full.at[pl.ds(links.dp_index * rows, rows)]
        self.first = links.copy(shard, mine, links.turn_peer())
        self.second = links.copy(shard, mine, links.cross_peer(), links.away)
        self.own = links.keep(shard, mine, links.home)
        unit = 2 * rows
        self.direct = []
        self.forward = []
        here = full.at[pl.ds(links.p * unit, unit)]
        for step in links.chip_steps():
            self.direct.append(links.copy(here, here, links.chip_peer(step)))
        if links.chips == 4:
            top = full.at[pl.ds(links.chip(2) * unit, rows)]
            bottom = full.at[pl.ds(links.chip(1) * unit + rows, rows)]
            self.forward.append(links.copy(top, top, links.chip_peer(1)))
            self.forward.append(links.copy(bottom, bottom, links.chip_peer(2)))

    def turn(self):
        self.first.start()
        self.second.start()
        self.own.start()

    def settle_unit(self):
        self.first.arrived()
        self.second.arrived()
        self.own.done()

    def spread(self):
        self.settle_unit()
        self.spread_unit()

    def spread_unit(self):
        for item in self.direct:
            item.start()

    def pass_on(self):
        for item in self.direct:
            item.arrived()
        for item in self.forward:
            item.start()

    def finish(self):
        for item in self.forward:
            item.arrived()


class RowGather:
    def __init__(self, links, full, rows):
        self.links = links
        mine = full.at[pl.ds(links.quarter * rows, rows)]
        self.to_core = links.copy(mine, mine, links.core_peer())
        self.to_low = []
        self.onward = []
        for step in range(1, links.low):
            self.to_low.append(links.copy(mine, mine, links.low_peer(step)))
            came = (links.tl + links.low - step) % links.low
            block = full.at[pl.ds((links.c * links.low + came) * rows, rows)]
            self.onward.append(links.copy(block, block, links.core_peer()))

    def start(self):
        for item in self.to_low:
            item.start()
        self.to_core.start()

    def pass_on(self):
        for arriving, item in zip(self.to_low, self.onward):
            arriving.arrived()
            item.start()

    def finish(self):
        self.to_core.arrived()
        for item in self.onward:
            item.arrived()


class RowScatter:
    def __init__(self, links, partial, mine, others, sums, arrivals, rows):
        self.links, self.rows = links, rows
        self.mine, self.others, self.sums, self.arrivals = mine, others, sums, arrivals
        low = links.low
        self.load = links.keep(partial.at[pl.ds(links.c * low * rows, low * rows)], mine)
        self.swap = links.copy(
            partial.at[pl.ds((1 - links.c) * low * rows, low * rows)], others, links.core_peer()
        )
        self.sends = [
            links.copy(sums.at[step - 1], arrivals.at[step - 1], links.low_peer(step))
            for step in range(1, low)
        ]

    def start(self):
        self.swap.start()
        self.load.start()

    def send_sums(self):
        self.load.done()
        self.swap.arrived()
        for step in range(1, self.links.low):
            base = ((self.links.tl + step) % self.links.low) * self.rows

            @pl.loop(0, self.rows // CHUNK)
            def _(i, base=base, step=step):
                span = pl.ds(pl.multiple_of(base + i * CHUNK, CHUNK), CHUNK)
                total = self.mine[span].astype(jnp.float32) + self.others[span].astype(jnp.float32)
                self.sums[step - 1, pl.ds(pl.multiple_of(i * CHUNK, CHUNK), CHUNK)] = total.astype(jnp.bfloat16)

            self.sends[step - 1].start()

    def collect(self, use):
        for item in self.sends:
            item.arrived()
        base = self.links.tl * self.rows

        @pl.loop(0, self.rows // CHUNK)
        def _(i):
            at = pl.multiple_of(i * CHUNK, CHUNK)
            span = pl.ds(pl.multiple_of(base + at, CHUNK), CHUNK)
            total = self.mine[span].astype(jnp.float32) + self.others[span].astype(jnp.float32)
            for step in range(1, self.links.low):
                total = total + self.arrivals[step - 1, pl.ds(at, CHUNK)].astype(jnp.float32)
            use(pl.ds(at, CHUNK), total)


def scatter_scratch(low, rows, width):
    return [
        pltpu.VMEM((low * rows, width), jnp.bfloat16),
        pltpu.VMEM((low * rows, width), jnp.bfloat16),
        pltpu.VMEM((low - 1, rows, width), jnp.bfloat16),
        pltpu.VMEM((low - 1, rows, width), jnp.bfloat16),
    ]


def semaphores(count, local_count):
    return [
        pltpu.SemaphoreType.DMA((count,)),
        pltpu.SemaphoreType.DMA((count,)),
        pltpu.SemaphoreType.DMA((local_count,)),
    ]


def anywhere(count):
    return [pl.BlockSpec(memory_space=pl.ANY)] * count


def in_vmem(count):
    return [pl.BlockSpec(memory_space=pltpu.VMEM)] * count


def link_params(number):
    return pltpu.CompilerParams(
        collective_id=number, has_side_effects=True, vmem_limit_bytes=LINK_VMEM_LIMIT
    )


ADD_ROWS = 32


def cut(columns, most):
    half = columns // 2
    return half if columns > most and half % 128 == 0 else columns


def product(left, right, out, left_dim, right_dim, rows, columns, finish=None, extra=(), extra_out=()):
    depth = left.shape[left_dim]
    count, width = out.shape
    rows, columns = math.gcd(count, rows), cut(width, columns)

    def body(left_ref, right_ref, *refs):
        value = times(left_ref[...], right_ref[...], left_dim, right_dim)
        if finish is None:
            refs[0][...] = value.astype(refs[0].dtype)
        else:
            finish(value, *refs)

    def block(shape, index):
        return pl.BlockSpec(shape, index)

    left_spec = (
        block((rows, depth), lambda j, i: (i, 0)) if left_dim == 1 else block((depth, rows), lambda j, i: (0, i))
    )
    right_spec = (
        block((columns, depth), lambda j, i: (j, 0))
        if right_dim == 1
        else block((depth, columns), lambda j, i: (0, j))
    )
    whole = block((rows, columns), lambda j, i: (i, j))
    extra_specs = [
        whole if ref.shape[1] == width else block((rows, ref.shape[1]), lambda j, i: (i, 0)) for ref in extra
    ]
    pltpu.emit_pipeline(
        body,
        grid=(width // columns, count // rows),
        in_specs=[left_spec, right_spec] + extra_specs,
        out_specs=[whole] * (1 + len(extra_out)),
    )(left, right, *extra, out, *extra_out)


def row_loop(rows, body):
    @pl.loop(0, rows // ADD_ROWS)
    def _(i):
        body(pl.ds(pl.multiple_of(i * ADD_ROWS, ADD_ROWS), ADD_ROWS))


class WeightScatter:
    def __init__(self, links, partial, result, inbox, turned, sums, leaving, stage):
        self.links, self.partial, self.result = links, partial, result
        self.inbox, self.turned, self.sums, self.leaving = inbox, turned, sums, leaving
        rows = partial.shape[0] // (2 * links.chips)
        self.rows = rows
        width = partial.shape[1]
        self.stage = [stage.at[i, pl.ds(0, rows), pl.ds(0, width)] for i in range(3)]
        self.both = links.chips == 4
        self.direct_started = False
        self.loads = [
            links.local_slot() for _ in range(3)
        ]
        if self.both:
            x_peer, y_peer = links.chip_peer(1), links.chip_peer(2)
            self.before = [
                links.copy(self.part(3, 0), inbox.at[0], x_peer),
                links.copy(self.part(3, 1), inbox.at[1], y_peer),
            ]
            self.direct = [
                links.copy(self.part(1, 0), inbox.at[2], x_peer),
                links.copy(self.part(2, 1), inbox.at[3], y_peer),
            ]
            self.summed = [
                links.copy(sums.at[0], inbox.at[4], y_peer),
                links.copy(sums.at[1], inbox.at[5], x_peer),
            ]
            self.arrivals = ((2, 4), (5, 3))
        else:
            self.before, self.summed, self.direct = [], [], []
            for step in links.chip_steps():
                for half in range(2):
                    at = 2 * (step - 1) + half
                    self.direct.append(
                        links.copy(self.part(step, half), inbox.at[at], links.chip_peer(step))
                    )
            self.arrivals = tuple(
                tuple(2 * (step - 1) + half for step in links.chip_steps()) for half in range(2)
            )
        self.first = links.copy(leaving.at[0], turned.at[0], links.back_peer())
        self.second = links.copy(leaving.at[1], turned.at[1], links.cross_peer(), links.away)

    def part(self, step, half):
        start = (2 * self.links.chip(step) + half) * self.rows
        return self.partial.at[pl.ds(start, self.rows)]

    def load(self, sources):
        copies = [
            pltpu.make_async_copy(source, stage, self.links.local.at[slot])
            for source, stage, slot in zip(sources, self.stage, self.loads)
        ]
        for copy in copies:
            copy.start()
        for copy in copies:
            copy.wait()

    def start(self, which):
        for item in getattr(self, which):
            item.start()

    def start_direct(self):
        if not self.direct_started:
            self.start("direct")
        self.direct_started = True

    def arrived(self, which):
        for item in getattr(self, which):
            item.arrived()

    def add_before(self):
        if not self.both:
            self.start_direct()
            return
        self.arrived("before")
        self.start_direct()
        for index, part in ((0, self.part(2, 0)), (1, self.part(1, 1))):
            self.load([part, self.inbox.at[index]])

            def body(span, index=index):
                total = self.stage[0][span].astype(jnp.float32) + self.stage[1][span].astype(jnp.float32)
                self.sums[index, span] = total.astype(jnp.bfloat16)

            row_loop(self.rows, body)
            self.summed[index].start()

    def turn(self):
        self.reduce()
        self.send_turned()

    def send_turned(self):
        self.first.start()
        self.second.start()

    def reduce(self):
        links = self.links
        for half in range(2):
            sources = [self.part(0, half)] + [self.inbox.at[at] for at in self.arrivals[half]]
            kept = links.c == half
            if len(sources) == 3:
                self.load(sources)

                def body(span, half=half, kept=kept):
                    total = self.stage[0][span].astype(jnp.float32)
                    total = total + self.stage[1][span].astype(jnp.float32)
                    self.settle(span, total + self.stage[2][span].astype(jnp.float32), kept)

                row_loop(self.rows, body)
            else:
                self.fold(sources, kept)

    def fold(self, sources, kept):
        rows = self.rows
        total = self.total
        self.load(sources[:1])
        row_loop(rows, lambda span: total.__setitem__(span, self.stage[0][span].astype(jnp.float32)))
        for source in sources[1:]:
            self.load([source])

            def body(span):
                total[span] = total[span] + self.stage[0][span].astype(jnp.float32)

            row_loop(rows, body)
        row_loop(rows, lambda span: self.settle(span, total[span], kept))

    def settle(self, span, total, kept):
        low = total.astype(jnp.bfloat16)
        links = self.links

        @pl.when(kept & links.home)
        def _():
            self.result[span] = total

        @pl.when(kept & links.away)
        def _():
            self.leaving[0, span] = low

        @pl.when(jnp.logical_not(kept) & links.home)
        def _():
            self.leaving[0, span] = low

        @pl.when(jnp.logical_not(kept) & links.away)
        def _():
            self.leaving[1, span] = low

    def finish(self):
        links = self.links
        self.first.arrived()
        self.second.arrived()

        @pl.when(links.home)
        def _():
            def body(span):
                self.result[span] = self.result[span] + self.turned[0, span].astype(jnp.float32)

            row_loop(self.rows, body)

        @pl.when(links.away)
        def _():
            def body(span):
                self.result[span] = self.turned[1, span].astype(jnp.float32) + self.turned[0, span].astype(
                    jnp.float32
                )

            row_loop(self.rows, body)


class TurnScatter:
    def __init__(self, links, mine, leaving, result, turned):
        self.links, self.mine, self.result, self.turned = links, mine, result, turned
        self.rows = mine.shape[0]
        self.first = links.copy(leaving.at[0], turned.at[0], links.back_peer())
        self.second = links.copy(leaving.at[1], turned.at[1], links.cross_peer(), links.away)

    def send_turned(self):
        self.first.start()
        self.second.start()

    def finish(self):
        self.first.arrived()
        self.second.arrived()

        @pl.when(self.links.home)
        def _():
            def body(span):
                self.result[span] = self.mine[span] + self.turned[0, span].astype(jnp.float32)

            row_loop(self.rows, body)

        @pl.when(self.links.away)
        def _():
            def body(span):
                self.result[span] = self.turned[1, span].astype(jnp.float32) + self.turned[0, span].astype(
                    jnp.float32
                )

            row_loop(self.rows, body)


def weight_scatter_scratch(chips, rows, width):
    return [pltpu.VMEM((2, rows, width), jnp.bfloat16)] * 3


def inbox_shape(chips, rows, width):
    count = 6 if chips == 4 else 2 * (chips - 1)
    return jax.ShapeDtypeStruct((count, rows, width), jnp.bfloat16)


def scatter_shapes(chips, partial):
    rows = partial.shape[0] // (2 * chips)
    width = partial.shape[1]
    return rows, width


def tail_kernel(
    dp_count,
    tensor_count,
    gain_column,
    partial,
    tokens_all,
    grad_rows,
    attended,
    normed,
    grad_heads,
    gain_parts,
    up_mine,
    up_leaving,
    grad_residual_ref,
    gain_ref,
    input_ref,
    up_ref,
    output_ref,
    first_ref,
    output_in,
    first_in,
    grad_output,
    grad_first,
    *scratch,
):
    output_work, first_work = scratch[:3], scratch[3:6]
    up_turned, stage, own_ref, leaving, crossed, mine, others, sums, arrivals = scratch[6:15]
    gains_out, gains_in, total = scratch[15:18]
    links = Links(dp_count, tensor_count, *scratch[18:])
    links.all_low = True
    rows = own_ref.shape[0]
    load_own = links.keep(tokens_all.at[pl.ds(links.quarter * rows, rows)], own_ref)
    scatter = RowScatter(links, partial, mine, others, sums, arrivals, rows)
    crossing = links.copy(leaving, crossed, links.cross_peer(), links.away)
    up = TurnScatter(links, up_mine, up_leaving, up_ref, up_turned)
    weights = []
    for grad, result, inbox, work in (
        (grad_output, output_ref, output_in, output_work),
        (grad_first, first_ref, first_in, first_work),
    ):
        turned, added, turning = work
        made = WeightScatter(links, grad, result, inbox, turned, added, turning, stage)
        made.total = None if made.both else total.at[pl.ds(0, made.rows), pl.ds(0, grad.shape[1])]
        weights.append(made)
    output, first = weights
    gain_sends = []
    for step in range(1, tensor_count):
        other = (links.tensor_index + step) % tensor_count
        gain_sends.append(
            links.copy(gains_out, gains_in.at[step - 1], links.at(links.p, links.c, other // links.low, other % links.low))
        )

    links.enter()
    scatter.start()
    load_own.start()
    up.send_turned()
    scatter.send_sums()
    load_own.done()

    def finish(value, parts_ref, out_ref):
        columns = value.shape[1]
        out_ref[:, : columns - 128] = value[:, : columns - 128].astype(jnp.bfloat16)
        out_ref[:, columns - 128 :] = (value[:, columns - 128 :] + parts_ref[...]).astype(jnp.bfloat16)

    product(normed, grad_heads, grad_first, 0, 0, 512, 1024, finish, (gain_parts,))
    first.start("before")
    product(grad_rows, attended, grad_output, 0, 0, 512, 1024)
    first.add_before()
    output.start("before")

    def use(span, grad_normed):
        own = own_ref[span].astype(jnp.float32)
        root = lax.rsqrt(jnp.mean(own * own, axis=-1, keepdims=True) + epsilon)
        unit = own * root
        scaled = grad_normed * gain_ref[...]
        grad = grad_residual_ref[span] + root * (
            scaled - unit * jnp.mean(scaled * unit, axis=-1, keepdims=True)
        )
        input_ref[span] = grad
        leaving[span] = grad.astype(jnp.bfloat16)

    scatter.collect(use)
    crossing.start()
    output.add_before()
    first.arrived("direct")
    first.arrived("summed")
    first.turn()
    crossing.arrived()

    @pl.when(links.away)
    def _():
        def body(span):
            input_ref[span] = crossed[span].astype(jnp.float32)

        row_loop(rows, body)

    output.arrived("direct")
    output.arrived("summed")
    output.turn()
    up.finish()
    first.finish()
    width = first_ref.shape[1]
    gains_out[...] = first_ref[:, width - 128 :]
    for item in gain_sends:
        item.start()
    output.finish()
    for item in gain_sends:
        item.arrived()
    summed = gains_out[...]
    for step in range(1, tensor_count):
        summed = summed + gains_in[step - 1]
    column = width - 128 + lax.broadcasted_iota(jnp.int32, summed.shape, 1)
    first_ref[:, width - 128 :] = jnp.where(column >= gain_column, summed, gains_out[...])
    links.leave()


def tail(
    dp_count,
    tensor_count,
    gain_column,
    partial,
    tokens_all,
    grad_rows,
    attended,
    normed,
    grad_heads,
    gain_parts,
    up_mine,
    up_leaving,
    grad_residual,
    gain,
):
    rows, width = grad_residual.shape
    low, chips = tensor_count // 2, dp_count // 2
    features = width
    partials = [
        jax.ShapeDtypeStruct((features, attended.shape[1]), jnp.bfloat16),
        jax.ShapeDtypeStruct((features, grad_heads.shape[1]), jnp.bfloat16),
    ]
    shapes = [scatter_shapes(chips, grad) for grad in partials]
    widest = max(columns for _, columns in shapes)
    most = shapes[0][0]
    scratch = []
    for block, columns in shapes:
        scratch += weight_scatter_scratch(chips, block, columns)
    scratch += [pltpu.VMEM(up_leaving.shape, jnp.bfloat16)]
    scratch += [pltpu.VMEM((3, most, widest), jnp.bfloat16)]
    scratch += [pltpu.VMEM((rows, width), jnp.bfloat16)] * 3
    scratch += scatter_scratch(low, rows, width)
    scratch += [
        pltpu.VMEM((most, 128), jnp.float32),
        pltpu.VMEM((tensor_count - 1, most, 128), jnp.float32),
        pltpu.VMEM((most, widest) if chips != 4 else (8, 128), jnp.float32),
    ]
    return pl.pallas_call(
        functools.partial(tail_kernel, dp_count, tensor_count, gain_column),
        out_shape=[jax.ShapeDtypeStruct((rows, width), jnp.float32)]
        + [jax.ShapeDtypeStruct(shape, jnp.float32) for shape in [up_mine.shape] + shapes]
        + [inbox_shape(chips, *shape) for shape in shapes]
        + partials,
        in_specs=anywhere(7) + in_vmem(4),
        out_specs=in_vmem(4) + anywhere(4),
        scratch_shapes=scratch + semaphores(96, 24),
        compiler_params=link_params(3),
        name="tail",
    )(
        partial,
        tokens_all,
        grad_rows,
        attended,
        normed,
        grad_heads,
        gain_parts,
        up_mine,
        up_leaving,
        grad_residual,
        gain,
    )[:4]


def gather_first_kernel(
    dp_count, tensor_count, tokens, first, output, gate, tokens_all, first_full, output_full, gate_unit, *sems
):
    links = Links(dp_count, tensor_count, *sems)
    rows = tokens.shape[0]
    mine = tokens_all.at[pl.ds(links.tensor_index * rows, rows)]
    crossing = links.copy(tokens, mine, links.cross_peer(), links.away)
    staying = links.keep(tokens, mine, links.home)
    gather_tokens = RowGather(links, tokens_all, rows)
    weights = [
        WeightGather(links, shard, full)
        for shard, full in ((first, first_full), (output, output_full))
    ]
    weights.append(UnitGather(links, gate, gate_unit))
    links.enter()
    weights[0].turn()
    crossing.start()
    staying.start()

    @pl.when(links.home)
    def _():
        staying.make().wait()
        gather_tokens.start()

    weights[0].spread()
    weights[1].turn()

    @pl.when(links.away)
    def _():
        crossing.make().wait_recv()
        gather_tokens.start()

    weights[1].spread()
    weights[2].turn()
    weights[0].pass_on()
    gather_tokens.pass_on()
    weights[1].pass_on()
    weights[0].finish()
    gather_tokens.finish()
    weights[1].finish()
    weights[2].settle_unit()
    links.leave()


def gather_first(dp_count, tensor_count, tokens, first, output, gate):
    def full(shard, times):
        return jax.ShapeDtypeStruct((shard.shape[0] * times, shard.shape[1]), shard.dtype)

    return pl.pallas_call(
        functools.partial(gather_first_kernel, dp_count, tensor_count),
        out_shape=[
            full(tokens, tensor_count),
            full(first, dp_count),
            full(output, dp_count),
            full(gate, 2),
        ],
        in_specs=in_vmem(4),
        out_specs=anywhere(4),
        scratch_shapes=semaphores(64, 8),
        compiler_params=link_params(0),
        name="gather_first",
    )(tokens, first, output, gate)


def middle_kernel(
    dp_count,
    tensor_count,
    moved_units,
    partial,
    tokens_all,
    cot,
    up,
    up_turned,
    up_crossed,
    down,
    gate_unit,
    *rest,
):
    gate_units, rest = rest[:moved_units], rest[moved_units:]
    gain_ref, residual_ref, normed_all, cot_all, up_full, down_full, gate_full = rest[:7]
    gate_values, up_values, hidden = rest[7:10]
    own, normed, mine, others, sums, arrivals = rest[10:16]
    links = Links(dp_count, tensor_count, *rest[16:])
    rows = cot.shape[0]
    scatter = RowScatter(links, partial, mine, others, sums, arrivals, rows)
    gather_normed = RowGather(links, normed_all, rows)
    gather_cot = RowGather(links, cot_all, rows)
    gate_gather = WeightGather(links, up, gate_full)
    up_gather = WeightGather(links, up, up_full)
    down_gather = WeightGather(links, down, down_full)
    shard = up.shape[0]
    here = up_full.at[pl.ds(links.dp_index * shard, shard)]
    beside = up_full.at[pl.ds((2 * links.p + 1 - links.c) * shard, shard)]
    quarter = pl.ds(links.quarter * rows, rows)
    placements = [
        links.keep(up, here, links.home),
        links.keep(up_turned, beside, links.home),
        links.keep(up_turned, here, links.away),
        links.keep(up_crossed, beside, links.away),
    ]
    gate_placements = [
        links.keep(unit, gate_full.at[pl.ds(links.chip(step) * 2 * shard, 2 * shard)])
        for step, unit in zip((0,) + links.chip_steps(), (gate_unit,) + tuple(gate_units))
    ]
    cot_crossing = links.copy(cot, cot_all.at[pl.ds(links.tensor_index * rows, rows)], links.cross_peer(), links.away)
    cot_staying = links.keep(cot, cot_all.at[quarter], links.home)
    load = links.keep(tokens_all.at[quarter], own)
    store = links.keep(normed, normed_all.at[quarter])
    links.drop([up_gather.first, up_gather.second, gate_gather.first, gate_gather.second] + gate_gather.direct)
    links.enter()
    scatter.start()
    load.start()
    for item in gate_placements + placements:
        item.start()
    for item in gate_placements:
        item.done()
    for item in gate_gather.forward:
        item.start()
    for item in placements:
        item.done()
    scatter.send_sums()
    up_gather.spread_unit()
    down_gather.turn()
    cot_staying.start()
    load.done()

    def use(span, total):
        residual = own[span].astype(jnp.float32) + total
        residual_ref[span] = residual
        root = lax.rsqrt(jnp.mean(residual * residual, axis=-1, keepdims=True) + epsilon)
        normed[span] = (residual * root * gain_ref[...]).astype(jnp.bfloat16)

    scatter.collect(use)
    store.start()
    store.done()
    gather_normed.start()
    down_gather.settle_unit()
    cot_crossing.start()
    up_gather.pass_on()
    down_gather.spread_unit()
    gate_gather.finish()
    gather_normed.pass_on()
    cot_staying.done()
    cot_crossing.arrived()
    gather_cot.start()
    up_gather.finish()
    gather_normed.finish()
    product(normed_all, gate_full, gate_values, 1, 0, 512, 1024)
    down_gather.pass_on()
    gather_cot.pass_on()

    def finish(up, gate_ref, up_ref, hidden_ref):
        gate = gate_ref[...]
        up_ref[...] = up
        hidden_ref[...] = (gate * jax.nn.sigmoid(gate) * up).astype(jnp.bfloat16)

    product(normed_all, up_full, up_values, 1, 0, 256, 1024, finish, (gate_values,), (hidden,))
    down_gather.finish()
    gather_cot.finish()
    links.leave()


def middle(
    dp_count, tensor_count, partial, tokens_all, cot, up, up_turned, up_crossed, down, gate_unit, gate_units, gain
):
    rows, width = cot.shape
    low = tensor_count // 2

    def full(shard, times):
        return jax.ShapeDtypeStruct((shard.shape[0] * times, shard.shape[1]), shard.dtype)

    return pl.pallas_call(
        functools.partial(middle_kernel, dp_count, tensor_count, len(gate_units)),
        out_shape=[
            jax.ShapeDtypeStruct((rows, width), jnp.float32),
            full(cot, tensor_count),
            full(cot, tensor_count),
            full(up, dp_count),
            full(down, dp_count),
            full(gate_unit, dp_count // 2),
            jax.ShapeDtypeStruct((rows * tensor_count, up.shape[1]), jnp.float32),
            jax.ShapeDtypeStruct((rows * tensor_count, up.shape[1]), jnp.float32),
            jax.ShapeDtypeStruct((rows * tensor_count, up.shape[1]), jnp.bfloat16),
        ],
        in_specs=anywhere(2) + in_vmem(len(gate_units) + 7),
        out_specs=in_vmem(1) + anywhere(8),
        scratch_shapes=[pltpu.VMEM((rows, width), jnp.bfloat16)] * 2
        + scatter_scratch(low, rows, width)
        + semaphores(64, 24),
        compiler_params=link_params(1),
        name="middle",
    )(partial, tokens_all, cot, up, up_turned, up_crossed, down, gate_unit, *gate_units, gain)


def turn_back_kernel(
    dp_count,
    tensor_count,
    partial,
    cot_all,
    normed_ffn,
    gate_signal,
    up_signal,
    hidden,
    down_full,
    residual_ref,
    gain_ref,
    grad_residual_ref,
    gain_part_ref,
    down_ref,
    gate_ref,
    gate_turning,
    grad_rows,
    down_in,
    gate_in,
    grad_down,
    grad_gate,
    grad_up,
    down_part,
    own,
    low_grad,
    turned,
    added,
    turning,
    gate_added,
    stage,
    total_ref,
    mine,
    others,
    sums,
    arrivals,
    *sems,
):
    links = Links(dp_count, tensor_count, *sems)
    rows = residual_ref.shape[0]
    down = WeightScatter(links, grad_down, down_ref, down_in, turned, added, turning, stage)
    gate = WeightScatter(links, grad_gate, gate_ref, gate_in, turned, gate_added, gate_turning, stage)
    down.total = gate.total = total_ref
    links.drop([gate.first, gate.second])
    scatter = RowScatter(links, partial, mine, others, sums, arrivals, rows)
    gather = RowGather(links, grad_rows, rows)
    quarter = pl.ds(links.quarter * rows, rows)
    load = links.keep(cot_all.at[quarter], own)
    store = links.keep(low_grad, grad_rows.at[quarter])
    links.enter()
    scatter.start()
    load.start()
    unit = 2 * down.rows

    def down_unit(step):
        at = pl.multiple_of(links.chip(step) * unit, 128)
        product(cot_all.at[:, pl.ds(at, unit)], hidden, grad_down.at[pl.ds(at, unit)], 0, 0, unit, 1024)

    if down.both and unit % 128 == 0:
        down_unit(3)
        down.start("before")
        scatter.send_sums()
        down_unit(1)
        down_unit(2)
        down.start_direct()
        down_unit(0)
    else:
        product(cot_all, hidden, grad_down, 0, 0, 512, 1024)
        down.start("before")
        scatter.send_sums()
    load.done()
    down.add_before()
    product(normed_ffn, gate_signal, grad_gate, 0, 0, 512, 1024)
    gate.start("before")
    gain_part_ref[...] = jnp.zeros_like(gain_part_ref)

    def use(span, grad_normed):
        residual = residual_ref[span]
        root = lax.rsqrt(jnp.mean(residual * residual, axis=-1, keepdims=True) + epsilon)
        unit = residual * root
        gain_part_ref[...] += jnp.sum(grad_normed * unit, axis=0, keepdims=True)
        scaled = grad_normed * gain_ref[...]
        grad = own[span].astype(jnp.float32) + root * (
            scaled - unit * jnp.mean(scaled * unit, axis=-1, keepdims=True)
        )
        grad_residual_ref[span] = grad
        low_grad[span] = grad.astype(jnp.bfloat16)

    scatter.collect(use)
    store.start()
    store.done()
    gather.start()
    down.arrived("direct")
    gate.start_direct()
    down.arrived("summed")
    down.turn()
    gate.add_before()
    product(normed_ffn, up_signal, grad_up, 0, 0, 512, 1024)
    gather.pass_on()
    product(hidden, down_full, down_part, 1, 1, 512, 1024)
    gate.arrived("direct")
    gate.arrived("summed")
    gate.reduce()
    down.finish()
    gather.finish()
    links.leave()


def turn_back(
    dp_count,
    tensor_count,
    partial,
    cot_all,
    normed_ffn,
    gate_signal,
    up_signal,
    hidden,
    down_full,
    residual,
    gain,
):
    rows, width = residual.shape
    low, chips = tensor_count // 2, dp_count // 2
    grad = jax.ShapeDtypeStruct((width, hidden.shape[1]), jnp.bfloat16)
    block, columns = scatter_shapes(chips, grad)
    return pl.pallas_call(
        functools.partial(turn_back_kernel, dp_count, tensor_count),
        out_shape=[
            jax.ShapeDtypeStruct((rows, width), jnp.float32),
            jax.ShapeDtypeStruct((1, width), jnp.float32),
            jax.ShapeDtypeStruct((block, columns), jnp.float32),
            jax.ShapeDtypeStruct((block, columns), jnp.float32),
            jax.ShapeDtypeStruct((2, block, columns), jnp.bfloat16),
            jax.ShapeDtypeStruct((rows * tensor_count, width), jnp.bfloat16),
            inbox_shape(chips, block, columns),
            inbox_shape(chips, block, columns),
            grad,
            grad,
            grad,
            jax.ShapeDtypeStruct((rows * tensor_count, width), jnp.bfloat16),
        ],
        in_specs=anywhere(7) + in_vmem(2),
        out_specs=in_vmem(5) + anywhere(7),
        scratch_shapes=[pltpu.VMEM((rows, width), jnp.bfloat16)] * 2
        + weight_scatter_scratch(chips, block, columns)
        + [
            pltpu.VMEM((2, block, columns), jnp.bfloat16),
            pltpu.VMEM((3, block, columns), jnp.bfloat16),
            pltpu.VMEM((block, columns) if chips != 4 else (8, 128), jnp.float32),
        ]
        + scatter_scratch(low, rows, width)
        + semaphores(64, 24),
        compiler_params=link_params(2),
        name="turn_back",
    )(partial, cot_all, normed_ffn, gate_signal, up_signal, hidden, down_full, residual, gain)


def hidden_back_kernel(
    cot_all, down_full, gate_values, up_values, gate_full, up_full, gate_signal, up_signal, partial
):
    def signals(grad_hidden, gate_ref, up_ref, gate_out, up_out):
        gate = gate_ref[...]
        sigmoid = jax.nn.sigmoid(gate)
        grad_hidden = grad_hidden * sigmoid
        gate_out[...] = (grad_hidden * up_ref[...] * (1.0 + gate * (1.0 - sigmoid))).astype(jnp.bfloat16)
        up_out[...] = (grad_hidden * gate).astype(jnp.bfloat16)

    product(
        cot_all, down_full, gate_signal, 1, 0, 256, 1024, signals, (gate_values, up_values), (up_signal,)
    )
    count, width = partial.shape
    depth = gate_full.shape[1]
    rows, columns = math.gcd(count, 512), cut(width, 1536)

    def body(gate_ref, up_ref, gate_weight, up_weight, out_ref):
        total = times(gate_ref[...], gate_weight[...], 1, 1) + times(up_ref[...], up_weight[...], 1, 1)
        out_ref[...] = total.astype(jnp.bfloat16)

    pltpu.emit_pipeline(
        body,
        grid=(width // columns, count // rows),
        in_specs=[pl.BlockSpec((rows, depth), lambda j, i: (i, 0))] * 2
        + [pl.BlockSpec((columns, depth), lambda j, i: (j, 0))] * 2,
        out_specs=[pl.BlockSpec((rows, columns), lambda j, i: (i, j))],
    )(gate_signal, up_signal, gate_full, up_full, partial)


def hidden_back(cot_all, down_full, gate_values, up_values, gate_full, up_full):
    signal = jax.ShapeDtypeStruct(gate_values.shape, jnp.bfloat16)
    flops = 6 * cot_all.size * gate_values.shape[1]
    return pl.pallas_call(
        hidden_back_kernel,
        out_shape=[signal, signal, jax.ShapeDtypeStruct(cot_all.shape, jnp.bfloat16)],
        in_specs=anywhere(6),
        out_specs=anywhere(3),
        compiler_params=pltpu.CompilerParams(vmem_limit_bytes=LINK_VMEM_LIMIT),
        cost_estimate=pl.CostEstimate(flops=flops, bytes_accessed=flops // 1000, transcendentals=0),
        name="hidden_back",
    )(cot_all, down_full, gate_values, up_values, gate_full, up_full)


def starts_of(positions, length_row):
    ends = jnp.cumsum(length_row)
    inside = positions[:, None] >= ends[None, :]
    return jnp.sum(jnp.where(inside, length_row[None, :], 0), axis=1)


def rotary_tables(positions):
    frequency = jnp.exp(
        jnp.arange(HALF, dtype=jnp.float32) * (-2.0 * math.log(rope_base) / HEAD_DIM)
    )
    angles = positions.astype(jnp.float32)[None, :] * frequency[:, None]
    return (jnp.cos(angles), jnp.sin(angles))


def per_device(
    dp_count,
    tensor_count,
    tokens,
    attention_gain,
    query_weight,
    key_weight,
    value_weight,
    output_weight,
    feedforward_gain,
    gate_weight,
    up_weight,
    down_weight,
    cotangent,
    lengths,
    storage_order,
    sequence_order,
    pad_mask,
):
    place = Placement(dp_count, tensor_count)
    count = storage_order.shape[0]
    rows = count // tensor_count
    kv_heads = key_weight.shape[1] // HEAD_DIM
    heads = query_weight.shape[1] // HEAD_DIM
    group = heads // kv_heads
    head_columns = (heads + 2 * kv_heads) * HEAD_DIM

    hidden_units = gate_weight.shape[1]
    hidden_padded = -(-hidden_units // 128) * 128
    output_padded = -(-heads * HEAD_DIM // 128) * 128
    first_padded = -(-(head_columns + 2) // 128) * 128

    def wide(array, columns):
        return jnp.pad(array, ((0, 0), (0, columns - array.shape[1])))

    gate_shard = wide(gate_weight, hidden_padded)
    up_shard = wide(up_weight, hidden_padded)
    down_shard = wide(down_weight.T, hidden_padded)
    tokens_all, first_weight, output_turned, gate_unit = gather_first(
        dp_count,
        tensor_count,
        tokens,
        wide(
            jnp.concatenate(
                [query_weight, key_weight, value_weight, attention_gain[:, None], feedforward_gain[:, None]],
                axis=1,
            ),
            first_padded,
        ),
        wide(output_weight.T, output_padded),
        gate_shard,
    )
    output_turned = output_turned[:, : heads * HEAD_DIM]
    late_up = after(up_shard, tokens_all)
    up_turned = place.home_turn(late_up)
    up_crossed = place.cross(late_up)
    steps = (1, 2) if place.chips == 4 else tuple(range(1, place.chips))
    gate_units = [place.to_chip(gate_unit, step) for step in steps]

    numbers = jnp.concatenate([storage_order, pad_mask, lengths[0]])
    numbers = jnp.where(place.home, numbers, place.to_core(numbers))
    pad_column = numbers[count : 2 * count][:, None]
    length_row = numbers[2 * count :]
    order = numbers[:count]

    places = jnp.arange(count, dtype=jnp.int32)
    starts = starts_of(places, length_row)
    cosine, sine = rotary_tables(places - starts)
    cosine_stored, sine_stored = rotary_tables(order - starts_of(order, length_row))
    to_sequence = (places[:, None] == order[None, :]).astype(jnp.bfloat16)
    to_storage = (order[:, None] == places[None, :]).astype(jnp.bfloat16)
    first_blocks = starts[:: math.gcd(count, QUERY_BLOCK)] // KEY_BLOCK
    start_row = starts[None, :]

    attention_scale = first_weight[:, head_columns].astype(jnp.float32)[None, :]
    feedforward_scale = first_weight[:, head_columns + 1].astype(jnp.float32)[None, :]
    normed, heads_stored, token_roots = project(
        tokens_all,
        attention_scale,
        first_weight,
        cosine_stored,
        sine_stored,
        heads + kv_heads,
        head_columns,
    )
    heads_all = contract(to_sequence, heads_stored, 1, 0, jnp.bfloat16)
    attended, log_totals = attend(first_blocks, heads_all, start_row, pad_column, kv_heads, group)
    attended_stored = contract(to_storage, attended, 1, 0, jnp.bfloat16)

    residual, normed_ffn, cot_all, up_full, down_turned, gate_full, gate_values, up_values, hidden = middle(
        dp_count,
        tensor_count,
        contract(attended_stored, output_turned, 1, 1, jnp.bfloat16),
        tokens_all,
        cotangent,
        up_shard,
        up_turned,
        up_crossed,
        down_shard,
        gate_unit,
        gate_units,
        feedforward_scale,
    )

    def leave(own):
        arrived = place.cross(own.astype(jnp.bfloat16)).astype(jnp.float32)
        return jnp.where(place.home, own, arrived)

    grad_gate, grad_up, grad_part = hidden_back(
        cot_all, down_turned, gate_values, up_values, gate_full, up_full
    )
    turned_back = turn_back(
        dp_count,
        tensor_count,
        grad_part,
        cot_all,
        normed_ffn,
        grad_gate,
        grad_up,
        hidden,
        down_turned,
        residual,
        feedforward_scale,
    )
    grad_residual, feedforward_part, down_grad, gate_grad, gate_turning, grad_rows = turned_back[:6]
    up_part, down_part = turned_back[10:]
    up_own, up_moves = place.plane_moves(up_part)
    gate_arrived = place.away_to_home(gate_turning)

    pairs = place.pair_rows(down_part)
    grad_attended = contract(grad_rows, output_turned, 1, 0, jnp.bfloat16)
    grad_attended = contract(to_sequence, grad_attended, 1, 0, jnp.bfloat16)
    grad_attended = after(grad_attended, *pairs)
    grad_query, grad_rest = attend_back(
        first_blocks,
        heads_all,
        start_row,
        pad_column,
        log_totals,
        attended,
        grad_attended,
        cosine,
        sine,
        kv_heads,
        group,
    )
    layer_own = after(residual, grad_query) + place.sum_rows(pairs)
    spare = jnp.zeros((count, first_padded - head_columns), jnp.bfloat16)
    up_mine, up_leaving = place.plane_sum(after(up_own, grad_query), up_moves)
    sequence_grads = after(jnp.concatenate([grad_query, grad_rest, spare], axis=1), layer_own)
    grad_heads = contract(to_storage, sequence_grads, 1, 0, jnp.bfloat16)
    grad_normed_part = contract(grad_heads, first_weight, 1, 1)
    tokens_wide = tokens_all.astype(jnp.float32)
    attention_part = jnp.sum(grad_normed_part * (tokens_wide * token_roots), axis=0)
    layer_output = leave(layer_own)
    gate_arrived = after(gate_arrived, grad_query).astype(jnp.float32)
    gate_other = place.home_to_core((gate_turning[0].astype(jnp.float32) + gate_arrived[1]).astype(jnp.bfloat16))
    gate_grad = jnp.where(place.home, gate_grad + gate_arrived[0], gate_other.astype(jnp.float32))
    gain_parts = jnp.stack([attention_part, feedforward_part[0]], axis=1)
    before = head_columns - (first_padded - 128)
    gain_parts = jnp.pad(gain_parts, ((0, 0), (before, 126 - before)))
    input_grad, up_grad, output_grad, first_grad = tail(
        dp_count,
        tensor_count,
        head_columns,
        after(grad_normed_part.astype(jnp.bfloat16), layer_own),
        tokens_all,
        grad_rows,
        wide(attended_stored, output_padded),
        normed,
        grad_heads,
        gain_parts,
        up_mine,
        up_leaving,
        grad_residual,
        attention_scale,
    )
    query_columns = heads * HEAD_DIM
    key_columns = kv_heads * HEAD_DIM
    return (
        layer_output,
        input_grad,
        first_grad[:, head_columns],
        first_grad[:, :query_columns],
        first_grad[:, query_columns : query_columns + key_columns],
        first_grad[:, query_columns + key_columns : head_columns],
        output_grad[:, :query_columns].T,
        first_grad[:, head_columns + 1],
        gate_grad[:, :hidden_units],
        up_grad[:, :hidden_units],
        down_grad[:, :hidden_units].T,
    )


def solution(mesh):
    placed = (
        P(("dp", "tensor"), None),
        P("dp"),
        P("dp", "tensor"),
        P("dp", "tensor"),
        P("dp", "tensor"),
        P("tensor", "dp"),
        P("dp"),
        P("dp", "tensor"),
        P("dp", "tensor"),
        P("tensor", "dp"),
        P(("dp", "tensor"), None),
        P("dp", None),
        P("dp"),
        P("dp"),
        P("dp"),
    )
    return jax.shard_map(
        functools.partial(per_device, mesh.shape["dp"], mesh.shape["tensor"]),
        mesh=mesh,
        in_specs=placed,
        out_specs=(
            P(("dp", "tensor"), None),
            P(("dp", "tensor"), None),
            P("dp"),
            P("dp", "tensor"),
            P("dp", "tensor"),
            P("dp", "tensor"),
            P("tensor", "dp"),
            P("dp"),
            P("dp", "tensor"),
            P("dp", "tensor"),
            P("tensor", "dp"),
        ),
        check_vma=False,
    )
```

```python
import functools
import math

import jax
import jax.numpy as jnp
from jax import lax
from jax.experimental import pallas as pl
from jax.experimental.pallas import tpu as pltpu
from jax.sharding import PartitionSpec as P

HEAD_DIM = 80
HALF = HEAD_DIM // 2
QUERY_BLOCK = 256
KEY_BLOCK = 256
MASKED = -1e30
VMEM_LIMIT = 48 * 1024 * 1024
LINK_VMEM_LIMIT = 60 * 1024 * 1024

epsilon = 1e-05
rope_base = 10000.0
AXES = ("dp", "tensor")


def contract(left, right, left_dim, right_dim, out_type=jnp.float32):
    product = lax.dot_general(
        left,
        right,
        (((left_dim,), (right_dim,)), ((), ())),
        preferred_element_type=jnp.float32,
    )
    return product.astype(out_type)


def after(value, *earlier):
    return lax.optimization_barrier((value,) + earlier)[0]


def inverse_root(vectors):
    return lax.rsqrt(jnp.mean(vectors * vectors, axis=-1, keepdims=True) + epsilon)


class Placement:
    def __init__(self, dp_count, tensor_count):
        self.dp_count = dp_count
        self.tensor_count = tensor_count
        self.chips = dp_count // 2
        self.low = tensor_count // 2
        dp_index = lax.axis_index("dp")
        tensor_index = lax.axis_index("tensor")
        self.p = dp_index // 2
        self.c = dp_index % 2
        self.th = tensor_index // self.low
        self.tl = tensor_index % self.low
        self.home = self.c == self.th

    def move(self, array, target):
        pairs = []
        for p in range(self.chips):
            for c in range(2):
                for th in range(2):
                    for tl in range(self.low):
                        goal = target(p, c, th, tl)
                        if goal is not None:
                            pairs.append((self.flat(p, c, th, tl), self.flat(*goal)))
        return lax.ppermute(array, AXES, pairs)

    def flat(self, p, c, th, tl):
        return (2 * p + c) * self.tensor_count + th * self.low + tl

    def to_core(self, array):
        return self.move(array, lambda p, c, th, tl: (p, 1 - c, th, tl))

    def to_chip(self, array, step):
        return self.move(array, lambda p, c, th, tl: (p ^ step, c, th, tl))

    def to_low(self, array, step):
        return self.move(array, lambda p, c, th, tl: (p, c, th, (tl + step) % self.low))

    def home_to_low(self, array, step):
        return self.move(
            array, lambda p, c, th, tl: (p, c, th, (tl + step) % self.low) if c == th else None
        )

    def cross(self, array):
        return self.move(
            array, lambda p, c, th, tl: (p, 1 - c, 1 - th, tl) if c != th else None
        )

    def home_turn(self, array):
        return self.move(
            array, lambda p, c, th, tl: (p, c, 1 - th, tl) if c == th else (p, 1 - c, th, tl)
        )

    def away_to_home(self, array):
        return self.move(array, lambda p, c, th, tl: (p, c, 1 - th, tl) if c != th else None)

    def home_to_core(self, array):
        return self.move(array, lambda p, c, th, tl: (p, 1 - c, th, tl) if c == th else None)

    def swap(self, array):
        return jnp.where(self.home, array, self.cross(array))

    def quarter_rows(self, array, step, other):
        rows = array.shape[0] // self.tensor_count
        index = (self.c ^ other) * self.low + (self.tl + step) % self.low
        return lax.dynamic_slice_in_dim(array, index * rows, rows, 0)

    def plane_moves(self, partial):
        rows, columns = partial.shape[0] // self.dp_count, partial.shape[1]

        def half(step, which):
            start = ((self.p ^ step) * 2 + which) * rows
            return lax.dynamic_slice(partial, (start, 0), (rows, columns))

        if self.chips == 4:
            return half, [
                self.to_chip(jnp.stack([half(3, 0), half(1, 0)]), 1),
                self.to_chip(jnp.stack([half(3, 1), half(2, 1)]), 2),
            ]
        return half, [
            self.to_chip(jnp.stack([half(step, 0), half(step, 1)]), step) for step in range(1, self.chips)
        ]

    def plane_sum(self, half, moves):
        def wide(value):
            return value.astype(jnp.float32)

        if self.chips == 4:
            by_x, by_y = moves
            first = self.to_chip((wide(half(2, 0)) + wide(by_x[0])).astype(jnp.bfloat16), 2)
            second = self.to_chip((wide(half(1, 1)) + wide(by_y[0])).astype(jnp.bfloat16), 1)
            parts = [[half(0, 0), by_x[1], first], [half(0, 1), by_y[1], second]]
        else:
            parts = [[half(0, which)] + [arrived[which] for arrived in moves] for which in range(2)]

        def total(which):
            return sum(wide(jnp.where(which == 0, one, two)) for one, two in zip(*parts))

        mine, other = total(self.c), total(1 - self.c)
        low = other.astype(jnp.bfloat16)
        return mine, jnp.where(self.home, low, mine.astype(jnp.bfloat16)), low


def project_kernel(heads, tokens_ref, gain_ref, weight_ref, cosine_ref, sine_ref, normed_ref, out_ref, root_ref):
    tokens = tokens_ref[...].astype(jnp.float32)
    root = lax.rsqrt(jnp.mean(tokens * tokens, axis=-1, keepdims=True) + epsilon)
    root_ref[...] = root
    normed = (tokens * root * gain_ref[...]).astype(jnp.bfloat16)
    normed_ref[...] = normed
    rows = jnp.dot(normed, weight_ref[...], preferred_element_type=jnp.float32)
    cosine, sine = cosine_ref[...].T, sine_ref[...].T
    pieces = []
    for head in range(heads):
        leading = rows[:, head * HEAD_DIM : head * HEAD_DIM + HALF]
        trailing = rows[:, head * HEAD_DIM + HALF : (head + 1) * HEAD_DIM]
        pieces.append(leading * cosine - trailing * sine)
        pieces.append(trailing * cosine + leading * sine)
    pieces.append(rows[:, heads * HEAD_DIM : out_ref.shape[1]])
    out_ref[...] = jnp.concatenate(pieces, axis=1).astype(jnp.bfloat16)


def project(tokens, gain, weight, cosine, sine, rotated_heads, out_columns):
    count, width = tokens.shape
    block = math.gcd(count, 256)
    return pl.pallas_call(
        functools.partial(project_kernel, rotated_heads),
        grid=(count // block,),
        in_specs=[
            pl.BlockSpec((block, width), lambda i: (i, 0)),
            pl.BlockSpec((1, width), lambda i: (0, 0)),
            pl.BlockSpec(weight.shape, lambda i: (0, 0)),
            pl.BlockSpec((HALF, block), lambda i: (0, i)),
            pl.BlockSpec((HALF, block), lambda i: (0, i)),
        ],
        out_specs=[
            pl.BlockSpec((block, width), lambda i: (i, 0)),
            pl.BlockSpec((block, out_columns), lambda i: (i, 0)),
            pl.BlockSpec((block, 1), lambda i: (i, 0)),
        ],
        out_shape=[
            jax.ShapeDtypeStruct((count, width), jnp.bfloat16),
            jax.ShapeDtypeStruct((count, out_columns), jnp.bfloat16),
            jax.ShapeDtypeStruct((count, 1), jnp.float32),
        ],
        compiler_params=pltpu.CompilerParams(vmem_limit_bytes=VMEM_LIMIT),
        cost_estimate=pl.CostEstimate(
            flops=2 * count * width * weight.shape[1],
            bytes_accessed=4 * count * width + 2 * weight.size,
            transcendentals=0,
        ),
        name="project",
    )(tokens, gain, weight, cosine, sine)


def block_bias(key_start, query_start, start_row, pad_column):
    shape = (pad_column.shape[0], start_row.shape[1])
    keys = key_start + lax.broadcasted_iota(jnp.int32, shape, 0)
    queries = query_start + lax.broadcasted_iota(jnp.int32, shape, 1)
    allowed = ((keys >= start_row) & (keys <= queries) & (pad_column == 1)) | (keys == queries)
    return jnp.where(allowed, 0.0, MASKED)


def stack_heads(rows, first, group):
    return jnp.concatenate(
        [rows[:, (first + g) * HEAD_DIM : (first + g + 1) * HEAD_DIM] for g in range(group)], axis=0
    )


def times(left, right, left_dim, right_dim):
    return lax.dot_general(
        left, right, (((left_dim,), (right_dim,)), ((), ())), preferred_element_type=jnp.float32
    )


def attend_kernel(
    kv_heads, group, first_ref, query_ref, all_ref, start_ref, pad_ref, out_ref, total_ref, key_heads, value_turned
):
    step = pl.program_id(0)
    heads = kv_heads * group
    query_rows = query_ref.shape[0]
    scale = 1.0 / math.sqrt(HEAD_DIM)

    @pl.when(step == 0)
    def _():
        for k in range(kv_heads):
            at = (heads + k) * HEAD_DIM
            key_heads[k] = all_ref[:, at : at + HEAD_DIM]
            at = (heads + kv_heads + k) * HEAD_DIM
            value_turned[k] = all_ref[:, at : at + HEAD_DIM].astype(jnp.float32).T.astype(jnp.bfloat16)

    query_start = step * query_rows
    last = (query_start + query_rows - 1) // KEY_BLOCK + 1
    pieces = []
    for k in range(kv_heads):
        queries = stack_heads(query_ref[:, : heads * HEAD_DIM], k * group, group)

        def body(block, carry, k=k, queries=queries):
            top, total, mixed = carry
            at = pl.multiple_of(block * KEY_BLOCK, KEY_BLOCK)
            bias = block_bias(at, query_start, start_ref[...], pad_ref[pl.ds(at, KEY_BLOCK), :])
            bias = jnp.concatenate([bias] * group, axis=1)
            scores = times(key_heads[k, pl.ds(at, KEY_BLOCK), :], queries, 1, 1) * scale + bias
            new_top = jnp.maximum(top, jnp.max(scores, axis=0, keepdims=True))
            weight = jnp.exp(scores - new_top)
            shrink = jnp.exp(top - new_top)
            total = total * shrink + jnp.sum(weight, axis=0, keepdims=True)
            mixed = mixed * shrink + times(
                value_turned[k, :, pl.ds(at, KEY_BLOCK)], weight.astype(jnp.bfloat16), 1, 0
            )
            return new_top, total, mixed

        columns = group * query_rows
        top, total, mixed = lax.fori_loop(
            first_ref[step],
            last,
            body,
            (
                jnp.full((1, columns), MASKED, jnp.float32),
                jnp.zeros((1, columns), jnp.float32),
                jnp.zeros((HEAD_DIM, columns), jnp.float32),
            ),
        )
        mixed = mixed / total
        log_total = top + jnp.log(total)
        for g in range(group):
            span = slice(g * query_rows, (g + 1) * query_rows)
            pieces.append(mixed[:, span].T)
            total_ref[k * group + g : k * group + g + 1, :] = log_total[:, span]
    out_ref[...] = jnp.concatenate(pieces, axis=1).astype(jnp.bfloat16)


def attend(first, heads_all, start_row, pad_column, kv_heads, group):
    count, columns = heads_all.shape
    heads = kv_heads * group
    block = math.gcd(count, QUERY_BLOCK)
    return pl.pallas_call(
        functools.partial(attend_kernel, kv_heads, group),
        grid_spec=pltpu.PrefetchScalarGridSpec(
            num_scalar_prefetch=1,
            grid=(count // block,),
            in_specs=[
                pl.BlockSpec((block, columns), lambda i, first: (i, 0)),
                pl.BlockSpec((count, columns), lambda i, first: (0, 0)),
                pl.BlockSpec((1, block), lambda i, first: (0, i)),
                pl.BlockSpec((count, 1), lambda i, first: (0, 0)),
            ],
            out_specs=[
                pl.BlockSpec((block, heads * HEAD_DIM), lambda i, first: (i, 0)),
                pl.BlockSpec((heads, block), lambda i, first: (0, i)),
            ],
            scratch_shapes=[
                pltpu.VMEM((kv_heads, count, HEAD_DIM), jnp.bfloat16),
                pltpu.VMEM((kv_heads, HEAD_DIM, count), jnp.bfloat16),
            ],
        ),
        out_shape=[
            jax.ShapeDtypeStruct((count, heads * HEAD_DIM), jnp.bfloat16),
            jax.ShapeDtypeStruct((heads, count), jnp.float32),
        ],
        compiler_params=pltpu.CompilerParams(vmem_limit_bytes=VMEM_LIMIT),
        cost_estimate=pl.CostEstimate(
            flops=50 * 10**9, bytes_accessed=count * columns, transcendentals=0
        ),
        name="attend",
    )(first, heads_all, heads_all, start_row, pad_column)


def attend_back_kernel(
    kv_heads,
    group,
    first_ref,
    query_ref,
    all_ref,
    start_ref,
    pad_ref,
    total_ref,
    attended_ref,
    grad_ref,
    cosine_turned_ref,
    sine_turned_ref,
    cosine_all_ref,
    sine_all_ref,
    grad_query_ref,
    grad_rest_ref,
    key_heads,
    value_heads,
    key_turned,
    grad_keys,
    grad_values,
):
    step = pl.program_id(0)
    heads = kv_heads * group
    query_rows = query_ref.shape[0]
    scale = 1.0 / math.sqrt(HEAD_DIM)

    @pl.when(step == 0)
    def _():
        for k in range(kv_heads):
            at = (heads + k) * HEAD_DIM
            keys = all_ref[:, at : at + HEAD_DIM]
            key_heads[k] = keys
            key_turned[k] = keys.astype(jnp.float32).T.astype(jnp.bfloat16)
            at = (heads + kv_heads + k) * HEAD_DIM
            value_heads[k] = all_ref[:, at : at + HEAD_DIM]
        grad_keys[...] = jnp.zeros_like(grad_keys)
        grad_values[...] = jnp.zeros_like(grad_values)

    query_start = step * query_rows
    last = (query_start + query_rows - 1) // KEY_BLOCK + 1
    cosine = cosine_turned_ref[...]
    sine = sine_turned_ref[...]
    pieces = []
    for k in range(kv_heads):
        queries = stack_heads(query_ref[:, : heads * HEAD_DIM], k * group, group)
        grads = stack_heads(grad_ref[...], k * group, group)
        attended = stack_heads(attended_ref[...], k * group, group)
        inner = jnp.sum(
            (grads.astype(jnp.float32) * attended.astype(jnp.float32)).T, axis=0, keepdims=True
        )
        log_total = jnp.concatenate(
            [total_ref[k * group + g : k * group + g + 1, :] for g in range(group)], axis=1
        )

        def body(block, turned, k=k, queries=queries, grads=grads, inner=inner, log_total=log_total):
            at = pl.multiple_of(block * KEY_BLOCK, KEY_BLOCK)
            span = pl.ds(at, KEY_BLOCK)
            bias = block_bias(at, query_start, start_ref[...], pad_ref[span, :])
            bias = jnp.concatenate([bias] * group, axis=1)
            scores = times(key_heads[k, span, :], queries, 1, 1) * scale + bias
            weight = jnp.exp(scores - log_total)
            grad_weight = times(value_heads[k, span, :], grads, 1, 1)
            grad_scores = (weight * (grad_weight - inner)).astype(jnp.bfloat16)
            grad_values[k, span, :] += times(weight.astype(jnp.bfloat16), grads, 1, 0)
            grad_keys[k, span, :] += times(grad_scores, queries, 1, 0)
            return turned + times(key_turned[k, :, span], grad_scores, 1, 0)

        turned = lax.fori_loop(
            first_ref[step], last, body, jnp.zeros((HEAD_DIM, group * query_rows), jnp.float32)
        )
        turned = turned * scale
        for g in range(group):
            part = turned[:, g * query_rows : (g + 1) * query_rows]
            leading, trailing = part[:HALF], part[HALF:]
            back = jnp.concatenate(
                [leading * cosine + trailing * sine, trailing * cosine - leading * sine], axis=0
            )
            pieces.append(back.T)
    grad_query_ref[...] = jnp.concatenate(pieces, axis=1).astype(jnp.bfloat16)

    @pl.when(step == pl.num_programs(0) - 1)
    def _():
        rest = []
        cosine_all, sine_all = cosine_all_ref[...].T, sine_all_ref[...].T
        for k in range(kv_heads):
            leading = grad_keys[k][:, :HALF] * scale
            trailing = grad_keys[k][:, HALF:] * scale
            rest.append(leading * cosine_all + trailing * sine_all)
            rest.append(trailing * cosine_all - leading * sine_all)
        for k in range(kv_heads):
            rest.append(grad_values[k])
        grad_rest_ref[...] = jnp.concatenate(rest, axis=1).astype(jnp.bfloat16)


def attend_back(
    first, heads_all, start_row, pad_column, log_totals, attended, grad_attended, cosine, sine, kv_heads, group
):
    count, columns = heads_all.shape
    heads = kv_heads * group
    block = math.gcd(count, QUERY_BLOCK)
    width = heads * HEAD_DIM
    rest = 2 * kv_heads * HEAD_DIM
    return pl.pallas_call(
        functools.partial(attend_back_kernel, kv_heads, group),
        grid_spec=pltpu.PrefetchScalarGridSpec(
            num_scalar_prefetch=1,
            grid=(count // block,),
            in_specs=[
                pl.BlockSpec((block, columns), lambda i, first: (i, 0)),
                pl.BlockSpec((count, columns), lambda i, first: (0, 0)),
                pl.BlockSpec((1, block), lambda i, first: (0, i)),
                pl.BlockSpec((count, 1), lambda i, first: (0, 0)),
                pl.BlockSpec((heads, block), lambda i, first: (0, i)),
                pl.BlockSpec((block, width), lambda i, first: (i, 0)),
                pl.BlockSpec((block, width), lambda i, first: (i, 0)),
                pl.BlockSpec((HALF, block), lambda i, first: (0, i)),
                pl.BlockSpec((HALF, block), lambda i, first: (0, i)),
                pl.BlockSpec((HALF, count), lambda i, first: (0, 0)),
                pl.BlockSpec((HALF, count), lambda i, first: (0, 0)),
            ],
            out_specs=[
                pl.BlockSpec((block, width), lambda i, first: (i, 0)),
                pl.BlockSpec((count, rest), lambda i, first: (0, 0)),
            ],
            scratch_shapes=[
                pltpu.VMEM((kv_heads, count, HEAD_DIM), jnp.bfloat16),
                pltpu.VMEM((kv_heads, count, HEAD_DIM), jnp.bfloat16),
                pltpu.VMEM((kv_heads, HEAD_DIM, count), jnp.bfloat16),
                pltpu.VMEM((kv_heads, count, HEAD_DIM), jnp.float32),
                pltpu.VMEM((kv_heads, count, HEAD_DIM), jnp.float32),
            ],
        ),
        out_shape=[
            jax.ShapeDtypeStruct((count, width), jnp.bfloat16),
            jax.ShapeDtypeStruct((count, rest), jnp.bfloat16),
        ],
        compiler_params=pltpu.CompilerParams(vmem_limit_bytes=VMEM_LIMIT),
        cost_estimate=pl.CostEstimate(
            flops=50 * 10**9, bytes_accessed=count * columns, transcendentals=0
        ),
        name="attend_back",
    )(
        first,
        heads_all,
        heads_all,
        start_row,
        pad_column,
        log_totals,
        attended,
        grad_attended,
        cosine,
        sine,
        cosine,
        sine,
    )


MESH = pl.DeviceIdType.MESH
CHUNK = 64


class Links:
    def __init__(self, dp_count, tensor_count, send, recv, local):
        self.chips, self.low = dp_count // 2, tensor_count // 2
        self.send, self.recv, self.local = send, recv, local
        self.used = 0
        self.used_local = 0
        self.unsent = []
        self.all_low = False
        dp_index, tensor_index = lax.axis_index("dp"), lax.axis_index("tensor")
        self.dp_index, self.tensor_index = dp_index, tensor_index
        self.p, self.c = dp_index // 2, dp_index % 2
        self.th, self.tl = tensor_index // self.low, tensor_index % self.low
        self.home = self.c == self.th
        self.away = self.c != self.th
        self.quarter = self.c * self.low + self.tl

    def at(self, p, c, th, tl):
        return (2 * p + c, th * self.low + tl)

    def chip(self, step):
        p = self.p
        moved = p
        for bit in (1, 2, 4):
            if step & bit:
                moved = moved + bit * (1 - 2 * ((p // bit) % 2))
        return moved

    def chip_peer(self, step):
        return self.at(self.chip(step), self.c, self.th, self.tl)

    def core_peer(self):
        return self.at(self.p, 1 - self.c, self.th, self.tl)

    def low_peer(self, step):
        return self.at(self.p, self.c, self.th, (self.tl + step) % self.low)

    def cross_peer(self):
        return self.at(self.p, 1 - self.c, 1 - self.th, self.tl)

    def turn_peer(self):
        home = self.home.astype(jnp.int32)
        return self.at(
            self.p,
            home * self.c + (1 - home) * (1 - self.c),
            home * (1 - self.th) + (1 - home) * self.th,
            self.tl,
        )

    def back_peer(self):
        home = self.home.astype(jnp.int32)
        return self.at(
            self.p,
            home * (1 - self.c) + (1 - home) * self.c,
            home * self.th + (1 - home) * (1 - self.th),
            self.tl,
        )

    def partner(self):
        return self.at(self.p, self.c, 1 - self.th, self.tl)

    def chip_steps(self):
        return (1, 2) if self.chips == 4 else tuple(range(1, self.chips))

    def enter(self):
        peers = [self.core_peer(), self.cross_peer(), self.partner()]
        peers += [self.chip_peer(step) for step in self.chip_steps()]
        peers += [self.low_peer(step) for step in range(1, self.low)]
        if self.all_low:
            peers += [
                self.at(self.p, self.c, 1 - self.th, (self.tl + step) % self.low)
                for step in range(1, self.low)
            ]
        barrier = pltpu.get_barrier_semaphore()
        for peer in peers:
            pl.semaphore_signal(barrier, inc=1, device_id=peer, device_id_type=MESH)
        pl.semaphore_wait(barrier, len(peers))

    def copy(self, source, target, peer, when=None):
        slot = self.used
        self.used += 1

        def make():
            return pltpu.make_async_remote_copy(
                src_ref=source,
                dst_ref=target,
                send_sem=self.send.at[slot],
                recv_sem=self.recv.at[slot],
                device_id=peer,
                device_id_type=MESH,
            )

        item = Item(make, when)
        self.unsent.append(item)
        return item

    def local_slot(self):
        self.used_local += 1
        return self.used_local - 1

    def keep(self, source, target, when=None):
        slot = self.used_local
        self.used_local += 1
        return Item(lambda: pltpu.make_async_copy(source, target, self.local.at[slot]), when)

    def drop(self, items):
        self.unsent = [item for item in self.unsent if item not in items]

    def leave(self):
        for item in self.unsent:
            item.sent()


class Item:
    def __init__(self, make, when):
        self.make, self.when = make, when

    def run(self, action):
        if self.when is None:
            action(self.make())
        else:
            pl.when(self.when)(lambda: action(self.make()))

    def start(self):
        self.run(lambda copy: copy.start())

    def arrived(self):
        self.run(lambda copy: copy.wait_recv())

    def sent(self):
        self.run(lambda copy: copy.wait_send())

    def done(self):
        self.run(lambda copy: copy.wait())


class UnitGather:
    def __init__(self, links, shard, unit):
        rows = shard.shape[0]
        mine = unit.at[pl.ds(links.c * rows, rows)]
        self.first = links.copy(shard, mine, links.turn_peer())
        self.second = links.copy(shard, mine, links.cross_peer(), links.away)
        self.own = links.keep(shard, mine, links.home)

    def turn(self):
        self.first.start()
        self.second.start()
        self.own.start()

    def settle_unit(self):
        self.first.arrived()
        self.second.arrived()
        self.own.done()


class WeightGather:
    def __init__(self, links, shard, full):
        self.links, self.shard, self.full = links, shard, full
        rows = shard.shape[0]
        self.rows = rows
        mine = full.at[pl.ds(links.dp_index * rows, rows)]
        self.first = links.copy(shard, mine, links.turn_peer())
        self.second = links.copy(shard, mine, links.cross_peer(), links.away)
        self.own = links.keep(shard, mine, links.home)
        unit = 2 * rows
        self.direct = []
        self.forward = []
        here = full.at[pl.ds(links.p * unit, unit)]
        for step in links.chip_steps():
            self.direct.append(links.copy(here, here, links.chip_peer(step)))
        if links.chips == 4:
            top = full.at[pl.ds(links.chip(2) * unit, rows)]
            bottom = full.at[pl.ds(links.chip(1) * unit + rows, rows)]
            self.forward.append(links.copy(top, top, links.chip_peer(1)))
            self.forward.append(links.copy(bottom, bottom, links.chip_peer(2)))

    def turn(self):
        self.first.start()
        self.second.start()
        self.own.start()

    def settle_unit(self):
        self.first.arrived()
        self.second.arrived()
        self.own.done()

    def spread(self):
        self.settle_unit()
        self.spread_unit()

    def spread_unit(self):
        for item in self.direct:
            item.start()

    def pass_on(self):
        for item in self.direct:
            item.arrived()
        for item in self.forward:
            item.start()

    def finish(self):
        for item in self.forward:
            item.arrived()


class RowGather:
    def __init__(self, links, full, rows, low_when=None):
        self.links = links
        mine = full.at[pl.ds(links.quarter * rows, rows)]
        self.to_core = links.copy(mine, mine, links.core_peer())
        self.to_low = []
        self.onward = []
        for step in range(1, links.low):
            self.to_low.append(links.copy(mine, mine, links.low_peer(step), low_when))
            came = (links.tl + links.low - step) % links.low
            block = full.at[pl.ds((links.c * links.low + came) * rows, rows)]
            self.onward.append(links.copy(block, block, links.core_peer()))

    def start(self):
        for item in self.to_low:
            item.start()
        self.to_core.start()

    def pass_on(self):
        for arriving, item in zip(self.to_low, self.onward):
            arriving.arrived()
            item.start()

    def finish(self):
        self.to_core.arrived()
        self.finish_onward()

    def finish_onward(self):
        for item in self.onward:
            item.arrived()


class RowScatter:
    def __init__(self, links, partial, mine, others, sums, arrivals, rows):
        self.links, self.rows = links, rows
        self.mine, self.others, self.sums, self.arrivals = mine, others, sums, arrivals
        low = links.low
        self.load = links.keep(partial.at[pl.ds(links.c * low * rows, low * rows)], mine)
        self.swap = links.copy(
            partial.at[pl.ds((1 - links.c) * low * rows, low * rows)], others, links.core_peer()
        )
        self.sends = [
            links.copy(sums.at[step - 1], arrivals.at[step - 1], links.low_peer(step))
            for step in range(1, low)
        ]

    def start(self):
        self.swap.start()
        self.load.start()

    def send_sums(self):
        self.load.done()
        self.swap.arrived()
        for step in range(1, self.links.low):
            base = ((self.links.tl + step) % self.links.low) * self.rows

            @pl.loop(0, self.rows // CHUNK)
            def _(i, base=base, step=step):
                span = pl.ds(pl.multiple_of(base + i * CHUNK, CHUNK), CHUNK)
                total = self.mine[span].astype(jnp.float32) + self.others[span].astype(jnp.float32)
                self.sums[step - 1, pl.ds(pl.multiple_of(i * CHUNK, CHUNK), CHUNK)] = total.astype(jnp.bfloat16)

            self.sends[step - 1].start()

    def collect(self, use):
        for item in self.sends:
            item.arrived()
        base = self.links.tl * self.rows

        @pl.loop(0, self.rows // CHUNK)
        def _(i):
            at = pl.multiple_of(i * CHUNK, CHUNK)
            span = pl.ds(pl.multiple_of(base + at, CHUNK), CHUNK)
            total = self.mine[span].astype(jnp.float32) + self.others[span].astype(jnp.float32)
            for step in range(1, self.links.low):
                total = total + self.arrivals[step - 1, pl.ds(at, CHUNK)].astype(jnp.float32)
            use(pl.ds(at, CHUNK), total)


def scatter_scratch(low, rows, width):
    return [
        pltpu.VMEM((low * rows, width), jnp.bfloat16),
        pltpu.VMEM((low * rows, width), jnp.bfloat16),
        pltpu.VMEM((low - 1, rows, width), jnp.bfloat16),
        pltpu.VMEM((low - 1, rows, width), jnp.bfloat16),
    ]


def semaphores(count, local_count):
    return [
        pltpu.SemaphoreType.DMA((count,)),
        pltpu.SemaphoreType.DMA((count,)),
        pltpu.SemaphoreType.DMA((local_count,)),
    ]


def anywhere(count):
    return [pl.BlockSpec(memory_space=pl.ANY)] * count


def in_vmem(count):
    return [pl.BlockSpec(memory_space=pltpu.VMEM)] * count


def link_params(number):
    return pltpu.CompilerParams(
        collective_id=number, has_side_effects=True, vmem_limit_bytes=LINK_VMEM_LIMIT
    )


ADD_ROWS = 32


def cut(columns, most):
    half = columns // 2
    return half if columns > most and half % 128 == 0 else columns


def product(left, right, out, left_dim, right_dim, rows, columns, finish=None, extra=(), extra_out=()):
    depth = left.shape[left_dim]
    count, width = out.shape
    rows, columns = math.gcd(count, rows), cut(width, columns)

    def body(left_ref, right_ref, *refs):
        value = times(left_ref[...], right_ref[...], left_dim, right_dim)
        if finish is None:
            refs[0][...] = value.astype(refs[0].dtype)
        else:
            finish(value, *refs)

    def block(shape, index):
        return pl.BlockSpec(shape, index)

    left_spec = (
        block((rows, depth), lambda j, i: (i, 0)) if left_dim == 1 else block((depth, rows), lambda j, i: (0, i))
    )
    right_spec = (
        block((columns, depth), lambda j, i: (j, 0))
        if right_dim == 1
        else block((depth, columns), lambda j, i: (0, j))
    )
    whole = block((rows, columns), lambda j, i: (i, j))
    extra_specs = [
        whole if ref.shape[1] == width else block((rows, ref.shape[1]), lambda j, i: (i, 0)) for ref in extra
    ]
    pltpu.emit_pipeline(
        body,
        grid=(width // columns, count // rows),
        in_specs=[left_spec, right_spec] + extra_specs,
        out_specs=[whole] * (1 + len(extra_out)),
    )(left, right, *extra, out, *extra_out)


def row_loop(rows, body):
    @pl.loop(0, rows // ADD_ROWS)
    def _(i):
        body(pl.ds(pl.multiple_of(i * ADD_ROWS, ADD_ROWS), ADD_ROWS))


class WeightScatter:
    def __init__(self, links, partial, result, inbox, turned, sums, leaving, stage):
        self.links, self.partial, self.result = links, partial, result
        self.inbox, self.turned, self.sums, self.leaving = inbox, turned, sums, leaving
        rows = partial.shape[0] // (2 * links.chips)
        self.rows = rows
        width = partial.shape[1]
        self.stage = [stage.at[i, pl.ds(0, rows), pl.ds(0, width)] for i in range(3)]
        self.both = links.chips == 4
        self.direct_started = False
        self.loads = [
            links.local_slot() for _ in range(3)
        ]
        if self.both:
            x_peer, y_peer = links.chip_peer(1), links.chip_peer(2)
            self.before = [
                links.copy(self.part(3, 0), inbox.at[0], x_peer),
                links.copy(self.part(3, 1), inbox.at[1], y_peer),
            ]
            self.direct = [
                links.copy(self.part(1, 0), inbox.at[2], x_peer),
                links.copy(self.part(2, 1), inbox.at[3], y_peer),
            ]
            self.summed = [
                links.copy(sums.at[0], inbox.at[4], y_peer),
                links.copy(sums.at[1], inbox.at[5], x_peer),
            ]
            self.arrivals = ((2, 4), (5, 3))
        else:
            self.before, self.summed, self.direct = [], [], []
            for step in links.chip_steps():
                for half in range(2):
                    at = 2 * (step - 1) + half
                    self.direct.append(
                        links.copy(self.part(step, half), inbox.at[at], links.chip_peer(step))
                    )
            self.arrivals = tuple(
                tuple(2 * (step - 1) + half for step in links.chip_steps()) for half in range(2)
            )
        self.first = links.copy(leaving.at[0], turned.at[0], links.back_peer())
        self.second = links.copy(leaving.at[1], turned.at[1], links.cross_peer(), links.away)

    def part(self, step, half):
        start = (2 * self.links.chip(step) + half) * self.rows
        return self.partial.at[pl.ds(start, self.rows)]

    def load(self, sources):
        copies = [
            pltpu.make_async_copy(source, stage, self.links.local.at[slot])
            for source, stage, slot in zip(sources, self.stage, self.loads)
        ]
        for copy in copies:
            copy.start()
        for copy in copies:
            copy.wait()

    def start(self, which):
        for item in getattr(self, which):
            item.start()

    def start_direct(self):
        if not self.direct_started:
            self.start("direct")
        self.direct_started = True

    def arrived(self, which):
        for item in getattr(self, which):
            item.arrived()

    def add_before(self):
        if not self.both:
            self.start_direct()
            return
        self.arrived("before")
        self.start_direct()
        for index, part in ((0, self.part(2, 0)), (1, self.part(1, 1))):
            self.load([part, self.inbox.at[index]])

            def body(span, index=index):
                total = self.stage[0][span].astype(jnp.float32) + self.stage[1][span].astype(jnp.float32)
                self.sums[index, span] = total.astype(jnp.bfloat16)

            row_loop(self.rows, body)
            self.summed[index].start()

    def turn(self):
        self.reduce()
        self.send_turned()

    def send_turned(self):
        self.first.start()
        self.second.start()

    def reduce(self):
        links = self.links
        for half in range(2):
            sources = [self.part(0, half)] + [self.inbox.at[at] for at in self.arrivals[half]]
            kept = links.c == half
            if len(sources) == 3:
                self.load(sources)

                def body(span, half=half, kept=kept):
                    total = self.stage[0][span].astype(jnp.float32)
                    total = total + self.stage[1][span].astype(jnp.float32)
                    self.settle(span, total + self.stage[2][span].astype(jnp.float32), kept)

                row_loop(self.rows, body)
            else:
                self.fold(sources, kept)

    def fold(self, sources, kept):
        rows = self.rows
        total = self.total
        self.load(sources[:1])
        row_loop(rows, lambda span: total.__setitem__(span, self.stage[0][span].astype(jnp.float32)))
        for source in sources[1:]:
            self.load([source])

            def body(span):
                total[span] = total[span] + self.stage[0][span].astype(jnp.float32)

            row_loop(rows, body)
        row_loop(rows, lambda span: self.settle(span, total[span], kept))

    def settle(self, span, total, kept):
        low = total.astype(jnp.bfloat16)
        links = self.links

        @pl.when(kept & links.home)
        def _():
            self.result[span] = total

        @pl.when(kept & links.away)
        def _():
            self.leaving[0, span] = low

        @pl.when(jnp.logical_not(kept) & links.home)
        def _():
            self.leaving[0, span] = low

        @pl.when(jnp.logical_not(kept) & links.away)
        def _():
            self.leaving[1, span] = low

    def finish(self):
        links = self.links
        self.first.arrived()
        self.second.arrived()

        @pl.when(links.home)
        def _():
            def body(span):
                self.result[span] = self.result[span] + self.turned[0, span].astype(jnp.float32)

            row_loop(self.rows, body)

        @pl.when(links.away)
        def _():
            def body(span):
                self.result[span] = self.turned[1, span].astype(jnp.float32) + self.turned[0, span].astype(
                    jnp.float32
                )

            row_loop(self.rows, body)


class TurnScatter:
    def __init__(self, links, mine, first, second, result, turned):
        self.links, self.mine, self.result, self.turned = links, mine, result, turned
        self.rows = mine.shape[0]
        self.first = links.copy(first, turned.at[0], links.back_peer())
        self.second = links.copy(second, turned.at[1], links.cross_peer(), links.away)

    def send_turned(self):
        self.first.start()
        self.second.start()

    def finish(self):
        self.first.arrived()
        self.second.arrived()

        @pl.when(self.links.home)
        def _():
            def body(span):
                self.result[span] = self.mine[span] + self.turned[0, span].astype(jnp.float32)

            row_loop(self.rows, body)

        @pl.when(self.links.away)
        def _():
            def body(span):
                self.result[span] = self.turned[1, span].astype(jnp.float32) + self.turned[0, span].astype(
                    jnp.float32
                )

            row_loop(self.rows, body)


def weight_scatter_scratch(chips, rows, width):
    return [pltpu.VMEM((2, rows, width), jnp.bfloat16)] * 3


def inbox_shape(chips, rows, width):
    count = 6 if chips == 4 else 2 * (chips - 1)
    return jax.ShapeDtypeStruct((count, rows, width), jnp.bfloat16)


def scatter_shapes(chips, partial):
    rows = partial.shape[0] // (2 * chips)
    width = partial.shape[1]
    return rows, width


def tail_kernel(
    dp_count,
    tensor_count,
    gain_column,
    partial,
    tokens_all,
    grad_rows,
    attended,
    normed,
    grad_heads,
    gain_parts,
    up_mine,
    up_first,
    up_second,
    grad_residual_ref,
    gain_ref,
    input_ref,
    up_ref,
    output_ref,
    first_ref,
    output_in,
    first_in,
    grad_output,
    grad_first,
    *scratch,
):
    output_work, first_work = scratch[:3], scratch[3:6]
    up_turned, stage, own_ref, leaving, crossed, mine, others, sums, arrivals = scratch[6:15]
    gains_out, gains_in, total = scratch[15:18]
    links = Links(dp_count, tensor_count, *scratch[18:])
    links.all_low = True
    rows = own_ref.shape[0]
    load_own = links.keep(tokens_all.at[pl.ds(links.quarter * rows, rows)], own_ref)
    scatter = RowScatter(links, partial, mine, others, sums, arrivals, rows)
    crossing = links.copy(leaving, crossed, links.cross_peer(), links.away)
    up = TurnScatter(links, up_mine, up_first, up_second, up_ref, up_turned)
    weights = []
    for grad, result, inbox, work in (
        (grad_output, output_ref, output_in, output_work),
        (grad_first, first_ref, first_in, first_work),
    ):
        turned, added, turning = work
        made = WeightScatter(links, grad, result, inbox, turned, added, turning, stage)
        made.total = None if made.both else total.at[pl.ds(0, made.rows), pl.ds(0, grad.shape[1])]
        weights.append(made)
    output, first = weights
    gain_sends = []
    for step in range(1, tensor_count):
        other = (links.tensor_index + step) % tensor_count
        gain_sends.append(
            links.copy(gains_out, gains_in.at[step - 1], links.at(links.p, links.c, other // links.low, other % links.low))
        )

    links.enter()
    scatter.start()
    load_own.start()
    up.send_turned()
    scatter.send_sums()
    load_own.done()

    def finish(value, parts_ref, out_ref):
        columns = value.shape[1]
        out_ref[:, : columns - 128] = value[:, : columns - 128].astype(jnp.bfloat16)
        out_ref[:, columns - 128 :] = (value[:, columns - 128 :] + parts_ref[...]).astype(jnp.bfloat16)

    product(normed, grad_heads, grad_first, 0, 0, 512, 1024, finish, (gain_parts,))
    first.start("before")
    product(grad_rows, attended, grad_output, 0, 0, 512, 1024)
    first.add_before()
    output.start("before")

    def use(span, grad_normed):
        own = own_ref[span].astype(jnp.float32)
        root = lax.rsqrt(jnp.mean(own * own, axis=-1, keepdims=True) + epsilon)
        unit = own * root
        scaled = grad_normed * gain_ref[...]
        grad = grad_residual_ref[span] + root * (
            scaled - unit * jnp.mean(scaled * unit, axis=-1, keepdims=True)
        )
        input_ref[span] = grad
        leaving[span] = grad.astype(jnp.bfloat16)

    scatter.collect(use)
    crossing.start()
    output.add_before()
    first.arrived("direct")
    first.arrived("summed")
    first.turn()
    crossing.arrived()

    @pl.when(links.away)
    def _():
        def body(span):
            input_ref[span] = crossed[span].astype(jnp.float32)

        row_loop(rows, body)

    output.arrived("direct")
    output.arrived("summed")
    output.turn()
    up.finish()
    first.finish()
    width = first_ref.shape[1]
    gains_out[...] = first_ref[:, width - 128 :]
    for item in gain_sends:
        item.start()
    output.finish()
    for item in gain_sends:
        item.arrived()
    summed = gains_out[...]
    for step in range(1, tensor_count):
        summed = summed + gains_in[step - 1]
    column = width - 128 + lax.broadcasted_iota(jnp.int32, summed.shape, 1)
    first_ref[:, width - 128 :] = jnp.where(column >= gain_column, summed, gains_out[...])
    links.leave()


def tail(
    dp_count,
    tensor_count,
    gain_column,
    partial,
    tokens_all,
    grad_rows,
    attended,
    normed,
    grad_heads,
    gain_parts,
    up_mine,
    up_first,
    up_second,
    grad_residual,
    gain,
):
    rows, width = grad_residual.shape
    low, chips = tensor_count // 2, dp_count // 2
    features = width
    partials = [
        jax.ShapeDtypeStruct((features, attended.shape[1]), jnp.bfloat16),
        jax.ShapeDtypeStruct((features, grad_heads.shape[1]), jnp.bfloat16),
    ]
    shapes = [scatter_shapes(chips, grad) for grad in partials]
    widest = max(columns for _, columns in shapes)
    most = shapes[0][0]
    scratch = []
    for block, columns in shapes:
        scratch += weight_scatter_scratch(chips, block, columns)
    scratch += [pltpu.VMEM((2,) + up_mine.shape, jnp.bfloat16)]
    scratch += [pltpu.VMEM((3, most, widest), jnp.bfloat16)]
    scratch += [pltpu.VMEM((rows, width), jnp.bfloat16)] * 3
    scratch += scatter_scratch(low, rows, width)
    scratch += [
        pltpu.VMEM((most, 128), jnp.float32),
        pltpu.VMEM((tensor_count - 1, most, 128), jnp.float32),
        pltpu.VMEM((most, widest) if chips != 4 else (8, 128), jnp.float32),
    ]
    return pl.pallas_call(
        functools.partial(tail_kernel, dp_count, tensor_count, gain_column),
        out_shape=[jax.ShapeDtypeStruct((rows, width), jnp.float32)]
        + [jax.ShapeDtypeStruct(shape, jnp.float32) for shape in [up_mine.shape] + shapes]
        + [inbox_shape(chips, *shape) for shape in shapes]
        + partials,
        in_specs=anywhere(7) + in_vmem(5),
        out_specs=in_vmem(4) + anywhere(4),
        scratch_shapes=scratch + semaphores(96, 24),
        compiler_params=link_params(3),
        name="tail",
    )(
        partial,
        tokens_all,
        grad_rows,
        attended,
        normed,
        grad_heads,
        gain_parts,
        up_mine,
        up_first,
        up_second,
        grad_residual,
        gain,
    )[:4]


def gather_first_kernel(
    dp_count, tensor_count, tokens, first, output, gate, tokens_all, first_full, output_full, gate_unit, *sems
):
    links = Links(dp_count, tensor_count, *sems)
    rows = tokens.shape[0]
    mine = tokens_all.at[pl.ds(links.tensor_index * rows, rows)]
    crossing = links.copy(tokens, mine, links.cross_peer(), links.away)
    staying = links.keep(tokens, mine, links.home)
    gather_tokens = RowGather(links, tokens_all, rows)
    weights = [
        WeightGather(links, shard, full)
        for shard, full in ((first, first_full), (output, output_full))
    ]
    weights.append(UnitGather(links, gate, gate_unit))
    links.enter()
    weights[0].turn()
    crossing.start()
    staying.start()

    @pl.when(links.home)
    def _():
        staying.make().wait()
        gather_tokens.start()

    weights[0].spread()
    weights[1].turn()

    @pl.when(links.away)
    def _():
        crossing.make().wait_recv()
        gather_tokens.start()

    weights[1].spread()
    weights[2].turn()
    weights[0].pass_on()
    gather_tokens.pass_on()
    weights[1].pass_on()
    weights[0].finish()
    gather_tokens.finish()
    weights[1].finish()
    weights[2].settle_unit()
    links.leave()


def gather_first(dp_count, tensor_count, tokens, first, output, gate):
    def full(shard, times):
        return jax.ShapeDtypeStruct((shard.shape[0] * times, shard.shape[1]), shard.dtype)

    return pl.pallas_call(
        functools.partial(gather_first_kernel, dp_count, tensor_count),
        out_shape=[
            full(tokens, tensor_count),
            full(first, dp_count),
            full(output, dp_count),
            full(gate, 2),
        ],
        in_specs=in_vmem(4),
        out_specs=anywhere(4),
        scratch_shapes=semaphores(64, 8),
        compiler_params=link_params(0),
        name="gather_first",
    )(tokens, first, output, gate)


def middle_kernel(
    dp_count,
    tensor_count,
    moved_units,
    partial,
    tokens_all,
    cot,
    cot_low,
    up,
    up_turned,
    up_crossed,
    down,
    gate_unit,
    *rest,
):
    gate_units, rest = rest[:moved_units], rest[moved_units:]
    gain_ref, residual_ref, normed_all, cot_all, up_full, down_full, gate_full = rest[:7]
    gate_values, up_values, hidden = rest[7:10]
    own, normed, mine, others, sums, arrivals = rest[10:16]
    links = Links(dp_count, tensor_count, *rest[16:])
    rows = cot.shape[0]
    scatter = RowScatter(links, partial, mine, others, sums, arrivals, rows)
    gather_normed = RowGather(links, normed_all, rows)
    gather_cot = RowGather(links, cot_all, rows, links.away)
    gate_gather = WeightGather(links, up, gate_full)
    up_gather = WeightGather(links, up, up_full)
    down_gather = WeightGather(links, down, down_full)
    shard = up.shape[0]
    here = up_full.at[pl.ds(links.dp_index * shard, shard)]
    beside = up_full.at[pl.ds((2 * links.p + 1 - links.c) * shard, shard)]
    quarter = pl.ds(links.quarter * rows, rows)
    placements = [
        links.keep(up, here, links.home),
        links.keep(up_turned, beside, links.home),
        links.keep(up_turned, here, links.away),
        links.keep(up_crossed, beside, links.away),
    ]
    gate_places = [links.chip(step) * 2 * shard for step in (0,) + links.chip_steps()]
    gate_placements = [
        links.keep(unit, gate_full.at[pl.ds(at, unit.shape[0])])
        for at, unit in zip(gate_places, (gate_unit,) + tuple(gate_units))
    ]
    cot_crossing = links.copy(cot, cot_all.at[pl.ds(links.tensor_index * rows, rows)], links.cross_peer(), links.away)
    cot_placements = [
        links.keep(
            cot_low.at[step - 1],
            cot_all.at[pl.ds((links.c * links.low + (links.tl + links.low - step) % links.low) * rows, rows)],
            links.home,
        )
        for step in range(1, links.low)
    ]
    cot_staying = links.keep(cot, cot_all.at[quarter], links.home)
    load = links.keep(tokens_all.at[quarter], own)
    store = links.keep(normed, normed_all.at[quarter])
    links.drop([up_gather.first, up_gather.second, gate_gather.first, gate_gather.second] + gate_gather.direct)
    links.enter()
    scatter.start()
    load.start()
    for item in gate_placements + placements:
        item.start()
    for item in gate_placements:
        item.done()
    for item in gate_gather.forward:
        item.start()
    for item in placements:
        item.done()
    scatter.send_sums()
    up_gather.spread_unit()
    down_gather.turn()
    cot_staying.start()
    for item in cot_placements:
        item.start()
    load.done()

    def use(span, total):
        residual = own[span].astype(jnp.float32) + total
        residual_ref[span] = residual
        root = lax.rsqrt(jnp.mean(residual * residual, axis=-1, keepdims=True) + epsilon)
        normed[span] = (residual * root * gain_ref[...]).astype(jnp.bfloat16)

    scatter.collect(use)
    store.start()
    store.done()
    gather_normed.start()
    down_gather.settle_unit()
    cot_crossing.start()
    up_gather.pass_on()
    down_gather.spread_unit()
    gate_gather.finish()
    gather_normed.pass_on()
    cot_staying.done()
    for item in cot_placements:
        item.done()
    cot_crossing.arrived()
    gather_cot.start()
    up_gather.finish()
    gather_normed.finish()
    product(normed_all, gate_full, gate_values, 1, 0, 512, 1024)
    down_gather.pass_on()
    gather_cot.pass_on()

    def finish(up, gate_ref, up_ref, hidden_ref):
        gate = gate_ref[...]
        up_ref[...] = up
        hidden_ref[...] = (gate * jax.nn.sigmoid(gate) * up).astype(jnp.bfloat16)

    product(normed_all, up_full, up_values, 1, 0, 256, 1024, finish, (gate_values,), (hidden,))
    down_gather.finish()
    gather_cot.finish()
    links.leave()


def middle(
    dp_count, tensor_count, partial, tokens_all, cot, cot_low, up, up_turned, up_crossed, down, gate_unit, gate_units, gain
):
    rows, width = cot.shape
    low = tensor_count // 2

    def full(shard, times):
        return jax.ShapeDtypeStruct((shard.shape[0] * times, shard.shape[1]), shard.dtype)

    return pl.pallas_call(
        functools.partial(middle_kernel, dp_count, tensor_count, len(gate_units)),
        out_shape=[
            jax.ShapeDtypeStruct((rows, width), jnp.float32),
            full(cot, tensor_count),
            full(cot, tensor_count),
            full(up, dp_count),
            full(down, dp_count),
            full(gate_unit, dp_count // 2),
            jax.ShapeDtypeStruct((rows * tensor_count, up.shape[1]), jnp.float32),
            jax.ShapeDtypeStruct((rows * tensor_count, up.shape[1]), jnp.float32),
            jax.ShapeDtypeStruct((rows * tensor_count, up.shape[1]), jnp.bfloat16),
        ],
        in_specs=anywhere(2) + in_vmem(len(gate_units) + 8),
        out_specs=in_vmem(1) + anywhere(8),
        scratch_shapes=[pltpu.VMEM((rows, width), jnp.bfloat16)] * 2
        + scatter_scratch(low, rows, width)
        + semaphores(64, 24),
        compiler_params=link_params(1),
        name="middle",
    )(partial, tokens_all, cot, cot_low, up, up_turned, up_crossed, down, gate_unit, *gate_units, gain)


def turn_back_kernel(
    dp_count,
    tensor_count,
    partial,
    cot_all,
    normed_ffn,
    gate_signal,
    up_signal,
    hidden,
    down_full,
    residual_ref,
    gain_ref,
    grad_residual_ref,
    gain_part_ref,
    down_ref,
    gate_ref,
    gate_turning,
    grad_rows,
    down_in,
    gate_in,
    grad_down,
    grad_gate,
    grad_up,
    down_part,
    pair_own,
    pair_low,
    own,
    low_grad,
    turned,
    added,
    turning,
    gate_added,
    stage,
    total_ref,
    mine,
    others,
    sums,
    arrivals,
    *sems,
):
    links = Links(dp_count, tensor_count, *sems)
    rows = residual_ref.shape[0]
    down = WeightScatter(links, grad_down, down_ref, down_in, turned, added, turning, stage)
    gate = WeightScatter(links, grad_gate, gate_ref, gate_in, turned, gate_added, gate_turning, stage)
    down.total = gate.total = total_ref
    links.drop([gate.first, gate.second])
    low = links.low
    half = low * residual_ref.shape[0]
    swap_layer = links.copy(down_part.at[pl.ds((1 - links.c) * half, half)], others, links.core_peer())
    load_layer = links.keep(down_part.at[pl.ds(links.c * half, half)], mine)
    keep_own = links.keep(low_grad, pair_own)
    keep_low = [links.keep(sums.at[step - 1], pair_low.at[step - 1]) for step in range(1, low)]
    scatter = RowScatter(links, partial, mine, others, sums, arrivals, rows)
    gather = RowGather(links, grad_rows, rows)
    quarter = pl.ds(links.quarter * rows, rows)
    load = links.keep(cot_all.at[quarter], own)
    store = links.keep(low_grad, grad_rows.at[quarter])
    links.enter()
    scatter.start()
    load.start()
    unit = 2 * down.rows

    def down_unit(step):
        at = pl.multiple_of(links.chip(step) * unit, 128)
        product(cot_all.at[:, pl.ds(at, unit)], hidden, grad_down.at[pl.ds(at, unit)], 0, 0, unit, 1024)

    if down.both and unit % 128 == 0:
        down_unit(3)
        down.start("before")
        scatter.send_sums()
        down_unit(1)
        down_unit(2)
        down.start_direct()
        down_unit(0)
    else:
        product(cot_all, hidden, grad_down, 0, 0, 512, 1024)
        down.start("before")
        scatter.send_sums()
    load.done()
    down.add_before()
    product(normed_ffn, gate_signal, grad_gate, 0, 0, 512, 1024)
    gate.start("before")
    gain_part_ref[...] = jnp.zeros_like(gain_part_ref)

    def use(span, grad_normed):
        residual = residual_ref[span]
        root = lax.rsqrt(jnp.mean(residual * residual, axis=-1, keepdims=True) + epsilon)
        unit = residual * root
        gain_part_ref[...] += jnp.sum(grad_normed * unit, axis=0, keepdims=True)
        scaled = grad_normed * gain_ref[...]
        grad = own[span].astype(jnp.float32) + root * (
            scaled - unit * jnp.mean(scaled * unit, axis=-1, keepdims=True)
        )
        grad_residual_ref[span] = grad
        low_grad[span] = grad.astype(jnp.bfloat16)

    scatter.collect(use)
    store.start()
    store.done()
    gather.start()
    down.arrived("direct")
    gate.start_direct()
    down.arrived("summed")
    down.turn()
    gate.add_before()
    product(normed_ffn, up_signal, grad_up, 0, 0, 512, 1024)
    gather.pass_on()
    product(hidden, down_full, down_part, 1, 1, 512, 1024)
    gather.to_core.arrived()
    swap_layer.start()
    load_layer.start()
    gate.arrived("direct")
    gate.arrived("summed")
    gate.reduce()
    for item in scatter.sends:
        item.sent()
    links.drop(scatter.sends)
    load_layer.done()
    swap_layer.arrived()
    for step in range(low):
        base = ((links.tl + step) % low) * rows

        @pl.loop(0, rows // CHUNK)
        def _(i, base=base, step=step):
            at = pl.multiple_of(i * CHUNK, CHUNK)
            span = pl.ds(pl.multiple_of(base + at, CHUNK), CHUNK)
            total = (mine[span].astype(jnp.float32) + others[span].astype(jnp.float32)).astype(jnp.bfloat16)
            if step:
                sums[step - 1, pl.ds(at, CHUNK)] = total
            else:
                low_grad[pl.ds(at, CHUNK)] = total

    keep_own.start()
    for item in keep_low:
        item.start()
    down.finish()
    gather.finish_onward()
    keep_own.done()
    for item in keep_low:
        item.done()
    links.leave()


def turn_back(
    dp_count,
    tensor_count,
    partial,
    cot_all,
    normed_ffn,
    gate_signal,
    up_signal,
    hidden,
    down_full,
    residual,
    gain,
):
    rows, width = residual.shape
    low, chips = tensor_count // 2, dp_count // 2
    grad = jax.ShapeDtypeStruct((width, hidden.shape[1]), jnp.bfloat16)
    block, columns = scatter_shapes(chips, grad)
    return pl.pallas_call(
        functools.partial(turn_back_kernel, dp_count, tensor_count),
        out_shape=[
            jax.ShapeDtypeStruct((rows, width), jnp.float32),
            jax.ShapeDtypeStruct((1, width), jnp.float32),
            jax.ShapeDtypeStruct((block, columns), jnp.float32),
            jax.ShapeDtypeStruct((block, columns), jnp.float32),
            jax.ShapeDtypeStruct((2, block, columns), jnp.bfloat16),
            jax.ShapeDtypeStruct((rows * tensor_count, width), jnp.bfloat16),
            inbox_shape(chips, block, columns),
            inbox_shape(chips, block, columns),
            grad,
            grad,
            grad,
            jax.ShapeDtypeStruct((rows * tensor_count, width), jnp.bfloat16),
            jax.ShapeDtypeStruct((rows, width), jnp.bfloat16),
            jax.ShapeDtypeStruct((low - 1, rows, width), jnp.bfloat16),
        ],
        in_specs=anywhere(7) + in_vmem(2),
        out_specs=in_vmem(5) + anywhere(9),
        scratch_shapes=[pltpu.VMEM((rows, width), jnp.bfloat16)] * 2
        + weight_scatter_scratch(chips, block, columns)
        + [
            pltpu.VMEM((2, block, columns), jnp.bfloat16),
            pltpu.VMEM((3, block, columns), jnp.bfloat16),
            pltpu.VMEM((block, columns) if chips != 4 else (8, 128), jnp.float32),
        ]
        + scatter_scratch(low, rows, width)
        + semaphores(64, 24),
        compiler_params=link_params(2),
        name="turn_back",
    )(partial, cot_all, normed_ffn, gate_signal, up_signal, hidden, down_full, residual, gain)


def hidden_back_kernel(
    cot_all, down_full, gate_values, up_values, gate_full, up_full, gate_signal, up_signal, partial
):
    def signals(grad_hidden, gate_ref, up_ref, gate_out, up_out):
        gate = gate_ref[...]
        sigmoid = jax.nn.sigmoid(gate)
        grad_hidden = grad_hidden * sigmoid
        gate_out[...] = (grad_hidden * up_ref[...] * (1.0 + gate * (1.0 - sigmoid))).astype(jnp.bfloat16)
        up_out[...] = (grad_hidden * gate).astype(jnp.bfloat16)

    product(
        cot_all, down_full, gate_signal, 1, 0, 256, 1024, signals, (gate_values, up_values), (up_signal,)
    )
    count, width = partial.shape
    depth = gate_full.shape[1]
    rows, columns = math.gcd(count, 512), cut(width, 1536)

    def body(gate_ref, up_ref, gate_weight, up_weight, out_ref):
        total = times(gate_ref[...], gate_weight[...], 1, 1) + times(up_ref[...], up_weight[...], 1, 1)
        out_ref[...] = total.astype(jnp.bfloat16)

    pltpu.emit_pipeline(
        body,
        grid=(width // columns, count // rows),
        in_specs=[pl.BlockSpec((rows, depth), lambda j, i: (i, 0))] * 2
        + [pl.BlockSpec((columns, depth), lambda j, i: (j, 0))] * 2,
        out_specs=[pl.BlockSpec((rows, columns), lambda j, i: (i, j))],
    )(gate_signal, up_signal, gate_full, up_full, partial)


def hidden_back(cot_all, down_full, gate_values, up_values, gate_full, up_full):
    signal = jax.ShapeDtypeStruct(gate_values.shape, jnp.bfloat16)
    flops = 6 * cot_all.size * gate_values.shape[1]
    return pl.pallas_call(
        hidden_back_kernel,
        out_shape=[signal, signal, jax.ShapeDtypeStruct(cot_all.shape, jnp.bfloat16)],
        in_specs=anywhere(6),
        out_specs=anywhere(3),
        compiler_params=pltpu.CompilerParams(vmem_limit_bytes=LINK_VMEM_LIMIT),
        cost_estimate=pl.CostEstimate(flops=flops, bytes_accessed=flops // 1000, transcendentals=0),
        name="hidden_back",
    )(cot_all, down_full, gate_values, up_values, gate_full, up_full)


def starts_of(positions, length_row):
    ends = jnp.cumsum(length_row)
    inside = positions[:, None] >= ends[None, :]
    return jnp.sum(jnp.where(inside, length_row[None, :], 0), axis=1)


def rotary_tables(positions):
    frequency = jnp.exp(
        jnp.arange(HALF, dtype=jnp.float32) * (-2.0 * math.log(rope_base) / HEAD_DIM)
    )
    angles = positions.astype(jnp.float32)[None, :] * frequency[:, None]
    return (jnp.cos(angles), jnp.sin(angles))


def per_device(
    dp_count,
    tensor_count,
    tokens,
    attention_gain,
    query_weight,
    key_weight,
    value_weight,
    output_weight,
    feedforward_gain,
    gate_weight,
    up_weight,
    down_weight,
    cotangent,
    lengths,
    storage_order,
    sequence_order,
    pad_mask,
):
    place = Placement(dp_count, tensor_count)
    count = storage_order.shape[0]
    rows = count // tensor_count
    kv_heads = key_weight.shape[1] // HEAD_DIM
    heads = query_weight.shape[1] // HEAD_DIM
    group = heads // kv_heads
    head_columns = (heads + 2 * kv_heads) * HEAD_DIM

    hidden_units = gate_weight.shape[1]
    hidden_padded = -(-hidden_units // 128) * 128
    output_padded = -(-heads * HEAD_DIM // 128) * 128
    first_padded = -(-(head_columns + 2) // 128) * 128

    def wide(array, columns):
        return jnp.pad(array, ((0, 0), (0, columns - array.shape[1])))

    gate_shard = wide(gate_weight, hidden_padded)
    up_shard = wide(up_weight, hidden_padded)
    down_shard = wide(down_weight.T, hidden_padded)
    tokens_all, first_weight, output_turned, gate_unit = gather_first(
        dp_count,
        tensor_count,
        tokens,
        wide(
            jnp.concatenate(
                [query_weight, key_weight, value_weight, attention_gain[:, None], feedforward_gain[:, None]],
                axis=1,
            ),
            first_padded,
        ),
        wide(output_weight.T, output_padded),
        gate_shard,
    )
    output_turned = output_turned[:, : heads * HEAD_DIM]
    late_up = after(up_shard, tokens_all)
    up_turned = place.home_turn(late_up)
    up_crossed = place.cross(late_up)
    steps = (1, 2) if place.chips == 4 else tuple(range(1, place.chips))
    gate_units = [place.to_chip(gate_unit, step) for step in steps]
    late_cot = after(cotangent, tokens_all)
    cot_low = jnp.stack([place.home_to_low(late_cot, step) for step in range(1, place.low)])

    numbers = jnp.concatenate([storage_order, pad_mask, lengths[0]])
    numbers = jnp.where(place.home, numbers, place.to_core(numbers))
    pad_column = numbers[count : 2 * count][:, None]
    length_row = numbers[2 * count :]
    order = numbers[:count]

    places = jnp.arange(count, dtype=jnp.int32)
    starts = starts_of(places, length_row)
    cosine, sine = rotary_tables(places - starts)
    cosine_stored, sine_stored = rotary_tables(order - starts_of(order, length_row))
    to_sequence = (places[:, None] == order[None, :]).astype(jnp.bfloat16)
    to_storage = (order[:, None] == places[None, :]).astype(jnp.bfloat16)
    first_blocks = starts[:: math.gcd(count, QUERY_BLOCK)] // KEY_BLOCK
    start_row = starts[None, :]

    attention_scale = first_weight[:, head_columns].astype(jnp.float32)[None, :]
    feedforward_scale = first_weight[:, head_columns + 1].astype(jnp.float32)[None, :]
    normed, heads_stored, token_roots = project(
        tokens_all,
        attention_scale,
        first_weight,
        cosine_stored,
        sine_stored,
        heads + kv_heads,
        head_columns,
    )
    heads_all = contract(to_sequence, heads_stored, 1, 0, jnp.bfloat16)
    attended, log_totals = attend(first_blocks, heads_all, start_row, pad_column, kv_heads, group)
    attended_stored = contract(to_storage, attended, 1, 0, jnp.bfloat16)

    residual, normed_ffn, cot_all, up_full, down_turned, gate_full, gate_values, up_values, hidden = middle(
        dp_count,
        tensor_count,
        contract(attended_stored, output_turned, 1, 1, jnp.bfloat16),
        tokens_all,
        cotangent,
        cot_low,
        up_shard,
        up_turned,
        up_crossed,
        down_shard,
        gate_unit,
        gate_units,
        feedforward_scale,
    )

    def leave(own):
        arrived = place.cross(own.astype(jnp.bfloat16)).astype(jnp.float32)
        return jnp.where(place.home, own, arrived)

    grad_gate, grad_up, grad_part = hidden_back(
        cot_all, down_turned, gate_values, up_values, gate_full, up_full
    )
    turned_back = turn_back(
        dp_count,
        tensor_count,
        grad_part,
        cot_all,
        normed_ffn,
        grad_gate,
        grad_up,
        hidden,
        down_turned,
        residual,
        feedforward_scale,
    )
    grad_residual, feedforward_part, down_grad, gate_grad, gate_turning, grad_rows = turned_back[:6]
    up_part, pair_own, pair_low = turned_back[10], turned_back[12], turned_back[13]
    up_half, up_moves = place.plane_moves(up_part)
    gate_arrived = place.away_to_home(gate_turning)

    layer_moves = [place.to_low(pair_low[step - 1], step) for step in range(1, place.low)]
    grad_attended = contract(grad_rows, output_turned, 1, 0, jnp.bfloat16)
    grad_attended = contract(to_sequence, grad_attended, 1, 0, jnp.bfloat16)
    grad_query, grad_rest = attend_back(
        first_blocks,
        heads_all,
        start_row,
        pad_column,
        log_totals,
        attended,
        grad_attended,
        cosine,
        sine,
        kv_heads,
        group,
    )
    layer_own = after(residual, grad_query) + pair_own.astype(jnp.float32)
    for arrived in layer_moves:
        layer_own = layer_own + arrived.astype(jnp.float32)
    spare = jnp.zeros((count, first_padded - head_columns), jnp.bfloat16)
    sequence_grads, _, *up_moves = lax.optimization_barrier(
        (jnp.concatenate([grad_query, grad_rest, spare], axis=1), layer_own, *up_moves)
    )
    up_mine, up_first, up_second = place.plane_sum(up_half, up_moves)
    grad_heads = contract(to_storage, sequence_grads, 1, 0, jnp.bfloat16)
    grad_normed_part = contract(grad_heads, first_weight, 1, 1)
    tokens_wide = tokens_all.astype(jnp.float32)
    attention_part = jnp.sum(grad_normed_part * (tokens_wide * token_roots), axis=0)
    layer_output = leave(layer_own)
    gate_arrived = after(gate_arrived, grad_query).astype(jnp.float32)
    gate_other = place.home_to_core((gate_turning[0].astype(jnp.float32) + gate_arrived[1]).astype(jnp.bfloat16))
    gate_grad = jnp.where(place.home, gate_grad + gate_arrived[0], gate_other.astype(jnp.float32))
    gain_parts = jnp.stack([attention_part, feedforward_part[0]], axis=1)
    before = head_columns - (first_padded - 128)
    gain_parts = jnp.pad(gain_parts, ((0, 0), (before, 126 - before)))
    input_grad, up_grad, output_grad, first_grad = tail(
        dp_count,
        tensor_count,
        head_columns,
        after(grad_normed_part.astype(jnp.bfloat16), layer_own),
        tokens_all,
        grad_rows,
        wide(attended_stored, output_padded),
        normed,
        grad_heads,
        gain_parts,
        up_mine,
        up_first,
        up_second,
        grad_residual,
        attention_scale,
    )
    query_columns = heads * HEAD_DIM
    key_columns = kv_heads * HEAD_DIM
    return (
        layer_output,
        input_grad,
        first_grad[:, head_columns],
        first_grad[:, :query_columns],
        first_grad[:, query_columns : query_columns + key_columns],
        first_grad[:, query_columns + key_columns : head_columns],
        output_grad[:, :query_columns].T,
        first_grad[:, head_columns + 1],
        gate_grad[:, :hidden_units],
        up_grad[:, :hidden_units],
        down_grad[:, :hidden_units].T,
    )


def solution(mesh):
    placed = (
        P(("dp", "tensor"), None),
        P("dp"),
        P("dp", "tensor"),
        P("dp", "tensor"),
        P("dp", "tensor"),
        P("tensor", "dp"),
        P("dp"),
        P("dp", "tensor"),
        P("dp", "tensor"),
        P("tensor", "dp"),
        P(("dp", "tensor"), None),
        P("dp", None),
        P("dp"),
        P("dp"),
        P("dp"),
    )
    return jax.shard_map(
        functools.partial(per_device, mesh.shape["dp"], mesh.shape["tensor"]),
        mesh=mesh,
        in_specs=placed,
        out_specs=(
            P(("dp", "tensor"), None),
            P(("dp", "tensor"), None),
            P("dp"),
            P("dp", "tensor"),
            P("dp", "tensor"),
            P("dp", "tensor"),
            P("tensor", "dp"),
            P("dp"),
            P("dp", "tensor"),
            P("dp", "tensor"),
            P("tensor", "dp"),
        ),
        check_vma=False,
    )
```

```python
import functools
import math

import jax
import jax.numpy as jnp
from jax import lax
from jax.experimental import pallas as pl
from jax.experimental.pallas import tpu as pltpu
from jax.sharding import PartitionSpec as P

HEAD_DIM = 80
HALF = HEAD_DIM // 2
QUERY_BLOCK = 256
KEY_BLOCK = 256
MASKED = -1e30
VMEM_LIMIT = 48 * 1024 * 1024
LINK_VMEM_LIMIT = 60 * 1024 * 1024

epsilon = 1e-05
rope_base = 10000.0
AXES = ("dp", "tensor")


def contract(left, right, left_dim, right_dim, out_type=jnp.float32):
    product = lax.dot_general(
        left,
        right,
        (((left_dim,), (right_dim,)), ((), ())),
        preferred_element_type=jnp.float32,
    )
    return product.astype(out_type)


def after(value, *earlier):
    return lax.optimization_barrier((value,) + earlier)[0]


def inverse_root(vectors):
    return lax.rsqrt(jnp.mean(vectors * vectors, axis=-1, keepdims=True) + epsilon)


class Placement:
    def __init__(self, dp_count, tensor_count):
        self.dp_count = dp_count
        self.tensor_count = tensor_count
        self.chips = dp_count // 2
        self.low = tensor_count // 2
        dp_index = lax.axis_index("dp")
        tensor_index = lax.axis_index("tensor")
        self.p = dp_index // 2
        self.c = dp_index % 2
        self.th = tensor_index // self.low
        self.tl = tensor_index % self.low
        self.home = self.c == self.th

    def move(self, array, target):
        pairs = []
        for p in range(self.chips):
            for c in range(2):
                for th in range(2):
                    for tl in range(self.low):
                        goal = target(p, c, th, tl)
                        if goal is not None:
                            pairs.append((self.flat(p, c, th, tl), self.flat(*goal)))
        return lax.ppermute(array, AXES, pairs)

    def flat(self, p, c, th, tl):
        return (2 * p + c) * self.tensor_count + th * self.low + tl

    def to_core(self, array):
        return self.move(array, lambda p, c, th, tl: (p, 1 - c, th, tl))

    def to_chip(self, array, step):
        return self.move(array, lambda p, c, th, tl: (p ^ step, c, th, tl))

    def to_low(self, array, step):
        return self.move(array, lambda p, c, th, tl: (p, c, th, (tl + step) % self.low))

    def home_to_low(self, array, step):
        return self.move(
            array, lambda p, c, th, tl: (p, c, th, (tl + step) % self.low) if c == th else None
        )

    def cross(self, array):
        return self.move(
            array, lambda p, c, th, tl: (p, 1 - c, 1 - th, tl) if c != th else None
        )

    def home_turn(self, array):
        return self.move(
            array, lambda p, c, th, tl: (p, c, 1 - th, tl) if c == th else (p, 1 - c, th, tl)
        )

    def away_to_home(self, array):
        return self.move(array, lambda p, c, th, tl: (p, c, 1 - th, tl) if c != th else None)

    def home_to_core(self, array):
        return self.move(array, lambda p, c, th, tl: (p, 1 - c, th, tl) if c == th else None)

    def swap(self, array):
        return jnp.where(self.home, array, self.cross(array))

    def quarter_rows(self, array, step, other):
        rows = array.shape[0] // self.tensor_count
        index = (self.c ^ other) * self.low + (self.tl + step) % self.low
        return lax.dynamic_slice_in_dim(array, index * rows, rows, 0)

    def plane_moves(self, partial):
        rows, columns = partial.shape[0] // self.dp_count, partial.shape[1]

        def half(step, which):
            start = ((self.p ^ step) * 2 + which) * rows
            return lax.dynamic_slice(partial, (start, 0), (rows, columns))

        if self.chips == 4:
            return half, [
                self.to_chip(jnp.stack([half(3, 0), half(1, 0)]), 1),
                self.to_chip(jnp.stack([half(3, 1), half(2, 1)]), 2),
            ]
        return half, [
            self.to_chip(jnp.stack([half(step, 0), half(step, 1)]), step) for step in range(1, self.chips)
        ]

    def plane_sum(self, half, moves):
        def wide(value):
            return value.astype(jnp.float32)

        if self.chips == 4:
            by_x, by_y = moves
            first = self.to_chip((wide(half(2, 0)) + wide(by_x[0])).astype(jnp.bfloat16), 2)
            second = self.to_chip((wide(half(1, 1)) + wide(by_y[0])).astype(jnp.bfloat16), 1)
            parts = [[half(0, 0), by_x[1], first], [half(0, 1), by_y[1], second]]
        else:
            parts = [[half(0, which)] + [arrived[which] for arrived in moves] for which in range(2)]

        def total(which):
            return sum(wide(jnp.where(which == 0, one, two)) for one, two in zip(*parts))

        mine, other = total(self.c), total(1 - self.c)
        low = other.astype(jnp.bfloat16)
        return mine, jnp.where(self.home, low, mine.astype(jnp.bfloat16)), low


def project_kernel(heads, tokens_ref, gain_ref, weight_ref, cosine_ref, sine_ref, normed_ref, out_ref, root_ref):
    tokens = tokens_ref[...].astype(jnp.float32)
    root = lax.rsqrt(jnp.mean(tokens * tokens, axis=-1, keepdims=True) + epsilon)
    root_ref[...] = root
    normed = (tokens * root * gain_ref[...]).astype(jnp.bfloat16)
    normed_ref[...] = normed
    rows = jnp.dot(normed, weight_ref[...], preferred_element_type=jnp.float32)
    cosine, sine = cosine_ref[...].T, sine_ref[...].T
    pieces = []
    for head in range(heads):
        leading = rows[:, head * HEAD_DIM : head * HEAD_DIM + HALF]
        trailing = rows[:, head * HEAD_DIM + HALF : (head + 1) * HEAD_DIM]
        pieces.append(leading * cosine - trailing * sine)
        pieces.append(trailing * cosine + leading * sine)
    pieces.append(rows[:, heads * HEAD_DIM : out_ref.shape[1]])
    out_ref[...] = jnp.concatenate(pieces, axis=1).astype(jnp.bfloat16)


def project(tokens, gain, weight, cosine, sine, rotated_heads, out_columns):
    count, width = tokens.shape
    block = math.gcd(count, 256)
    return pl.pallas_call(
        functools.partial(project_kernel, rotated_heads),
        grid=(count // block,),
        in_specs=[
            pl.BlockSpec((block, width), lambda i: (i, 0)),
            pl.BlockSpec((1, width), lambda i: (0, 0)),
            pl.BlockSpec(weight.shape, lambda i: (0, 0)),
            pl.BlockSpec((HALF, block), lambda i: (0, i)),
            pl.BlockSpec((HALF, block), lambda i: (0, i)),
        ],
        out_specs=[
            pl.BlockSpec((block, width), lambda i: (i, 0)),
            pl.BlockSpec((block, out_columns), lambda i: (i, 0)),
            pl.BlockSpec((block, 1), lambda i: (i, 0)),
        ],
        out_shape=[
            jax.ShapeDtypeStruct((count, width), jnp.bfloat16),
            jax.ShapeDtypeStruct((count, out_columns), jnp.bfloat16),
            jax.ShapeDtypeStruct((count, 1), jnp.float32),
        ],
        compiler_params=pltpu.CompilerParams(vmem_limit_bytes=VMEM_LIMIT),
        cost_estimate=pl.CostEstimate(
            flops=2 * count * width * weight.shape[1],
            bytes_accessed=4 * count * width + 2 * weight.size,
            transcendentals=0,
        ),
        name="project",
    )(tokens, gain, weight, cosine, sine)


def block_bias(key_start, query_start, start_row, pad_column):
    shape = (pad_column.shape[0], start_row.shape[1])
    keys = key_start + lax.broadcasted_iota(jnp.int32, shape, 0)
    queries = query_start + lax.broadcasted_iota(jnp.int32, shape, 1)
    allowed = ((keys >= start_row) & (keys <= queries) & (pad_column == 1)) | (keys == queries)
    return jnp.where(allowed, 0.0, MASKED)


def stack_heads(rows, first, group):
    return jnp.concatenate(
        [rows[:, (first + g) * HEAD_DIM : (first + g + 1) * HEAD_DIM] for g in range(group)], axis=0
    )


def times(left, right, left_dim, right_dim):
    return lax.dot_general(
        left, right, (((left_dim,), (right_dim,)), ((), ())), preferred_element_type=jnp.float32
    )


def attend_kernel(
    kv_heads, group, first_ref, query_ref, all_ref, start_ref, pad_ref, out_ref, total_ref, key_heads, value_turned
):
    step = pl.program_id(0)
    heads = kv_heads * group
    query_rows = query_ref.shape[0]
    scale = math.log2(math.e) / math.sqrt(HEAD_DIM)

    @pl.when(step == 0)
    def _():
        for k in range(kv_heads):
            at = (heads + k) * HEAD_DIM
            key_heads[k] = all_ref[:, at : at + HEAD_DIM]
            at = (heads + kv_heads + k) * HEAD_DIM
            value_turned[k] = all_ref[:, at : at + HEAD_DIM].astype(jnp.float32).T.astype(jnp.bfloat16)

    query_start = step * query_rows
    last = (query_start + query_rows - 1) // KEY_BLOCK + 1
    pieces = []
    for k in range(kv_heads):
        queries = stack_heads(query_ref[:, : heads * HEAD_DIM], k * group, group)

        def body(block, carry, k=k, queries=queries):
            top, total, mixed = carry
            at = pl.multiple_of(block * KEY_BLOCK, KEY_BLOCK)
            bias = block_bias(at, query_start, start_ref[...], pad_ref[pl.ds(at, KEY_BLOCK), :])
            bias = jnp.concatenate([bias] * group, axis=1)
            scores = times(key_heads[k, pl.ds(at, KEY_BLOCK), :], queries, 1, 1) * scale + bias
            new_top = jnp.maximum(top, jnp.max(scores, axis=0, keepdims=True))
            weight = jnp.exp2(scores - new_top)
            shrink = jnp.exp2(top - new_top)
            total = total * shrink + jnp.sum(weight, axis=0, keepdims=True)
            mixed = mixed * shrink + times(
                value_turned[k, :, pl.ds(at, KEY_BLOCK)], weight.astype(jnp.bfloat16), 1, 0
            )
            return new_top, total, mixed

        columns = group * query_rows
        top, total, mixed = lax.fori_loop(
            first_ref[step],
            last,
            body,
            (
                jnp.full((1, columns), MASKED, jnp.float32),
                jnp.zeros((1, columns), jnp.float32),
                jnp.zeros((HEAD_DIM, columns), jnp.float32),
            ),
        )
        mixed = mixed / total
        log_total = top + jnp.log2(total)
        for g in range(group):
            span = slice(g * query_rows, (g + 1) * query_rows)
            pieces.append(mixed[:, span].T)
            total_ref[k * group + g : k * group + g + 1, :] = log_total[:, span]
    out_ref[...] = jnp.concatenate(pieces, axis=1).astype(jnp.bfloat16)


def attend(first, heads_all, start_row, pad_column, kv_heads, group):
    count, columns = heads_all.shape
    heads = kv_heads * group
    block = math.gcd(count, QUERY_BLOCK)
    return pl.pallas_call(
        functools.partial(attend_kernel, kv_heads, group),
        grid_spec=pltpu.PrefetchScalarGridSpec(
            num_scalar_prefetch=1,
            grid=(count // block,),
            in_specs=[
                pl.BlockSpec((block, columns), lambda i, first: (i, 0)),
                pl.BlockSpec((count, columns), lambda i, first: (0, 0)),
                pl.BlockSpec((1, block), lambda i, first: (0, i)),
                pl.BlockSpec((count, 1), lambda i, first: (0, 0)),
            ],
            out_specs=[
                pl.BlockSpec((block, heads * HEAD_DIM), lambda i, first: (i, 0)),
                pl.BlockSpec((heads, block), lambda i, first: (0, i)),
            ],
            scratch_shapes=[
                pltpu.VMEM((kv_heads, count, HEAD_DIM), jnp.bfloat16),
                pltpu.VMEM((kv_heads, HEAD_DIM, count), jnp.bfloat16),
            ],
        ),
        out_shape=[
            jax.ShapeDtypeStruct((count, heads * HEAD_DIM), jnp.bfloat16),
            jax.ShapeDtypeStruct((heads, count), jnp.float32),
        ],
        compiler_params=pltpu.CompilerParams(vmem_limit_bytes=VMEM_LIMIT),
        cost_estimate=pl.CostEstimate(
            flops=50 * 10**9, bytes_accessed=count * columns, transcendentals=0
        ),
        name="attend",
    )(first, heads_all, heads_all, start_row, pad_column)


def attend_back_kernel(
    kv_heads,
    group,
    first_ref,
    query_ref,
    all_ref,
    start_ref,
    pad_ref,
    total_ref,
    attended_ref,
    grad_ref,
    cosine_turned_ref,
    sine_turned_ref,
    cosine_all_ref,
    sine_all_ref,
    grad_query_ref,
    grad_rest_ref,
    key_heads,
    value_heads,
    key_turned,
    grad_keys,
    grad_values,
):
    step = pl.program_id(0)
    heads = kv_heads * group
    query_rows = query_ref.shape[0]
    scale = 1.0 / math.sqrt(HEAD_DIM)

    @pl.when(step == 0)
    def _():
        for k in range(kv_heads):
            at = (heads + k) * HEAD_DIM
            keys = all_ref[:, at : at + HEAD_DIM]
            key_heads[k] = keys
            key_turned[k] = keys.astype(jnp.float32).T.astype(jnp.bfloat16)
            at = (heads + kv_heads + k) * HEAD_DIM
            value_heads[k] = all_ref[:, at : at + HEAD_DIM]
        grad_keys[...] = jnp.zeros_like(grad_keys)
        grad_values[...] = jnp.zeros_like(grad_values)

    query_start = step * query_rows
    last = (query_start + query_rows - 1) // KEY_BLOCK + 1
    cosine = cosine_turned_ref[...]
    sine = sine_turned_ref[...]
    pieces = []
    for k in range(kv_heads):
        queries = stack_heads(query_ref[:, : heads * HEAD_DIM], k * group, group)
        grads = stack_heads(grad_ref[...], k * group, group)
        attended = stack_heads(attended_ref[...], k * group, group)
        inner = jnp.sum(
            (grads.astype(jnp.float32) * attended.astype(jnp.float32)).T, axis=0, keepdims=True
        )
        log_total = jnp.concatenate(
            [total_ref[k * group + g : k * group + g + 1, :] for g in range(group)], axis=1
        )

        def body(block, turned, k=k, queries=queries, grads=grads, inner=inner, log_total=log_total):
            at = pl.multiple_of(block * KEY_BLOCK, KEY_BLOCK)
            span = pl.ds(at, KEY_BLOCK)
            bias = block_bias(at, query_start, start_ref[...], pad_ref[span, :])
            bias = jnp.concatenate([bias] * group, axis=1)
            scores = times(key_heads[k, span, :], queries, 1, 1) * (scale * math.log2(math.e)) + bias
            weight = jnp.exp2(scores - log_total)
            grad_weight = times(value_heads[k, span, :], grads, 1, 1)
            grad_scores = (weight * (grad_weight - inner)).astype(jnp.bfloat16)
            grad_values[k, span, :] += times(weight.astype(jnp.bfloat16), grads, 1, 0)
            grad_keys[k, span, :] += times(grad_scores, queries, 1, 0)
            return turned + times(key_turned[k, :, span], grad_scores, 1, 0)

        turned = lax.fori_loop(
            first_ref[step], last, body, jnp.zeros((HEAD_DIM, group * query_rows), jnp.float32)
        )
        turned = turned * scale
        for g in range(group):
            part = turned[:, g * query_rows : (g + 1) * query_rows]
            leading, trailing = part[:HALF], part[HALF:]
            back = jnp.concatenate(
                [leading * cosine + trailing * sine, trailing * cosine - leading * sine], axis=0
            )
            pieces.append(back.T)
    grad_query_ref[...] = jnp.concatenate(pieces, axis=1).astype(jnp.bfloat16)

    @pl.when(step == pl.num_programs(0) - 1)
    def _():
        rest = []
        cosine_all, sine_all = cosine_all_ref[...].T, sine_all_ref[...].T
        for k in range(kv_heads):
            leading = grad_keys[k][:, :HALF] * scale
            trailing = grad_keys[k][:, HALF:] * scale
            rest.append(leading * cosine_all + trailing * sine_all)
            rest.append(trailing * cosine_all - leading * sine_all)
        for k in range(kv_heads):
            rest.append(grad_values[k])
        grad_rest_ref[...] = jnp.concatenate(rest, axis=1).astype(jnp.bfloat16)


def attend_back(
    first, heads_all, start_row, pad_column, log_totals, attended, grad_attended, cosine, sine, kv_heads, group
):
    count, columns = heads_all.shape
    heads = kv_heads * group
    block = math.gcd(count, QUERY_BLOCK)
    width = heads * HEAD_DIM
    rest = 2 * kv_heads * HEAD_DIM
    return pl.pallas_call(
        functools.partial(attend_back_kernel, kv_heads, group),
        grid_spec=pltpu.PrefetchScalarGridSpec(
            num_scalar_prefetch=1,
            grid=(count // block,),
            in_specs=[
                pl.BlockSpec((block, columns), lambda i, first: (i, 0)),
                pl.BlockSpec((count, columns), lambda i, first: (0, 0)),
                pl.BlockSpec((1, block), lambda i, first: (0, i)),
                pl.BlockSpec((count, 1), lambda i, first: (0, 0)),
                pl.BlockSpec((heads, block), lambda i, first: (0, i)),
                pl.BlockSpec((block, width), lambda i, first: (i, 0)),
                pl.BlockSpec((block, width), lambda i, first: (i, 0)),
                pl.BlockSpec((HALF, block), lambda i, first: (0, i)),
                pl.BlockSpec((HALF, block), lambda i, first: (0, i)),
                pl.BlockSpec((HALF, count), lambda i, first: (0, 0)),
                pl.BlockSpec((HALF, count), lambda i, first: (0, 0)),
            ],
            out_specs=[
                pl.BlockSpec((block, width), lambda i, first: (i, 0)),
                pl.BlockSpec((count, rest), lambda i, first: (0, 0)),
            ],
            scratch_shapes=[
                pltpu.VMEM((kv_heads, count, HEAD_DIM), jnp.bfloat16),
                pltpu.VMEM((kv_heads, count, HEAD_DIM), jnp.bfloat16),
                pltpu.VMEM((kv_heads, HEAD_DIM, count), jnp.bfloat16),
                pltpu.VMEM((kv_heads, count, HEAD_DIM), jnp.float32),
                pltpu.VMEM((kv_heads, count, HEAD_DIM), jnp.float32),
            ],
        ),
        out_shape=[
            jax.ShapeDtypeStruct((count, width), jnp.bfloat16),
            jax.ShapeDtypeStruct((count, rest), jnp.bfloat16),
        ],
        compiler_params=pltpu.CompilerParams(vmem_limit_bytes=VMEM_LIMIT),
        cost_estimate=pl.CostEstimate(
            flops=50 * 10**9, bytes_accessed=count * columns, transcendentals=0
        ),
        name="attend_back",
    )(
        first,
        heads_all,
        heads_all,
        start_row,
        pad_column,
        log_totals,
        attended,
        grad_attended,
        cosine,
        sine,
        cosine,
        sine,
    )


MESH = pl.DeviceIdType.MESH
CHUNK = 64


class Links:
    def __init__(self, dp_count, tensor_count, send, recv, local):
        self.chips, self.low = dp_count // 2, tensor_count // 2
        self.send, self.recv, self.local = send, recv, local
        self.used = 0
        self.used_local = 0
        self.unsent = []
        self.all_low = False
        dp_index, tensor_index = lax.axis_index("dp"), lax.axis_index("tensor")
        self.dp_index, self.tensor_index = dp_index, tensor_index
        self.p, self.c = dp_index // 2, dp_index % 2
        self.th, self.tl = tensor_index // self.low, tensor_index % self.low
        self.home = self.c == self.th
        self.away = self.c != self.th
        self.quarter = self.c * self.low + self.tl

    def at(self, p, c, th, tl):
        return (2 * p + c, th * self.low + tl)

    def chip(self, step):
        p = self.p
        moved = p
        for bit in (1, 2, 4):
            if step & bit:
                moved = moved + bit * (1 - 2 * ((p // bit) % 2))
        return moved

    def chip_peer(self, step):
        return self.at(self.chip(step), self.c, self.th, self.tl)

    def core_peer(self):
        return self.at(self.p, 1 - self.c, self.th, self.tl)

    def low_peer(self, step):
        return self.at(self.p, self.c, self.th, (self.tl + step) % self.low)

    def cross_peer(self):
        return self.at(self.p, 1 - self.c, 1 - self.th, self.tl)

    def turn_peer(self):
        home = self.home.astype(jnp.int32)
        return self.at(
            self.p,
            home * self.c + (1 - home) * (1 - self.c),
            home * (1 - self.th) + (1 - home) * self.th,
            self.tl,
        )

    def back_peer(self):
        home = self.home.astype(jnp.int32)
        return self.at(
            self.p,
            home * (1 - self.c) + (1 - home) * self.c,
            home * self.th + (1 - home) * (1 - self.th),
            self.tl,
        )

    def partner(self):
        return self.at(self.p, self.c, 1 - self.th, self.tl)

    def chip_steps(self):
        return (1, 2) if self.chips == 4 else tuple(range(1, self.chips))

    def enter(self):
        peers = [self.core_peer(), self.cross_peer(), self.partner()]
        peers += [self.chip_peer(step) for step in self.chip_steps()]
        peers += [self.low_peer(step) for step in range(1, self.low)]
        if self.all_low:
            peers += [
                self.at(self.p, self.c, 1 - self.th, (self.tl + step) % self.low)
                for step in range(1, self.low)
            ]
        barrier = pltpu.get_barrier_semaphore()
        for peer in peers:
            pl.semaphore_signal(barrier, inc=1, device_id=peer, device_id_type=MESH)
        pl.semaphore_wait(barrier, len(peers))

    def copy(self, source, target, peer, when=None):
        slot = self.used
        self.used += 1

        def make():
            return pltpu.make_async_remote_copy(
                src_ref=source,
                dst_ref=target,
                send_sem=self.send.at[slot],
                recv_sem=self.recv.at[slot],
                device_id=peer,
                device_id_type=MESH,
            )

        item = Item(make, when)
        self.unsent.append(item)
        return item

    def local_slot(self):
        self.used_local += 1
        return self.used_local - 1

    def keep(self, source, target, when=None):
        slot = self.used_local
        self.used_local += 1
        return Item(lambda: pltpu.make_async_copy(source, target, self.local.at[slot]), when)

    def drop(self, items):
        self.unsent = [item for item in self.unsent if item not in items]

    def leave(self):
        for item in self.unsent:
            item.sent()


class Item:
    def __init__(self, make, when):
        self.make, self.when = make, when

    def run(self, action):
        if self.when is None:
            action(self.make())
        else:
            pl.when(self.when)(lambda: action(self.make()))

    def start(self):
        self.run(lambda copy: copy.start())

    def arrived(self):
        self.run(lambda copy: copy.wait_recv())

    def sent(self):
        self.run(lambda copy: copy.wait_send())

    def done(self):
        self.run(lambda copy: copy.wait())


class UnitGather:
    def __init__(self, links, shard, unit):
        rows = shard.shape[0]
        mine = unit.at[pl.ds(links.c * rows, rows)]
        self.first = links.copy(shard, mine, links.turn_peer())
        self.second = links.copy(shard, mine, links.cross_peer(), links.away)
        self.own = links.keep(shard, mine, links.home)

    def turn(self):
        self.first.start()
        self.second.start()
        self.own.start()

    def settle_unit(self):
        self.first.arrived()
        self.second.arrived()
        self.own.done()


class WeightGather:
    def __init__(self, links, shard, full):
        self.links, self.shard, self.full = links, shard, full
        rows = shard.shape[0]
        self.rows = rows
        mine = full.at[pl.ds(links.dp_index * rows, rows)]
        self.first = links.copy(shard, mine, links.turn_peer())
        self.second = links.copy(shard, mine, links.cross_peer(), links.away)
        self.own = links.keep(shard, mine, links.home)
        unit = 2 * rows
        self.direct = []
        self.forward = []
        here = full.at[pl.ds(links.p * unit, unit)]
        for step in links.chip_steps():
            self.direct.append(links.copy(here, here, links.chip_peer(step)))
        if links.chips == 4:
            top = full.at[pl.ds(links.chip(2) * unit, rows)]
            bottom = full.at[pl.ds(links.chip(1) * unit + rows, rows)]
            self.forward.append(links.copy(top, top, links.chip_peer(1)))
            self.forward.append(links.copy(bottom, bottom, links.chip_peer(2)))

    def turn(self):
        self.first.start()
        self.second.start()
        self.own.start()

    def settle_unit(self):
        self.first.arrived()
        self.second.arrived()
        self.own.done()

    def spread(self):
        self.settle_unit()
        self.spread_unit()

    def spread_unit(self):
        for item in self.direct:
            item.start()

    def pass_on(self):
        for item in self.direct:
            item.arrived()
        for item in self.forward:
            item.start()

    def finish(self):
        for item in self.forward:
            item.arrived()


class RowGather:
    def __init__(self, links, full, rows, low_when=None):
        self.links = links
        mine = full.at[pl.ds(links.quarter * rows, rows)]
        self.to_core = links.copy(mine, mine, links.core_peer())
        self.to_low = []
        self.onward = []
        for step in range(1, links.low):
            self.to_low.append(links.copy(mine, mine, links.low_peer(step), low_when))
            came = (links.tl + links.low - step) % links.low
            block = full.at[pl.ds((links.c * links.low + came) * rows, rows)]
            self.onward.append(links.copy(block, block, links.core_peer()))

    def start(self):
        for item in self.to_low:
            item.start()
        self.to_core.start()

    def pass_on(self):
        for arriving, item in zip(self.to_low, self.onward):
            arriving.arrived()
            item.start()

    def finish(self):
        self.to_core.arrived()
        self.finish_onward()

    def finish_onward(self):
        for item in self.onward:
            item.arrived()


class RowScatter:
    def __init__(self, links, partial, mine, others, sums, arrivals, rows):
        self.links, self.rows = links, rows
        self.mine, self.others, self.sums, self.arrivals = mine, others, sums, arrivals
        low = links.low
        self.load = links.keep(partial.at[pl.ds(links.c * low * rows, low * rows)], mine)
        self.swap = links.copy(
            partial.at[pl.ds((1 - links.c) * low * rows, low * rows)], others, links.core_peer()
        )
        self.sends = [
            links.copy(sums.at[step - 1], arrivals.at[step - 1], links.low_peer(step))
            for step in range(1, low)
        ]

    def start(self):
        self.swap.start()
        self.load.start()

    def send_sums(self):
        self.load.done()
        self.swap.arrived()
        for step in range(1, self.links.low):
            base = ((self.links.tl + step) % self.links.low) * self.rows

            @pl.loop(0, self.rows // CHUNK)
            def _(i, base=base, step=step):
                span = pl.ds(pl.multiple_of(base + i * CHUNK, CHUNK), CHUNK)
                total = self.mine[span].astype(jnp.float32) + self.others[span].astype(jnp.float32)
                self.sums[step - 1, pl.ds(pl.multiple_of(i * CHUNK, CHUNK), CHUNK)] = total.astype(jnp.bfloat16)

            self.sends[step - 1].start()

    def collect(self, use):
        for item in self.sends:
            item.arrived()
        base = self.links.tl * self.rows

        @pl.loop(0, self.rows // CHUNK)
        def _(i):
            at = pl.multiple_of(i * CHUNK, CHUNK)
            span = pl.ds(pl.multiple_of(base + at, CHUNK), CHUNK)
            total = self.mine[span].astype(jnp.float32) + self.others[span].astype(jnp.float32)
            for step in range(1, self.links.low):
                total = total + self.arrivals[step - 1, pl.ds(at, CHUNK)].astype(jnp.float32)
            use(pl.ds(at, CHUNK), total)


def scatter_scratch(low, rows, width):
    return [
        pltpu.VMEM((low * rows, width), jnp.bfloat16),
        pltpu.VMEM((low * rows, width), jnp.bfloat16),
        pltpu.VMEM((low - 1, rows, width), jnp.bfloat16),
        pltpu.VMEM((low - 1, rows, width), jnp.bfloat16),
    ]


def semaphores(count, local_count):
    return [
        pltpu.SemaphoreType.DMA((count,)),
        pltpu.SemaphoreType.DMA((count,)),
        pltpu.SemaphoreType.DMA((local_count,)),
    ]


def anywhere(count):
    return [pl.BlockSpec(memory_space=pl.ANY)] * count


def in_vmem(count):
    return [pl.BlockSpec(memory_space=pltpu.VMEM)] * count


def link_params(number):
    return pltpu.CompilerParams(
        collective_id=number, has_side_effects=True, vmem_limit_bytes=LINK_VMEM_LIMIT
    )


ADD_ROWS = 32


def cut(columns, most):
    half = columns // 2
    return half if columns > most and half % 128 == 0 else columns


def product(left, right, out, left_dim, right_dim, rows, columns, finish=None, extra=(), extra_out=()):
    depth = left.shape[left_dim]
    count, width = out.shape
    rows, columns = math.gcd(count, rows), cut(width, columns)

    def body(left_ref, right_ref, *refs):
        value = times(left_ref[...], right_ref[...], left_dim, right_dim)
        if finish is None:
            refs[0][...] = value.astype(refs[0].dtype)
        else:
            finish(value, *refs)

    def block(shape, index):
        return pl.BlockSpec(shape, index)

    left_spec = (
        block((rows, depth), lambda j, i: (i, 0)) if left_dim == 1 else block((depth, rows), lambda j, i: (0, i))
    )
    right_spec = (
        block((columns, depth), lambda j, i: (j, 0))
        if right_dim == 1
        else block((depth, columns), lambda j, i: (0, j))
    )
    whole = block((rows, columns), lambda j, i: (i, j))
    extra_specs = [
        whole if ref.shape[1] == width else block((rows, ref.shape[1]), lambda j, i: (i, 0)) for ref in extra
    ]
    pltpu.emit_pipeline(
        body,
        grid=(width // columns, count // rows),
        in_specs=[left_spec, right_spec] + extra_specs,
        out_specs=[whole] * (1 + len(extra_out)),
    )(left, right, *extra, out, *extra_out)


def row_loop(rows, body):
    @pl.loop(0, rows // ADD_ROWS)
    def _(i):
        body(pl.ds(pl.multiple_of(i * ADD_ROWS, ADD_ROWS), ADD_ROWS))


class WeightScatter:
    def __init__(self, links, partial, result, inbox, turned, sums, leaving, stage):
        self.links, self.partial, self.result = links, partial, result
        self.inbox, self.turned, self.sums, self.leaving = inbox, turned, sums, leaving
        rows = partial.shape[0] // (2 * links.chips)
        self.rows = rows
        width = partial.shape[1]
        self.stage = [stage.at[i, pl.ds(0, rows), pl.ds(0, width)] for i in range(3)]
        self.both = links.chips == 4
        self.direct_started = False
        self.loads = [
            links.local_slot() for _ in range(3)
        ]
        if self.both:
            x_peer, y_peer = links.chip_peer(1), links.chip_peer(2)
            self.before = [
                links.copy(self.part(3, 0), inbox.at[0], x_peer),
                links.copy(self.part(3, 1), inbox.at[1], y_peer),
            ]
            self.direct = [
                links.copy(self.part(1, 0), inbox.at[2], x_peer),
                links.copy(self.part(2, 1), inbox.at[3], y_peer),
            ]
            self.summed = [
                links.copy(sums.at[0], inbox.at[4], y_peer),
                links.copy(sums.at[1], inbox.at[5], x_peer),
            ]
            self.arrivals = ((2, 4), (5, 3))
        else:
            self.before, self.summed, self.direct = [], [], []
            for step in links.chip_steps():
                for half in range(2):
                    at = 2 * (step - 1) + half
                    self.direct.append(
                        links.copy(self.part(step, half), inbox.at[at], links.chip_peer(step))
                    )
            self.arrivals = tuple(
                tuple(2 * (step - 1) + half for step in links.chip_steps()) for half in range(2)
            )
        self.first = links.copy(leaving.at[0], turned.at[0], links.back_peer())
        self.second = links.copy(leaving.at[1], turned.at[1], links.cross_peer(), links.away)

    def part(self, step, half):
        start = (2 * self.links.chip(step) + half) * self.rows
        return self.partial.at[pl.ds(start, self.rows)]

    def load(self, sources):
        copies = [
            pltpu.make_async_copy(source, stage, self.links.local.at[slot])
            for source, stage, slot in zip(sources, self.stage, self.loads)
        ]
        for copy in copies:
            copy.start()
        for copy in copies:
            copy.wait()

    def start(self, which):
        for item in getattr(self, which):
            item.start()

    def start_direct(self):
        if not self.direct_started:
            self.start("direct")
        self.direct_started = True

    def arrived(self, which):
        for item in getattr(self, which):
            item.arrived()

    def add_before(self):
        if not self.both:
            self.start_direct()
            return
        self.arrived("before")
        self.start_direct()
        for index, part in ((0, self.part(2, 0)), (1, self.part(1, 1))):
            self.load([part, self.inbox.at[index]])

            def body(span, index=index):
                total = self.stage[0][span].astype(jnp.float32) + self.stage[1][span].astype(jnp.float32)
                self.sums[index, span] = total.astype(jnp.bfloat16)

            row_loop(self.rows, body)
            self.summed[index].start()

    def turn(self):
        self.reduce()
        self.send_turned()

    def send_turned(self):
        self.first.start()
        self.second.start()

    def reduce(self):
        links = self.links
        for half in range(2):
            sources = [self.part(0, half)] + [self.inbox.at[at] for at in self.arrivals[half]]
            kept = links.c == half
            if len(sources) == 3:
                self.load(sources)

                def body(span, half=half, kept=kept):
                    total = self.stage[0][span].astype(jnp.float32)
                    total = total + self.stage[1][span].astype(jnp.float32)
                    self.settle(span, total + self.stage[2][span].astype(jnp.float32), kept)

                row_loop(self.rows, body)
            else:
                self.fold(sources, kept)

    def fold(self, sources, kept):
        rows = self.rows
        total = self.total
        self.load(sources[:1])
        row_loop(rows, lambda span: total.__setitem__(span, self.stage[0][span].astype(jnp.float32)))
        for source in sources[1:]:
            self.load([source])

            def body(span):
                total[span] = total[span] + self.stage[0][span].astype(jnp.float32)

            row_loop(rows, body)
        row_loop(rows, lambda span: self.settle(span, total[span], kept))

    def settle(self, span, total, kept):
        low = total.astype(jnp.bfloat16)
        links = self.links

        @pl.when(kept & links.home)
        def _():
            self.result[span] = total

        @pl.when(kept & links.away)
        def _():
            self.leaving[0, span] = low

        @pl.when(jnp.logical_not(kept) & links.home)
        def _():
            self.leaving[0, span] = low

        @pl.when(jnp.logical_not(kept) & links.away)
        def _():
            self.leaving[1, span] = low

    def finish(self):
        links = self.links
        self.first.arrived()
        self.second.arrived()

        @pl.when(links.home)
        def _():
            def body(span):
                self.result[span] = self.result[span] + self.turned[0, span].astype(jnp.float32)

            row_loop(self.rows, body)

        @pl.when(links.away)
        def _():
            def body(span):
                self.result[span] = self.turned[1, span].astype(jnp.float32) + self.turned[0, span].astype(
                    jnp.float32
                )

            row_loop(self.rows, body)


class TurnScatter:
    def __init__(self, links, mine, first, second, result, turned):
        self.links, self.mine, self.result, self.turned = links, mine, result, turned
        self.rows = mine.shape[0]
        self.first = links.copy(first, turned.at[0], links.back_peer())
        self.second = links.copy(second, turned.at[1], links.cross_peer(), links.away)

    def send_turned(self):
        self.first.start()
        self.second.start()

    def finish(self):
        self.first.arrived()
        self.second.arrived()

        @pl.when(self.links.home)
        def _():
            def body(span):
                self.result[span] = self.mine[span] + self.turned[0, span].astype(jnp.float32)

            row_loop(self.rows, body)

        @pl.when(self.links.away)
        def _():
            def body(span):
                self.result[span] = self.turned[1, span].astype(jnp.float32) + self.turned[0, span].astype(
                    jnp.float32
                )

            row_loop(self.rows, body)


def weight_scatter_scratch(chips, rows, width):
    return [pltpu.VMEM((2, rows, width), jnp.bfloat16)] * 3


def inbox_shape(chips, rows, width):
    count = 6 if chips == 4 else 2 * (chips - 1)
    return jax.ShapeDtypeStruct((count, rows, width), jnp.bfloat16)


def scatter_shapes(chips, partial):
    rows = partial.shape[0] // (2 * chips)
    width = partial.shape[1]
    return rows, width


def tail_kernel(
    dp_count,
    tensor_count,
    gain_column,
    partial,
    tokens_all,
    grad_rows,
    attended,
    normed,
    grad_heads,
    gain_parts,
    up_mine,
    up_first,
    up_second,
    grad_residual_ref,
    gain_ref,
    input_ref,
    up_ref,
    output_ref,
    first_ref,
    output_in,
    first_in,
    grad_output,
    grad_first,
    *scratch,
):
    output_work, first_work = scratch[:3], scratch[3:6]
    up_turned, stage, own_ref, leaving, crossed, mine, others, sums, arrivals = scratch[6:15]
    gains_out, gains_in, total = scratch[15:18]
    links = Links(dp_count, tensor_count, *scratch[18:])
    links.all_low = True
    rows = own_ref.shape[0]
    load_own = links.keep(tokens_all.at[pl.ds(links.quarter * rows, rows)], own_ref)
    scatter = RowScatter(links, partial, mine, others, sums, arrivals, rows)
    crossing = links.copy(leaving, crossed, links.cross_peer(), links.away)
    up = TurnScatter(links, up_mine, up_first, up_second, up_ref, up_turned)
    weights = []
    for grad, result, inbox, work in (
        (grad_output, output_ref, output_in, output_work),
        (grad_first, first_ref, first_in, first_work),
    ):
        turned, added, turning = work
        made = WeightScatter(links, grad, result, inbox, turned, added, turning, stage)
        made.total = None if made.both else total.at[pl.ds(0, made.rows), pl.ds(0, grad.shape[1])]
        weights.append(made)
    output, first = weights
    gain_sends = []
    for step in range(1, tensor_count):
        other = (links.tensor_index + step) % tensor_count
        gain_sends.append(
            links.copy(gains_out, gains_in.at[step - 1], links.at(links.p, links.c, other // links.low, other % links.low))
        )

    links.enter()
    scatter.start()
    load_own.start()
    up.send_turned()
    scatter.send_sums()
    load_own.done()

    def finish(value, parts_ref, out_ref):
        columns = value.shape[1]
        out_ref[:, : columns - 128] = value[:, : columns - 128].astype(jnp.bfloat16)
        out_ref[:, columns - 128 :] = (value[:, columns - 128 :] + parts_ref[...]).astype(jnp.bfloat16)

    product(grad_rows, attended, grad_output, 0, 0, 512, 1024)
    output.start("before")
    product(normed, grad_heads, grad_first, 0, 0, 512, 1024, finish, (gain_parts,))
    output.add_before()
    first.start("before")

    def use(span, grad_normed):
        own = own_ref[span].astype(jnp.float32)
        root = lax.rsqrt(jnp.mean(own * own, axis=-1, keepdims=True) + epsilon)
        unit = own * root
        scaled = grad_normed * gain_ref[...]
        grad = grad_residual_ref[span] + root * (
            scaled - unit * jnp.mean(scaled * unit, axis=-1, keepdims=True)
        )
        input_ref[span] = grad
        leaving[span] = grad.astype(jnp.bfloat16)

    output.arrived("direct")
    output.arrived("summed")
    output.turn()
    first.add_before()
    scatter.collect(use)
    crossing.start()
    first.arrived("direct")
    first.arrived("summed")
    first.turn()
    crossing.arrived()

    @pl.when(links.away)
    def _():
        def body(span):
            input_ref[span] = crossed[span].astype(jnp.float32)

        row_loop(rows, body)

    up.finish()
    output.finish()
    first.finish()
    width = first_ref.shape[1]
    gains_out[...] = first_ref[:, width - 128 :]
    for item in gain_sends:
        item.start()
    for item in gain_sends:
        item.arrived()
    summed = gains_out[...]
    for step in range(1, tensor_count):
        summed = summed + gains_in[step - 1]
    column = width - 128 + lax.broadcasted_iota(jnp.int32, summed.shape, 1)
    first_ref[:, width - 128 :] = jnp.where(column >= gain_column, summed, gains_out[...])
    links.leave()


def tail(
    dp_count,
    tensor_count,
    gain_column,
    partial,
    tokens_all,
    grad_rows,
    attended,
    normed,
    grad_heads,
    gain_parts,
    up_mine,
    up_first,
    up_second,
    grad_residual,
    gain,
):
    rows, width = grad_residual.shape
    low, chips = tensor_count // 2, dp_count // 2
    features = width
    partials = [
        jax.ShapeDtypeStruct((features, attended.shape[1]), jnp.bfloat16),
        jax.ShapeDtypeStruct((features, grad_heads.shape[1]), jnp.bfloat16),
    ]
    shapes = [scatter_shapes(chips, grad) for grad in partials]
    widest = max(columns for _, columns in shapes)
    most = shapes[0][0]
    scratch = []
    for block, columns in shapes:
        scratch += weight_scatter_scratch(chips, block, columns)
    scratch += [pltpu.VMEM((2,) + up_mine.shape, jnp.bfloat16)]
    scratch += [pltpu.VMEM((3, most, widest), jnp.bfloat16)]
    scratch += [pltpu.VMEM((rows, width), jnp.bfloat16)] * 3
    scratch += scatter_scratch(low, rows, width)
    scratch += [
        pltpu.VMEM((most, 128), jnp.float32),
        pltpu.VMEM((tensor_count - 1, most, 128), jnp.float32),
        pltpu.VMEM((most, widest) if chips != 4 else (8, 128), jnp.float32),
    ]
    return pl.pallas_call(
        functools.partial(tail_kernel, dp_count, tensor_count, gain_column),
        out_shape=[jax.ShapeDtypeStruct((rows, width), jnp.float32)]
        + [jax.ShapeDtypeStruct(shape, jnp.float32) for shape in [up_mine.shape] + shapes]
        + [inbox_shape(chips, *shape) for shape in shapes]
        + partials,
        in_specs=anywhere(7) + in_vmem(5),
        out_specs=in_vmem(4) + anywhere(4),
        scratch_shapes=scratch + semaphores(96, 24),
        compiler_params=link_params(3),
        name="tail",
    )(
        partial,
        tokens_all,
        grad_rows,
        attended,
        normed,
        grad_heads,
        gain_parts,
        up_mine,
        up_first,
        up_second,
        grad_residual,
        gain,
    )[:4]


def gather_first_kernel(
    dp_count, tensor_count, tokens, first, output, gate, tokens_all, first_full, output_full, gate_unit, *sems
):
    links = Links(dp_count, tensor_count, *sems)
    rows = tokens.shape[0]
    mine = tokens_all.at[pl.ds(links.tensor_index * rows, rows)]
    crossing = links.copy(tokens, mine, links.cross_peer(), links.away)
    staying = links.keep(tokens, mine, links.home)
    gather_tokens = RowGather(links, tokens_all, rows)
    weights = [
        WeightGather(links, shard, full)
        for shard, full in ((first, first_full), (output, output_full))
    ]
    weights.append(UnitGather(links, gate, gate_unit))
    links.enter()
    weights[0].turn()
    crossing.start()
    staying.start()

    @pl.when(links.home)
    def _():
        staying.make().wait()
        gather_tokens.start()

    weights[0].spread()
    weights[1].turn()

    @pl.when(links.away)
    def _():
        crossing.make().wait_recv()
        gather_tokens.start()

    weights[1].spread()
    weights[2].turn()
    weights[0].pass_on()
    gather_tokens.pass_on()
    weights[1].pass_on()
    weights[0].finish()
    gather_tokens.finish()
    weights[1].finish()
    weights[2].settle_unit()
    links.leave()


def gather_first(dp_count, tensor_count, tokens, first, output, gate):
    def full(shard, times):
        return jax.ShapeDtypeStruct((shard.shape[0] * times, shard.shape[1]), shard.dtype)

    return pl.pallas_call(
        functools.partial(gather_first_kernel, dp_count, tensor_count),
        out_shape=[
            full(tokens, tensor_count),
            full(first, dp_count),
            full(output, dp_count),
            full(gate, 2),
        ],
        in_specs=in_vmem(4),
        out_specs=anywhere(4),
        scratch_shapes=semaphores(64, 8),
        compiler_params=link_params(0),
        name="gather_first",
    )(tokens, first, output, gate)


def middle_kernel(
    dp_count,
    tensor_count,
    moved_units,
    partial,
    tokens_all,
    cot,
    cot_low,
    up,
    up_turned,
    up_crossed,
    down,
    gate_unit,
    *rest,
):
    gate_units, rest = rest[:moved_units], rest[moved_units:]
    gain_ref, residual_ref, normed_all, cot_all, up_full, down_full, gate_full = rest[:7]
    gate_values, up_values, hidden = rest[7:10]
    own, normed, mine, others, sums, arrivals = rest[10:16]
    links = Links(dp_count, tensor_count, *rest[16:])
    rows = cot.shape[0]
    scatter = RowScatter(links, partial, mine, others, sums, arrivals, rows)
    gather_normed = RowGather(links, normed_all, rows)
    gather_cot = RowGather(links, cot_all, rows, links.away)
    gate_gather = WeightGather(links, up, gate_full)
    up_gather = WeightGather(links, up, up_full)
    down_gather = WeightGather(links, down, down_full)
    shard = up.shape[0]
    here = up_full.at[pl.ds(links.dp_index * shard, shard)]
    beside = up_full.at[pl.ds((2 * links.p + 1 - links.c) * shard, shard)]
    quarter = pl.ds(links.quarter * rows, rows)
    placements = [
        links.keep(up, here, links.home),
        links.keep(up_turned, beside, links.home),
        links.keep(up_turned, here, links.away),
        links.keep(up_crossed, beside, links.away),
    ]
    gate_places = [links.chip(step) * 2 * shard for step in (0,) + links.chip_steps()]
    gate_placements = [
        links.keep(unit, gate_full.at[pl.ds(at, unit.shape[0])])
        for at, unit in zip(gate_places, (gate_unit,) + tuple(gate_units))
    ]
    cot_crossing = links.copy(cot, cot_all.at[pl.ds(links.tensor_index * rows, rows)], links.cross_peer(), links.away)
    cot_placements = [
        links.keep(
            cot_low.at[step - 1],
            cot_all.at[pl.ds((links.c * links.low + (links.tl + links.low - step) % links.low) * rows, rows)],
            links.home,
        )
        for step in range(1, links.low)
    ]
    cot_staying = links.keep(cot, cot_all.at[quarter], links.home)
    load = links.keep(tokens_all.at[quarter], own)
    store = links.keep(normed, normed_all.at[quarter])
    links.drop([up_gather.first, up_gather.second, gate_gather.first, gate_gather.second] + gate_gather.direct)
    links.enter()
    scatter.start()
    load.start()
    for item in gate_placements + placements:
        item.start()
    for item in gate_placements:
        item.done()
    for item in gate_gather.forward:
        item.start()
    for item in placements:
        item.done()
    scatter.send_sums()
    up_gather.spread_unit()
    down_gather.turn()
    cot_staying.start()
    for item in cot_placements:
        item.start()
    load.done()

    def use(span, total):
        residual = own[span].astype(jnp.float32) + total
        residual_ref[span] = residual
        root = lax.rsqrt(jnp.mean(residual * residual, axis=-1, keepdims=True) + epsilon)
        normed[span] = (residual * root * gain_ref[...]).astype(jnp.bfloat16)

    scatter.collect(use)
    store.start()
    store.done()
    gather_normed.start()
    down_gather.settle_unit()
    cot_crossing.start()
    up_gather.pass_on()
    down_gather.spread_unit()
    gate_gather.finish()
    gather_normed.pass_on()
    cot_staying.done()
    for item in cot_placements:
        item.done()
    cot_crossing.arrived()
    gather_cot.start()
    up_gather.finish()
    gather_normed.finish()
    product(normed_all, gate_full, gate_values, 1, 0, 512, 1024)
    down_gather.pass_on()
    gather_cot.pass_on()

    def finish(up, gate_ref, up_ref, hidden_ref):
        gate = gate_ref[...]
        up_ref[...] = up
        hidden_ref[...] = (gate * jax.nn.sigmoid(gate) * up).astype(jnp.bfloat16)

    product(normed_all, up_full, up_values, 1, 0, 256, 1024, finish, (gate_values,), (hidden,))
    down_gather.finish()
    gather_cot.finish()
    links.leave()


def middle(
    dp_count, tensor_count, partial, tokens_all, cot, cot_low, up, up_turned, up_crossed, down, gate_unit, gate_units, gain
):
    rows, width = cot.shape
    low = tensor_count // 2

    def full(shard, times):
        return jax.ShapeDtypeStruct((shard.shape[0] * times, shard.shape[1]), shard.dtype)

    return pl.pallas_call(
        functools.partial(middle_kernel, dp_count, tensor_count, len(gate_units)),
        out_shape=[
            jax.ShapeDtypeStruct((rows, width), jnp.float32),
            full(cot, tensor_count),
            full(cot, tensor_count),
            full(up, dp_count),
            full(down, dp_count),
            full(gate_unit, dp_count // 2),
            jax.ShapeDtypeStruct((rows * tensor_count, up.shape[1]), jnp.float32),
            jax.ShapeDtypeStruct((rows * tensor_count, up.shape[1]), jnp.float32),
            jax.ShapeDtypeStruct((rows * tensor_count, up.shape[1]), jnp.bfloat16),
        ],
        in_specs=anywhere(2) + in_vmem(len(gate_units) + 8),
        out_specs=in_vmem(1) + anywhere(8),
        scratch_shapes=[pltpu.VMEM((rows, width), jnp.bfloat16)] * 2
        + scatter_scratch(low, rows, width)
        + semaphores(64, 24),
        compiler_params=link_params(1),
        name="middle",
    )(partial, tokens_all, cot, cot_low, up, up_turned, up_crossed, down, gate_unit, *gate_units, gain)


def turn_back_kernel(
    dp_count,
    tensor_count,
    partial,
    cot_all,
    normed_ffn,
    gate_signal,
    up_signal,
    hidden,
    down_full,
    residual_ref,
    gain_ref,
    grad_residual_ref,
    gain_part_ref,
    down_ref,
    gate_ref,
    gate_turning,
    grad_rows,
    down_in,
    gate_in,
    grad_down,
    grad_gate,
    grad_up,
    down_part,
    pair_own,
    pair_low,
    own,
    low_grad,
    turned,
    added,
    turning,
    gate_added,
    stage,
    total_ref,
    mine,
    others,
    sums,
    arrivals,
    *sems,
):
    links = Links(dp_count, tensor_count, *sems)
    rows = residual_ref.shape[0]
    down = WeightScatter(links, grad_down, down_ref, down_in, turned, added, turning, stage)
    gate = WeightScatter(links, grad_gate, gate_ref, gate_in, turned, gate_added, gate_turning, stage)
    down.total = gate.total = total_ref
    links.drop([gate.first, gate.second])
    low = links.low
    half = low * residual_ref.shape[0]
    swap_layer = links.copy(down_part.at[pl.ds((1 - links.c) * half, half)], others, links.core_peer())
    load_layer = links.keep(down_part.at[pl.ds(links.c * half, half)], mine)
    keep_own = links.keep(low_grad, pair_own)
    keep_low = [links.keep(sums.at[step - 1], pair_low.at[step - 1]) for step in range(1, low)]
    scatter = RowScatter(links, partial, mine, others, sums, arrivals, rows)
    gather = RowGather(links, grad_rows, rows)
    quarter = pl.ds(links.quarter * rows, rows)
    load = links.keep(cot_all.at[quarter], own)
    store = links.keep(low_grad, grad_rows.at[quarter])
    links.enter()
    scatter.start()
    load.start()
    unit = 2 * down.rows

    def down_unit(step):
        at = pl.multiple_of(links.chip(step) * unit, 128)
        product(cot_all.at[:, pl.ds(at, unit)], hidden, grad_down.at[pl.ds(at, unit)], 0, 0, unit, 1024)

    if down.both and unit % 128 == 0:
        down_unit(3)
        down.start("before")
        scatter.send_sums()
        down_unit(1)
        down_unit(2)
        down.start_direct()
        down_unit(0)
    else:
        product(cot_all, hidden, grad_down, 0, 0, 512, 1024)
        down.start("before")
        scatter.send_sums()
    load.done()
    down.add_before()
    product(normed_ffn, gate_signal, grad_gate, 0, 0, 512, 1024)
    gate.start("before")
    gain_part_ref[...] = jnp.zeros_like(gain_part_ref)

    def use(span, grad_normed):
        residual = residual_ref[span]
        root = lax.rsqrt(jnp.mean(residual * residual, axis=-1, keepdims=True) + epsilon)
        unit = residual * root
        gain_part_ref[...] += jnp.sum(grad_normed * unit, axis=0, keepdims=True)
        scaled = grad_normed * gain_ref[...]
        grad = own[span].astype(jnp.float32) + root * (
            scaled - unit * jnp.mean(scaled * unit, axis=-1, keepdims=True)
        )
        grad_residual_ref[span] = grad
        low_grad[span] = grad.astype(jnp.bfloat16)

    scatter.collect(use)
    store.start()
    store.done()
    gather.start()
    down.arrived("direct")
    gate.start_direct()
    down.arrived("summed")
    down.turn()
    gate.add_before()
    product(normed_ffn, up_signal, grad_up, 0, 0, 512, 1024)
    gather.pass_on()
    product(hidden, down_full, down_part, 1, 1, 512, 1024)
    gather.to_core.arrived()
    swap_layer.start()
    load_layer.start()
    gate.arrived("direct")
    gate.arrived("summed")
    gate.reduce()
    for item in scatter.sends:
        item.sent()
    links.drop(scatter.sends)
    load_layer.done()
    swap_layer.arrived()
    for step in range(low):
        base = ((links.tl + step) % low) * rows

        @pl.loop(0, rows // CHUNK)
        def _(i, base=base, step=step):
            at = pl.multiple_of(i * CHUNK, CHUNK)
            span = pl.ds(pl.multiple_of(base + at, CHUNK), CHUNK)
            total = (mine[span].astype(jnp.float32) + others[span].astype(jnp.float32)).astype(jnp.bfloat16)
            if step:
                sums[step - 1, pl.ds(at, CHUNK)] = total
            else:
                low_grad[pl.ds(at, CHUNK)] = total

    keep_own.start()
    for item in keep_low:
        item.start()
    down.finish()
    gather.finish_onward()
    keep_own.done()
    for item in keep_low:
        item.done()
    links.leave()


def turn_back(
    dp_count,
    tensor_count,
    partial,
    cot_all,
    normed_ffn,
    gate_signal,
    up_signal,
    hidden,
    down_full,
    residual,
    gain,
):
    rows, width = residual.shape
    low, chips = tensor_count // 2, dp_count // 2
    grad = jax.ShapeDtypeStruct((width, hidden.shape[1]), jnp.bfloat16)
    block, columns = scatter_shapes(chips, grad)
    return pl.pallas_call(
        functools.partial(turn_back_kernel, dp_count, tensor_count),
        out_shape=[
            jax.ShapeDtypeStruct((rows, width), jnp.float32),
            jax.ShapeDtypeStruct((1, width), jnp.float32),
            jax.ShapeDtypeStruct((block, columns), jnp.float32),
            jax.ShapeDtypeStruct((block, columns), jnp.float32),
            jax.ShapeDtypeStruct((2, block, columns), jnp.bfloat16),
            jax.ShapeDtypeStruct((rows * tensor_count, width), jnp.bfloat16),
            inbox_shape(chips, block, columns),
            inbox_shape(chips, block, columns),
            grad,
            grad,
            grad,
            jax.ShapeDtypeStruct((rows * tensor_count, width), jnp.bfloat16),
            jax.ShapeDtypeStruct((rows, width), jnp.bfloat16),
            jax.ShapeDtypeStruct((low - 1, rows, width), jnp.bfloat16),
        ],
        in_specs=anywhere(7) + in_vmem(2),
        out_specs=in_vmem(5) + anywhere(9),
        scratch_shapes=[pltpu.VMEM((rows, width), jnp.bfloat16)] * 2
        + weight_scatter_scratch(chips, block, columns)
        + [
            pltpu.VMEM((2, block, columns), jnp.bfloat16),
            pltpu.VMEM((3, block, columns), jnp.bfloat16),
            pltpu.VMEM((block, columns) if chips != 4 else (8, 128), jnp.float32),
        ]
        + scatter_scratch(low, rows, width)
        + semaphores(64, 24),
        compiler_params=link_params(2),
        name="turn_back",
    )(partial, cot_all, normed_ffn, gate_signal, up_signal, hidden, down_full, residual, gain)


def hidden_back_kernel(
    cot_all, down_full, gate_values, up_values, gate_full, up_full, gate_signal, up_signal, partial
):
    def signals(grad_hidden, gate_ref, up_ref, gate_out, up_out):
        gate = gate_ref[...]
        sigmoid = jax.nn.sigmoid(gate)
        grad_hidden = grad_hidden * sigmoid
        gate_out[...] = (grad_hidden * up_ref[...] * (1.0 + gate * (1.0 - sigmoid))).astype(jnp.bfloat16)
        up_out[...] = (grad_hidden * gate).astype(jnp.bfloat16)

    product(
        cot_all, down_full, gate_signal, 1, 0, 256, 1024, signals, (gate_values, up_values), (up_signal,)
    )
    count, width = partial.shape
    depth = gate_full.shape[1]
    rows, columns = math.gcd(count, 512), cut(width, 1536)

    def body(gate_ref, up_ref, gate_weight, up_weight, out_ref):
        total = times(gate_ref[...], gate_weight[...], 1, 1) + times(up_ref[...], up_weight[...], 1, 1)
        out_ref[...] = total.astype(jnp.bfloat16)

    pltpu.emit_pipeline(
        body,
        grid=(width // columns, count // rows),
        in_specs=[pl.BlockSpec((rows, depth), lambda j, i: (i, 0))] * 2
        + [pl.BlockSpec((columns, depth), lambda j, i: (j, 0))] * 2,
        out_specs=[pl.BlockSpec((rows, columns), lambda j, i: (i, j))],
    )(gate_signal, up_signal, gate_full, up_full, partial)


def hidden_back(cot_all, down_full, gate_values, up_values, gate_full, up_full):
    signal = jax.ShapeDtypeStruct(gate_values.shape, jnp.bfloat16)
    flops = 6 * cot_all.size * gate_values.shape[1]
    return pl.pallas_call(
        hidden_back_kernel,
        out_shape=[signal, signal, jax.ShapeDtypeStruct(cot_all.shape, jnp.bfloat16)],
        in_specs=anywhere(6),
        out_specs=anywhere(3),
        compiler_params=pltpu.CompilerParams(vmem_limit_bytes=LINK_VMEM_LIMIT),
        cost_estimate=pl.CostEstimate(flops=flops, bytes_accessed=flops // 1000, transcendentals=0),
        name="hidden_back",
    )(cot_all, down_full, gate_values, up_values, gate_full, up_full)


def starts_of(positions, length_row):
    ends = jnp.cumsum(length_row)
    inside = positions[:, None] >= ends[None, :]
    return jnp.sum(jnp.where(inside, length_row[None, :], 0), axis=1)


def rotary_tables(positions):
    frequency = jnp.exp(
        jnp.arange(HALF, dtype=jnp.float32) * (-2.0 * math.log(rope_base) / HEAD_DIM)
    )
    angles = positions.astype(jnp.float32)[None, :] * frequency[:, None]
    return (jnp.cos(angles), jnp.sin(angles))


def per_device(
    dp_count,
    tensor_count,
    tokens,
    attention_gain,
    query_weight,
    key_weight,
    value_weight,
    output_weight,
    feedforward_gain,
    gate_weight,
    up_weight,
    down_weight,
    cotangent,
    lengths,
    storage_order,
    sequence_order,
    pad_mask,
):
    place = Placement(dp_count, tensor_count)
    count = storage_order.shape[0]
    rows = count // tensor_count
    kv_heads = key_weight.shape[1] // HEAD_DIM
    heads = query_weight.shape[1] // HEAD_DIM
    group = heads // kv_heads
    head_columns = (heads + 2 * kv_heads) * HEAD_DIM

    hidden_units = gate_weight.shape[1]
    hidden_padded = -(-hidden_units // 128) * 128
    output_padded = -(-heads * HEAD_DIM // 128) * 128
    first_padded = -(-(head_columns + 2) // 128) * 128

    def wide(array, columns):
        return jnp.pad(array, ((0, 0), (0, columns - array.shape[1])))

    gate_shard = wide(gate_weight, hidden_padded)
    up_shard = wide(up_weight, hidden_padded)
    down_shard = wide(down_weight.T, hidden_padded)
    tokens_all, first_weight, output_turned, gate_unit = gather_first(
        dp_count,
        tensor_count,
        tokens,
        wide(
            jnp.concatenate(
                [query_weight, key_weight, value_weight, attention_gain[:, None], feedforward_gain[:, None]],
                axis=1,
            ),
            first_padded,
        ),
        wide(output_weight.T, output_padded),
        gate_shard,
    )
    output_turned = output_turned[:, : heads * HEAD_DIM]
    late_up = after(up_shard, tokens_all)
    up_turned = place.home_turn(late_up)
    up_crossed = place.cross(late_up)
    steps = (1, 2) if place.chips == 4 else tuple(range(1, place.chips))
    gate_units = [place.to_chip(gate_unit, step) for step in steps]
    late_cot = after(cotangent, tokens_all)
    cot_low = jnp.stack([place.home_to_low(late_cot, step) for step in range(1, place.low)])

    numbers = jnp.concatenate([storage_order, pad_mask, lengths[0]])
    numbers = jnp.where(place.home, numbers, place.to_core(numbers))
    pad_column = numbers[count : 2 * count][:, None]
    length_row = numbers[2 * count :]
    order = numbers[:count]

    places = jnp.arange(count, dtype=jnp.int32)
    starts = starts_of(places, length_row)
    cosine, sine = rotary_tables(places - starts)
    cosine_stored, sine_stored = rotary_tables(order - starts_of(order, length_row))
    to_sequence = (places[:, None] == order[None, :]).astype(jnp.bfloat16)
    to_storage = (order[:, None] == places[None, :]).astype(jnp.bfloat16)
    first_blocks = starts[:: math.gcd(count, QUERY_BLOCK)] // KEY_BLOCK
    start_row = starts[None, :]

    attention_scale = first_weight[:, head_columns].astype(jnp.float32)[None, :]
    feedforward_scale = first_weight[:, head_columns + 1].astype(jnp.float32)[None, :]
    normed, heads_stored, token_roots = project(
        tokens_all,
        attention_scale,
        first_weight,
        cosine_stored,
        sine_stored,
        heads + kv_heads,
        head_columns,
    )
    heads_all = contract(to_sequence, heads_stored, 1, 0, jnp.bfloat16)
    attended, log_totals = attend(first_blocks, heads_all, start_row, pad_column, kv_heads, group)
    attended_stored = contract(to_storage, attended, 1, 0, jnp.bfloat16)

    residual, normed_ffn, cot_all, up_full, down_turned, gate_full, gate_values, up_values, hidden = middle(
        dp_count,
        tensor_count,
        contract(attended_stored, output_turned, 1, 1, jnp.bfloat16),
        tokens_all,
        cotangent,
        cot_low,
        up_shard,
        up_turned,
        up_crossed,
        down_shard,
        gate_unit,
        gate_units,
        feedforward_scale,
    )

    def leave(own):
        arrived = place.cross(own.astype(jnp.bfloat16)).astype(jnp.float32)
        return jnp.where(place.home, own, arrived)

    grad_gate, grad_up, grad_part = hidden_back(
        cot_all, down_turned, gate_values, up_values, gate_full, up_full
    )
    turned_back = turn_back(
        dp_count,
        tensor_count,
        grad_part,
        cot_all,
        normed_ffn,
        grad_gate,
        grad_up,
        hidden,
        down_turned,
        residual,
        feedforward_scale,
    )
    grad_residual, feedforward_part, down_grad, gate_grad, gate_turning, grad_rows = turned_back[:6]
    up_part, pair_own, pair_low = turned_back[10], turned_back[12], turned_back[13]
    up_half, up_moves = place.plane_moves(up_part)
    gate_arrived = place.away_to_home(gate_turning)

    layer_moves = [place.to_low(pair_low[step - 1], step) for step in range(1, place.low)]
    grad_attended = contract(grad_rows, output_turned, 1, 0, jnp.bfloat16)
    grad_attended = contract(to_sequence, grad_attended, 1, 0, jnp.bfloat16)
    grad_query, grad_rest = attend_back(
        first_blocks,
        heads_all,
        start_row,
        pad_column,
        log_totals,
        attended,
        grad_attended,
        cosine,
        sine,
        kv_heads,
        group,
    )
    layer_own = after(residual, grad_query) + pair_own.astype(jnp.float32)
    for arrived in layer_moves:
        layer_own = layer_own + arrived.astype(jnp.float32)
    spare = jnp.zeros((count, first_padded - head_columns), jnp.bfloat16)
    sequence_grads, _, *up_moves = lax.optimization_barrier(
        (jnp.concatenate([grad_query, grad_rest, spare], axis=1), layer_own, *up_moves)
    )
    up_mine, up_first, up_second = place.plane_sum(up_half, up_moves)
    grad_heads = contract(to_storage, sequence_grads, 1, 0, jnp.bfloat16)
    grad_normed_part = contract(grad_heads, first_weight, 1, 1)
    tokens_wide = tokens_all.astype(jnp.float32)
    attention_part = jnp.sum(grad_normed_part * (tokens_wide * token_roots), axis=0)
    layer_output = leave(layer_own)
    gate_arrived = after(gate_arrived, grad_query).astype(jnp.float32)
    gate_other = place.home_to_core((gate_turning[0].astype(jnp.float32) + gate_arrived[1]).astype(jnp.bfloat16))
    gate_grad = jnp.where(place.home, gate_grad + gate_arrived[0], gate_other.astype(jnp.float32))
    gain_parts = jnp.stack([attention_part, feedforward_part[0]], axis=1)
    before = head_columns - (first_padded - 128)
    gain_parts = jnp.pad(gain_parts, ((0, 0), (before, 126 - before)))
    input_grad, up_grad, output_grad, first_grad = tail(
        dp_count,
        tensor_count,
        head_columns,
        after(grad_normed_part.astype(jnp.bfloat16), layer_own),
        tokens_all,
        grad_rows,
        wide(attended_stored, output_padded),
        normed,
        grad_heads,
        gain_parts,
        up_mine,
        up_first,
        up_second,
        grad_residual,
        attention_scale,
    )
    query_columns = heads * HEAD_DIM
    key_columns = kv_heads * HEAD_DIM
    return (
        layer_output,
        input_grad,
        first_grad[:, head_columns],
        first_grad[:, :query_columns],
        first_grad[:, query_columns : query_columns + key_columns],
        first_grad[:, query_columns + key_columns : head_columns],
        output_grad[:, :query_columns].T,
        first_grad[:, head_columns + 1],
        gate_grad[:, :hidden_units],
        up_grad[:, :hidden_units],
        down_grad[:, :hidden_units].T,
    )


def solution(mesh):
    placed = (
        P(("dp", "tensor"), None),
        P("dp"),
        P("dp", "tensor"),
        P("dp", "tensor"),
        P("dp", "tensor"),
        P("tensor", "dp"),
        P("dp"),
        P("dp", "tensor"),
        P("dp", "tensor"),
        P("tensor", "dp"),
        P(("dp", "tensor"), None),
        P("dp", None),
        P("dp"),
        P("dp"),
        P("dp"),
    )
    return jax.shard_map(
        functools.partial(per_device, mesh.shape["dp"], mesh.shape["tensor"]),
        mesh=mesh,
        in_specs=placed,
        out_specs=(
            P(("dp", "tensor"), None),
            P(("dp", "tensor"), None),
            P("dp"),
            P("dp", "tensor"),
            P("dp", "tensor"),
            P("dp", "tensor"),
            P("tensor", "dp"),
            P("dp"),
            P("dp", "tensor"),
            P("dp", "tensor"),
            P("tensor", "dp"),
        ),
        check_vma=False,
    )
```

```python
import functools
import math

import jax
import jax.numpy as jnp
from jax import lax
from jax.experimental import pallas as pl
from jax.experimental.pallas import tpu as pltpu
from jax.sharding import PartitionSpec as P

HEAD_DIM = 80
HALF = HEAD_DIM // 2
QUERY_BLOCK = 256
KEY_BLOCK = 256
MASKED = -1e30
VMEM_LIMIT = 48 * 1024 * 1024
LINK_VMEM_LIMIT = 60 * 1024 * 1024

epsilon = 1e-05
rope_base = 10000.0
AXES = ("dp", "tensor")


def contract(left, right, left_dim, right_dim, out_type=jnp.float32):
    product = lax.dot_general(
        left,
        right,
        (((left_dim,), (right_dim,)), ((), ())),
        preferred_element_type=jnp.float32,
    )
    return product.astype(out_type)


def after(value, *earlier):
    return lax.optimization_barrier((value,) + earlier)[0]


def inverse_root(vectors):
    return lax.rsqrt(jnp.mean(vectors * vectors, axis=-1, keepdims=True) + epsilon)


class Placement:
    def __init__(self, dp_count, tensor_count):
        self.dp_count = dp_count
        self.tensor_count = tensor_count
        self.chips = dp_count // 2
        self.low = tensor_count // 2
        dp_index = lax.axis_index("dp")
        tensor_index = lax.axis_index("tensor")
        self.p = dp_index // 2
        self.c = dp_index % 2
        self.th = tensor_index // self.low
        self.tl = tensor_index % self.low
        self.home = self.c == self.th

    def move(self, array, target):
        pairs = []
        for p in range(self.chips):
            for c in range(2):
                for th in range(2):
                    for tl in range(self.low):
                        goal = target(p, c, th, tl)
                        if goal is not None:
                            pairs.append((self.flat(p, c, th, tl), self.flat(*goal)))
        return lax.ppermute(array, AXES, pairs)

    def flat(self, p, c, th, tl):
        return (2 * p + c) * self.tensor_count + th * self.low + tl

    def to_core(self, array):
        return self.move(array, lambda p, c, th, tl: (p, 1 - c, th, tl))

    def to_chip(self, array, step):
        return self.move(array, lambda p, c, th, tl: (p ^ step, c, th, tl))

    def to_low(self, array, step):
        return self.move(array, lambda p, c, th, tl: (p, c, th, (tl + step) % self.low))

    def home_to_low(self, array, step):
        return self.move(
            array, lambda p, c, th, tl: (p, c, th, (tl + step) % self.low) if c == th else None
        )

    def cross(self, array):
        return self.move(
            array, lambda p, c, th, tl: (p, 1 - c, 1 - th, tl) if c != th else None
        )

    def home_turn(self, array):
        return self.move(
            array, lambda p, c, th, tl: (p, c, 1 - th, tl) if c == th else (p, 1 - c, th, tl)
        )

    def away_to_home(self, array):
        return self.move(array, lambda p, c, th, tl: (p, c, 1 - th, tl) if c != th else None)

    def home_to_core(self, array):
        return self.move(array, lambda p, c, th, tl: (p, 1 - c, th, tl) if c == th else None)

    def swap(self, array):
        return jnp.where(self.home, array, self.cross(array))

    def quarter_rows(self, array, step, other):
        rows = array.shape[0] // self.tensor_count
        index = (self.c ^ other) * self.low + (self.tl + step) % self.low
        return lax.dynamic_slice_in_dim(array, index * rows, rows, 0)

    def plane_moves(self, partial):
        rows, columns = partial.shape[0] // self.dp_count, partial.shape[1]

        def half(step, which):
            start = ((self.p ^ step) * 2 + which) * rows
            return lax.dynamic_slice(partial, (start, 0), (rows, columns))

        if self.chips == 4:
            return half, [
                self.to_chip(jnp.stack([half(3, 0), half(1, 0)]), 1),
                self.to_chip(jnp.stack([half(3, 1), half(2, 1)]), 2),
            ]
        return half, [
            self.to_chip(jnp.stack([half(step, 0), half(step, 1)]), step) for step in range(1, self.chips)
        ]

    def plane_sum(self, half, moves):
        def wide(value):
            return value.astype(jnp.float32)

        if self.chips == 4:
            by_x, by_y = moves
            first = self.to_chip((wide(half(2, 0)) + wide(by_x[0])).astype(jnp.bfloat16), 2)
            second = self.to_chip((wide(half(1, 1)) + wide(by_y[0])).astype(jnp.bfloat16), 1)
            parts = [[half(0, 0), by_x[1], first], [half(0, 1), by_y[1], second]]
        else:
            parts = [[half(0, which)] + [arrived[which] for arrived in moves] for which in range(2)]

        def total(which):
            return sum(wide(jnp.where(which == 0, one, two)) for one, two in zip(*parts))

        mine, other = total(self.c), total(1 - self.c)
        low = other.astype(jnp.bfloat16)
        return mine, jnp.where(self.home, low, mine.astype(jnp.bfloat16)), low


def project_kernel(heads, tokens_ref, gain_ref, weight_ref, cosine_ref, sine_ref, normed_ref, out_ref, root_ref):
    tokens = tokens_ref[...].astype(jnp.float32)
    root = lax.rsqrt(jnp.mean(tokens * tokens, axis=-1, keepdims=True) + epsilon)
    root_ref[...] = root
    normed = (tokens * root * gain_ref[...]).astype(jnp.bfloat16)
    normed_ref[...] = normed
    rows = jnp.dot(normed, weight_ref[...], preferred_element_type=jnp.float32)
    cosine, sine = cosine_ref[...].T, sine_ref[...].T
    pieces = []
    for head in range(heads):
        leading = rows[:, head * HEAD_DIM : head * HEAD_DIM + HALF]
        trailing = rows[:, head * HEAD_DIM + HALF : (head + 1) * HEAD_DIM]
        pieces.append(leading * cosine - trailing * sine)
        pieces.append(trailing * cosine + leading * sine)
    pieces.append(rows[:, heads * HEAD_DIM : out_ref.shape[1]])
    out_ref[...] = jnp.concatenate(pieces, axis=1).astype(jnp.bfloat16)


def project(tokens, gain, weight, cosine, sine, rotated_heads, out_columns):
    count, width = tokens.shape
    block = math.gcd(count, 256)
    return pl.pallas_call(
        functools.partial(project_kernel, rotated_heads),
        grid=(count // block,),
        in_specs=[
            pl.BlockSpec((block, width), lambda i: (i, 0)),
            pl.BlockSpec((1, width), lambda i: (0, 0)),
            pl.BlockSpec(weight.shape, lambda i: (0, 0)),
            pl.BlockSpec((HALF, block), lambda i: (0, i)),
            pl.BlockSpec((HALF, block), lambda i: (0, i)),
        ],
        out_specs=[
            pl.BlockSpec((block, width), lambda i: (i, 0)),
            pl.BlockSpec((block, out_columns), lambda i: (i, 0)),
            pl.BlockSpec((block, 1), lambda i: (i, 0)),
        ],
        out_shape=[
            jax.ShapeDtypeStruct((count, width), jnp.bfloat16),
            jax.ShapeDtypeStruct((count, out_columns), jnp.bfloat16),
            jax.ShapeDtypeStruct((count, 1), jnp.float32),
        ],
        compiler_params=pltpu.CompilerParams(vmem_limit_bytes=VMEM_LIMIT),
        cost_estimate=pl.CostEstimate(
            flops=2 * count * width * weight.shape[1],
            bytes_accessed=4 * count * width + 2 * weight.size,
            transcendentals=0,
        ),
        name="project",
    )(tokens, gain, weight, cosine, sine)


def block_bias(key_start, query_start, start_row, pad_column):
    shape = (pad_column.shape[0], start_row.shape[1])
    keys = key_start + lax.broadcasted_iota(jnp.int32, shape, 0)
    queries = query_start + lax.broadcasted_iota(jnp.int32, shape, 1)
    allowed = ((keys >= start_row) & (keys <= queries) & (pad_column == 1)) | (keys == queries)
    return jnp.where(allowed, 0.0, MASKED)


def stack_heads(rows, first, group):
    return jnp.concatenate(
        [rows[:, (first + g) * HEAD_DIM : (first + g + 1) * HEAD_DIM] for g in range(group)], axis=0
    )


def times(left, right, left_dim, right_dim):
    return lax.dot_general(
        left, right, (((left_dim,), (right_dim,)), ((), ())), preferred_element_type=jnp.float32
    )


def attend_kernel(
    kv_heads, group, first_ref, query_ref, all_ref, start_ref, pad_ref, out_ref, total_ref, key_heads, value_turned
):
    step = pl.program_id(0)
    heads = kv_heads * group
    query_rows = query_ref.shape[0]
    scale = math.log2(math.e) / math.sqrt(HEAD_DIM)

    @pl.when(step == 0)
    def _():
        for k in range(kv_heads):
            at = (heads + k) * HEAD_DIM
            key_heads[k] = all_ref[:, at : at + HEAD_DIM]
            at = (heads + kv_heads + k) * HEAD_DIM
            value_turned[k] = all_ref[:, at : at + HEAD_DIM].astype(jnp.float32).T.astype(jnp.bfloat16)

    query_start = step * query_rows
    last = (query_start + query_rows - 1) // KEY_BLOCK + 1
    pieces = []
    for k in range(kv_heads):
        queries = stack_heads(query_ref[:, : heads * HEAD_DIM], k * group, group)

        def body(block, carry, k=k, queries=queries):
            top, total, mixed = carry
            at = pl.multiple_of(block * KEY_BLOCK, KEY_BLOCK)
            bias = block_bias(at, query_start, start_ref[...], pad_ref[pl.ds(at, KEY_BLOCK), :])
            bias = jnp.concatenate([bias] * group, axis=1)
            scores = times(key_heads[k, pl.ds(at, KEY_BLOCK), :], queries, 1, 1) * scale + bias
            new_top = jnp.maximum(top, jnp.max(scores, axis=0, keepdims=True))
            weight = jnp.exp2(scores - new_top)
            shrink = jnp.exp2(top - new_top)
            total = total * shrink + jnp.sum(weight, axis=0, keepdims=True)
            mixed = mixed * shrink + times(
                value_turned[k, :, pl.ds(at, KEY_BLOCK)], weight.astype(jnp.bfloat16), 1, 0
            )
            return new_top, total, mixed

        columns = group * query_rows
        top, total, mixed = lax.fori_loop(
            first_ref[step],
            last,
            body,
            (
                jnp.full((1, columns), MASKED, jnp.float32),
                jnp.zeros((1, columns), jnp.float32),
                jnp.zeros((HEAD_DIM, columns), jnp.float32),
            ),
        )
        mixed = mixed / total
        log_total = top + jnp.log2(total)
        for g in range(group):
            span = slice(g * query_rows, (g + 1) * query_rows)
            pieces.append(mixed[:, span].T)
            total_ref[k * group + g : k * group + g + 1, :] = log_total[:, span]
    out_ref[...] = jnp.concatenate(pieces, axis=1).astype(jnp.bfloat16)


def attend(first, heads_all, start_row, pad_column, kv_heads, group):
    count, columns = heads_all.shape
    heads = kv_heads * group
    block = math.gcd(count, QUERY_BLOCK)
    return pl.pallas_call(
        functools.partial(attend_kernel, kv_heads, group),
        grid_spec=pltpu.PrefetchScalarGridSpec(
            num_scalar_prefetch=1,
            grid=(count // block,),
            in_specs=[
                pl.BlockSpec((block, columns), lambda i, first: (i, 0)),
                pl.BlockSpec((count, columns), lambda i, first: (0, 0)),
                pl.BlockSpec((1, block), lambda i, first: (0, i)),
                pl.BlockSpec((count, 1), lambda i, first: (0, 0)),
            ],
            out_specs=[
                pl.BlockSpec((block, heads * HEAD_DIM), lambda i, first: (i, 0)),
                pl.BlockSpec((heads, block), lambda i, first: (0, i)),
            ],
            scratch_shapes=[
                pltpu.VMEM((kv_heads, count, HEAD_DIM), jnp.bfloat16),
                pltpu.VMEM((kv_heads, HEAD_DIM, count), jnp.bfloat16),
            ],
        ),
        out_shape=[
            jax.ShapeDtypeStruct((count, heads * HEAD_DIM), jnp.bfloat16),
            jax.ShapeDtypeStruct((heads, count), jnp.float32),
        ],
        compiler_params=pltpu.CompilerParams(vmem_limit_bytes=VMEM_LIMIT),
        cost_estimate=pl.CostEstimate(
            flops=50 * 10**9, bytes_accessed=count * columns, transcendentals=0
        ),
        name="attend",
    )(first, heads_all, heads_all, start_row, pad_column)


def attend_back_kernel(
    kv_heads,
    group,
    first_ref,
    query_ref,
    all_ref,
    start_ref,
    pad_ref,
    total_ref,
    attended_ref,
    grad_ref,
    cosine_turned_ref,
    sine_turned_ref,
    cosine_all_ref,
    sine_all_ref,
    grad_query_ref,
    grad_rest_ref,
    key_heads,
    value_heads,
    key_turned,
    grad_keys,
    grad_values,
):
    step = pl.program_id(0)
    heads = kv_heads * group
    query_rows = query_ref.shape[0]
    scale = 1.0 / math.sqrt(HEAD_DIM)

    @pl.when(step == 0)
    def _():
        for k in range(kv_heads):
            at = (heads + k) * HEAD_DIM
            keys = all_ref[:, at : at + HEAD_DIM]
            key_heads[k] = keys
            key_turned[k] = keys.astype(jnp.float32).T.astype(jnp.bfloat16)
            at = (heads + kv_heads + k) * HEAD_DIM
            value_heads[k] = all_ref[:, at : at + HEAD_DIM]
        grad_keys[...] = jnp.zeros_like(grad_keys)
        grad_values[...] = jnp.zeros_like(grad_values)

    query_start = step * query_rows
    last = (query_start + query_rows - 1) // KEY_BLOCK + 1
    cosine = cosine_turned_ref[...]
    sine = sine_turned_ref[...]
    pieces = []
    for k in range(kv_heads):
        queries = stack_heads(query_ref[:, : heads * HEAD_DIM], k * group, group)
        grads = stack_heads(grad_ref[...], k * group, group)
        attended = stack_heads(attended_ref[...], k * group, group)
        inner = jnp.sum(
            (grads.astype(jnp.float32) * attended.astype(jnp.float32)).T, axis=0, keepdims=True
        )
        log_total = jnp.concatenate(
            [total_ref[k * group + g : k * group + g + 1, :] for g in range(group)], axis=1
        )

        def body(block, turned, k=k, queries=queries, grads=grads, inner=inner, log_total=log_total):
            at = pl.multiple_of(block * KEY_BLOCK, KEY_BLOCK)
            span = pl.ds(at, KEY_BLOCK)
            bias = block_bias(at, query_start, start_ref[...], pad_ref[span, :])
            bias = jnp.concatenate([bias] * group, axis=1)
            scores = times(key_heads[k, span, :], queries, 1, 1) * (scale * math.log2(math.e)) + bias
            weight = jnp.exp2(scores - log_total)
            grad_weight = times(value_heads[k, span, :], grads, 1, 1)
            grad_scores = (weight * (grad_weight - inner)).astype(jnp.bfloat16)
            grad_values[k, span, :] += times(weight.astype(jnp.bfloat16), grads, 1, 0)
            grad_keys[k, span, :] += times(grad_scores, queries, 1, 0)
            return turned + times(key_turned[k, :, span], grad_scores, 1, 0)

        turned = lax.fori_loop(
            first_ref[step], last, body, jnp.zeros((HEAD_DIM, group * query_rows), jnp.float32)
        )
        turned = turned * scale
        for g in range(group):
            part = turned[:, g * query_rows : (g + 1) * query_rows]
            leading, trailing = part[:HALF], part[HALF:]
            back = jnp.concatenate(
                [leading * cosine + trailing * sine, trailing * cosine - leading * sine], axis=0
            )
            pieces.append(back.T)
    grad_query_ref[...] = jnp.concatenate(pieces, axis=1).astype(jnp.bfloat16)

    @pl.when(step == pl.num_programs(0) - 1)
    def _():
        rest = []
        cosine_all, sine_all = cosine_all_ref[...].T, sine_all_ref[...].T
        for k in range(kv_heads):
            leading = grad_keys[k][:, :HALF] * scale
            trailing = grad_keys[k][:, HALF:] * scale
            rest.append(leading * cosine_all + trailing * sine_all)
            rest.append(trailing * cosine_all - leading * sine_all)
        for k in range(kv_heads):
            rest.append(grad_values[k])
        grad_rest_ref[...] = jnp.concatenate(rest, axis=1).astype(jnp.bfloat16)


def attend_back(
    first, heads_all, start_row, pad_column, log_totals, attended, grad_attended, cosine, sine, kv_heads, group
):
    count, columns = heads_all.shape
    heads = kv_heads * group
    block = math.gcd(count, QUERY_BLOCK)
    width = heads * HEAD_DIM
    rest = 2 * kv_heads * HEAD_DIM
    return pl.pallas_call(
        functools.partial(attend_back_kernel, kv_heads, group),
        grid_spec=pltpu.PrefetchScalarGridSpec(
            num_scalar_prefetch=1,
            grid=(count // block,),
            in_specs=[
                pl.BlockSpec((block, columns), lambda i, first: (i, 0)),
                pl.BlockSpec((count, columns), lambda i, first: (0, 0)),
                pl.BlockSpec((1, block), lambda i, first: (0, i)),
                pl.BlockSpec((count, 1), lambda i, first: (0, 0)),
                pl.BlockSpec((heads, block), lambda i, first: (0, i)),
                pl.BlockSpec((block, width), lambda i, first: (i, 0)),
                pl.BlockSpec((block, width), lambda i, first: (i, 0)),
                pl.BlockSpec((HALF, block), lambda i, first: (0, i)),
                pl.BlockSpec((HALF, block), lambda i, first: (0, i)),
                pl.BlockSpec((HALF, count), lambda i, first: (0, 0)),
                pl.BlockSpec((HALF, count), lambda i, first: (0, 0)),
            ],
            out_specs=[
                pl.BlockSpec((block, width), lambda i, first: (i, 0)),
                pl.BlockSpec((count, rest), lambda i, first: (0, 0)),
            ],
            scratch_shapes=[
                pltpu.VMEM((kv_heads, count, HEAD_DIM), jnp.bfloat16),
                pltpu.VMEM((kv_heads, count, HEAD_DIM), jnp.bfloat16),
                pltpu.VMEM((kv_heads, HEAD_DIM, count), jnp.bfloat16),
                pltpu.VMEM((kv_heads, count, HEAD_DIM), jnp.float32),
                pltpu.VMEM((kv_heads, count, HEAD_DIM), jnp.float32),
            ],
        ),
        out_shape=[
            jax.ShapeDtypeStruct((count, width), jnp.bfloat16),
            jax.ShapeDtypeStruct((count, rest), jnp.bfloat16),
        ],
        compiler_params=pltpu.CompilerParams(vmem_limit_bytes=VMEM_LIMIT),
        cost_estimate=pl.CostEstimate(
            flops=50 * 10**9, bytes_accessed=count * columns, transcendentals=0
        ),
        name="attend_back",
    )(
        first,
        heads_all,
        heads_all,
        start_row,
        pad_column,
        log_totals,
        attended,
        grad_attended,
        cosine,
        sine,
        cosine,
        sine,
    )


MESH = pl.DeviceIdType.MESH
CHUNK = 64


class Links:
    def __init__(self, dp_count, tensor_count, send, recv, local):
        self.chips, self.low = dp_count // 2, tensor_count // 2
        self.send, self.recv, self.local = send, recv, local
        self.used = 0
        self.used_local = 0
        self.unsent = []
        self.all_low = False
        dp_index, tensor_index = lax.axis_index("dp"), lax.axis_index("tensor")
        self.dp_index, self.tensor_index = dp_index, tensor_index
        self.p, self.c = dp_index // 2, dp_index % 2
        self.th, self.tl = tensor_index // self.low, tensor_index % self.low
        self.home = self.c == self.th
        self.away = self.c != self.th
        self.quarter = self.c * self.low + self.tl

    def at(self, p, c, th, tl):
        return (2 * p + c, th * self.low + tl)

    def chip(self, step):
        p = self.p
        moved = p
        for bit in (1, 2, 4):
            if step & bit:
                moved = moved + bit * (1 - 2 * ((p // bit) % 2))
        return moved

    def chip_peer(self, step):
        return self.at(self.chip(step), self.c, self.th, self.tl)

    def core_peer(self):
        return self.at(self.p, 1 - self.c, self.th, self.tl)

    def low_peer(self, step):
        return self.at(self.p, self.c, self.th, (self.tl + step) % self.low)

    def cross_peer(self):
        return self.at(self.p, 1 - self.c, 1 - self.th, self.tl)

    def turn_peer(self):
        home = self.home.astype(jnp.int32)
        return self.at(
            self.p,
            home * self.c + (1 - home) * (1 - self.c),
            home * (1 - self.th) + (1 - home) * self.th,
            self.tl,
        )

    def back_peer(self):
        home = self.home.astype(jnp.int32)
        return self.at(
            self.p,
            home * (1 - self.c) + (1 - home) * self.c,
            home * self.th + (1 - home) * (1 - self.th),
            self.tl,
        )

    def partner(self):
        return self.at(self.p, self.c, 1 - self.th, self.tl)

    def chip_steps(self):
        return (1, 2) if self.chips == 4 else tuple(range(1, self.chips))

    def enter(self):
        peers = [self.core_peer(), self.cross_peer(), self.partner()]
        peers += [self.chip_peer(step) for step in self.chip_steps()]
        peers += [self.low_peer(step) for step in range(1, self.low)]
        if self.all_low:
            peers += [
                self.at(self.p, self.c, 1 - self.th, (self.tl + step) % self.low)
                for step in range(1, self.low)
            ]
        barrier = pltpu.get_barrier_semaphore()
        for peer in peers:
            pl.semaphore_signal(barrier, inc=1, device_id=peer, device_id_type=MESH)
        pl.semaphore_wait(barrier, len(peers))

    def copy(self, source, target, peer, when=None):
        slot = self.used
        self.used += 1

        def make():
            return pltpu.make_async_remote_copy(
                src_ref=source,
                dst_ref=target,
                send_sem=self.send.at[slot],
                recv_sem=self.recv.at[slot],
                device_id=peer,
                device_id_type=MESH,
            )

        item = Item(make, when)
        self.unsent.append(item)
        return item

    def local_slot(self):
        self.used_local += 1
        return self.used_local - 1

    def keep(self, source, target, when=None):
        slot = self.used_local
        self.used_local += 1
        return Item(lambda: pltpu.make_async_copy(source, target, self.local.at[slot]), when)

    def drop(self, items):
        self.unsent = [item for item in self.unsent if item not in items]

    def leave(self):
        for item in self.unsent:
            item.sent()


class Item:
    def __init__(self, make, when):
        self.make, self.when = make, when

    def run(self, action):
        if self.when is None:
            action(self.make())
        else:
            pl.when(self.when)(lambda: action(self.make()))

    def start(self):
        self.run(lambda copy: copy.start())

    def arrived(self):
        self.run(lambda copy: copy.wait_recv())

    def sent(self):
        self.run(lambda copy: copy.wait_send())

    def done(self):
        self.run(lambda copy: copy.wait())


class UnitGather:
    def __init__(self, links, shard, unit):
        rows = shard.shape[0]
        mine = unit.at[pl.ds(links.c * rows, rows)]
        self.first = links.copy(shard, mine, links.turn_peer())
        self.second = links.copy(shard, mine, links.cross_peer(), links.away)
        self.own = links.keep(shard, mine, links.home)

    def turn(self):
        self.first.start()
        self.second.start()
        self.own.start()

    def settle_unit(self):
        self.first.arrived()
        self.second.arrived()
        self.own.done()


class WeightGather:
    def __init__(self, links, shard, full):
        self.links, self.shard, self.full = links, shard, full
        rows = shard.shape[0]
        self.rows = rows
        mine = full.at[pl.ds(links.dp_index * rows, rows)]
        self.first = links.copy(shard, mine, links.turn_peer())
        self.second = links.copy(shard, mine, links.cross_peer(), links.away)
        self.own = links.keep(shard, mine, links.home)
        unit = 2 * rows
        self.direct = []
        self.forward = []
        here = full.at[pl.ds(links.p * unit, unit)]
        for step in links.chip_steps():
            self.direct.append(links.copy(here, here, links.chip_peer(step)))
        if links.chips == 4:
            top = full.at[pl.ds(links.chip(2) * unit, rows)]
            bottom = full.at[pl.ds(links.chip(1) * unit + rows, rows)]
            self.forward.append(links.copy(top, top, links.chip_peer(1)))
            self.forward.append(links.copy(bottom, bottom, links.chip_peer(2)))

    def turn(self):
        self.first.start()
        self.second.start()
        self.own.start()

    def settle_unit(self):
        self.first.arrived()
        self.second.arrived()
        self.own.done()

    def spread(self):
        self.settle_unit()
        self.spread_unit()

    def spread_unit(self):
        for item in self.direct:
            item.start()

    def pass_on(self):
        for item in self.direct:
            item.arrived()
        for item in self.forward:
            item.start()

    def finish(self):
        for item in self.forward:
            item.arrived()


class RowGather:
    def __init__(self, links, full, rows, low_when=None):
        self.links = links
        mine = full.at[pl.ds(links.quarter * rows, rows)]
        self.to_core = links.copy(mine, mine, links.core_peer())
        self.to_low = []
        self.onward = []
        for step in range(1, links.low):
            self.to_low.append(links.copy(mine, mine, links.low_peer(step), low_when))
            came = (links.tl + links.low - step) % links.low
            block = full.at[pl.ds((links.c * links.low + came) * rows, rows)]
            self.onward.append(links.copy(block, block, links.core_peer()))

    def start(self):
        for item in self.to_low:
            item.start()
        self.to_core.start()

    def pass_on(self):
        for arriving, item in zip(self.to_low, self.onward):
            arriving.arrived()
            item.start()

    def finish(self):
        self.to_core.arrived()
        self.finish_onward()

    def finish_onward(self):
        for item in self.onward:
            item.arrived()


class RowScatter:
    def __init__(self, links, partial, mine, others, sums, arrivals, rows):
        self.links, self.rows = links, rows
        self.mine, self.others, self.sums, self.arrivals = mine, others, sums, arrivals
        low = links.low
        self.load = links.keep(partial.at[pl.ds(links.c * low * rows, low * rows)], mine)
        self.swap = links.copy(
            partial.at[pl.ds((1 - links.c) * low * rows, low * rows)], others, links.core_peer()
        )
        self.sends = [
            links.copy(sums.at[step - 1], arrivals.at[step - 1], links.low_peer(step))
            for step in range(1, low)
        ]

    def start(self):
        self.swap.start()
        self.load.start()

    def send_sums(self):
        self.load.done()
        self.swap.arrived()
        for step in range(1, self.links.low):
            base = ((self.links.tl + step) % self.links.low) * self.rows

            @pl.loop(0, self.rows // CHUNK)
            def _(i, base=base, step=step):
                span = pl.ds(pl.multiple_of(base + i * CHUNK, CHUNK), CHUNK)
                total = self.mine[span].astype(jnp.float32) + self.others[span].astype(jnp.float32)
                self.sums[step - 1, pl.ds(pl.multiple_of(i * CHUNK, CHUNK), CHUNK)] = total.astype(jnp.bfloat16)

            self.sends[step - 1].start()

    def collect(self, use):
        for item in self.sends:
            item.arrived()
        base = self.links.tl * self.rows

        @pl.loop(0, self.rows // CHUNK)
        def _(i):
            at = pl.multiple_of(i * CHUNK, CHUNK)
            span = pl.ds(pl.multiple_of(base + at, CHUNK), CHUNK)
            total = self.mine[span].astype(jnp.float32) + self.others[span].astype(jnp.float32)
            for step in range(1, self.links.low):
                total = total + self.arrivals[step - 1, pl.ds(at, CHUNK)].astype(jnp.float32)
            use(pl.ds(at, CHUNK), total)


def scatter_scratch(low, rows, width):
    return [
        pltpu.VMEM((low * rows, width), jnp.bfloat16),
        pltpu.VMEM((low * rows, width), jnp.bfloat16),
        pltpu.VMEM((low - 1, rows, width), jnp.bfloat16),
        pltpu.VMEM((low - 1, rows, width), jnp.bfloat16),
    ]


def semaphores(count, local_count):
    return [
        pltpu.SemaphoreType.DMA((count,)),
        pltpu.SemaphoreType.DMA((count,)),
        pltpu.SemaphoreType.DMA((local_count,)),
    ]


def anywhere(count):
    return [pl.BlockSpec(memory_space=pl.ANY)] * count


def in_vmem(count):
    return [pl.BlockSpec(memory_space=pltpu.VMEM)] * count


def link_params(number):
    return pltpu.CompilerParams(
        collective_id=number, has_side_effects=True, vmem_limit_bytes=LINK_VMEM_LIMIT
    )


ADD_ROWS = 32


def cut(columns, most):
    half = columns // 2
    return half if columns > most and half % 128 == 0 else columns


def product(left, right, out, left_dim, right_dim, rows, columns, finish=None, extra=(), extra_out=()):
    depth = left.shape[left_dim]
    count, width = out.shape
    rows, columns = math.gcd(count, rows), cut(width, columns)

    def body(left_ref, right_ref, *refs):
        value = times(left_ref[...], right_ref[...], left_dim, right_dim)
        if finish is None:
            refs[0][...] = value.astype(refs[0].dtype)
        else:
            finish(value, *refs)

    def block(shape, index):
        return pl.BlockSpec(shape, index)

    left_spec = (
        block((rows, depth), lambda j, i: (i, 0)) if left_dim == 1 else block((depth, rows), lambda j, i: (0, i))
    )
    right_spec = (
        block((columns, depth), lambda j, i: (j, 0))
        if right_dim == 1
        else block((depth, columns), lambda j, i: (0, j))
    )
    whole = block((rows, columns), lambda j, i: (i, j))
    extra_specs = [
        whole if ref.shape[1] == width else block((rows, ref.shape[1]), lambda j, i: (i, 0)) for ref in extra
    ]
    pltpu.emit_pipeline(
        body,
        grid=(width // columns, count // rows),
        in_specs=[left_spec, right_spec] + extra_specs,
        out_specs=[whole] * (1 + len(extra_out)),
    )(left, right, *extra, out, *extra_out)


def row_loop(rows, body):
    @pl.loop(0, rows // ADD_ROWS)
    def _(i):
        body(pl.ds(pl.multiple_of(i * ADD_ROWS, ADD_ROWS), ADD_ROWS))


class WeightScatter:
    def __init__(self, links, partial, result, inbox, turned, sums, leaving, stage):
        self.links, self.partial, self.result = links, partial, result
        self.inbox, self.turned, self.sums, self.leaving = inbox, turned, sums, leaving
        rows = partial.shape[0] // (2 * links.chips)
        self.rows = rows
        width = partial.shape[1]
        self.stage = [stage.at[i, pl.ds(0, rows), pl.ds(0, width)] for i in range(3)]
        self.both = links.chips == 4
        self.direct_started = False
        self.loads = [
            links.local_slot() for _ in range(3)
        ]
        if self.both:
            x_peer, y_peer = links.chip_peer(1), links.chip_peer(2)
            self.before = [
                links.copy(self.part(3, 0), inbox.at[0], x_peer),
                links.copy(self.part(3, 1), inbox.at[1], y_peer),
            ]
            self.direct = [
                links.copy(self.part(1, 0), inbox.at[2], x_peer),
                links.copy(self.part(2, 1), inbox.at[3], y_peer),
            ]
            self.summed = [
                links.copy(sums.at[0], inbox.at[4], y_peer),
                links.copy(sums.at[1], inbox.at[5], x_peer),
            ]
            self.arrivals = ((2, 4), (5, 3))
        else:
            self.before, self.summed, self.direct = [], [], []
            for step in links.chip_steps():
                for half in range(2):
                    at = 2 * (step - 1) + half
                    self.direct.append(
                        links.copy(self.part(step, half), inbox.at[at], links.chip_peer(step))
                    )
            self.arrivals = tuple(
                tuple(2 * (step - 1) + half for step in links.chip_steps()) for half in range(2)
            )
        self.first = links.copy(leaving.at[0], turned.at[0], links.back_peer())
        self.second = links.copy(leaving.at[1], turned.at[1], links.cross_peer(), links.away)

    def part(self, step, half):
        start = (2 * self.links.chip(step) + half) * self.rows
        return self.partial.at[pl.ds(start, self.rows)]

    def load(self, sources):
        copies = [
            pltpu.make_async_copy(source, stage, self.links.local.at[slot])
            for source, stage, slot in zip(sources, self.stage, self.loads)
        ]
        for copy in copies:
            copy.start()
        for copy in copies:
            copy.wait()

    def start(self, which):
        for item in getattr(self, which):
            item.start()

    def start_direct(self):
        if not self.direct_started:
            self.start("direct")
        self.direct_started = True

    def arrived(self, which):
        for item in getattr(self, which):
            item.arrived()

    def add_before(self):
        if not self.both:
            self.start_direct()
            return
        self.arrived("before")
        self.start_direct()
        for index, part in ((0, self.part(2, 0)), (1, self.part(1, 1))):
            self.load([part, self.inbox.at[index]])

            def body(span, index=index):
                total = self.stage[0][span].astype(jnp.float32) + self.stage[1][span].astype(jnp.float32)
                self.sums[index, span] = total.astype(jnp.bfloat16)

            row_loop(self.rows, body)
            self.summed[index].start()

    def turn(self):
        self.reduce()
        self.send_turned()

    def send_turned(self):
        self.first.start()
        self.second.start()

    def reduce(self):
        links = self.links
        for half in range(2):
            sources = [self.part(0, half)] + [self.inbox.at[at] for at in self.arrivals[half]]
            kept = links.c == half
            if len(sources) == 3:
                self.load(sources)

                def body(span, half=half, kept=kept):
                    total = self.stage[0][span].astype(jnp.float32)
                    total = total + self.stage[1][span].astype(jnp.float32)
                    self.settle(span, total + self.stage[2][span].astype(jnp.float32), kept)

                row_loop(self.rows, body)
            else:
                self.fold(sources, kept)

    def fold(self, sources, kept):
        rows = self.rows
        total = self.total
        self.load(sources[:1])
        row_loop(rows, lambda span: total.__setitem__(span, self.stage[0][span].astype(jnp.float32)))
        for source in sources[1:]:
            self.load([source])

            def body(span):
                total[span] = total[span] + self.stage[0][span].astype(jnp.float32)

            row_loop(rows, body)
        row_loop(rows, lambda span: self.settle(span, total[span], kept))

    def settle(self, span, total, kept):
        low = total.astype(jnp.bfloat16)
        links = self.links

        @pl.when(kept & links.home)
        def _():
            self.result[span] = total

        @pl.when(kept & links.away)
        def _():
            self.leaving[0, span] = low

        @pl.when(jnp.logical_not(kept) & links.home)
        def _():
            self.leaving[0, span] = low

        @pl.when(jnp.logical_not(kept) & links.away)
        def _():
            self.leaving[1, span] = low

    def finish(self):
        links = self.links
        self.first.arrived()
        self.second.arrived()

        @pl.when(links.home)
        def _():
            def body(span):
                self.result[span] = self.result[span] + self.turned[0, span].astype(jnp.float32)

            row_loop(self.rows, body)

        @pl.when(links.away)
        def _():
            def body(span):
                self.result[span] = self.turned[1, span].astype(jnp.float32) + self.turned[0, span].astype(
                    jnp.float32
                )

            row_loop(self.rows, body)


class TurnScatter:
    def __init__(self, links, mine, first, second, result, turned):
        self.links, self.mine, self.result, self.turned = links, mine, result, turned
        self.rows = mine.shape[0]
        self.first = links.copy(first, turned.at[0], links.back_peer())
        self.second = links.copy(second, turned.at[1], links.cross_peer(), links.away)

    def send_turned(self):
        self.first.start()
        self.second.start()

    def finish(self):
        self.first.arrived()
        self.second.arrived()

        @pl.when(self.links.home)
        def _():
            def body(span):
                self.result[span] = self.mine[span] + self.turned[0, span].astype(jnp.float32)

            row_loop(self.rows, body)

        @pl.when(self.links.away)
        def _():
            def body(span):
                self.result[span] = self.turned[1, span].astype(jnp.float32) + self.turned[0, span].astype(
                    jnp.float32
                )

            row_loop(self.rows, body)


def weight_scatter_scratch(chips, rows, width):
    return [pltpu.VMEM((2, rows, width), jnp.bfloat16)] * 3


def inbox_shape(chips, rows, width):
    count = 6 if chips == 4 else 2 * (chips - 1)
    return jax.ShapeDtypeStruct((count, rows, width), jnp.bfloat16)


def scatter_shapes(chips, partial):
    rows = partial.shape[0] // (2 * chips)
    width = partial.shape[1]
    return rows, width


def tail_kernel(
    dp_count,
    tensor_count,
    gain_column,
    partial,
    tokens_all,
    grad_rows,
    attended,
    normed,
    grad_heads,
    gain_parts,
    up_mine,
    up_first,
    up_second,
    grad_residual_ref,
    gain_ref,
    input_ref,
    up_ref,
    output_ref,
    first_ref,
    output_in,
    first_in,
    grad_output,
    grad_first,
    *scratch,
):
    output_work, first_work = scratch[:3], scratch[3:6]
    up_turned, stage, own_ref, leaving, crossed, mine, others, sums, arrivals = scratch[6:15]
    gains_out, gains_in, total = scratch[15:18]
    links = Links(dp_count, tensor_count, *scratch[18:])
    links.all_low = True
    rows = own_ref.shape[0]
    load_own = links.keep(tokens_all.at[pl.ds(links.quarter * rows, rows)], own_ref)
    scatter = RowScatter(links, partial, mine, others, sums, arrivals, rows)
    crossing = links.copy(leaving, crossed, links.cross_peer(), links.away)
    up = TurnScatter(links, up_mine, up_first, up_second, up_ref, up_turned)
    weights = []
    for grad, result, inbox, work in (
        (grad_output, output_ref, output_in, output_work),
        (grad_first, first_ref, first_in, first_work),
    ):
        turned, added, turning = work
        made = WeightScatter(links, grad, result, inbox, turned, added, turning, stage)
        made.total = None if made.both else total.at[pl.ds(0, made.rows), pl.ds(0, grad.shape[1])]
        weights.append(made)
    output, first = weights
    gain_sends = []
    for step in range(1, tensor_count):
        other = (links.tensor_index + step) % tensor_count
        gain_sends.append(
            links.copy(gains_out, gains_in.at[step - 1], links.at(links.p, links.c, other // links.low, other % links.low))
        )

    links.enter()
    scatter.start()
    load_own.start()
    up.send_turned()
    scatter.send_sums()
    load_own.done()

    def finish(value, parts_ref, out_ref):
        columns = value.shape[1]
        out_ref[:, : columns - 128] = value[:, : columns - 128].astype(jnp.bfloat16)
        out_ref[:, columns - 128 :] = (value[:, columns - 128 :] + parts_ref[...]).astype(jnp.bfloat16)

    product(grad_rows, attended, grad_output, 0, 0, 512, 1024)
    output.start("before")
    product(normed, grad_heads, grad_first, 0, 0, 512, 1024, finish, (gain_parts,))
    output.add_before()
    first.start("before")

    def use(span, grad_normed):
        own = own_ref[span].astype(jnp.float32)
        root = lax.rsqrt(jnp.mean(own * own, axis=-1, keepdims=True) + epsilon)
        unit = own * root
        scaled = grad_normed * gain_ref[...]
        grad = grad_residual_ref[span] + root * (
            scaled - unit * jnp.mean(scaled * unit, axis=-1, keepdims=True)
        )
        input_ref[span] = grad
        leaving[span] = grad.astype(jnp.bfloat16)

    output.arrived("direct")
    output.arrived("summed")
    output.turn()
    first.add_before()
    scatter.collect(use)
    crossing.start()
    first.arrived("direct")
    first.arrived("summed")
    first.turn()
    crossing.arrived()

    @pl.when(links.away)
    def _():
        def body(span):
            input_ref[span] = crossed[span].astype(jnp.float32)

        row_loop(rows, body)

    up.finish()
    output.finish()
    first.finish()
    width = first_ref.shape[1]
    gains_out[...] = first_ref[:, width - 128 :]
    for item in gain_sends:
        item.start()
    for item in gain_sends:
        item.arrived()
    summed = gains_out[...]
    for step in range(1, tensor_count):
        summed = summed + gains_in[step - 1]
    column = width - 128 + lax.broadcasted_iota(jnp.int32, summed.shape, 1)
    first_ref[:, width - 128 :] = jnp.where(column >= gain_column, summed, gains_out[...])
    links.leave()


def tail(
    dp_count,
    tensor_count,
    gain_column,
    partial,
    tokens_all,
    grad_rows,
    attended,
    normed,
    grad_heads,
    gain_parts,
    up_mine,
    up_first,
    up_second,
    grad_residual,
    gain,
):
    rows, width = grad_residual.shape
    low, chips = tensor_count // 2, dp_count // 2
    features = width
    partials = [
        jax.ShapeDtypeStruct((features, attended.shape[1]), jnp.bfloat16),
        jax.ShapeDtypeStruct((features, grad_heads.shape[1]), jnp.bfloat16),
    ]
    shapes = [scatter_shapes(chips, grad) for grad in partials]
    widest = max(columns for _, columns in shapes)
    most = shapes[0][0]
    scratch = []
    for block, columns in shapes:
        scratch += weight_scatter_scratch(chips, block, columns)
    scratch += [pltpu.VMEM((2,) + up_mine.shape, jnp.bfloat16)]
    scratch += [pltpu.VMEM((3, most, widest), jnp.bfloat16)]
    scratch += [pltpu.VMEM((rows, width), jnp.bfloat16)] * 3
    scratch += scatter_scratch(low, rows, width)
    scratch += [
        pltpu.VMEM((most, 128), jnp.float32),
        pltpu.VMEM((tensor_count - 1, most, 128), jnp.float32),
        pltpu.VMEM((most, widest) if chips != 4 else (8, 128), jnp.float32),
    ]
    return pl.pallas_call(
        functools.partial(tail_kernel, dp_count, tensor_count, gain_column),
        out_shape=[jax.ShapeDtypeStruct((rows, width), jnp.float32)]
        + [jax.ShapeDtypeStruct(shape, jnp.float32) for shape in [up_mine.shape] + shapes]
        + [inbox_shape(chips, *shape) for shape in shapes]
        + partials,
        in_specs=anywhere(7) + in_vmem(5),
        out_specs=in_vmem(4) + anywhere(4),
        scratch_shapes=scratch + semaphores(96, 24),
        compiler_params=link_params(3),
        name="tail",
    )(
        partial,
        tokens_all,
        grad_rows,
        attended,
        normed,
        grad_heads,
        gain_parts,
        up_mine,
        up_first,
        up_second,
        grad_residual,
        gain,
    )[:4]


def gather_first_kernel(
    dp_count, tensor_count, tokens, first, output, gate, tokens_all, first_full, output_full, gate_unit, *sems
):
    links = Links(dp_count, tensor_count, *sems)
    rows = tokens.shape[0]
    mine = tokens_all.at[pl.ds(links.tensor_index * rows, rows)]
    crossing = links.copy(tokens, mine, links.cross_peer(), links.away)
    staying = links.keep(tokens, mine, links.home)
    gather_tokens = RowGather(links, tokens_all, rows)
    weights = [
        WeightGather(links, shard, full)
        for shard, full in ((first, first_full), (output, output_full))
    ]
    weights.append(UnitGather(links, gate, gate_unit))
    links.enter()
    weights[0].turn()
    crossing.start()
    staying.start()

    @pl.when(links.home)
    def _():
        staying.make().wait()
        gather_tokens.start()

    weights[0].spread()
    weights[1].turn()

    @pl.when(links.away)
    def _():
        crossing.make().wait_recv()
        gather_tokens.start()

    weights[1].spread()
    weights[2].turn()
    weights[0].pass_on()
    gather_tokens.pass_on()
    weights[1].pass_on()
    weights[0].finish()
    gather_tokens.finish()
    weights[1].finish()
    weights[2].settle_unit()
    links.leave()


def gather_first(dp_count, tensor_count, tokens, first, output, gate):
    def full(shard, times):
        return jax.ShapeDtypeStruct((shard.shape[0] * times, shard.shape[1]), shard.dtype)

    return pl.pallas_call(
        functools.partial(gather_first_kernel, dp_count, tensor_count),
        out_shape=[
            full(tokens, tensor_count),
            full(first, dp_count),
            full(output, dp_count),
            full(gate, 2),
        ],
        in_specs=in_vmem(4),
        out_specs=anywhere(4),
        scratch_shapes=semaphores(64, 8),
        compiler_params=link_params(0),
        name="gather_first",
    )(tokens, first, output, gate)


def middle_kernel(
    dp_count,
    tensor_count,
    moved_units,
    partial,
    tokens_all,
    cot,
    cot_low,
    up,
    up_turned,
    up_crossed,
    down,
    gate_unit,
    *rest,
):
    gate_units, rest = rest[:moved_units], rest[moved_units:]
    gain_ref, residual_ref, normed_all, cot_all, up_full, down_full, gate_full = rest[:7]
    gate_values, up_values, hidden = rest[7:10]
    own, normed, mine, others, sums, arrivals = rest[10:16]
    links = Links(dp_count, tensor_count, *rest[16:])
    rows = cot.shape[0]
    scatter = RowScatter(links, partial, mine, others, sums, arrivals, rows)
    gather_normed = RowGather(links, normed_all, rows)
    gather_cot = RowGather(links, cot_all, rows, links.away)
    gate_gather = WeightGather(links, up, gate_full)
    up_gather = WeightGather(links, up, up_full)
    down_gather = WeightGather(links, down, down_full)
    shard = up.shape[0]
    here = up_full.at[pl.ds(links.dp_index * shard, shard)]
    beside = up_full.at[pl.ds((2 * links.p + 1 - links.c) * shard, shard)]
    quarter = pl.ds(links.quarter * rows, rows)
    placements = [
        links.keep(up, here, links.home),
        links.keep(up_turned, beside, links.home),
        links.keep(up_turned, here, links.away),
        links.keep(up_crossed, beside, links.away),
    ]
    gate_places = [links.chip(step) * 2 * shard for step in (0,) + links.chip_steps()]
    gate_placements = [
        links.keep(unit, gate_full.at[pl.ds(at, unit.shape[0])])
        for at, unit in zip(gate_places, (gate_unit,) + tuple(gate_units))
    ]
    cot_crossing = links.copy(cot, cot_all.at[pl.ds(links.tensor_index * rows, rows)], links.cross_peer(), links.away)
    cot_placements = [
        links.keep(
            cot_low.at[step - 1],
            cot_all.at[pl.ds((links.c * links.low + (links.tl + links.low - step) % links.low) * rows, rows)],
            links.home,
        )
        for step in range(1, links.low)
    ]
    cot_staying = links.keep(cot, cot_all.at[quarter], links.home)
    load = links.keep(tokens_all.at[quarter], own)
    store = links.keep(normed, normed_all.at[quarter])
    links.drop([up_gather.first, up_gather.second, gate_gather.first, gate_gather.second] + gate_gather.direct)
    links.enter()
    scatter.start()
    load.start()
    for item in gate_placements + placements:
        item.start()
    for item in gate_placements:
        item.done()
    for item in gate_gather.forward:
        item.start()
    for item in placements:
        item.done()
    scatter.send_sums()
    up_gather.spread_unit()
    down_gather.turn()
    cot_staying.start()
    for item in cot_placements:
        item.start()
    load.done()

    def use(span, total):
        residual = own[span].astype(jnp.float32) + total
        residual_ref[span] = residual
        root = lax.rsqrt(jnp.mean(residual * residual, axis=-1, keepdims=True) + epsilon)
        normed[span] = (residual * root * gain_ref[...]).astype(jnp.bfloat16)

    scatter.collect(use)
    store.start()
    store.done()
    gather_normed.start()
    down_gather.settle_unit()
    cot_crossing.start()
    up_gather.pass_on()
    down_gather.spread_unit()
    gate_gather.finish()
    gather_normed.pass_on()
    cot_staying.done()
    for item in cot_placements:
        item.done()
    cot_crossing.arrived()
    gather_cot.start()
    up_gather.finish()
    gather_normed.finish()
    product(normed_all, gate_full, gate_values, 1, 0, 512, 1024)
    down_gather.pass_on()
    gather_cot.pass_on()

    def finish(up, gate_ref, up_ref, hidden_ref):
        gate = gate_ref[...]
        up_ref[...] = up
        hidden_ref[...] = (gate * jax.nn.sigmoid(gate) * up).astype(jnp.bfloat16)

    product(normed_all, up_full, up_values, 1, 0, 256, 1024, finish, (gate_values,), (hidden,))
    down_gather.finish()
    gather_cot.finish()
    links.leave()


def middle(
    dp_count, tensor_count, partial, tokens_all, cot, cot_low, up, up_turned, up_crossed, down, gate_unit, gate_units, gain
):
    rows, width = cot.shape
    low = tensor_count // 2

    def full(shard, times):
        return jax.ShapeDtypeStruct((shard.shape[0] * times, shard.shape[1]), shard.dtype)

    return pl.pallas_call(
        functools.partial(middle_kernel, dp_count, tensor_count, len(gate_units)),
        out_shape=[
            jax.ShapeDtypeStruct((rows, width), jnp.float32),
            full(cot, tensor_count),
            full(cot, tensor_count),
            full(up, dp_count),
            full(down, dp_count),
            full(gate_unit, dp_count // 2),
            jax.ShapeDtypeStruct((rows * tensor_count, up.shape[1]), jnp.float32),
            jax.ShapeDtypeStruct((rows * tensor_count, up.shape[1]), jnp.float32),
            jax.ShapeDtypeStruct((rows * tensor_count, up.shape[1]), jnp.bfloat16),
        ],
        in_specs=anywhere(2) + in_vmem(len(gate_units) + 8),
        out_specs=in_vmem(1) + anywhere(8),
        scratch_shapes=[pltpu.VMEM((rows, width), jnp.bfloat16)] * 2
        + scatter_scratch(low, rows, width)
        + semaphores(64, 24),
        compiler_params=link_params(1),
        name="middle",
    )(partial, tokens_all, cot, cot_low, up, up_turned, up_crossed, down, gate_unit, *gate_units, gain)


def turn_back_kernel(
    dp_count,
    tensor_count,
    partial,
    cot_all,
    normed_ffn,
    gate_signal,
    up_signal,
    hidden,
    down_full,
    residual_ref,
    gain_ref,
    grad_residual_ref,
    gain_part_ref,
    down_ref,
    gate_ref,
    gate_turning,
    grad_rows,
    down_in,
    gate_in,
    grad_down,
    grad_gate,
    grad_up,
    down_part,
    pair_own,
    pair_low,
    own,
    low_grad,
    turned,
    added,
    turning,
    gate_added,
    stage,
    total_ref,
    mine,
    others,
    sums,
    arrivals,
    *sems,
):
    links = Links(dp_count, tensor_count, *sems)
    rows = residual_ref.shape[0]
    down = WeightScatter(links, grad_down, down_ref, down_in, turned, added, turning, stage)
    gate = WeightScatter(links, grad_gate, gate_ref, gate_in, turned, gate_added, gate_turning, stage)
    down.total = gate.total = total_ref
    links.drop([gate.first, gate.second])
    low = links.low
    half = low * residual_ref.shape[0]
    swap_layer = links.copy(down_part.at[pl.ds((1 - links.c) * half, half)], others, links.core_peer())
    load_layer = links.keep(down_part.at[pl.ds(links.c * half, half)], mine)
    keep_own = links.keep(low_grad, pair_own)
    keep_low = [links.keep(sums.at[step - 1], pair_low.at[step - 1]) for step in range(1, low)]
    scatter = RowScatter(links, partial, mine, others, sums, arrivals, rows)
    gather = RowGather(links, grad_rows, rows)
    quarter = pl.ds(links.quarter * rows, rows)
    load = links.keep(cot_all.at[quarter], own)
    store = links.keep(low_grad, grad_rows.at[quarter])
    links.enter()
    scatter.start()
    load.start()
    unit = 2 * down.rows

    def down_unit(step):
        at = pl.multiple_of(links.chip(step) * unit, 128)
        product(cot_all.at[:, pl.ds(at, unit)], hidden, grad_down.at[pl.ds(at, unit)], 0, 0, unit, 1024)

    if down.both and unit % 128 == 0:
        down_unit(3)
        down.start("before")
        scatter.send_sums()
        down_unit(1)
        down_unit(2)
        down.start_direct()
        down_unit(0)
    else:
        product(cot_all, hidden, grad_down, 0, 0, 512, 1024)
        down.start("before")
        scatter.send_sums()
    load.done()
    down.add_before()
    product(normed_ffn, gate_signal, grad_gate, 0, 0, 512, 1024)
    gate.start("before")
    gain_part_ref[...] = jnp.zeros_like(gain_part_ref)

    def use(span, grad_normed):
        residual = residual_ref[span]
        root = lax.rsqrt(jnp.mean(residual * residual, axis=-1, keepdims=True) + epsilon)
        unit = residual * root
        gain_part_ref[...] += jnp.sum(grad_normed * unit, axis=0, keepdims=True)
        scaled = grad_normed * gain_ref[...]
        grad = own[span].astype(jnp.float32) + root * (
            scaled - unit * jnp.mean(scaled * unit, axis=-1, keepdims=True)
        )
        grad_residual_ref[span] = grad
        low_grad[span] = grad.astype(jnp.bfloat16)

    scatter.collect(use)
    store.start()
    store.done()
    gather.start()
    down.arrived("direct")
    gate.start_direct()
    down.arrived("summed")
    down.turn()
    gate.add_before()
    product(normed_ffn, up_signal, grad_up, 0, 0, 512, 1024)
    gather.pass_on()
    product(hidden, down_full, down_part, 1, 1, 512, 1024)
    gather.to_core.arrived()
    swap_layer.start()
    load_layer.start()
    gate.arrived("direct")
    gate.arrived("summed")
    gate.reduce()
    for item in scatter.sends:
        item.sent()
    links.drop(scatter.sends)
    load_layer.done()
    swap_layer.arrived()
    for step in range(low):
        base = ((links.tl + step) % low) * rows

        @pl.loop(0, rows // CHUNK)
        def _(i, base=base, step=step):
            at = pl.multiple_of(i * CHUNK, CHUNK)
            span = pl.ds(pl.multiple_of(base + at, CHUNK), CHUNK)
            total = (mine[span].astype(jnp.float32) + others[span].astype(jnp.float32)).astype(jnp.bfloat16)
            if step:
                sums[step - 1, pl.ds(at, CHUNK)] = total
            else:
                low_grad[pl.ds(at, CHUNK)] = total

    keep_own.start()
    for item in keep_low:
        item.start()
    down.finish()
    gather.finish_onward()
    keep_own.done()
    for item in keep_low:
        item.done()
    links.leave()


def turn_back(
    dp_count,
    tensor_count,
    partial,
    cot_all,
    normed_ffn,
    gate_signal,
    up_signal,
    hidden,
    down_full,
    residual,
    gain,
):
    rows, width = residual.shape
    low, chips = tensor_count // 2, dp_count // 2
    grad = jax.ShapeDtypeStruct((width, hidden.shape[1]), jnp.bfloat16)
    block, columns = scatter_shapes(chips, grad)
    return pl.pallas_call(
        functools.partial(turn_back_kernel, dp_count, tensor_count),
        out_shape=[
            jax.ShapeDtypeStruct((rows, width), jnp.float32),
            jax.ShapeDtypeStruct((1, width), jnp.float32),
            jax.ShapeDtypeStruct((block, columns), jnp.float32),
            jax.ShapeDtypeStruct((block, columns), jnp.float32),
            jax.ShapeDtypeStruct((2, block, columns), jnp.bfloat16),
            jax.ShapeDtypeStruct((rows * tensor_count, width), jnp.bfloat16),
            inbox_shape(chips, block, columns),
            inbox_shape(chips, block, columns),
            grad,
            grad,
            grad,
            jax.ShapeDtypeStruct((rows * tensor_count, width), jnp.bfloat16),
            jax.ShapeDtypeStruct((rows, width), jnp.bfloat16),
            jax.ShapeDtypeStruct((low - 1, rows, width), jnp.bfloat16),
        ],
        in_specs=anywhere(7) + in_vmem(2),
        out_specs=in_vmem(5) + anywhere(9),
        scratch_shapes=[pltpu.VMEM((rows, width), jnp.bfloat16)] * 2
        + weight_scatter_scratch(chips, block, columns)
        + [
            pltpu.VMEM((2, block, columns), jnp.bfloat16),
            pltpu.VMEM((3, block, columns), jnp.bfloat16),
            pltpu.VMEM((block, columns) if chips != 4 else (8, 128), jnp.float32),
        ]
        + scatter_scratch(low, rows, width)
        + semaphores(64, 24),
        compiler_params=link_params(2),
        name="turn_back",
    )(partial, cot_all, normed_ffn, gate_signal, up_signal, hidden, down_full, residual, gain)


def hidden_back_kernel(
    cot_all, down_full, gate_values, up_values, gate_full, up_full, gate_signal, up_signal, partial
):
    def signals(grad_hidden, gate_ref, up_ref, gate_out, up_out):
        gate = gate_ref[...]
        sigmoid = jax.nn.sigmoid(gate)
        grad_hidden = grad_hidden * sigmoid
        gate_out[...] = (grad_hidden * up_ref[...] * (1.0 + gate * (1.0 - sigmoid))).astype(jnp.bfloat16)
        up_out[...] = (grad_hidden * gate).astype(jnp.bfloat16)

    product(
        cot_all, down_full, gate_signal, 1, 0, 512, 1024, signals, (gate_values, up_values), (up_signal,)
    )
    count, width = partial.shape
    depth = gate_full.shape[1]
    rows, columns = math.gcd(count, 512), cut(width, 1536)

    def body(gate_ref, up_ref, gate_weight, up_weight, out_ref):
        total = times(gate_ref[...], gate_weight[...], 1, 1) + times(up_ref[...], up_weight[...], 1, 1)
        out_ref[...] = total.astype(jnp.bfloat16)

    pltpu.emit_pipeline(
        body,
        grid=(width // columns, count // rows),
        in_specs=[pl.BlockSpec((rows, depth), lambda j, i: (i, 0))] * 2
        + [pl.BlockSpec((columns, depth), lambda j, i: (j, 0))] * 2,
        out_specs=[pl.BlockSpec((rows, columns), lambda j, i: (i, j))],
    )(gate_signal, up_signal, gate_full, up_full, partial)


def hidden_back(cot_all, down_full, gate_values, up_values, gate_full, up_full):
    signal = jax.ShapeDtypeStruct(gate_values.shape, jnp.bfloat16)
    flops = 6 * cot_all.size * gate_values.shape[1]
    return pl.pallas_call(
        hidden_back_kernel,
        out_shape=[signal, signal, jax.ShapeDtypeStruct(cot_all.shape, jnp.bfloat16)],
        in_specs=anywhere(6),
        out_specs=anywhere(3),
        compiler_params=pltpu.CompilerParams(vmem_limit_bytes=LINK_VMEM_LIMIT),
        cost_estimate=pl.CostEstimate(flops=flops, bytes_accessed=flops // 1000, transcendentals=0),
        name="hidden_back",
    )(cot_all, down_full, gate_values, up_values, gate_full, up_full)


def starts_of(positions, length_row):
    ends = jnp.cumsum(length_row)
    inside = positions[:, None] >= ends[None, :]
    return jnp.sum(jnp.where(inside, length_row[None, :], 0), axis=1)


def rotary_tables(positions):
    frequency = jnp.exp(
        jnp.arange(HALF, dtype=jnp.float32) * (-2.0 * math.log(rope_base) / HEAD_DIM)
    )
    angles = positions.astype(jnp.float32)[None, :] * frequency[:, None]
    return (jnp.cos(angles), jnp.sin(angles))


def per_device(
    dp_count,
    tensor_count,
    tokens,
    attention_gain,
    query_weight,
    key_weight,
    value_weight,
    output_weight,
    feedforward_gain,
    gate_weight,
    up_weight,
    down_weight,
    cotangent,
    lengths,
    storage_order,
    sequence_order,
    pad_mask,
):
    place = Placement(dp_count, tensor_count)
    count = storage_order.shape[0]
    rows = count // tensor_count
    kv_heads = key_weight.shape[1] // HEAD_DIM
    heads = query_weight.shape[1] // HEAD_DIM
    group = heads // kv_heads
    head_columns = (heads + 2 * kv_heads) * HEAD_DIM

    hidden_units = gate_weight.shape[1]
    hidden_padded = -(-hidden_units // 128) * 128
    output_padded = -(-heads * HEAD_DIM // 128) * 128
    first_padded = -(-(head_columns + 2) // 128) * 128

    def wide(array, columns):
        return jnp.pad(array, ((0, 0), (0, columns - array.shape[1])))

    gate_shard = wide(gate_weight, hidden_padded)
    up_shard = wide(up_weight, hidden_padded)
    down_shard = wide(down_weight.T, hidden_padded)
    tokens_all, first_weight, output_turned, gate_unit = gather_first(
        dp_count,
        tensor_count,
        tokens,
        wide(
            jnp.concatenate(
                [query_weight, key_weight, value_weight, attention_gain[:, None], feedforward_gain[:, None]],
                axis=1,
            ),
            first_padded,
        ),
        wide(output_weight.T, output_padded),
        gate_shard,
    )
    output_turned = output_turned[:, : heads * HEAD_DIM]
    late_up = after(up_shard, tokens_all)
    up_turned = place.home_turn(late_up)
    up_crossed = place.cross(late_up)
    steps = (1, 2) if place.chips == 4 else tuple(range(1, place.chips))
    gate_units = [place.to_chip(gate_unit, step) for step in steps]
    late_cot = after(cotangent, tokens_all)
    cot_low = jnp.stack([place.home_to_low(late_cot, step) for step in range(1, place.low)])

    numbers = jnp.concatenate([storage_order, pad_mask, lengths[0]])
    numbers = jnp.where(place.home, numbers, place.to_core(numbers))
    pad_column = numbers[count : 2 * count][:, None]
    length_row = numbers[2 * count :]
    order = numbers[:count]

    places = jnp.arange(count, dtype=jnp.int32)
    starts = starts_of(places, length_row)
    cosine, sine = rotary_tables(places - starts)
    cosine_stored, sine_stored = rotary_tables(order - starts_of(order, length_row))
    to_sequence = (places[:, None] == order[None, :]).astype(jnp.bfloat16)
    to_storage = (order[:, None] == places[None, :]).astype(jnp.bfloat16)
    first_blocks = starts[:: math.gcd(count, QUERY_BLOCK)] // KEY_BLOCK
    start_row = starts[None, :]

    attention_scale = first_weight[:, head_columns].astype(jnp.float32)[None, :]
    feedforward_scale = first_weight[:, head_columns + 1].astype(jnp.float32)[None, :]
    normed, heads_stored, token_roots = project(
        tokens_all,
        attention_scale,
        first_weight,
        cosine_stored,
        sine_stored,
        heads + kv_heads,
        head_columns,
    )
    heads_all = contract(to_sequence, heads_stored, 1, 0, jnp.bfloat16)
    attended, log_totals = attend(first_blocks, heads_all, start_row, pad_column, kv_heads, group)
    attended_stored = contract(to_storage, attended, 1, 0, jnp.bfloat16)

    residual, normed_ffn, cot_all, up_full, down_turned, gate_full, gate_values, up_values, hidden = middle(
        dp_count,
        tensor_count,
        contract(attended_stored, output_turned, 1, 1, jnp.bfloat16),
        tokens_all,
        cotangent,
        cot_low,
        up_shard,
        up_turned,
        up_crossed,
        down_shard,
        gate_unit,
        gate_units,
        feedforward_scale,
    )

    def leave(own):
        arrived = place.cross(own.astype(jnp.bfloat16)).astype(jnp.float32)
        return jnp.where(place.home, own, arrived)

    grad_gate, grad_up, grad_part = hidden_back(
        cot_all, down_turned, gate_values, up_values, gate_full, up_full
    )
    turned_back = turn_back(
        dp_count,
        tensor_count,
        grad_part,
        cot_all,
        normed_ffn,
        grad_gate,
        grad_up,
        hidden,
        down_turned,
        residual,
        feedforward_scale,
    )
    grad_residual, feedforward_part, down_grad, gate_grad, gate_turning, grad_rows = turned_back[:6]
    up_part, pair_own, pair_low = turned_back[10], turned_back[12], turned_back[13]
    up_half, up_moves = place.plane_moves(up_part)
    gate_arrived = place.away_to_home(gate_turning)

    layer_moves = [place.to_low(pair_low[step - 1], step) for step in range(1, place.low)]
    grad_attended = contract(grad_rows, output_turned, 1, 0, jnp.bfloat16)
    grad_attended = contract(to_sequence, grad_attended, 1, 0, jnp.bfloat16)
    grad_query, grad_rest = attend_back(
        first_blocks,
        heads_all,
        start_row,
        pad_column,
        log_totals,
        attended,
        grad_attended,
        cosine,
        sine,
        kv_heads,
        group,
    )
    layer_own = after(residual, grad_query) + pair_own.astype(jnp.float32)
    for arrived in layer_moves:
        layer_own = layer_own + arrived.astype(jnp.float32)
    spare = jnp.zeros((count, first_padded - head_columns), jnp.bfloat16)
    sequence_grads, _, *up_moves = lax.optimization_barrier(
        (jnp.concatenate([grad_query, grad_rest, spare], axis=1), layer_own, *up_moves)
    )
    up_mine, up_first, up_second = place.plane_sum(up_half, up_moves)
    grad_heads = contract(to_storage, sequence_grads, 1, 0, jnp.bfloat16)
    grad_normed_part = contract(grad_heads, first_weight, 1, 1)
    tokens_wide = tokens_all.astype(jnp.float32)
    attention_part = jnp.sum(grad_normed_part * (tokens_wide * token_roots), axis=0)
    layer_output = leave(layer_own)
    gate_arrived = after(gate_arrived, grad_query).astype(jnp.float32)
    gate_other = place.home_to_core((gate_turning[0].astype(jnp.float32) + gate_arrived[1]).astype(jnp.bfloat16))
    gate_grad = jnp.where(place.home, gate_grad + gate_arrived[0], gate_other.astype(jnp.float32))
    gain_parts = jnp.stack([attention_part, feedforward_part[0]], axis=1)
    before = head_columns - (first_padded - 128)
    gain_parts = jnp.pad(gain_parts, ((0, 0), (before, 126 - before)))
    input_grad, up_grad, output_grad, first_grad = tail(
        dp_count,
        tensor_count,
        head_columns,
        after(grad_normed_part.astype(jnp.bfloat16), layer_own),
        tokens_all,
        grad_rows,
        wide(attended_stored, output_padded),
        normed,
        grad_heads,
        gain_parts,
        up_mine,
        up_first,
        up_second,
        grad_residual,
        attention_scale,
    )
    query_columns = heads * HEAD_DIM
    key_columns = kv_heads * HEAD_DIM
    return (
        layer_output,
        input_grad,
        first_grad[:, head_columns],
        first_grad[:, :query_columns],
        first_grad[:, query_columns : query_columns + key_columns],
        first_grad[:, query_columns + key_columns : head_columns],
        output_grad[:, :query_columns].T,
        first_grad[:, head_columns + 1],
        gate_grad[:, :hidden_units],
        up_grad[:, :hidden_units],
        down_grad[:, :hidden_units].T,
    )


def solution(mesh):
    placed = (
        P(("dp", "tensor"), None),
        P("dp"),
        P("dp", "tensor"),
        P("dp", "tensor"),
        P("dp", "tensor"),
        P("tensor", "dp"),
        P("dp"),
        P("dp", "tensor"),
        P("dp", "tensor"),
        P("tensor", "dp"),
        P(("dp", "tensor"), None),
        P("dp", None),
        P("dp"),
        P("dp"),
        P("dp"),
    )
    return jax.shard_map(
        functools.partial(per_device, mesh.shape["dp"], mesh.shape["tensor"]),
        mesh=mesh,
        in_specs=placed,
        out_specs=(
            P(("dp", "tensor"), None),
            P(("dp", "tensor"), None),
            P("dp"),
            P("dp", "tensor"),
            P("dp", "tensor"),
            P("dp", "tensor"),
            P("tensor", "dp"),
            P("dp"),
            P("dp", "tensor"),
            P("dp", "tensor"),
            P("tensor", "dp"),
        ),
        check_vma=False,
    )
```
